32 devices in a mesh: grp: 2 (over x), blk: 16 (over z, y, core).
Axes of the slice: x: 2, y: 2, z: 4, core: 2. Of those that a mesh axis runs over, the one named last changes fastest.
Arguments:
- embed: bfloat16 [1024, 256], P(('grp', 'blk')), parts along dimension 0, may hold values from -6 to 6
- pair_weight: bfloat16 [256, 64], replicated, may hold values from -0.375 to 0.375
- conv_kernel: bfloat16 [64, 9, 64], replicated, may hold values from -0.25 to 0.25
- dilations: int32 [4], replicated, may hold values from 0 to 3, each once
- tile_order: int32 [32, 2], P(('grp', 'blk')), parts along dimension 0, may hold values from 0 to 1, each once within a row
- cotangent: bfloat16 [32, 2, 64, 1024], P(('grp', 'blk')), parts along dimension 0, may hold values from -6 to 6
Outputs:
- pair_out: bfloat16 [32, 2, 64, 1024], P(('grp', 'blk')), parts along dimension 0
- grad_embed: float32 [1024, 256], P(('grp', 'blk')), parts along dimension 0
- grad_weight: float32 [512, 64], P('grp'), parts along dimension 0
- grad_kernel: float32 [128, 9, 64], P('grp'), parts along dimension 0
The draws below stay inside these ranges and needn't reach their ends.
There are 2 independent parts, one for each index of `grp`. The reference program is written for one: setup_inputs(seed, part) draws one part's arguments, and reference() takes and returns one part's arrays. A program takes and returns all parts, laid end to end along the dimension named above; an argument that names none is the same for every part. Nothing has to cross between parts.
Inputs may be any that keep to these rules, and one draw needn't show every extreme that they name: A permutation of 0 to 3: channel group g uses dilation 2 ** dilations[g]. Each row is a permutation of 0 and 1: slot t of block b holds the tile at diagonal offset tile_order[b, t].
All inputs are finite; a program needn't handle non-finite values.
Results may differ from the reference program's by a relative error of at most 0.003.
The reference program's roundings to bfloat16 on the way count: a program that leaves them out, or rounds other values in their place, can miss the bound.
Values may be sent and summed in bfloat16 or wider, within the bound.
No kernel may reach another device: no remote copies, remote signals or barrier semaphores. Data moves between devices by JAX's collectives and lax.ppermute only.
A program may use at most 128 MiB of HBM per device.

```python
import jax
import jax.numpy as jnp
from jax import lax

CH = 256
PAIR_CH = 64
GROUPS = 4
TILE = 32
HALO = 8
BLOCKS = 16
BINS = 512


def block_scale(rng, dims, cuts, least, top_value):
    def one(position, parts):
        draws = jax.random.uniform(jax.random.fold_in(jax.random.fold_in(rng, 6), position), (parts,), jnp.float32, least / len(cuts), top_value / len(cuts))
        return jnp.repeat(jnp.exp(draws), dims[position] // parts).reshape((-1,) + (1,) * (len(dims) - position - 1))

    loudness = one(*cuts[0])
    for cut in cuts[1:]:
        loudness = loudness * one(*cut)
    return loudness


def normal_values(key, shape, scale, reach, cuts=(), kind=jnp.bfloat16):
    drawn = scale * jax.random.normal(key, shape, jnp.float32)
    if cuts:
        drawn = drawn * block_scale(key, shape, cuts, -0.22, 0.18)
    return jnp.clip(drawn, -reach, reach).astype(kind)


def setup_inputs(seed: int = 0, part: int = 0) -> dict:
    key_list = jax.random.split(jax.random.key(seed), 7)
    part_keys = jax.random.split(jax.random.fold_in(key_list[6], part), 7)
    embed = normal_values(part_keys[0], (BINS, CH), 1.0, 6.0, ((0, 16),))
    pair_weight = normal_values(key_list[1], (CH, PAIR_CH), CH ** -0.5, 0.375)
    conv_kernel = normal_values(key_list[2], (PAIR_CH, 9, PAIR_CH), (9 * PAIR_CH) ** -0.5, 0.25)
    dilations = jax.random.permutation(key_list[3], GROUPS).astype(jnp.int32)
    tile_order = jax.vmap(lambda own: jax.random.permutation(own, 2))(jax.random.split(part_keys[4], BLOCKS)).reshape((BLOCKS, 2)).astype(jnp.int32)
    cotangent = normal_values(part_keys[5], (BLOCKS, 2, PAIR_CH, TILE * TILE), 1.0, 6.0, ((0, 16),))
    return {"embed": embed, "pair_weight": pair_weight, "conv_kernel": conv_kernel, "dilations": dilations, "tile_order": tile_order, "cotangent": cotangent}


HIGHEST = lax.Precision.HIGHEST


def scale_rows(embed_rows, pair_weight):
    widened = embed_rows.astype(jnp.float32)[None, :, :] * pair_weight.astype(jnp.float32).T[:, None, :]
    return widened.astype(jnp.bfloat16)


def pair_block(scaled, columns):
    product = jnp.einsum("krc,sc->krs", scaled.astype(jnp.float32), columns.astype(jnp.float32), precision=HIGHEST)
    return product.astype(jnp.bfloat16)


def assemble(corner_before, rows_before, tile_zero, tile_one, rows_after, corner_after):
    channels = tile_zero.shape[0]
    tile_width = tile_zero.shape[1]
    margin = corner_before.shape[1]
    upper_rows = jnp.concatenate([corner_before, rows_before, jnp.zeros((channels, margin, tile_width + margin), tile_zero.dtype)], 2)
    middle = jnp.concatenate([jnp.transpose(rows_before, (0, 2, 1)), tile_zero, tile_one, jnp.zeros((channels, tile_width, margin), tile_zero.dtype)], 2)
    lower_rows = jnp.concatenate([jnp.zeros((channels, margin, margin), tile_zero.dtype), jnp.transpose(tile_one[:, :, :margin], (0, 2, 1)), rows_after, corner_after], 2)
    return jnp.concatenate([upper_rows, middle, lower_rows], 1)


def tap_starts(dilations, groups, margin):
    starts = []
    for u in (-1, 0, 1):
        for v in (-1, 0, 1):
            per_group = []
            for g in range(groups):
                spacing = jnp.left_shift(jnp.int32(1), dilations[g]).astype(jnp.int32)
                per_group.append(((margin + u * spacing).astype(jnp.int32), (margin + v * spacing).astype(jnp.int32)))
            starts.append(per_group)
    return starts


def tap_stack(extended, dilations, groups, margin, tile_width):
    group_width = extended.shape[0] // groups
    tap_pieces = []
    for per_group in tap_starts(dilations, groups, margin):
        group_slices = []
        for g in range(groups):
            row_start, col_start = per_group[g]
            group_slices.append(lax.dynamic_slice(extended, (jnp.int32(g * group_width), row_start, col_start), (group_width, tile_width, 2 * tile_width)))
        tap_pieces.append(jnp.concatenate(group_slices, 0))
    return jnp.stack(tap_pieces, 0).reshape(9 * extended.shape[0], 2 * tile_width * tile_width)


def conv_adjoint(grad_flat, conv_kernel, dilations, groups, margin, tile_width):
    channels = conv_kernel.shape[0]
    group_width = channels // groups
    totals = [jnp.zeros((group_width, tile_width + 2 * margin, 2 * tile_width + 2 * margin), jnp.float32) for g in range(groups)]
    for t, per_group in enumerate(tap_starts(dilations, groups, margin)):
        spread = lax.dot_general(conv_kernel[:, t, :], grad_flat, (((0,), (0,)), ((), ())), preferred_element_type=jnp.float32)
        spread = spread.reshape(channels, tile_width, 2 * tile_width)
        for g in range(groups):
            row_start, col_start = per_group[g]
            earlier = lax.dynamic_slice(totals[g], (jnp.int32(0), row_start, col_start), (group_width, tile_width, 2 * tile_width))
            totals[g] = lax.dynamic_update_slice(totals[g], earlier + spread[g * group_width:(g + 1) * group_width], (jnp.int32(0), row_start, col_start))
    return jnp.concatenate(totals, 0)


def split_adjoint(grad_ext, margin, tile_width):
    channels = grad_ext.shape[0]
    upper_rows = grad_ext[:, :margin]
    middle = grad_ext[:, margin:margin + tile_width]
    lower_rows = grad_ext[:, margin + tile_width:]
    filler = jnp.zeros((channels, margin, tile_width - margin), jnp.float32)
    send_up = jnp.stack([jnp.concatenate([filler, upper_rows[:, :, :margin]], 2),
                         upper_rows[:, :, margin:margin + tile_width] + jnp.transpose(middle[:, :, :margin], (0, 2, 1))], 0)
    send_down = jnp.stack([lower_rows[:, :, margin + tile_width:margin + 2 * tile_width],
                           jnp.concatenate([lower_rows[:, :, margin + 2 * tile_width:], filler], 2)], 0)
    own_one = middle[:, :, margin + tile_width:margin + 2 * tile_width]
    own_one = own_one.at[:, :, :margin].add(jnp.transpose(lower_rows[:, :, margin:margin + tile_width], (0, 2, 1)))
    own_grad = jnp.stack([middle[:, :, margin:margin + tile_width], own_one], 0)
    return send_up, send_down, own_grad


def reference(embed, pair_weight, conv_kernel, dilations, tile_order, cotangent):
    margin = HALO
    cotangent = cotangent.reshape(BLOCKS, 2, PAIR_CH, TILE, TILE)
    blocks = embed.reshape(BLOCKS, TILE, CH)
    next_blocks = jnp.concatenate([blocks[1:], jnp.zeros((1, TILE, CH), embed.dtype)], 0)

    def make_tiles(inputs):
        block_rows, next_rows = inputs
        scaled = scale_rows(block_rows, pair_weight)
        return scaled, jnp.stack([pair_block(scaled, block_rows), pair_block(scaled, next_rows)], 0)

    scaled_all, pair_tiles = lax.map(make_tiles, (blocks, next_blocks))
    hidden_map = jnp.maximum(pair_tiles, 0)
    zero_rim = jnp.zeros((1, 2, PAIR_CH, margin, TILE), jnp.bfloat16)
    prev_bottom = jnp.concatenate([zero_rim, hidden_map[:-1, :, :, -margin:, :]], 0)
    next_top = jnp.concatenate([hidden_map[1:, :, :, :margin, :], zero_rim], 0)
    has_next = jnp.arange(BLOCKS) < BLOCKS - 1
    first_slot = tile_order[:, 0][:, None, None, None]
    second_slot = tile_order[:, 1][:, None, None, None]
    cot_zero = jnp.where(first_slot == 0, cotangent[:, 0], cotangent[:, 1])
    cot_one = jnp.where(first_slot == 1, cotangent[:, 0], cotangent[:, 1])
    cot_one = jnp.where(has_next[:, None, None, None], cot_one, jnp.zeros_like(cot_one))
    grad_out = jnp.stack([cot_zero, cot_one], 1)

    def conv_step(inputs):
        before, hidden, after, grads = inputs
        extended = assemble(before[0][:, :, -margin:], before[1], hidden[0], hidden[1], after[0], after[1][:, :, :margin])
        columns = tap_stack(extended, dilations, GROUPS, margin, TILE)
        response = jnp.dot(conv_kernel.reshape(PAIR_CH, 9 * PAIR_CH), columns, preferred_element_type=jnp.float32)
        grad_flat = jnp.concatenate([grads[0], grads[1]], 2).reshape(PAIR_CH, 2 * TILE * TILE)
        kernel_part = lax.dot_general(grad_flat, columns, (((1,), (1,)), ((), ())), preferred_element_type=jnp.float32)
        send_up, send_down, own_grad = split_adjoint(conv_adjoint(grad_flat, conv_kernel, dilations, GROUPS, margin, TILE), margin, TILE)
        return response.reshape(PAIR_CH, TILE, 2 * TILE), kernel_part, send_up, send_down, own_grad

    responses, kernel_parts, sends_up, sends_down, own_grads = lax.map(conv_step, (prev_bottom, hidden_map, next_top, grad_out))
    response_tiles = jnp.stack([responses[..., :TILE], responses[..., TILE:]], 1)
    tile_mask = jnp.stack([jnp.ones((BLOCKS,), jnp.float32), has_next.astype(jnp.float32)], 1)[:, :, None, None, None]
    out_tiles = (tile_mask * (pair_tiles.astype(jnp.float32) + response_tiles)).astype(jnp.bfloat16)
    pair_out = jnp.stack([jnp.where(first_slot == 0, out_tiles[:, 0], out_tiles[:, 1]),
                          jnp.where(second_slot == 0, out_tiles[:, 0], out_tiles[:, 1])], 1)
    pair_out = pair_out.reshape(BLOCKS, 2, PAIR_CH, TILE * TILE)
    grad_kernel = jnp.sum(kernel_parts, 0).reshape(PAIR_CH, 9, PAIR_CH)
    zero_send = jnp.zeros((1, 2, PAIR_CH, margin, TILE), jnp.float32)
    grad_hidden = own_grads.at[:, :, :, :margin, :].add(jnp.concatenate([zero_send, sends_down[:-1]], 0))
    grad_hidden = grad_hidden.at[:, :, :, -margin:, :].add(jnp.concatenate([sends_up[1:], zero_send], 0))
    grad_pair = (grad_out.astype(jnp.float32) + jnp.where(pair_tiles > 0, grad_hidden, 0.0)).astype(jnp.bfloat16)

    def pair_backward(inputs):
        grads, block_rows, next_rows, scaled = inputs
        grad_scaled = jnp.einsum("krs,sc->krc", grads[0].astype(jnp.float32), block_rows.astype(jnp.float32), precision=HIGHEST)
        grad_scaled = grad_scaled + jnp.einsum("krs,sc->krc", grads[1].astype(jnp.float32), next_rows.astype(jnp.float32), precision=HIGHEST)
        local_grad = jnp.sum(grad_scaled * pair_weight.astype(jnp.float32).T[:, None, :], 0)
        weight_part = jnp.sum(grad_scaled * block_rows.astype(jnp.float32)[None], 1)
        near_term = jnp.einsum("krs,krc->sc", grads[0].astype(jnp.float32), scaled.astype(jnp.float32), precision=HIGHEST)
        far_term = jnp.einsum("krs,krc->sc", grads[1].astype(jnp.float32), scaled.astype(jnp.float32), precision=HIGHEST)
        return local_grad + near_term, far_term, weight_part

    near_terms, far_terms, weight_parts = lax.map(pair_backward, (grad_pair, blocks, next_blocks, scaled_all))
    carried = jnp.concatenate([jnp.zeros((1, TILE, CH), jnp.float32), far_terms[:-1]], 0)
    grad_embed = (near_terms + carried).reshape(BINS, CH)
    grad_weight = jnp.sum(weight_parts, 0).T
    return pair_out, grad_embed, grad_weight, grad_kernel
```

```python
import jax
import jax.numpy as jnp
from jax import lax
from jax.sharding import PartitionSpec as P

GROUPS = 4
HALO = 8


def shifted(shard, axis, by):
    length = lax.axis_size(axis)
    pairs = [(i, i + by) for i in range(length) if 0 <= i + by < length]
    return lax.ppermute(shard, axis, pairs)


def extended_2(cells, sides, width):
    for axis, dim in sides:
        count = lax.axis_size(axis)
        ends = count - 1
        head = lax.slice_in_dim(cells, 0, width, axis=dim)
        tail = lax.slice_in_dim(cells, cells.shape[dim] - width, cells.shape[dim], axis=dim)
        cells = jnp.concatenate(
            [
                lax.ppermute(tail, axis, [(i, (i + 1) % count) for i in range(ends)]),
                cells,
                lax.ppermute(head, axis, [((i + 1) % count, i) for i in range(ends)]),
            ],
            axis=dim,
        )
    return cells


def scale_rows(embed_rows, pair_weight):
    widened = (
        embed_rows.astype(jnp.float32)[None, :, :] * pair_weight.astype(jnp.float32).T[:, None, :]
    )
    return widened.astype(jnp.bfloat16)


def pair_block(scaled, columns):
    return jnp.einsum("krc,sc->krs", scaled, columns, preferred_element_type=jnp.float32).astype(
        jnp.bfloat16
    )


def assemble(corner_before, rows_before, tile_zero, tile_one, rows_after, corner_after):
    channels = tile_zero.shape[0]
    tile_width = tile_zero.shape[1]
    margin = corner_before.shape[1]
    upper_rows = jnp.concatenate(
        [
            corner_before,
            rows_before,
            jnp.zeros((channels, margin, tile_width + margin), tile_zero.dtype),
        ],
        2,
    )
    middle = jnp.concatenate(
        [
            jnp.transpose(rows_before, (0, 2, 1)),
            tile_zero,
            tile_one,
            jnp.zeros((channels, tile_width, margin), tile_zero.dtype),
        ],
        2,
    )
    lower_rows = jnp.concatenate(
        [
            jnp.zeros((channels, margin, margin), tile_zero.dtype),
            jnp.transpose(tile_one[:, :, :margin], (0, 2, 1)),
            rows_after,
            corner_after,
        ],
        2,
    )
    return jnp.concatenate([upper_rows, middle, lower_rows], 1)


def tap_starts(dilations, groups, margin):
    starts = []
    for u in (-1, 0, 1):
        for v in (-1, 0, 1):
            per_group = []
            for g in range(groups):
                spacing = jnp.left_shift(jnp.int32(1), dilations[g])
                per_group.append((margin + u * spacing, margin + v * spacing))
            starts.append(per_group)
    return starts


def tap_stack(extended, dilations, groups, margin, tile_width):
    group_width = extended.shape[0] // groups
    tap_pieces = []
    for per_group in tap_starts(dilations, groups, margin):
        group_slices = []
        for g in range(groups):
            row_start, col_start = per_group[g]
            group_slices.append(
                lax.dynamic_slice(
                    extended,
                    (jnp.int32(g * group_width), row_start, col_start),
                    (group_width, tile_width, 2 * tile_width),
                )
            )
        tap_pieces.append(jnp.concatenate(group_slices, 0))
    return jnp.stack(tap_pieces, 0).reshape(9 * extended.shape[0], 2 * tile_width * tile_width)


def conv_adjoint(grad_flat, conv_kernel, dilations, groups, margin, tile_width):
    channels = conv_kernel.shape[0]
    group_width = channels // groups
    totals = [
        jnp.zeros((group_width, tile_width + 2 * margin, 2 * tile_width + 2 * margin), jnp.float32)
        for g in range(groups)
    ]
    for t, per_group in enumerate(tap_starts(dilations, groups, margin)):
        spread = lax.dot_general(
            conv_kernel[:, t, :],
            grad_flat,
            (((0,), (0,)), ((), ())),
            preferred_element_type=jnp.float32,
        )
        spread = spread.reshape(channels, tile_width, 2 * tile_width)
        for g in range(groups):
            row_start, col_start = per_group[g]
            earlier = lax.dynamic_slice(
                totals[g],
                (jnp.int32(0), row_start, col_start),
                (group_width, tile_width, 2 * tile_width),
            )
            totals[g] = lax.dynamic_update_slice(
                totals[g],
                earlier + spread[g * group_width : (g + 1) * group_width],
                (jnp.int32(0), row_start, col_start),
            )
    return jnp.concatenate(totals, 0)


def split_adjoint(grad_ext, margin, tile_width):
    channels = grad_ext.shape[0]
    upper_rows = grad_ext[:, :margin]
    middle = grad_ext[:, margin : margin + tile_width]
    lower_rows = grad_ext[:, margin + tile_width :]
    filler = jnp.zeros((channels, margin, tile_width - margin), jnp.float32)
    send_up = jnp.stack(
        [
            jnp.concatenate([filler, upper_rows[:, :, :margin]], 2),
            upper_rows[:, :, margin : margin + tile_width]
            + jnp.transpose(middle[:, :, :margin], (0, 2, 1)),
        ],
        0,
    )
    send_down = jnp.stack(
        [
            lower_rows[:, :, margin + tile_width : margin + 2 * tile_width],
            jnp.concatenate([lower_rows[:, :, margin + 2 * tile_width :], filler], 2),
        ],
        0,
    )
    own_one = middle[:, :, margin + tile_width : margin + 2 * tile_width]
    own_one = own_one.at[:, :, :margin].add(
        jnp.transpose(lower_rows[:, :, margin : margin + tile_width], (0, 2, 1))
    )
    own_grad = jnp.stack([middle[:, :, margin : margin + tile_width], own_one], 0)
    return (send_up, send_down, own_grad)


def sum_exchange(flat, axis):
    count = lax.axis_size(axis)
    shares = flat.reshape(count, flat.size // count)
    arrived = lax.all_to_all(shares, axis, 0, 0)
    mine = jnp.sum(arrived, 0, keepdims=True)
    spread = jnp.broadcast_to(mine, shares.shape)
    return lax.all_to_all(spread, axis, 0, 0).reshape(-1)


def per_device(embed, pair_weight, conv_kernel, dilations, tile_order, cotangent):
    tile_width = embed.shape[0]
    channels = conv_kernel.shape[0]
    margin = HALO
    groups = GROUPS
    cotangent = cotangent.reshape(1, 2, channels, tile_width, tile_width)
    following = shifted(embed, "blk", -1)
    scaled = scale_rows(embed, pair_weight)
    pair_zero = pair_block(scaled, embed)
    pair_one = pair_block(scaled, following)
    hidden_zero = jnp.maximum(pair_zero, 0)
    hidden_one = jnp.maximum(pair_one, 0)
    edge_rows = jnp.concatenate(
        [
            jnp.stack([hidden_zero[:, :margin], hidden_one[:, :margin]], 0),
            jnp.stack([hidden_zero[:, -margin:], hidden_one[:, -margin:]], 0),
        ],
        2,
    )
    widened = extended_2(edge_rows, (("blk", 2),), margin)
    rims_above = widened[:, :, :margin]
    rims_below = widened[:, :, -margin:]
    corner_before = rims_above[0][:, :, -margin:]
    rows_before = rims_above[1]
    rows_after = rims_below[0]
    corner_after = rims_below[1][:, :, :margin]
    extended = assemble(
        corner_before, rows_before, hidden_zero, hidden_one, rows_after, corner_after
    )
    columns = tap_stack(extended, dilations, groups, margin, tile_width)
    response = jnp.dot(
        conv_kernel.reshape(channels, 9 * channels), columns, preferred_element_type=jnp.float32
    )
    response = response.reshape(channels, tile_width, 2 * tile_width)
    has_next = lax.axis_index("blk") < lax.axis_size("blk") - 1
    first_slot = tile_order[0, 0]
    second_slot = tile_order[0, 1]
    cot_zero = jnp.where(first_slot == 0, cotangent[0, 0], cotangent[0, 1])
    cot_one = jnp.where(
        has_next,
        jnp.where(first_slot == 1, cotangent[0, 0], cotangent[0, 1]),
        jnp.zeros_like(cotangent[0, 0]),
    )
    out_zero = (pair_zero.astype(jnp.float32) + response[:, :, :tile_width]).astype(jnp.bfloat16)
    out_one = jnp.where(
        has_next, pair_one.astype(jnp.float32) + response[:, :, tile_width:], 0.0
    ).astype(jnp.bfloat16)
    pair_out = jnp.stack(
        [
            jnp.where(first_slot == 0, out_zero, out_one),
            jnp.where(second_slot == 0, out_zero, out_one),
        ],
        0,
    )
    pair_out = pair_out.reshape(1, 2, channels, tile_width * tile_width)
    grad_flat = jnp.concatenate([cot_zero, cot_one], 2).reshape(
        channels, 2 * tile_width * tile_width
    )
    kernel_part = lax.dot_general(
        grad_flat, columns, (((1,), (1,)), ((), ())), preferred_element_type=jnp.float32
    )
    send_up, send_down, own_grad = split_adjoint(
        conv_adjoint(grad_flat, conv_kernel, dilations, groups, margin, tile_width),
        margin,
        tile_width,
    )
    upward = jnp.concatenate([send_up[1], send_up[0][:, :, -margin:]], 2)
    downward = jnp.concatenate([send_down[0], send_down[1][:, :, :margin]], 2)
    packed = jnp.concatenate([upward, downward], 1)
    received = extended_2(packed.astype(jnp.bfloat16), (("blk", 1),), margin).astype(packed.dtype)
    from_before = received[:, :margin]
    from_after = received[:, -margin:]
    tile_zero_grad = own_grad[0].at[:, :margin].add(from_before[:, :, :tile_width])
    tile_zero_grad = tile_zero_grad.at[:, -margin:, -margin:].add(from_after[:, :, tile_width:])
    tile_one_grad = own_grad[1].at[:, :margin, :margin].add(from_before[:, :, tile_width:])
    tile_one_grad = tile_one_grad.at[:, -margin:].add(from_after[:, :, :tile_width])
    grad_hidden = jnp.stack([tile_zero_grad, tile_one_grad], 0)
    grad_zero = (
        cot_zero.astype(jnp.float32) + jnp.where(pair_zero > 0, grad_hidden[0], 0.0)
    ).astype(jnp.bfloat16)
    grad_one = (cot_one.astype(jnp.float32) + jnp.where(pair_one > 0, grad_hidden[1], 0.0)).astype(
        jnp.bfloat16
    )
    grad_scaled = jnp.einsum("krs,sc->krc", grad_zero, embed, preferred_element_type=jnp.float32)
    grad_scaled = grad_scaled + jnp.einsum(
        "krs,sc->krc", grad_one, following, preferred_element_type=jnp.float32
    )
    local_grad = jnp.sum(grad_scaled * pair_weight.astype(jnp.float32).T[:, None, :], 0)
    weight_part = jnp.sum(grad_scaled * embed.astype(jnp.float32)[None], 1).T
    near_term = jnp.einsum("krs,krc->sc", grad_zero, scaled, preferred_element_type=jnp.float32)
    far_term = jnp.einsum("krs,krc->sc", grad_one, scaled, preferred_element_type=jnp.float32)
    carried = shifted(far_term.astype(jnp.bfloat16), "blk", 1).astype(far_term.dtype)
    grad_embed = local_grad + near_term + carried
    flat = jnp.concatenate([kernel_part.reshape(-1), weight_part.reshape(-1)])
    total = sum_exchange(flat, "blk")
    kernel_sum = total[: kernel_part.size]
    grad_weight = total[kernel_part.size :].reshape(weight_part.shape)
    return (pair_out, grad_embed, grad_weight, kernel_sum.reshape(channels, 9, channels))


def solution(mesh):
    placed = (
        P(("grp", "blk"), None),
        P(),
        P(),
        P(),
        P(("grp", "blk"), None),
        P(("grp", "blk"), None, None, None),
    )
    return jax.shard_map(
        per_device,
        mesh=mesh,
        in_specs=placed,
        out_specs=(
            P(("grp", "blk"), None, None, None),
            P(("grp", "blk"), None),
            P("grp", None),
            P("grp", None, None),
        ),
        check_vma=False,
    )
```

```python
import jax
import jax.numpy as jnp
import numpy as np
from jax import lax
from jax.experimental import pallas as pl
from jax.experimental.pallas import tpu as pltpu
from jax.sharding import PartitionSpec as P

GROUPS = 4
HALO = 8
TILE = 32
LANES = 128
TAPS = 9
F32 = jnp.float32
BF16 = jnp.bfloat16
NN = (((1,), (0,)), ((), ()))
NT = (((1,), (1,)), ((), ()))
TN = (((0,), (0,)), ((), ()))


def dot(a, b, dims=NN):
    return lax.dot_general(a, b, dims, preferred_element_type=F32)


def turn(x, by):
    by = by % LANES
    return x if by == 0 else pltpu.roll(x, by, 1)


def lane_ids(rows):
    return lax.broadcasted_iota(jnp.int32, (rows, LANES), 1)


def within(lane, low, high):
    return jnp.logical_and(lane >= low, lane < high)


def placing_tables():
    spread = np.zeros((2 * LANES, 4 * LANES), np.float32)
    for m in range(4):
        for s in range(TILE):
            spread[TILE * m + s, LANES * m + s] = 1
            spread[LANES + TILE * m + s, LANES * m + TILE + s] = 1
    swap = np.zeros((HALO * TILE, HALO * TILE), np.float32)
    for i in range(HALO):
        for a in range(TILE):
            swap[TILE * i + a, HALO * a + i] = 1
    edge = np.zeros((TILE * TILE, HALO * TILE), np.float32)
    for r in range(TILE):
        for s in range(HALO):
            edge[TILE * r + s, TILE * s + r] = 1
    return tuple(jnp.asarray(t, BF16) for t in (spread, swap, edge))


def has_next_flag():
    return lax.axis_index("blk") < lax.axis_size("blk") - 1


def prepare(
    order_ref, cot_ref, kern_ref, spread_ref, swap_ref, edge_ref,
    g_ref, first_ref, last_ref, tail_ref, flat_ref, both_ref,
):
    slot = order_ref[0, 0]
    keep = jnp.where(has_next_flag(), 1.0, 0.0).astype(F32)
    zero = cot_ref[slot]
    one = (cot_ref[1 - slot].astype(F32) * keep).astype(BF16)
    swap = swap_ref[...]
    tail_at = TILE * (TILE - HALO)
    y_zero = dot(zero[:, tail_at:], swap)
    y_one = dot(one[:, tail_at:], swap)
    columns = dot(zero, edge_ref[...])
    lane = lane_ids(zero.shape[0])
    own_side = within(lane, 72, 80)
    far_side = within(lane, 80, 112)
    spread = spread_ref[...]
    for j in range(8):
        at = slice(LANES * j, LANES * (j + 1))
        rows = dot(jnp.concatenate([zero[:, at], one[:, at]], 1), spread)
        for m in range(4):
            r = 4 * j + m
            row = rows[:, LANES * m : LANES * (m + 1)]
            half = LANES * (r // 16)
            side = turn(y_zero[:, half : half + LANES], 72 - 8 * (r % 16))
            whole = (row + jnp.where(own_side, side, 0.0)).astype(BF16)
            g_ref[r] = whole
            if r >= TILE - HALO:
                last_ref[r - (TILE - HALO)] = whole
            if r < HALO:
                quarter = LANES * (r // 4)
                column = turn(columns[:, quarter : quarter + LANES], 80 - TILE * (r % 4))
                first_ref[r] = (row + jnp.where(far_side, column, 0.0)).astype(BF16)
                rest = turn(y_one[:, :LANES], 72 - 8 * r)
                tail_ref[r] = jnp.where(own_side, rest, 0.0).astype(BF16)
    channels = kern_ref.shape[1]
    eye = (
        lax.broadcasted_iota(jnp.int32, (channels, channels), 0)
        == lax.broadcasted_iota(jnp.int32, (channels, channels), 1)
    )
    eye = jnp.where(eye, 1.0, 0.0).astype(BF16)
    for u in range(3):
        for v in range(3):
            t = 3 * u + v
            pair = jnp.concatenate([kern_ref[t], kern_ref[3 * v + u]], 0)
            both_ref[channels * t : channels * (t + 1), :] = dot(eye, pair, NT).astype(BF16)
    for t in range(0, TAPS - 1, 2):
        flat_ref[:, channels * t : channels * (t + 2)] = jnp.concatenate(
            [kern_ref[t].astype(F32), kern_ref[t + 1].astype(F32)], 1
        ).astype(BF16)
    flat_ref[:, channels * (TAPS - 1) : channels * TAPS] = kern_ref[TAPS - 1]


def forward(
    dil_ref, order_ref, weight_ref, own_ref, next_ref, second_ref, before_ref, g_ref, flat_ref,
    spread_ref, swap_ref,
    out_ref, part_ref, pair_ref, scaled_ref,
    map_ref, rolled_ref, rows_ref,
):
    channels = flat_ref.shape[0]
    width = channels // GROUPS
    weight = weight_ref[...].astype(F32)
    own = own_ref[...].astype(F32)
    after = next_ref[...].astype(F32)
    head = second_ref[...].astype(F32)[:HALO]
    before = before_ref[...].astype(F32)[TILE - HALO :]
    rows = jnp.concatenate([before, own, after[:HALO]], 0)
    filler = jnp.zeros((LANES - 2 * TILE - 2 * HALO, own.shape[1]), F32)
    columns = jnp.concatenate([own, after, head, filler, before], 0).astype(BF16)
    lane = lane_ids(channels)
    kept = (
        jnp.logical_or(lane < TILE, lane >= LANES - HALO),
        lane < 2 * TILE,
        within(lane, TILE, 2 * TILE + HALO),
    )
    for c in range(6):
        part = 0 if c == 0 else (2 if c == 5 else 1)
        scaled = jnp.concatenate(
            [(rows[8 * c + i : 8 * c + i + 1, :] * weight).astype(BF16) for i in range(8)], 0
        )
        if part == 1:
            scaled_ref[8 * channels * (c - 1) : 8 * channels * c, :] = scaled
        pair = dot(scaled, columns, NT).astype(BF16)
        for i in range(8):
            one = pair[channels * i : channels * (i + 1)]
            if part == 1:
                pair_ref[8 * (c - 1) + i] = one
            map_ref[8 * c + i] = jnp.where(kept[part], jnp.maximum(one.astype(F32), 0.0), 0.0)
    swap = swap_ref[...]

    def gathered(first, per, low, high, move):
        halves = []
        for half in range(2):
            total = None
            for m in range(per):
                piece = jnp.where(within(lane, low, high), map_ref[first + per * half + m], 0.0)
                piece = turn(piece, move(m))
                total = piece if total is None else total + piece
            halves.append(total.astype(BF16))
        return jnp.concatenate(halves, 1)

    above = dot(gathered(0, 4, 0, TILE, lambda m: TILE * m), swap)
    below = dot(gathered(8, 16, TILE, TILE + HALO, lambda m: HALO * m - TILE), swap, NT)
    for r in range(TILE):
        half = LANES * (r // 16)
        side = turn(above[:, half : half + LANES], LANES - HALO - HALO * (r % 16))
        map_ref[HALO + r] += jnp.where(lane >= LANES - HALO, side, 0.0)
    for i in range(HALO):
        half = LANES * (i // 4)
        side = turn(below[:, half : half + LANES], -TILE * (i % 4))
        map_ref[HALO + TILE + i] += jnp.where(lane < TILE, side, 0.0)

    spacing = [jnp.left_shift(jnp.int32(1), dil_ref[g]) for g in range(GROUPS)]

    def roll_row(i, carry):
        for g in range(GROUPS):
            at = width * g
            x = map_ref[i, at : at + width, :]
            rolled_ref[i, at : at + width, :] = pltpu.roll(x, spacing[g], 1).astype(BF16)
            rolled_ref[i, channels + at : channels + at + width, :] = x.astype(BF16)
            rolled_ref[i, 2 * channels + at : 2 * channels + at + width, :] = pltpu.roll(
                x, LANES - spacing[g], 1
            ).astype(BF16)
        return carry

    lax.fori_loop(0, TILE + 2 * HALO, roll_row, 0, unroll=2)
    part_ref[...] = jnp.zeros_like(part_ref)
    inner = jnp.where(lane < 2 * TILE, 1.0, 0.0).astype(BF16)

    def taps_of(r):
        pieces = []
        for u in range(3):
            for v in range(3):
                for g in range(GROUPS):
                    at = channels * v + width * g
                    pieces.append(rolled_ref[r + HALO + (u - 1) * spacing[g], at : at + width, :])
        return jnp.concatenate(pieces, 0)

    def conv_rows(j, carry):
        for h in range(2):
            r = 4 * j + 2 * h
            stack = jnp.concatenate([taps_of(r), taps_of(r + 1)], 1)
            response = dot(flat_ref[...], stack)
            grads = jnp.concatenate([g_ref[r] * inner, g_ref[r + 1] * inner], 1)
            part_ref[...] += dot(grads, stack, NT)
            for m in range(2):
                row = pair_ref[r + m].astype(F32) + response[:, LANES * m : LANES * (m + 1)]
                at = LANES * (2 * h + m)
                rows_ref[j, :, at : at + LANES] = row.astype(BF16)
        return carry

    lax.fori_loop(0, TILE // 4, conv_rows, 0)
    slot = order_ref[0, 0]
    keep = jnp.where(has_next_flag(), 1.0, 0.0).astype(F32)
    spread = spread_ref[...]
    for j in range(TILE // 4):
        chunk = dot(rows_ref[j], spread, NT)
        at = slice(LANES * j, LANES * (j + 1))
        out_ref[slot, :, at] = chunk[:, :LANES].astype(BF16)
        out_ref[1 - slot, :, at] = (chunk[:, LANES:] * keep).astype(BF16)


def backward(
    dil_ref, weight_ref, own_ref, next_ref, g_ref, above_ref, below_ref, tail_ref, both_ref,
    pair_ref, scaled_ref, part_ref,
    sums_ref, near_ref, far_ref,
    map_ref, spread_ref, grad_ref,
):
    channels = weight_ref.shape[0]
    width = channels // GROUPS
    lane = lane_ids(channels)
    zeros = jnp.zeros((channels, LANES), BF16)

    def masked(x, keep):
        return jnp.where(keep, x, 0.0).astype(BF16)

    upper = jnp.logical_or(lane < TILE, lane >= LANES - HALO)
    for i in range(HALO):
        map_ref[i, :channels] = masked(turn(above_ref[i].astype(F32), -TILE), upper)
        map_ref[i, channels:] = zeros
        x = below_ref[i].astype(F32)
        at = HALO + TILE + i
        map_ref[at, :channels] = masked(turn(x, TILE), within(lane, TILE, 2 * TILE + HALO))
        map_ref[at, channels:] = masked(x, within(lane, 80, 112)) + tail_ref[i]
    inner = jnp.where(lane < 2 * TILE, 1.0, 0.0).astype(BF16)
    side = jnp.where(within(lane, 72, 80), 1.0, 0.0).astype(BF16)

    def own_rows(r, carry):
        x = g_ref[r]
        map_ref[HALO + r, :channels] = x * inner
        map_ref[HALO + r, channels:] = x * side
        return carry

    lax.fori_loop(0, TILE, own_rows, 0, unroll=4)

    def spread_rows(i, carry):
        x = jnp.concatenate([map_ref[2 * i], map_ref[2 * i + 1]], 1)
        y = dot(both_ref[...], x)
        spread_ref[2 * i] = y[:, :LANES]
        spread_ref[2 * i + 1] = y[:, LANES:]
        return carry

    lax.fori_loop(0, (TILE + 2 * HALO) // 2, spread_rows, 0)
    spacing = [jnp.left_shift(jnp.int32(1), dil_ref[g]) for g in range(GROUPS)]
    second = within(lane, TILE, 2 * TILE)

    def gather_row(r, carry):
        pieces = []
        for g in range(GROUPS):
            totals = []
            for v in range(3):
                total = None
                for u in range(3):
                    at = channels * (3 * u + v) + width * g
                    piece = spread_ref[r + HALO - (u - 1) * spacing[g], at : at + width, :]
                    total = piece if total is None else total + piece
                totals.append(total)
            pieces.append(
                totals[1]
                + pltpu.roll(totals[0], LANES - spacing[g], 1)
                + pltpu.roll(totals[2], spacing[g], 1)
            )
        grad = jnp.concatenate(pieces, 0)
        grad = grad + jnp.where(second, turn(grad, -48), 0.0)
        own = g_ref[r].astype(F32)
        own = own + jnp.where(pair_ref[r].astype(F32) > 0, grad, 0.0)
        grad_ref[pl.ds(pl.multiple_of(r * channels, channels), channels), :] = jnp.where(
            lane < 2 * TILE, own, 0.0
        ).astype(BF16)
        return carry

    lax.fori_loop(0, TILE, gather_row, 0)
    weight = weight_ref[...].astype(F32)
    own = own_ref[...].astype(F32)
    columns = jnp.concatenate(
        [own_ref[...], next_ref[...], jnp.zeros((LANES - 2 * TILE, own.shape[1]), BF16)], 0
    )
    weight_part = jnp.zeros_like(weight)
    local = []
    for c in range(4):
        at = slice(8 * channels * c, 8 * channels * (c + 1))
        grad_scaled = dot(grad_ref[at, :], columns)
        for i in range(8):
            one = grad_scaled[channels * i : channels * (i + 1)]
            local.append(jnp.sum(one * weight, 0, keepdims=True))
            weight_part = weight_part + one * own[8 * c + i : 8 * c + i + 1, :]
    both = dot(grad_ref[...], scaled_ref[...], TN)
    near_ref[...] = jnp.concatenate(local, 0) + both[:TILE]
    far_ref[...] = both[TILE : 2 * TILE].astype(BF16)
    features = own.shape[1]
    sums_ref[:, :features] = weight_part
    sums_ref[:, features:] = part_ref[...]


def finish(mine_ref, other_ref, near_ref, carried_ref, weight_ref, kernel_ref, embed_ref):
    total = mine_ref[...] + other_ref[...]
    features = weight_ref.shape[1]
    channels = kernel_ref.shape[1]
    weight_ref[...] = total[:, :features]
    for t in range(TAPS):
        at = features + channels * t
        kernel_ref[t] = total[:, at : at + channels]
    embed_ref[...] = near_ref[...] + carried_ref[...].astype(F32)


def shifted(shard, axis, by):
    length = lax.axis_size(axis)
    pairs = [(i, i + by) for i in range(length) if 0 <= i + by < length]
    return lax.ppermute(shard, axis, pairs)


VMEM = pl.BlockSpec(memory_space=pltpu.VMEM)
SMEM = pl.BlockSpec(memory_space=pltpu.SMEM)


def shape(dims, kind):
    return jax.ShapeDtypeStruct(dims, kind)


def call(kernel, outs, scalars, operands, scratch=(), flops=0, moved=0):
    specs = [SMEM] * scalars + [VMEM] * (len(operands) - scalars)
    return pl.pallas_call(
        kernel,
        out_shape=outs,
        in_specs=specs,
        out_specs=[VMEM] * len(outs),
        scratch_shapes=list(scratch),
        compiler_params=pltpu.CompilerParams(vmem_limit_bytes=48 * 1024 * 1024),
        cost_estimate=pl.CostEstimate(flops=flops, bytes_accessed=moved, transcendentals=0),
    )(*operands)


def per_device(embed, pair_weight, conv_kernel, dilations, tile_order, cotangent):
    features = embed.shape[1]
    channels = conv_kernel.shape[0]
    spread, swap, edge = placing_tables()
    weight = pair_weight.T
    taps = jnp.transpose(conv_kernel, (1, 0, 2))
    cot = cotangent.reshape(2, channels, TILE * TILE)
    following = shifted(embed, "blk", -1)
    before = shifted(embed, "blk", 1)
    second = shifted(embed, "blk", -2)
    rim = shape((HALO, channels, LANES), BF16)
    body = shape((TILE, channels, LANES), BF16)
    grads, first, last, tail, flat, both = call(
        prepare,
        [
            body, rim, rim, rim,
            shape((channels, TAPS * channels), BF16),
            shape((TAPS * channels, 2 * channels), BF16),
        ],
        1,
        (tile_order, cot, taps, spread, swap, edge),
        flops=2 * 10**8,
        moved=3 * 10**6,
    )
    from_above = shifted(last, "blk", 1)
    from_below = shifted(first, "blk", -1)
    out, part, pair, scaled = call(
        forward,
        [
            shape((2, channels, TILE * TILE), BF16),
            shape((channels, TAPS * channels), F32),
            body,
            shape((TILE * channels, features), BF16),
        ],
        2,
        (
            dilations, tile_order, weight, embed, following, second, before, grads, flat,
            spread, swap,
        ),
        [
            pltpu.VMEM((TILE + 2 * HALO, channels, LANES), F32),
            pltpu.VMEM((TILE + 2 * HALO, 3 * channels, LANES), BF16),
            pltpu.VMEM((TILE // 4, channels, 4 * LANES), BF16),
        ],
        flops=8 * 10**8,
        moved=4 * 10**6,
    )
    sums, near, far = call(
        backward,
        [
            shape((channels, features + TAPS * channels), F32),
            shape((TILE, features), F32),
            shape((TILE, features), BF16),
        ],
        1,
        (
            dilations, weight, embed, following, grads, from_above, from_below, tail, both,
            pair, scaled, part,
        ),
        [
            pltpu.VMEM((TILE + 2 * HALO, 2 * channels, LANES), BF16),
            pltpu.VMEM((TILE + 2 * HALO, TAPS * channels, LANES), F32),
            pltpu.VMEM((TILE * channels, LANES), BF16),
        ],
        flops=8 * 10**8,
        moved=4 * 10**6,
    )
    carried = shifted(far, "blk", 1)
    count = lax.axis_size("blk")
    step = 1
    while step < count:
        other = lax.ppermute(sums, "blk", [(i, i ^ step) for i in range(count)])
        step *= 2
        if step < count:
            sums = sums + other
    grad_weight, grad_kernel, grad_embed = call(
        finish,
        [
            shape((channels, features), F32),
            shape((TAPS, channels, channels), F32),
            shape((TILE, features), F32),
        ],
        0,
        (sums, other, near, carried),
        moved=10**6,
    )
    return (
        out.reshape(1, 2, channels, TILE * TILE),
        grad_embed,
        grad_weight.T,
        jnp.transpose(grad_kernel, (1, 0, 2)),
    )


def solution(mesh):
    placed = (
        P(("grp", "blk"), None),
        P(),
        P(),
        P(),
        P(("grp", "blk"), None),
        P(("grp", "blk"), None, None, None),
    )
    return jax.shard_map(
        per_device,
        mesh=mesh,
        in_specs=placed,
        out_specs=(
            P(("grp", "blk"), None, None, None),
            P(("grp", "blk"), None),
            P("grp", None),
            P("grp", None, None),
        ),
        check_vma=False,
    )
```

```python
import jax
import jax.numpy as jnp
from jax import lax
from jax.experimental import pallas as pl
from jax.experimental.pallas import tpu as pltpu
from jax.sharding import PartitionSpec as P

GROUPS = 4
HALO = 8
TILE = 32
LANES = 128
TAPS = 9
F32 = jnp.float32
BF16 = jnp.bfloat16
NN = (((1,), (0,)), ((), ()))
NT = (((1,), (1,)), ((), ()))
TN = (((0,), (0,)), ((), ()))


def dot(a, b, dims=NN):
    return lax.dot_general(a, b, dims, preferred_element_type=F32)


def turn(x, by):
    by = by % LANES
    return x if by == 0 else pltpu.roll(x, by, 1)


def lane_ids(rows):
    return lax.broadcasted_iota(jnp.int32, (rows, LANES), 1)


def within(lane, low, high):
    return jnp.logical_and(lane >= low, lane < high)


def one_hot(target, chunks):
    lane = lane_ids(target.shape[0])
    hits = [jnp.where(target == lane + LANES * c, 1.0, 0.0).astype(BF16) for c in range(chunks)]
    return jnp.concatenate(hits, 1)


def row_ids(rows):
    return lax.broadcasted_iota(jnp.int32, (rows, LANES), 0)


def spread_table(chunks):
    x = row_ids(LANES * chunks)
    return one_hot((((x >> 5) & 3) << 7) + ((x >> 7) << 5) + (x & 31), 4)


def swap_table():
    x = row_ids(HALO * TILE)
    return one_hot(((x & 31) << 3) + (x >> 5), 2)


def edge_table():
    x = row_ids(LANES)
    return one_hot(jnp.where((x & 31) < HALO, ((x & 31) << 5) + (x >> 5), -1), 2)


def has_next_flag():
    return lax.axis_index("blk") < lax.axis_size("blk") - 1


def tiles_of(order_ref, cot_ref):
    slot = order_ref[0, 0]
    keep = jnp.where(has_next_flag(), 1.0, 0.0).astype(F32)
    return cot_ref[slot], (cot_ref[1 - slot].astype(F32) * keep).astype(BF16)


def pack(order_ref, cot_ref, embed_ref, up_ref, down_ref):
    zero, one = tiles_of(order_ref, cot_ref)
    lane = lane_ids(zero.shape[0])
    far_side = within(lane, 80, 112)
    edge = edge_table()
    halves = [None, None]
    for j in range(8):
        moved = dot(zero[:, LANES * j : LANES * (j + 1)], edge)
        for h in range(2):
            piece = turn(moved[:, LANES * h : LANES * (h + 1)], 4 * j)
            halves[h] = piece if halves[h] is None else halves[h] + piece
    spread = spread_table(2)
    for j in (0, 1, 6, 7):
        at = slice(LANES * j, LANES * (j + 1))
        rows = dot(jnp.concatenate([zero[:, at], one[:, at]], 1), spread)
        for m in range(4):
            row = rows[:, LANES * m : LANES * (m + 1)]
            r = 4 * j + m
            if r < HALO:
                column = turn(halves[r // 4], 80 - TILE * (r % 4))
                up_ref[r] = (row + jnp.where(far_side, column, 0.0)).astype(BF16)
            else:
                down_ref[r - (TILE - HALO)] = row.astype(BF16)
    both = jnp.concatenate([embed_ref[:, :LANES], embed_ref[:, LANES:]], 0)
    up_ref[HALO] = both
    down_ref[HALO] = both


def prepare(
    order_ref, cot_ref, kern_ref, weight_ref, embed_ref,
    g_ref, dense_ref, tail_ref, flat_ref, both_ref, scaled_ref,
):
    zero, one = tiles_of(order_ref, cot_ref)
    channels = kern_ref.shape[1]
    swap = swap_table()
    tail_at = TILE * (TILE - HALO)
    y_zero = dot(zero[:, tail_at:], swap)
    y_one = dot(one[:, tail_at:], swap)
    lane = lane_ids(channels)
    own_side = within(lane, 72, 80)
    low = lane < 2 * TILE
    spread = spread_table(4)
    for j in range(4):
        at = slice(LANES * j, LANES * (j + 1))
        later = slice(LANES * (j + 4), LANES * (j + 5))
        rows = dot(
            jnp.concatenate([zero[:, at], one[:, at], zero[:, later], one[:, later]], 1), spread
        )
        for m in range(4):
            row = rows[:, LANES * m : LANES * (m + 1)]
            dense_ref[4 * j + m] = row.astype(BF16)
            for h in range(2):
                r = 16 * h + 4 * j + m
                side = turn(y_zero[:, LANES * h : LANES * (h + 1)], 72 - 8 * (r % 16))
                side = jnp.where(own_side, side, 0.0)
                g_ref[r] = jnp.where(low, turn(row, 64 * h), side).astype(BF16)
    for i in range(HALO):
        rest = turn(y_one[:, :LANES], 72 - 8 * i)
        tail_ref[i] = jnp.where(own_side, rest, 0.0).astype(BF16)
    eye = (
        lax.broadcasted_iota(jnp.int32, (channels, channels), 0)
        == lax.broadcasted_iota(jnp.int32, (channels, channels), 1)
    )
    eye = jnp.where(eye, 1.0, 0.0).astype(BF16)
    for u in range(3):
        for v in range(3):
            t = 3 * u + v
            pair = jnp.concatenate([kern_ref[t], kern_ref[3 * v + u]], 0)
            both_ref[channels * t : channels * (t + 1), :] = dot(eye, pair, NT).astype(BF16)
    for t in range(0, TAPS - 1, 2):
        flat_ref[:, channels * t : channels * (t + 2)] = jnp.concatenate(
            [kern_ref[t].astype(F32), kern_ref[t + 1].astype(F32)], 1
        ).astype(BF16)
    flat_ref[:, channels * (TAPS - 1) : channels * TAPS] = kern_ref[TAPS - 1]
    weight = weight_ref[...].astype(F32)
    own = embed_ref[...].astype(F32)
    for r in range(TILE):
        scaled_ref[channels * r : channels * (r + 1), :] = (own[r : r + 1, :] * weight).astype(
            BF16
        )


def unpacked(ref):
    x = ref[HALO].astype(F32)
    return jnp.concatenate([x[:TILE], x[TILE:]], 1)


def forward(
    dil_ref, order_ref, weight_ref, own_ref, second_ref, above_ref, below_ref, dense_ref,
    flat_ref, scaled_ref,
    out_ref, part_ref, pair_ref,
    map_ref, rolled_ref, rows_ref,
):
    channels = flat_ref.shape[0]
    width = channels // GROUPS
    weight = weight_ref[...].astype(F32)
    own = own_ref[...].astype(F32)
    after = unpacked(below_ref)
    head = second_ref[...].astype(F32)[:HALO]
    before = unpacked(above_ref)[TILE - HALO :]
    filler = jnp.zeros((LANES - 2 * TILE - 2 * HALO, own.shape[1]), F32)
    columns = jnp.concatenate([own, after, head, filler, before], 0).astype(BF16)
    lane = lane_ids(channels)
    kept = (
        jnp.logical_or(lane < TILE, lane >= LANES - HALO),
        lane < 2 * TILE,
        within(lane, TILE, 2 * TILE + HALO),
    )
    for c in range(6):
        part = 0 if c == 0 else (2 if c == 5 else 1)
        if part == 1:
            scaled = scaled_ref[8 * channels * (c - 1) : 8 * channels * c, :]
        else:
            rim = before if part == 0 else after
            scaled = jnp.concatenate(
                [(rim[i : i + 1, :] * weight).astype(BF16) for i in range(HALO)], 0
            )
        pair = dot(scaled, columns, NT).astype(BF16)
        for i in range(8):
            one = pair[channels * i : channels * (i + 1)]
            if part == 1:
                pair_ref[8 * (c - 1) + i] = one
            map_ref[8 * c + i] = jnp.where(kept[part], jnp.maximum(one.astype(F32), 0.0), 0.0)
    swap = swap_table()

    def gathered(first, per, low, high, move):
        halves = []
        for half in range(2):
            total = None
            for m in range(per):
                piece = jnp.where(within(lane, low, high), map_ref[first + per * half + m], 0.0)
                piece = turn(piece, move(m))
                total = piece if total is None else total + piece
            halves.append(total.astype(BF16))
        return jnp.concatenate(halves, 1)

    above = dot(gathered(0, 4, 0, TILE, lambda m: TILE * m), swap)
    below = dot(gathered(8, 16, TILE, TILE + HALO, lambda m: HALO * m - TILE), swap, NT)
    for r in range(TILE):
        half = LANES * (r // 16)
        side = turn(above[:, half : half + LANES], LANES - HALO - HALO * (r % 16))
        map_ref[HALO + r] += jnp.where(lane >= LANES - HALO, side, 0.0)
    for i in range(HALO):
        half = LANES * (i // 4)
        side = turn(below[:, half : half + LANES], -TILE * (i % 4))
        map_ref[HALO + TILE + i] += jnp.where(lane < TILE, side, 0.0)

    spacing = [jnp.left_shift(jnp.int32(1), dil_ref[g]) for g in range(GROUPS)]
    left = lane_ids(width) < 2 * TILE

    def roll_row(i, carry):
        for g in range(GROUPS):
            at = width * g
            x = map_ref[i, at : at + width, :]
            y = turn(map_ref[i + 16, at : at + width, :], 2 * TILE)
            for v, by in enumerate((spacing[g], None, LANES - spacing[g])):
                one, two = (x, y) if by is None else (pltpu.roll(x, by, 1), pltpu.roll(y, by, 1))
                to = channels * v + at
                rolled_ref[i, to : to + width, :] = jnp.where(left, one, two).astype(BF16)
        return carry

    lax.fori_loop(0, TILE, roll_row, 0, unroll=4)
    part_ref[...] = jnp.zeros_like(part_ref)

    def taps_of(r):
        pieces = []
        for u in range(3):
            for v in range(3):
                for g in range(GROUPS):
                    at = channels * v + width * g
                    pieces.append(rolled_ref[r + HALO + (u - 1) * spacing[g], at : at + width, :])
        return jnp.concatenate(pieces, 0)

    low = lane < 2 * TILE

    def conv_rows(j, carry):
        for h in range(2):
            r = 4 * j + 2 * h
            stack = jnp.concatenate([taps_of(r), taps_of(r + 1)], 1)
            response = dot(flat_ref[...], stack)
            part_ref[...] += dot(
                jnp.concatenate([dense_ref[r], dense_ref[r + 1]], 1), stack, NT
            )
            for m in range(2):
                row = jnp.where(
                    low,
                    pair_ref[r + m].astype(F32),
                    turn(pair_ref[r + m + 16].astype(F32), 2 * TILE),
                )
                row = row + response[:, LANES * m : LANES * (m + 1)]
                at = LANES * (2 * h + m)
                rows_ref[j, :, at : at + LANES] = row.astype(BF16)
        return carry

    lax.fori_loop(0, 4, conv_rows, 0)
    slot = order_ref[0, 0]
    keep = jnp.where(has_next_flag(), 1.0, 0.0).astype(F32)
    spread = spread_table(4)
    for j in range(4):
        chunk = dot(rows_ref[j], spread, NT)
        for h in range(2):
            at = slice(LANES * (j + 4 * h), LANES * (j + 4 * h + 1))
            to = 2 * LANES * h
            out_ref[slot, :, at] = chunk[:, to : to + LANES].astype(BF16)
            out_ref[1 - slot, :, at] = (chunk[:, to + LANES : to + 2 * LANES] * keep).astype(BF16)


def adjoint(
    dil_ref, g_ref, above_ref, below_ref, tail_ref, both_ref, pair_ref,
    grad_ref,
    map_ref, spread_ref,
):
    channels = g_ref.shape[1]
    width = channels // GROUPS
    lane = lane_ids(channels)
    zeros = jnp.zeros((channels, LANES), BF16)

    def masked(x, keep):
        return jnp.where(keep, x, 0.0).astype(BF16)

    upper = jnp.logical_or(lane < TILE, lane >= LANES - HALO)
    for i in range(HALO):
        map_ref[i, :channels] = masked(turn(above_ref[i].astype(F32), -TILE), upper)
        map_ref[i, channels:] = zeros
        x = below_ref[i].astype(F32)
        at = HALO + TILE + i
        map_ref[at, :channels] = masked(turn(x, TILE), within(lane, TILE, 2 * TILE + HALO))
        map_ref[at, channels:] = masked(x, within(lane, 80, 112)) + tail_ref[i]
    inner = jnp.where(lane < 2 * TILE, 1.0, 0.0).astype(BF16)
    side = jnp.where(within(lane, 72, 80), 1.0, 0.0).astype(BF16)

    def own_rows(r, carry):
        x = g_ref[r]
        map_ref[HALO + r, :channels] = x * inner
        map_ref[HALO + r, channels:] = x * side
        return carry

    lax.fori_loop(0, TILE, own_rows, 0, unroll=4)

    def spread_rows(i, carry):
        x = jnp.concatenate([map_ref[2 * i], map_ref[2 * i + 1]], 1)
        y = dot(both_ref[...], x)
        spread_ref[2 * i] = y[:, :LANES]
        spread_ref[2 * i + 1] = y[:, LANES:]
        return carry

    lax.fori_loop(0, (TILE + 2 * HALO) // 2, spread_rows, 0, unroll=2)
    spacing = [jnp.left_shift(jnp.int32(1), dil_ref[g]) for g in range(GROUPS)]
    second = within(lane, TILE, 2 * TILE)

    def gather_row(r, carry):
        pieces = []
        for g in range(GROUPS):
            totals = []
            for v in range(3):
                total = None
                for u in range(3):
                    at = channels * (3 * u + v) + width * g
                    piece = spread_ref[r + HALO - (u - 1) * spacing[g], at : at + width, :]
                    total = piece if total is None else total + piece
                totals.append(total)
            pieces.append(
                totals[1]
                + pltpu.roll(totals[0], LANES - spacing[g], 1)
                + pltpu.roll(totals[2], spacing[g], 1)
            )
        grad = jnp.concatenate(pieces, 0)
        grad = grad + jnp.where(second, turn(grad, -48), 0.0)
        own = g_ref[r].astype(F32)
        own = own + jnp.where(pair_ref[r].astype(F32) > 0, grad, 0.0)
        grad_ref[pl.ds(pl.multiple_of(r * channels, channels), channels), :] = jnp.where(
            lane < 2 * TILE, own, 0.0
        ).astype(BF16)
        return carry

    lax.fori_loop(0, TILE, gather_row, 0, unroll=4)


def project(
    weight_ref, own_ref, below_ref, scaled_ref, grad_ref, sums_ref, near_ref
):
    channels = weight_ref.shape[0]
    weight = weight_ref[...].astype(F32)
    own = own_ref[...].astype(F32)
    columns = jnp.concatenate(
        [own, unpacked(below_ref), jnp.zeros((LANES - 2 * TILE, own.shape[1]), F32)], 0
    ).astype(BF16)
    weight_part = jnp.zeros_like(weight)
    local = []
    for c in range(4):
        at = slice(8 * channels * c, 8 * channels * (c + 1))
        grad_scaled = dot(grad_ref[at, :], columns)
        for i in range(8):
            one = grad_scaled[channels * i : channels * (i + 1)]
            local.append(jnp.sum(one * weight, 0, keepdims=True))
            weight_part = weight_part + one * own[8 * c + i : 8 * c + i + 1, :]
    both = dot(grad_ref[...], scaled_ref[...], TN)
    near_ref[...] = jnp.concatenate(local, 0) + both[:TILE]
    sums_ref[:channels] = weight_part
    sums_ref[channels:] = both[TILE : 2 * TILE]


def finish(
    sums_ref, more_ref, part_ref, other_ref, near_ref, carried_ref,
    weight_ref, kernel_ref, embed_ref,
):
    channels = kernel_ref.shape[1]
    weight_ref[...] = sums_ref[...] + more_ref[...]
    total = part_ref[...] + other_ref[...]
    for t in range(TAPS):
        kernel_ref[t] = total[:, channels * t : channels * (t + 1)]
    embed_ref[...] = near_ref[...] + carried_ref[...]


def shifted(shard, axis, by):
    length = lax.axis_size(axis)
    pairs = [(i, i + by) for i in range(length) if 0 <= i + by < length]
    return lax.ppermute(shard, axis, pairs)


VMEM = pl.BlockSpec(memory_space=pltpu.VMEM)
SMEM = pl.BlockSpec(memory_space=pltpu.SMEM)


def shape(dims, kind):
    return jax.ShapeDtypeStruct(dims, kind)


def call(kernel, outs, scalars, operands, scratch=(), flops=0, moved=0, room=40):
    specs = [SMEM] * scalars + [VMEM] * (len(operands) - scalars)
    return pl.pallas_call(
        kernel,
        out_shape=outs,
        in_specs=specs,
        out_specs=[VMEM] * len(outs),
        scratch_shapes=list(scratch),
        compiler_params=pltpu.CompilerParams(vmem_limit_bytes=room * 1024 * 1024),
        cost_estimate=pl.CostEstimate(flops=flops, bytes_accessed=moved, transcendentals=0),
    )(*operands)


def paired(shard, axis, step):
    return lax.ppermute(shard, axis, [(i, i ^ step) for i in range(lax.axis_size(axis))])


def per_device(embed, pair_weight, conv_kernel, dilations, tile_order, cotangent):
    features = embed.shape[1]
    channels = conv_kernel.shape[0]
    weight = pair_weight.T
    taps = jnp.transpose(conv_kernel, (1, 0, 2))
    cot = cotangent.reshape(2, channels, TILE * TILE)
    second = shifted(embed, "blk", -2)
    rim = shape((HALO, channels, LANES), BF16)
    packed = shape((HALO + 1, channels, LANES), BF16)
    body = shape((TILE, channels, LANES), BF16)
    up, down = call(
        pack, [packed, packed], 1, (tile_order, cot, embed), flops=10**7, moved=10**6, room=60
    )
    from_above = shifted(down, "blk", 1)
    from_below = shifted(up, "blk", -1)
    grads, dense, tail, flat, both, scaled = call(
        prepare,
        [
            body,
            shape((TILE // 2, channels, LANES), BF16),
            rim,
            shape((channels, TAPS * channels), BF16),
            shape((TAPS * channels, 2 * channels), BF16),
            shape((TILE * channels, features), BF16),
        ],
        1,
        (tile_order, cot, taps, weight, embed),
        flops=2 * 10**8,
        moved=3 * 10**6,
    )
    out, part, pair = call(
        forward,
        [
            shape((2, channels, TILE * TILE), BF16),
            shape((channels, TAPS * channels), F32),
            body,
        ],
        2,
        (
            dilations, tile_order, weight, embed, second, from_above, from_below, dense, flat,
            scaled,
        ),
        [
            pltpu.VMEM((TILE + 2 * HALO, channels, LANES), F32),
            pltpu.VMEM((TILE, 3 * channels, LANES), BF16),
            pltpu.VMEM((4, channels, 4 * LANES), BF16),
        ],
        flops=8 * 10**8,
        moved=4 * 10**6,
    )
    (grad_pair,) = call(
        adjoint,
        [shape((TILE * channels, LANES), BF16)],
        1,
        (dilations, grads, from_above, from_below, tail, both, pair),
        [
            pltpu.VMEM((TILE + 2 * HALO, 2 * channels, LANES), BF16),
            pltpu.VMEM((TILE + 2 * HALO, TAPS * channels, LANES), F32),
        ],
        flops=8 * 10**8,
        moved=4 * 10**6,
    )
    sums, near = call(
        project,
        [shape((channels + TILE, features), F32), shape((TILE, features), F32)],
        0,
        (weight, embed, from_below, scaled, grad_pair),
        flops=4 * 10**8,
        moved=4 * 10**6,
    )
    count = lax.axis_size("blk")
    other = paired(part, "blk", 1)
    arrived = lax.ppermute(sums, "blk", [(i, (i + 1) % count) for i in range(count)])
    carried = arrived[channels:]
    sums, more = sums[:channels], arrived[:channels]
    step = 2
    while step < count:
        part = part + other
        other = paired(part, "blk", step)
        sums = sums + more
        more = paired(sums, "blk", step)
        step *= 2
    grad_weight, grad_kernel, grad_embed = call(
        finish,
        [
            shape((channels, features), F32),
            shape((TAPS, channels, channels), F32),
            shape((TILE, features), F32),
        ],
        0,
        (sums, more, part, other, near, carried),
        moved=10**6,
    )
    return (
        out.reshape(1, 2, channels, TILE * TILE),
        grad_embed,
        grad_weight.T,
        jnp.transpose(grad_kernel, (1, 0, 2)),
    )


def solution(mesh):
    placed = (
        P(("grp", "blk"), None),
        P(),
        P(),
        P(),
        P(("grp", "blk"), None),
        P(("grp", "blk"), None, None, None),
    )
    return jax.shard_map(
        per_device,
        mesh=mesh,
        in_specs=placed,
        out_specs=(
            P(("grp", "blk"), None, None, None),
            P(("grp", "blk"), None),
            P("grp", None),
            P("grp", None, None),
        ),
        check_vma=False,
    )
```

```python
import jax
import jax.numpy as jnp
from jax import lax
from jax.experimental import pallas as pl
from jax.experimental.pallas import tpu as pltpu
from jax.sharding import PartitionSpec as P

GROUPS = 4
HALO = 8
TILE = 32
LANES = 128
TAPS = 9
F32 = jnp.float32
BF16 = jnp.bfloat16
NN = (((1,), (0,)), ((), ()))
NT = (((1,), (1,)), ((), ()))
TN = (((0,), (0,)), ((), ()))


def dot(a, b, dims=NN):
    return lax.dot_general(a, b, dims, preferred_element_type=F32)


def turn(x, by):
    by = by % LANES
    return x if by == 0 else pltpu.roll(x, by, 1)


def lane_ids(rows):
    return lax.broadcasted_iota(jnp.int32, (rows, LANES), 1)


def within(lane, low, high):
    return jnp.logical_and(lane >= low, lane < high)


def one_hot(target, chunks):
    lane = lane_ids(target.shape[0])
    hits = [jnp.where(target == lane + LANES * c, 1.0, 0.0).astype(BF16) for c in range(chunks)]
    return jnp.concatenate(hits, 1)


def row_ids(rows):
    return lax.broadcasted_iota(jnp.int32, (rows, LANES), 0)


def spread_table(chunks):
    x = row_ids(LANES * chunks)
    return one_hot((((x >> 5) & 3) << 7) + ((x >> 7) << 5) + (x & 31), 4)


def swap_table():
    x = row_ids(HALO * TILE)
    return one_hot(((x & 31) << 3) + (x >> 5), 2)


def edge_table():
    x = row_ids(LANES)
    return one_hot(jnp.where((x & 31) < HALO, ((x & 31) << 5) + (x >> 5), -1), 2)


def as_float(flag):
    return jnp.where(flag, 1.0, 0.0).astype(F32)


def place():
    index = lax.axis_index("blk")
    last = lax.axis_size("blk") - 1
    return index, as_float(index % 2 == 0), as_float(index > 0), as_float(index < last)


def half_of(index):
    return (index + index // 2) % 2


def tiles_of(order_ref, cot_ref):
    slot = order_ref[0, 0]
    _, _, _, keep = place()
    return cot_ref[slot], (cot_ref[1 - slot].astype(F32) * keep).astype(BF16)


def fetch(sources, targets, sems):
    copies = [
        pltpu.make_async_copy(source, target, sems.at[i])
        for i, (source, target) in enumerate(zip(sources, targets))
    ]
    for copy in copies:
        copy.start()
    for copy in copies:
        copy.wait()


def pack(
    order_hbm, cot_hbm, embed_hbm,
    core_ref, chip_ref,
    order_ref, cot_ref, embed_ref, sems,
):
    fetch((order_hbm, cot_hbm, embed_hbm), (order_ref, cot_ref, embed_ref), sems)
    zero, one = tiles_of(order_ref, cot_ref)
    _, even, _, _ = place()
    channels = zero.shape[0]
    lane = lane_ids(channels)
    far_side = within(lane, 80, 112)
    moved = dot(
        jnp.concatenate([zero[:, LANES * j : LANES * (j + 1)] for j in range(8)], 0), edge_table()
    )
    halves = [None, None]
    for j in range(8):
        for h in range(2):
            piece = moved[channels * j : channels * (j + 1), LANES * h : LANES * (h + 1)]
            piece = turn(piece, 4 * j)
            halves[h] = piece if halves[h] is None else halves[h] + piece
    pieces = []
    for j in (0, 1, 6, 7):
        at = slice(LANES * j, LANES * (j + 1))
        pieces.append(jnp.concatenate([zero[:, at], one[:, at]], 1))
    rows = dot(jnp.concatenate(pieces, 0), spread_table(2))

    def row_of(i):
        at = channels * (i // 4)
        to = LANES * (i % 4)
        return rows[at : at + channels, to : to + LANES]

    for r in range(HALO):
        column = turn(halves[r // 4], 80 - TILE * (r % 4))
        up = row_of(r) + jnp.where(far_side, column, 0.0)
        down = row_of(HALO + r)
        core_ref[r] = (down * even + up * (1.0 - even)).astype(BF16)
        chip_ref[r] = (up * even + down * (1.0 - even)).astype(BF16)
    both = jnp.concatenate([embed_ref[:, :LANES], embed_ref[:, LANES:]], 0)
    core_ref[HALO] = both
    chip_ref[HALO] = both


def from_above(core_ref, chip_ref, i):
    _, even, before, _ = place()
    x = chip_ref[i].astype(F32) * (even * before)
    return x + core_ref[i].astype(F32) * ((1.0 - even) * before)


def from_below(core_ref, chip_ref, i):
    _, even, _, after = place()
    x = core_ref[i].astype(F32) * (even * after)
    return x + chip_ref[i].astype(F32) * ((1.0 - even) * after)


def prepare(
    order_ref, dil_ref, cot_ref, kern_ref, weight_ref, embed_ref,
    g_ref, dense_ref, tail_ref, flat_ref, both_ref, scaled_ref, meta_ref,
):
    for g in range(GROUPS):
        meta_ref[g] = jnp.left_shift(jnp.int32(1), dil_ref[g])
    meta_ref[GROUPS] = order_ref[0, 0]
    zero, one = tiles_of(order_ref, cot_ref)
    channels = kern_ref.shape[1]
    swap = swap_table()
    tail_at = TILE * (TILE - HALO)
    y_zero = dot(zero[:, tail_at:], swap)
    y_one = dot(one[:, tail_at:], swap)
    lane = lane_ids(channels)
    own_side = within(lane, 72, 80)
    low = lane < 2 * TILE
    pieces = []
    for j in range(4):
        at = slice(LANES * j, LANES * (j + 1))
        later = slice(LANES * (j + 4), LANES * (j + 5))
        pieces.append(
            jnp.concatenate([zero[:, at], one[:, at], zero[:, later], one[:, later]], 1)
        )
    rows = dot(jnp.concatenate(pieces, 0), spread_table(4))
    for j in range(4):
        for m in range(4):
            row = rows[channels * j : channels * (j + 1), LANES * m : LANES * (m + 1)]
            dense_ref[4 * j + m] = row.astype(BF16)
            for h in range(2):
                r = 16 * h + 4 * j + m
                side = turn(y_zero[:, LANES * h : LANES * (h + 1)], 72 - 8 * (r % 16))
                side = jnp.where(own_side, side, 0.0)
                g_ref[r] = jnp.where(low, turn(row, 64 * h), side).astype(BF16)
    for i in range(HALO):
        rest = turn(y_one[:, :LANES], 72 - 8 * i)
        tail_ref[i] = jnp.where(own_side, rest, 0.0).astype(BF16)
    eye = (
        lax.broadcasted_iota(jnp.int32, (channels, channels), 0)
        == lax.broadcasted_iota(jnp.int32, (channels, channels), 1)
    )
    eye = jnp.where(eye, 1.0, 0.0).astype(BF16)
    for u in range(3):
        for v in range(3):
            t = 3 * u + v
            pair = jnp.concatenate([kern_ref[t], kern_ref[3 * v + u]], 0)
            both_ref[channels * t : channels * (t + 1), :] = dot(eye, pair, NT).astype(BF16)
    for t in range(0, TAPS - 1, 2):
        flat_ref[:, channels * t : channels * (t + 2)] = jnp.concatenate(
            [kern_ref[t].astype(F32), kern_ref[t + 1].astype(F32)], 1
        ).astype(BF16)
    flat_ref[:, channels * (TAPS - 1) : channels * TAPS] = kern_ref[TAPS - 1]
    weight = weight_ref[...].astype(F32)
    own = embed_ref[...].astype(F32)
    for r in range(TILE):
        scaled_ref[channels * r : channels * (r + 1), :] = (own[r : r + 1, :] * weight).astype(
            BF16
        )


def unpacked(x):
    return jnp.concatenate([x[:TILE], x[TILE:]], 1)


def forward(
    meta_ref, weight_ref, own_ref, second_ref, core_ref, chip_ref, dense_ref, scaled_ref,
    part_ref, pair_ref, rolled_ref,
    map_ref,
):
    channels = weight_ref.shape[0]
    width = channels // GROUPS
    weight = weight_ref[...].astype(F32)
    own = own_ref[...].astype(F32)
    after = unpacked(from_below(core_ref, chip_ref, HALO))
    near_end = as_float(lax.axis_index("blk") < lax.axis_size("blk") - 2)
    head = second_ref[...].astype(F32)[:HALO] * near_end
    before = unpacked(from_above(core_ref, chip_ref, HALO))[TILE - HALO :]
    filler = jnp.zeros((LANES - 2 * TILE - 2 * HALO, own.shape[1]), F32)
    columns = jnp.concatenate([own, after, head, filler, before], 0).astype(BF16)
    lane = lane_ids(channels)
    kept = (
        jnp.logical_or(lane < TILE, lane >= LANES - HALO),
        lane < 2 * TILE,
        within(lane, TILE, 2 * TILE + HALO),
    )
    for c in range(6):
        part = 0 if c == 0 else (2 if c == 5 else 1)
        if part == 1:
            scaled = scaled_ref[8 * channels * (c - 1) : 8 * channels * c, :]
        else:
            rim = before if part == 0 else after
            scaled = jnp.concatenate(
                [(rim[i : i + 1, :] * weight).astype(BF16) for i in range(HALO)], 0
            )
        pair = dot(scaled, columns, NT).astype(BF16)
        for i in range(8):
            one = pair[channels * i : channels * (i + 1)]
            if part == 1:
                pair_ref[8 * (c - 1) + i] = one
            map_ref[8 * c + i] = jnp.where(kept[part], jnp.maximum(one.astype(F32), 0.0), 0.0)
    swap = swap_table()

    def gathered(first, per, low, high, move):
        halves = []
        for half in range(2):
            total = None
            for m in range(per):
                piece = jnp.where(within(lane, low, high), map_ref[first + per * half + m], 0.0)
                piece = turn(piece, move(m))
                total = piece if total is None else total + piece
            halves.append(total.astype(BF16))
        return jnp.concatenate(halves, 1)

    above = dot(gathered(0, 4, 0, TILE, lambda m: TILE * m), swap)
    below = dot(gathered(8, 16, TILE, TILE + HALO, lambda m: HALO * m - TILE), swap, NT)
    for r in range(TILE):
        half = LANES * (r // 16)
        side = turn(above[:, half : half + LANES], LANES - HALO - HALO * (r % 16))
        map_ref[HALO + r] += jnp.where(lane >= LANES - HALO, side, 0.0)
    for i in range(HALO):
        half = LANES * (i // 4)
        side = turn(below[:, half : half + LANES], -TILE * (i % 4))
        map_ref[HALO + TILE + i] += jnp.where(lane < TILE, side, 0.0)

    spacing = [meta_ref[g] for g in range(GROUPS)]
    left = lane_ids(width) < 2 * TILE

    def roll_row(i, carry):
        for g in range(GROUPS):
            at = width * g
            x = map_ref[i, at : at + width, :]
            y = turn(map_ref[i + 16, at : at + width, :], 2 * TILE)
            for v, by in enumerate((spacing[g], None, LANES - spacing[g])):
                one, two = (x, y) if by is None else (pltpu.roll(x, by, 1), pltpu.roll(y, by, 1))
                to = channels * v + at
                rolled_ref[i, to : to + width, :] = jnp.where(left, one, two).astype(BF16)
        return carry

    lax.fori_loop(0, TILE, roll_row, 0, unroll=4)
    part_ref[...] = jnp.zeros_like(part_ref)

    def sum_rows(j, carry):
        stack = jnp.concatenate([taps_of(rolled_ref, spacing, 2 * j + m) for m in range(2)], 1)
        grads = jnp.concatenate([dense_ref[2 * j], dense_ref[2 * j + 1]], 1)
        part_ref[...] += dot(grads, stack, NT)
        return carry

    lax.fori_loop(0, 8, sum_rows, 0, unroll=2)


def taps_of(rolled_ref, spacing, r):
    channels = rolled_ref.shape[1] // 3
    width = channels // GROUPS
    pieces = []
    for u in range(3):
        for v in range(3):
            for g in range(GROUPS):
                at = channels * v + width * g
                pieces.append(rolled_ref[r + HALO + (u - 1) * spacing[g], at : at + width, :])
    return jnp.concatenate(pieces, 0)


def respond(meta_ref, flat_ref, rolled_ref, pair_ref, out_ref, rows_ref):
    channels = flat_ref.shape[0]
    spacing = [meta_ref[g] for g in range(GROUPS)]
    low = lane_ids(channels) < 2 * TILE

    def conv_rows(j, carry):
        for h in range(2):
            r = 4 * j + 2 * h
            stack = jnp.concatenate([taps_of(rolled_ref, spacing, r + m) for m in range(2)], 1)
            response = dot(flat_ref[...], stack)
            for m in range(2):
                row = jnp.where(
                    low,
                    pair_ref[r + m].astype(F32),
                    turn(pair_ref[r + m + 16].astype(F32), 2 * TILE),
                )
                row = row + response[:, LANES * m : LANES * (m + 1)]
                at = LANES * (2 * h + m)
                to = pl.ds(pl.multiple_of(channels * j, channels), channels)
                rows_ref[to, at : at + LANES] = row.astype(BF16)
        return carry

    lax.fori_loop(0, 4, conv_rows, 0)
    slot = meta_ref[GROUPS]
    _, _, _, keep = place()
    chunks = dot(rows_ref[...], spread_table(4), NT)
    for j in range(4):
        chunk = chunks[channels * j : channels * (j + 1)]
        for h in range(2):
            at = slice(LANES * (j + 4 * h), LANES * (j + 4 * h + 1))
            to = 2 * LANES * h
            out_ref[slot, :, at] = chunk[:, to : to + LANES].astype(BF16)
            out_ref[1 - slot, :, at] = (chunk[:, to + LANES : to + 2 * LANES] * keep).astype(BF16)


def adjoint(
    meta_ref, g_ref, core_ref, chip_ref, tail_ref, both_ref, pair_ref,
    grad_ref,
    map_ref, spread_ref,
):
    channels = g_ref.shape[1]
    width = channels // GROUPS
    lane = lane_ids(channels)
    zeros = jnp.zeros((channels, LANES), BF16)

    def masked(x, keep):
        return jnp.where(keep, x, 0.0).astype(BF16)

    upper = jnp.logical_or(lane < TILE, lane >= LANES - HALO)
    for i in range(HALO):
        map_ref[i, :channels] = masked(turn(from_above(core_ref, chip_ref, i), -TILE), upper)
        map_ref[i, channels:] = zeros
        x = from_below(core_ref, chip_ref, i)
        at = HALO + TILE + i
        map_ref[at, :channels] = masked(turn(x, TILE), within(lane, TILE, 2 * TILE + HALO))
        map_ref[at, channels:] = masked(x, within(lane, 80, 112)) + tail_ref[i]
    inner = jnp.where(lane < 2 * TILE, 1.0, 0.0).astype(BF16)
    side = jnp.where(within(lane, 72, 80), 1.0, 0.0).astype(BF16)

    def own_rows(r, carry):
        x = g_ref[r]
        map_ref[HALO + r, :channels] = x * inner
        map_ref[HALO + r, channels:] = x * side
        return carry

    lax.fori_loop(0, TILE, own_rows, 0, unroll=4)

    def spread_rows(i, carry):
        x = jnp.concatenate([map_ref[2 * i], map_ref[2 * i + 1]], 1)
        y = dot(both_ref[...], x)
        spread_ref[2 * i] = y[:, :LANES]
        spread_ref[2 * i + 1] = y[:, LANES:]
        return carry

    lax.fori_loop(0, (TILE + 2 * HALO) // 2, spread_rows, 0, unroll=2)
    spacing = [meta_ref[g] for g in range(GROUPS)]
    second = within(lane, TILE, 2 * TILE)

    def gather_row(r, carry):
        pieces = []
        for g in range(GROUPS):
            totals = []
            for v in range(3):
                total = None
                for u in range(3):
                    at = channels * (3 * u + v) + width * g
                    piece = spread_ref[r + HALO - (u - 1) * spacing[g], at : at + width, :]
                    total = piece if total is None else total + piece
                totals.append(total)
            pieces.append(
                totals[1]
                + pltpu.roll(totals[0], LANES - spacing[g], 1)
                + pltpu.roll(totals[2], spacing[g], 1)
            )
        grad = jnp.concatenate(pieces, 0)
        grad = grad + jnp.where(second, turn(grad, -48), 0.0)
        own = g_ref[r].astype(F32)
        own = own + jnp.where(pair_ref[r].astype(F32) > 0, grad, 0.0)
        grad_ref[pl.ds(pl.multiple_of(r * channels, channels), channels), :] = jnp.where(
            lane < 2 * TILE, own, 0.0
        ).astype(BF16)
        return carry

    lax.fori_loop(0, TILE, gather_row, 0, unroll=4)


def project(
    weight_ref, own_ref, core_ref, chip_ref, scaled_ref, grad_ref, part_ref,
    keep_ref, send_ref, far_ref, near_ref,
    sum_ref,
):
    channels = weight_ref.shape[0]
    weight = weight_ref[...].astype(F32)
    own = own_ref[...].astype(F32)
    columns = jnp.concatenate(
        [own, unpacked(from_below(core_ref, chip_ref, HALO)), jnp.zeros((LANES - 2 * TILE, own.shape[1]), F32)], 0
    ).astype(BF16)
    weight_part = jnp.zeros_like(weight)
    local = []
    for c in range(4):
        at = slice(8 * channels * c, 8 * channels * (c + 1))
        grad_scaled = dot(grad_ref[at, :], columns)
        for i in range(8):
            one = grad_scaled[channels * i : channels * (i + 1)]
            local.append(jnp.sum(one * weight, 0, keepdims=True))
            weight_part = weight_part + one * own[8 * c + i : 8 * c + i + 1, :]
    both = dot(grad_ref[...], scaled_ref[...], TN)
    near_ref[...] = jnp.concatenate(local, 0) + both[:TILE]
    far = both[TILE : 2 * TILE]
    far_ref[...] = far
    sum_ref[...] = weight_part
    rows = channels // 2
    features = own.shape[1]
    half = half_of(lax.axis_index("blk"))
    mine = pl.ds(pl.multiple_of(rows * half, rows), rows)
    other = pl.ds(pl.multiple_of(rows * (1 - half), rows), rows)
    keep_ref[:, :features] = sum_ref[mine, :]
    keep_ref[:, features:] = part_ref[mine, :]
    send_ref[:, :features] = far
    send_ref[:, features : 2 * features] = sum_ref[other, :]
    send_ref[:, 2 * features :] = part_ref[other, :]


def finish(
    mine_ref, other_ref, core_ref, chip_ref, near_ref,
    weight_ref, kernel_ref, embed_ref,
):
    index, even, _, _ = place()
    rows = mine_ref.shape[0]
    channels = 2 * rows
    features = weight_ref.shape[1]
    half = half_of(index)
    for ref, which in ((mine_ref, half), (other_ref, 1 - half)):
        at = pl.ds(pl.multiple_of(rows * which, rows), rows)
        weight_ref[at, :] = ref[:, :features]
        for t in range(TAPS):
            to = features + channels * t
            kernel_ref[t, at, :] = ref[:, to : to + channels]
    carried = core_ref[:, :features] * (1.0 - even) + chip_ref[:, :features] * even
    embed_ref[...] = near_ref[...] + carried


VMEM = pl.BlockSpec(memory_space=pltpu.VMEM)
SMEM = pl.BlockSpec(memory_space=pltpu.SMEM)
HBM = pl.BlockSpec(memory_space=pltpu.HBM)


def shape(dims, kind):
    return jax.ShapeDtypeStruct(dims, kind)


def call(kernel, outs, scalars, operands, scratch=(), flops=0, moved=0, first=None, room=40):
    specs = [first or SMEM] * scalars + [VMEM] * (len(operands) - scalars)
    return pl.pallas_call(
        kernel,
        out_shape=outs,
        in_specs=specs,
        out_specs=[SMEM if out.dtype == jnp.int32 else VMEM for out in outs],
        scratch_shapes=list(scratch),
        compiler_params=pltpu.CompilerParams(vmem_limit_bytes=room * 1024 * 1024),
        cost_estimate=pl.CostEstimate(flops=flops, bytes_accessed=moved, transcendentals=0),
    )(*operands)


def swap_with(shard, step):
    return lax.ppermute(shard, "blk", [(i, i ^ step) for i in range(lax.axis_size("blk"))])


def swap_chips(shard):
    count = lax.axis_size("blk")
    pairs = [(i, (i + (1 if i % 2 else -1)) % count) for i in range(count)]
    return lax.ppermute(shard, "blk", pairs)


def per_device(embed, pair_weight, conv_kernel, dilations, tile_order, cotangent):
    features = embed.shape[1]
    channels = conv_kernel.shape[0]
    count = lax.axis_size("blk")
    weight = pair_weight.T
    taps = jnp.transpose(conv_kernel, (1, 0, 2))
    cot = cotangent.reshape(2, channels, TILE * TILE)
    packed = shape((HALO + 1, channels, LANES), BF16)
    body = shape((TILE, channels, LANES), BF16)
    to_core, to_chip = call(
        pack,
        [packed, packed],
        3,
        (tile_order, cot, embed),
        [
            pltpu.SMEM(tile_order.shape, jnp.int32),
            pltpu.VMEM(cot.shape, BF16),
            pltpu.VMEM(embed.shape, BF16),
            pltpu.SemaphoreType.DMA((3,)),
        ],
        flops=10**7,
        moved=10**6,
        first=HBM,
        room=60,
    )
    core = swap_with(to_core, 1)
    chip = swap_chips(to_chip)
    second = lax.ppermute(embed, "blk", [(i, (i - 2) % count) for i in range(count)])
    grads, dense, tail, flat, both, scaled, meta = call(
        prepare,
        [
            body,
            shape((TILE // 2, channels, LANES), BF16),
            shape((HALO, channels, LANES), BF16),
            shape((channels, TAPS * channels), BF16),
            shape((TAPS * channels, 2 * channels), BF16),
            shape((TILE * channels, features), BF16),
            shape((2 * GROUPS,), jnp.int32),
        ],
        2,
        (tile_order, dilations, cot, taps, weight, embed),
        flops=2 * 10**8,
        moved=3 * 10**6,
    )
    part, pair, rolled = call(
        forward,
        [
            shape((channels, TAPS * channels), F32),
            body,
            shape((TILE, 3 * channels, LANES), BF16),
        ],
        1,
        (meta, weight, embed, second, core, chip, dense, scaled),
        [pltpu.VMEM((TILE + 2 * HALO, channels, LANES), F32)],
        flops=8 * 10**8,
        moved=4 * 10**6,
    )
    (grad_pair,) = call(
        adjoint,
        [shape((TILE * channels, LANES), BF16)],
        1,
        (meta, grads, core, chip, tail, both, pair),
        [
            pltpu.VMEM((TILE + 2 * HALO, 2 * channels, LANES), BF16),
            pltpu.VMEM((TILE + 2 * HALO, TAPS * channels, LANES), F32),
        ],
        flops=8 * 10**8,
        moved=4 * 10**6,
    )
    width = features + TAPS * channels
    keep, send, far, near = call(
        project,
        [
            shape((channels // 2, width), F32),
            shape((channels // 2, features + width), F32),
            shape((TILE, features), F32),
            shape((TILE, features), F32),
        ],
        0,
        (weight, embed, core, chip, scaled, grad_pair, part),
        [pltpu.VMEM((channels, features), F32)],
        flops=4 * 10**8,
        moved=4 * 10**6,
    )
    by_core = swap_with(send, 1)
    total = keep + by_core[:, features:]
    by_chip = swap_chips(jnp.concatenate([far, total], 1))
    total = total + by_chip[:, features:]
    step = 4
    while 2 * step < count:
        total = total + swap_with(total, step)
        step *= 2
    rolled, total = lax.optimization_barrier((rolled, total))
    last = swap_with(total, step)
    (out,) = call(
        respond,
        [shape((2, channels, TILE * TILE), BF16)],
        1,
        (meta, flat, rolled, pair),
        [pltpu.VMEM((4 * channels, 4 * LANES), BF16)],
        flops=2 * 10**8,
        moved=2 * 10**6,
    )
    out, last = lax.optimization_barrier((out, last))
    total = total + last
    rest = swap_with(total, 1)
    grad_weight, grad_kernel, grad_embed = call(
        finish,
        [
            shape((channels, features), F32),
            shape((TAPS, channels, channels), F32),
            shape((TILE, features), F32),
        ],
        0,
        (total, rest, by_core, by_chip, near),
        moved=10**6,
    )
    return (
        out.reshape(1, 2, channels, TILE * TILE),
        grad_embed,
        grad_weight.T,
        jnp.transpose(grad_kernel, (1, 0, 2)),
    )


def solution(mesh):
    placed = (
        P(("grp", "blk"), None),
        P(),
        P(),
        P(),
        P(("grp", "blk"), None),
        P(("grp", "blk"), None, None, None),
    )
    return jax.shard_map(
        per_device,
        mesh=mesh,
        in_specs=placed,
        out_specs=(
            P(("grp", "blk"), None, None, None),
            P(("grp", "blk"), None),
            P("grp", None),
            P("grp", None, None),
        ),
        check_vma=False,
    )
```

```python
import jax
import jax.numpy as jnp
from jax import lax
from jax.experimental import pallas as pl
from jax.experimental.pallas import tpu as pltpu
from jax.sharding import PartitionSpec as P

GROUPS = 4
HALO = 8
TILE = 32
LANES = 128
TAPS = 9
F32 = jnp.float32
BF16 = jnp.bfloat16
NN = (((1,), (0,)), ((), ()))
NT = (((1,), (1,)), ((), ()))
TN = (((0,), (0,)), ((), ()))


def dot(a, b, dims=NN):
    return lax.dot_general(a, b, dims, preferred_element_type=F32)


def turn(x, by):
    by = by % LANES
    return x if by == 0 else pltpu.roll(x, by, 1)


def lane_ids(rows):
    return lax.broadcasted_iota(jnp.int32, (rows, LANES), 1)


def within(lane, low, high):
    return jnp.logical_and(lane >= low, lane < high)


def one_hot(target, chunks):
    lane = lane_ids(target.shape[0])
    hits = [jnp.where(target == lane + LANES * c, 1.0, 0.0).astype(BF16) for c in range(chunks)]
    return jnp.concatenate(hits, 1)


def row_ids(rows):
    return lax.broadcasted_iota(jnp.int32, (rows, LANES), 0)


def spread_table(chunks):
    x = row_ids(LANES * chunks)
    return one_hot((((x >> 5) & 3) << 7) + ((x >> 7) << 5) + (x & 31), 4)


def swap_table():
    x = row_ids(HALO * TILE)
    return one_hot(((x & 31) << 3) + (x >> 5), 2)


def edge_table():
    x = row_ids(LANES)
    return one_hot(jnp.where((x & 31) < HALO, ((x & 31) << 5) + (x >> 5), -1), 2)


def as_float(flag):
    return jnp.where(flag, 1.0, 0.0).astype(F32)


def place():
    index = lax.axis_index("blk")
    last = lax.axis_size("blk") - 1
    return index, as_float(index % 2 == 0), as_float(index > 0), as_float(index < last)


def corner_shift(flat, spacing):
    width = flat.shape[0] // GROUPS
    lane = lane_ids(width)
    pieces = []
    for g in range(GROUPS):
        d = spacing[g]
        kept = jnp.logical_and(jnp.logical_and(lane < 8 * HALO, (lane >> 3) < d), (lane & 7) < d)
        x = jnp.where(kept, flat[width * g : width * (g + 1)], 0.0)
        pieces.append(pltpu.roll(x, (HALO + 1) * (HALO - d), 1))
    return jnp.concatenate(pieces, 0).astype(BF16)


def tiles_of(order_ref, cot_ref):
    slot = order_ref[0, 0]
    _, _, _, keep = place()
    return cot_ref[slot], (cot_ref[1 - slot].astype(F32) * keep).astype(BF16)


def fetch(sources, targets, sems):
    copies = [
        pltpu.make_async_copy(source, target, sems.at[i])
        for i, (source, target) in enumerate(zip(sources, targets))
    ]
    for copy in copies:
        copy.start()
    for copy in copies:
        copy.wait()


def pack(
    order_hbm, cot_hbm, embed_hbm,
    core_ref, chip_ref,
    order_ref, cot_ref, embed_ref, sems,
):
    fetch((order_hbm, cot_hbm, embed_hbm), (order_ref, cot_ref, embed_ref), sems)
    zero, one = tiles_of(order_ref, cot_ref)
    _, even, _, _ = place()
    channels = zero.shape[0]
    lane = lane_ids(channels)
    far_side = within(lane, 80, 112)
    moved = dot(
        jnp.concatenate([zero[:, LANES * j : LANES * (j + 1)] for j in range(8)], 0), edge_table()
    )
    halves = [None, None]
    for j in range(8):
        for h in range(2):
            piece = moved[channels * j : channels * (j + 1), LANES * h : LANES * (h + 1)]
            piece = turn(piece, 4 * j)
            halves[h] = piece if halves[h] is None else halves[h] + piece
    pieces = []
    for j in (0, 1, 6, 7):
        at = slice(LANES * j, LANES * (j + 1))
        pieces.append(jnp.concatenate([zero[:, at], one[:, at]], 1))
    rows = dot(jnp.concatenate(pieces, 0), spread_table(2))

    def row_of(i):
        at = channels * (i // 4)
        to = LANES * (i % 4)
        return rows[at : at + channels, to : to + LANES]

    for r in range(HALO):
        column = turn(halves[r // 4], 80 - TILE * (r % 4))
        up = row_of(r) + jnp.where(far_side, column, 0.0)
        down = row_of(HALO + r)
        core_ref[r] = (down * even + up * (1.0 - even)).astype(BF16)
        chip_ref[r] = (up * even + down * (1.0 - even)).astype(BF16)
    both = jnp.concatenate([embed_ref[:, :LANES], embed_ref[:, LANES:]], 0)
    core_ref[HALO] = both
    chip_ref[HALO] = both


def from_above(core_ref, chip_ref, i):
    _, even, before, _ = place()
    x = chip_ref[i].astype(F32) * (even * before)
    return x + core_ref[i].astype(F32) * ((1.0 - even) * before)


def from_below(core_ref, chip_ref, i):
    _, even, _, after = place()
    x = core_ref[i].astype(F32) * (even * after)
    return x + chip_ref[i].astype(F32) * ((1.0 - even) * after)


def prepare(
    order_ref, dil_ref, cot_ref, kern_ref, weight_ref, embed_ref,
    g_ref, dense_ref, tail_ref, flat_ref, both_ref, scaled_ref, meta_ref,
):
    for g in range(GROUPS):
        meta_ref[g] = jnp.left_shift(jnp.int32(1), dil_ref[g])
    meta_ref[GROUPS] = order_ref[0, 0]
    zero, one = tiles_of(order_ref, cot_ref)
    channels = kern_ref.shape[1]
    swap = swap_table()
    tail_at = TILE * (TILE - HALO)
    y_zero = dot(zero[:, tail_at:], swap)
    y_one = dot(one[:, tail_at:], swap)
    lane = lane_ids(channels)
    own_side = within(lane, 72, 80)
    low = lane < 2 * TILE
    pieces = []
    for j in range(4):
        at = slice(LANES * j, LANES * (j + 1))
        later = slice(LANES * (j + 4), LANES * (j + 5))
        pieces.append(
            jnp.concatenate([zero[:, at], one[:, at], zero[:, later], one[:, later]], 1)
        )
    rows = dot(jnp.concatenate(pieces, 0), spread_table(4))
    for j in range(4):
        for m in range(4):
            row = rows[channels * j : channels * (j + 1), LANES * m : LANES * (m + 1)]
            dense_ref[4 * j + m] = row.astype(BF16)
            for h in range(2):
                r = 16 * h + 4 * j + m
                side = turn(y_zero[:, LANES * h : LANES * (h + 1)], 72 - 8 * (r % 16))
                side = jnp.where(own_side, side, 0.0)
                g_ref[r] = jnp.where(low, turn(row, 64 * h), side).astype(BF16)
    for i in range(HALO):
        rest = turn(y_one[:, :LANES], 72 - 8 * i)
        tail_ref[i] = jnp.where(own_side, rest, 0.0).astype(BF16)
    eye = (
        lax.broadcasted_iota(jnp.int32, (channels, channels), 0)
        == lax.broadcasted_iota(jnp.int32, (channels, channels), 1)
    )
    eye = jnp.where(eye, 1.0, 0.0).astype(BF16)
    for u in range(3):
        for v in range(3):
            t = 3 * u + v
            pair = jnp.concatenate([kern_ref[t], kern_ref[3 * v + u]], 0)
            both_ref[channels * t : channels * (t + 1), :] = dot(eye, pair, NT).astype(BF16)
    for t in range(0, TAPS - 1, 2):
        flat_ref[:, channels * t : channels * (t + 2)] = jnp.concatenate(
            [kern_ref[t].astype(F32), kern_ref[t + 1].astype(F32)], 1
        ).astype(BF16)
    flat_ref[:, channels * (TAPS - 1) : channels * TAPS] = kern_ref[TAPS - 1]
    weight = weight_ref[...].astype(F32)
    own = embed_ref[...].astype(F32)
    for r in range(TILE):
        scaled_ref[channels * r : channels * (r + 1), :] = (own[r : r + 1, :] * weight).astype(
            BF16
        )


def unpacked(x):
    return jnp.concatenate([x[:TILE], x[TILE:]], 1)


def forward(
    meta_ref, weight_ref, own_ref, core_ref, chip_ref, dense_ref, scaled_ref,
    part_ref, pair_ref, rolled_ref, corner_ref,
    map_ref,
):
    channels = weight_ref.shape[0]
    width = channels // GROUPS
    weight = weight_ref[...].astype(F32)
    own = own_ref[...].astype(F32)
    after = unpacked(from_below(core_ref, chip_ref, HALO))
    before = unpacked(from_above(core_ref, chip_ref, HALO))[TILE - HALO :]
    filler = jnp.zeros((LANES - 2 * TILE - HALO, own.shape[1]), F32)
    columns = jnp.concatenate([own, after, filler, before], 0).astype(BF16)
    lane = lane_ids(channels)
    kept = (
        jnp.logical_or(lane < TILE, lane >= LANES - HALO),
        lane < 2 * TILE,
        within(lane, TILE, 2 * TILE),
    )
    for c in range(6):
        part = 0 if c == 0 else (2 if c == 5 else 1)
        if part == 1:
            scaled = scaled_ref[8 * channels * (c - 1) : 8 * channels * c, :]
        else:
            rim = before if part == 0 else after
            scaled = jnp.concatenate(
                [(rim[i : i + 1, :] * weight).astype(BF16) for i in range(HALO)], 0
            )
        pair = dot(scaled, columns, NT).astype(BF16)
        for i in range(8):
            one = pair[channels * i : channels * (i + 1)]
            if part == 1:
                pair_ref[8 * (c - 1) + i] = one
            map_ref[8 * c + i] = jnp.where(kept[part], jnp.maximum(one.astype(F32), 0.0), 0.0)
    swap = swap_table()

    def gathered(first, per, low, high, move):
        halves = []
        for half in range(2):
            total = None
            for m in range(per):
                piece = jnp.where(within(lane, low, high), map_ref[first + per * half + m], 0.0)
                piece = turn(piece, move(m))
                total = piece if total is None else total + piece
            halves.append(total.astype(BF16))
        return jnp.concatenate(halves, 1)

    above = dot(gathered(0, 4, 0, TILE, lambda m: TILE * m), swap)
    below = dot(gathered(8, 16, TILE, TILE + HALO, lambda m: HALO * m - TILE), swap, NT)
    for r in range(TILE):
        half = LANES * (r // 16)
        side = turn(above[:, half : half + LANES], LANES - HALO - HALO * (r % 16))
        map_ref[HALO + r] += jnp.where(lane >= LANES - HALO, side, 0.0)
    for i in range(HALO):
        half = LANES * (i // 4)
        side = turn(below[:, half : half + LANES], -TILE * (i % 4))
        map_ref[HALO + TILE + i] += jnp.where(lane < TILE, side, 0.0)

    spacing = [meta_ref[g] for g in range(GROUPS)]
    left = lane_ids(width) < 2 * TILE

    def roll_row(i, carry):
        for g in range(GROUPS):
            at = width * g
            x = map_ref[i, at : at + width, :]
            y = turn(map_ref[i + 16, at : at + width, :], 2 * TILE)
            for v, by in enumerate((spacing[g], None, LANES - spacing[g])):
                one, two = (x, y) if by is None else (pltpu.roll(x, by, 1), pltpu.roll(y, by, 1))
                to = channels * v + at
                rolled_ref[i, to : to + width, :] = jnp.where(left, one, two).astype(BF16)
        return carry

    lax.fori_loop(0, TILE, roll_row, 0, unroll=8)

    corner = None
    ends = None
    for i in range(HALO):
        x = jnp.where(within(lane, TILE, TILE + HALO), map_ref[HALO + i], 0.0)
        y = jnp.where(
            within(lane, 2 * TILE - HALO, 2 * TILE), from_above(core_ref, chip_ref, i), 0.0
        )
        x, y = turn(x, HALO * i - TILE), turn(y, HALO * i - 2 * TILE + HALO)
        corner, ends = (x, y) if i == 0 else (corner + x, ends + y)
    corner_ref[...] = corner[: channels // 2] + turn(corner[channels // 2 :], 8 * HALO)
    part_ref[...] = jnp.zeros_like(part_ref)
    part_ref[:, channels * (TAPS - 1) :] = dot(
        ends.astype(BF16), corner_shift(corner, spacing), NT
    )

    def sum_rows(j, carry):
        stack = jnp.concatenate([taps_of(rolled_ref, spacing, 2 * j + m) for m in range(2)], 1)
        grads = jnp.concatenate([dense_ref[2 * j], dense_ref[2 * j + 1]], 1)
        part_ref[...] += dot(grads, stack, NT)
        return carry

    lax.fori_loop(0, 8, sum_rows, 0, unroll=4)


def taps_of(rolled_ref, spacing, r):
    channels = rolled_ref.shape[1] // 3
    width = channels // GROUPS
    pieces = []
    for u in range(3):
        for v in range(3):
            for g in range(GROUPS):
                at = channels * v + width * g
                pieces.append(rolled_ref[r + HALO + (u - 1) * spacing[g], at : at + width, :])
    return jnp.concatenate(pieces, 0)


def respond(
    meta_ref, flat_ref, rolled_ref, pair_ref, core_ref, chip_ref,
    out_ref,
    rows_ref, share_ref,
):
    channels = flat_ref.shape[0]
    spacing = [meta_ref[g] for g in range(GROUPS)]
    lane = lane_ids(channels)
    low = lane < 2 * TILE
    _, even, _, keep = place()
    corner = core_ref[...] * even + chip_ref[...] * ((1.0 - even) * keep)
    corner = jnp.concatenate([corner, turn(corner, 8 * HALO)], 0)
    share = dot(flat_ref[:, channels * (TAPS - 1) :], corner_shift(corner, spacing))
    share_ref[:HALO] = jnp.zeros((HALO, channels, LANES), F32)
    for i in range(HALO):
        share_ref[HALO + i] = jnp.where(
            lane >= LANES - HALO, turn(share, LANES - HALO - HALO * i), 0.0
        )

    def conv_rows(j, carry):
        for h in range(2):
            r = 4 * j + 2 * h
            stack = jnp.concatenate([taps_of(rolled_ref, spacing, r + m) for m in range(2)], 1)
            response = dot(flat_ref[...], stack)
            for m in range(2):
                row = jnp.where(
                    low,
                    pair_ref[r + m].astype(F32),
                    turn(pair_ref[r + m + 16].astype(F32), 2 * TILE),
                )
                row = row + (response[:, LANES * m : LANES * (m + 1)] + share_ref[r + m])
                at = LANES * (2 * h + m)
                to = pl.ds(pl.multiple_of(channels * j, channels), channels)
                rows_ref[to, at : at + LANES] = row.astype(BF16)
        return carry

    lax.fori_loop(0, 4, conv_rows, 0)
    slot = meta_ref[GROUPS]
    chunks = dot(rows_ref[...], spread_table(4), NT)
    for j in range(4):
        chunk = chunks[channels * j : channels * (j + 1)]
        for h in range(2):
            at = slice(LANES * (j + 4 * h), LANES * (j + 4 * h + 1))
            to = 2 * LANES * h
            out_ref[slot, :, at] = chunk[:, to : to + LANES].astype(BF16)
            out_ref[1 - slot, :, at] = (chunk[:, to + LANES : to + 2 * LANES] * keep).astype(BF16)


def adjoint(
    meta_ref, g_ref, core_ref, chip_ref, tail_ref, both_ref, pair_ref,
    grad_ref,
    map_ref, spread_ref,
):
    channels = g_ref.shape[1]
    width = channels // GROUPS
    lane = lane_ids(channels)
    zeros = jnp.zeros((channels, LANES), BF16)

    def masked(x, keep):
        return jnp.where(keep, x, 0.0).astype(BF16)

    upper = jnp.logical_or(lane < TILE, lane >= LANES - HALO)
    for i in range(HALO):
        map_ref[i, :channels] = masked(turn(from_above(core_ref, chip_ref, i), -TILE), upper)
        map_ref[i, channels:] = zeros
        x = from_below(core_ref, chip_ref, i)
        at = HALO + TILE + i
        map_ref[at, :channels] = masked(turn(x, TILE), within(lane, TILE, 2 * TILE + HALO))
        map_ref[at, channels:] = masked(x, within(lane, 80, 112)) + tail_ref[i]
    inner = jnp.where(lane < 2 * TILE, 1.0, 0.0).astype(BF16)
    side = jnp.where(within(lane, 72, 80), 1.0, 0.0).astype(BF16)

    def own_rows(r, carry):
        x = g_ref[r]
        map_ref[HALO + r, :channels] = x * inner
        map_ref[HALO + r, channels:] = x * side
        return carry

    lax.fori_loop(0, TILE, own_rows, 0, unroll=8)
    span = 3 * channels

    def spread_rows(i, low, high):
        x = jnp.concatenate([map_ref[2 * i], map_ref[2 * i + 1]], 1)
        y = dot(both_ref[low:high, :], x)
        spread_ref[2 * i, low:high, :] = y[:, :LANES]
        spread_ref[2 * i + 1, low:high, :] = y[:, LANES:]

    for i in range(HALO // 2):
        spread_rows(i, 2 * span, 3 * span)
        spread_rows((HALO + TILE) // 2 + i, 0, span)

    def spread_own(i, carry):
        spread_rows(HALO // 2 + i, 0, 3 * span)
        return carry

    lax.fori_loop(0, TILE // 2, spread_own, 0, unroll=4)
    spacing = [meta_ref[g] for g in range(GROUPS)]
    second = within(lane, TILE, 2 * TILE)

    def gather_row(r, carry):
        pieces = []
        for g in range(GROUPS):
            totals = []
            for v in range(3):
                total = None
                for u in range(3):
                    at = channels * (3 * u + v) + width * g
                    piece = spread_ref[r + HALO - (u - 1) * spacing[g], at : at + width, :]
                    total = piece if total is None else total + piece
                totals.append(total)
            pieces.append(
                totals[1]
                + pltpu.roll(totals[0], LANES - spacing[g], 1)
                + pltpu.roll(totals[2], spacing[g], 1)
            )
        grad = jnp.concatenate(pieces, 0)
        grad = grad + jnp.where(second, turn(grad, -48), 0.0)
        own = g_ref[r].astype(F32)
        own = own + jnp.where(pair_ref[r].astype(F32) > 0, grad, 0.0)
        grad_ref[pl.ds(pl.multiple_of(r * channels, channels), channels), :] = jnp.where(
            lane < 2 * TILE, own, 0.0
        ).astype(BF16)
        return carry

    lax.fori_loop(0, TILE, gather_row, 0, unroll=8)


def project(
    weight_ref, own_ref, core_ref, chip_ref, scaled_ref, grad_ref, part_ref, corner_ref,
    keep_ref, send_ref, side_ref, near_ref,
    sum_ref,
):
    channels = weight_ref.shape[0]
    weight = weight_ref[...].astype(F32)
    own = own_ref[...].astype(F32)
    columns = jnp.concatenate(
        [own, unpacked(from_below(core_ref, chip_ref, HALO)), jnp.zeros((LANES - 2 * TILE, own.shape[1]), F32)], 0
    ).astype(BF16)
    weight_part = jnp.zeros_like(weight)
    local = []
    for c in range(4):
        at = slice(8 * channels * c, 8 * channels * (c + 1))
        grad_scaled = dot(grad_ref[at, :], columns)
        for i in range(8):
            one = grad_scaled[channels * i : channels * (i + 1)]
            local.append(jnp.sum(one * weight, 0, keepdims=True))
            weight_part = weight_part + one * own[8 * c + i : 8 * c + i + 1, :]
    both = dot(grad_ref[...], scaled_ref[...], TN)
    near_ref[...] = jnp.concatenate(local, 0) + both[:TILE]
    sum_ref[...] = weight_part
    rows = channels // 2
    features = own.shape[1]
    half = lax.axis_index("blk") % 2
    mine = pl.ds(pl.multiple_of(rows * half, rows), rows)
    other = pl.ds(pl.multiple_of(rows * (1 - half), rows), rows)
    keep_ref[:, :features] = sum_ref[mine, :]
    keep_ref[:, features:] = part_ref[mine, :]
    side = features + LANES
    for ref in (send_ref, side_ref):
        ref[:, :features] = both[TILE : 2 * TILE]
        ref[:, features:side] = corner_ref[...]
    send_ref[:, side : side + features] = sum_ref[other, :]
    send_ref[:, side + features :] = part_ref[other, :]


def finish(
    mine_ref, other_ref, core_ref, chip_ref, near_ref,
    weight_ref, kernel_ref, embed_ref,
):
    index, even, before, _ = place()
    rows = mine_ref.shape[0]
    channels = 2 * rows
    features = weight_ref.shape[1]
    half = index % 2
    for ref, which in ((mine_ref, half), (other_ref, 1 - half)):
        at = pl.ds(pl.multiple_of(rows * which, rows), rows)
        weight_ref[at, :] = ref[:, :features]
        for t in range(TAPS):
            to = features + channels * t
            kernel_ref[t, at, :] = ref[:, to : to + channels]
    carried = core_ref[:, :features] * (1.0 - even) + chip_ref[:, :features] * (even * before)
    embed_ref[...] = near_ref[...] + carried


VMEM = pl.BlockSpec(memory_space=pltpu.VMEM)
SMEM = pl.BlockSpec(memory_space=pltpu.SMEM)
HBM = pl.BlockSpec(memory_space=pltpu.HBM)


def shape(dims, kind):
    return jax.ShapeDtypeStruct(dims, kind)


def call(kernel, outs, scalars, operands, scratch=(), flops=0, moved=0, first=None, room=40):
    specs = [first or SMEM] * scalars + [VMEM] * (len(operands) - scalars)
    return pl.pallas_call(
        kernel,
        out_shape=outs,
        in_specs=specs,
        out_specs=[SMEM if out.dtype == jnp.int32 else VMEM for out in outs],
        scratch_shapes=list(scratch),
        compiler_params=pltpu.CompilerParams(vmem_limit_bytes=room * 1024 * 1024),
        cost_estimate=pl.CostEstimate(flops=flops, bytes_accessed=moved, transcendentals=0),
    )(*operands)


def swap_with(shard, step):
    return lax.ppermute(shard, "blk", [(i, i ^ step) for i in range(lax.axis_size("blk"))])


def swap_chips(shard):
    last = lax.axis_size("blk") - 1
    pairs = [(i, min(max(i + (1 if i % 2 else -1), 0), last)) for i in range(last + 1)]
    return lax.ppermute(shard, "blk", pairs)


def per_device(embed, pair_weight, conv_kernel, dilations, tile_order, cotangent):
    features = embed.shape[1]
    channels = conv_kernel.shape[0]
    count = lax.axis_size("blk")
    weight = pair_weight.T
    taps = jnp.transpose(conv_kernel, (1, 0, 2))
    cot = cotangent.reshape(2, channels, TILE * TILE)
    packed = shape((HALO + 1, channels, LANES), BF16)
    body = shape((TILE, channels, LANES), BF16)
    to_core, to_chip = call(
        pack,
        [packed, packed],
        3,
        (tile_order, cot, embed),
        [
            pltpu.SMEM(tile_order.shape, jnp.int32),
            pltpu.VMEM(cot.shape, BF16),
            pltpu.VMEM(embed.shape, BF16),
            pltpu.SemaphoreType.DMA((3,)),
        ],
        flops=10**9,
        moved=10**6,
        first=HBM,
        room=60,
    )
    core = swap_with(to_core, 1)
    chip = swap_chips(to_chip)
    grads, dense, tail, flat, both, scaled, meta = call(
        prepare,
        [
            body,
            shape((TILE // 2, channels, LANES), BF16),
            shape((HALO, channels, LANES), BF16),
            shape((channels, TAPS * channels), BF16),
            shape((TAPS * channels, 2 * channels), BF16),
            shape((TILE * channels, features), BF16),
            shape((2 * GROUPS,), jnp.int32),
        ],
        2,
        (tile_order, dilations, cot, taps, weight, embed),
        flops=2 * 10**8,
        moved=3 * 10**6,
    )
    part, pair, rolled, corner = call(
        forward,
        [
            shape((channels, TAPS * channels), F32),
            body,
            shape((TILE, 3 * channels, LANES), BF16),
            shape((channels // 2, LANES), F32),
        ],
        1,
        (meta, weight, embed, core, chip, dense, scaled),
        [pltpu.VMEM((TILE + 2 * HALO, channels, LANES), F32)],
        flops=8 * 10**8,
        moved=4 * 10**6,
    )
    (grad_pair,) = call(
        adjoint,
        [shape((TILE * channels, LANES), BF16)],
        1,
        (meta, grads, core, chip, tail, both, pair),
        [
            pltpu.VMEM((TILE + 2 * HALO, 2 * channels, LANES), BF16),
            pltpu.VMEM((TILE + 2 * HALO, TAPS * channels, LANES), F32),
        ],
        flops=8 * 10**8,
        moved=4 * 10**6,
    )
    width = features + TAPS * channels
    side = features + LANES
    total, send, sided, near = call(
        project,
        [
            shape((channels // 2, width), F32),
            shape((channels // 2, side + width), F32),
            shape((channels // 2, side), F32),
            shape((TILE, features), F32),
        ],
        0,
        (weight, embed, core, chip, scaled, grad_pair, part, corner),
        [pltpu.VMEM((channels, features), F32)],
        flops=4 * 10**8,
        moved=4 * 10**6,
    )
    by_core = swap_with(send, 1)
    by_chip = swap_chips(sided)
    total = total + by_core[:, side:]
    by_core = by_core[:, :side]
    step = 2
    while 2 * step < count:
        total = total + swap_with(total, step)
        if step == 2:
            total, by_chip = lax.optimization_barrier((total, by_chip))
        step *= 2
    rolled, total = lax.optimization_barrier((rolled, total))
    last = swap_with(total, step)
    (out,) = call(
        respond,
        [shape((2, channels, TILE * TILE), BF16)],
        1,
        (meta, flat, rolled, pair, by_core[:, features:], by_chip[:, features:]),
        [
            pltpu.VMEM((4 * channels, 4 * LANES), BF16),
            pltpu.VMEM((TILE // 2, channels, LANES), F32),
        ],
        flops=2 * 10**8,
        moved=2 * 10**6,
    )
    out, last = lax.optimization_barrier((out, last))
    total = total + last
    rest = swap_with(total, 1)
    grad_weight, grad_kernel, grad_embed = call(
        finish,
        [
            shape((channels, features), F32),
            shape((TAPS, channels, channels), F32),
            shape((TILE, features), F32),
        ],
        0,
        (total, rest, by_core, by_chip, near),
        moved=10**6,
    )
    return (
        out.reshape(1, 2, channels, TILE * TILE),
        grad_embed,
        grad_weight.T,
        jnp.transpose(grad_kernel, (1, 0, 2)),
    )


def solution(mesh):
    placed = (
        P(("grp", "blk"), None),
        P(),
        P(),
        P(),
        P(("grp", "blk"), None),
        P(("grp", "blk"), None, None, None),
    )
    return jax.shard_map(
        per_device,
        mesh=mesh,
        in_specs=placed,
        out_specs=(
            P(("grp", "blk"), None, None, None),
            P(("grp", "blk"), None),
            P("grp", None),
            P("grp", None, None),
        ),
        check_vma=False,
    )
```

```python
import jax
import jax.numpy as jnp
from jax import lax
from jax.experimental import pallas as pl
from jax.experimental.pallas import tpu as pltpu
from jax.sharding import PartitionSpec as P

GROUPS = 4
HALO = 8
TILE = 32
LANES = 128
TAPS = 9
F32 = jnp.float32
BF16 = jnp.bfloat16
NN = (((1,), (0,)), ((), ()))
NT = (((1,), (1,)), ((), ()))
TN = (((0,), (0,)), ((), ()))


def dot(a, b, dims=NN):
    return lax.dot_general(a, b, dims, preferred_element_type=F32)


def turn(x, by):
    by = by % LANES
    return x if by == 0 else pltpu.roll(x, by, 1)


def lane_ids(rows):
    return lax.broadcasted_iota(jnp.int32, (rows, LANES), 1)


def within(lane, low, high):
    return jnp.logical_and(lane >= low, lane < high)


def one_hot(target, chunks):
    lane = lane_ids(target.shape[0])
    hits = [jnp.where(target == lane + LANES * c, 1.0, 0.0).astype(BF16) for c in range(chunks)]
    return jnp.concatenate(hits, 1)


def row_ids(rows):
    return lax.broadcasted_iota(jnp.int32, (rows, LANES), 0)


def spread_table(chunks):
    x = row_ids(LANES * chunks)
    return one_hot((((x >> 5) & 3) << 7) + ((x >> 7) << 5) + (x & 31), 4)


def swap_table():
    x = row_ids(HALO * TILE)
    return one_hot(((x & 31) << 3) + (x >> 5), 2)


def edge_table():
    x = row_ids(LANES)
    return one_hot(jnp.where((x & 31) < HALO, ((x & 31) << 5) + (x >> 5), -1), 2)


def corner_table(first):
    x = row_ids(HALO * TILE)
    c = (x & 31) - first
    return one_hot(jnp.where(within(c, 0, HALO), ((x >> 5) << 3) + c, -1), 1)


def as_float(flag):
    return jnp.where(flag, 1.0, 0.0).astype(F32)


def place():
    index = lax.axis_index("blk")
    last = lax.axis_size("blk") - 1
    return index, as_float(index % 2 == 0), as_float(index > 0), as_float(index < last)


def corner_shift(flat, spacing):
    width = flat.shape[0] // GROUPS
    lane = lane_ids(width)
    pieces = []
    for g in range(GROUPS):
        d = spacing[g]
        kept = jnp.logical_and(jnp.logical_and(lane < 8 * HALO, (lane >> 3) < d), (lane & 7) < d)
        x = jnp.where(kept, flat[width * g : width * (g + 1)], 0.0)
        pieces.append(pltpu.roll(x, (HALO + 1) * (HALO - d), 1))
    return jnp.concatenate(pieces, 0).astype(BF16)


def tiles_of(order_ref, cot_ref):
    slot = order_ref[0, 0]
    _, _, _, keep = place()
    return cot_ref[slot], (cot_ref[1 - slot].astype(F32) * keep).astype(BF16)


def fetch(sources, targets, sems):
    copies = [
        pltpu.make_async_copy(source, target, sems.at[i])
        for i, (source, target) in enumerate(zip(sources, targets))
    ]
    for copy in copies:
        copy.start()
    for copy in copies:
        copy.wait()


def pack(
    order_hbm, cot_hbm, embed_hbm,
    core_ref, chip_ref,
    order_ref, cot_ref, embed_ref, sems,
):
    fetch((order_hbm, cot_hbm, embed_hbm), (order_ref, cot_ref, embed_ref), sems)
    zero, one = tiles_of(order_ref, cot_ref)
    _, even, _, _ = place()
    channels = zero.shape[0]
    moved = dot(
        jnp.concatenate([zero[:, LANES * j : LANES * (j + 1)] for j in range(8)], 0), edge_table()
    )
    columns = []
    for h in range(2):
        total = None
        for j in range(8):
            piece = moved[channels * j : channels * (j + 1), LANES * h : LANES * (h + 1)]
            piece = turn(piece, 4 * j)
            total = piece if total is None else total + piece
        columns.append(total)
    rim = HALO * TILE
    tail_at = TILE * (TILE - HALO)
    up = [zero[:, :rim].astype(F32)] + columns + [dot(one[:, :rim], corner_table(0))]
    down = [one[:, tail_at:].astype(F32)] + [jnp.zeros_like(x) for x in columns]
    down += [dot(zero[:, tail_at:], corner_table(TILE - HALO))]
    up, down = jnp.concatenate(up, 1), jnp.concatenate(down, 1)
    width = up.shape[1]
    both = jnp.concatenate([embed_ref[:, :LANES], embed_ref[:, LANES:]], 0)
    core_ref[:, :width] = (down * even + up * (1.0 - even)).astype(BF16)
    core_ref[:, width:] = both
    chip_ref[:, :width] = (up * even + down * (1.0 - even)).astype(BF16)
    chip_ref[:, width:] = both


RIM_SIDE, RIM_CORNER, RIM_EMBED, RIM = 256, 512, 640, 768


def from_above(core_ref, chip_ref, at):
    _, even, before, _ = place()
    x = chip_ref[:, at].astype(F32) * (even * before)
    return x + core_ref[:, at].astype(F32) * ((1.0 - even) * before)


def from_below(core_ref, chip_ref, at):
    _, even, _, after = place()
    x = core_ref[:, at].astype(F32) * (even * after)
    return x + chip_ref[:, at].astype(F32) * ((1.0 - even) * after)


def prepare(
    order_ref, dil_ref, cot_ref, kern_ref, weight_ref, embed_ref,
    g_ref, dense_ref, tail_ref, flat_ref, both_ref, scaled_ref, meta_ref,
):
    for g in range(GROUPS):
        meta_ref[g] = jnp.left_shift(jnp.int32(1), dil_ref[g])
    meta_ref[GROUPS] = order_ref[0, 0]
    zero, one = tiles_of(order_ref, cot_ref)
    channels = kern_ref.shape[1]
    swap = swap_table()
    tail_at = TILE * (TILE - HALO)
    y_zero = dot(zero[:, tail_at:], swap)
    y_one = dot(one[:, tail_at:], swap)
    lane = lane_ids(channels)
    own_side = within(lane, 72, 80)
    low = lane < 2 * TILE
    pieces = []
    for j in range(4):
        at = slice(LANES * j, LANES * (j + 1))
        later = slice(LANES * (j + 4), LANES * (j + 5))
        pieces.append(
            jnp.concatenate([zero[:, at], one[:, at], zero[:, later], one[:, later]], 1)
        )
    rows = dot(jnp.concatenate(pieces, 0), spread_table(4))
    for j in range(4):
        for m in range(4):
            row = rows[channels * j : channels * (j + 1), LANES * m : LANES * (m + 1)]
            dense_ref[4 * j + m] = row.astype(BF16)
            for h in range(2):
                r = 16 * h + 4 * j + m
                side = turn(y_zero[:, LANES * h : LANES * (h + 1)], 72 - 8 * (r % 16))
                side = jnp.where(own_side, side, 0.0)
                g_ref[r] = jnp.where(low, turn(row, 64 * h), side).astype(BF16)
    for i in range(HALO):
        rest = turn(y_one[:, :LANES], 72 - 8 * i)
        tail_ref[i] = jnp.where(own_side, rest, 0.0).astype(BF16)
    eye = (
        lax.broadcasted_iota(jnp.int32, (channels, channels), 0)
        == lax.broadcasted_iota(jnp.int32, (channels, channels), 1)
    )
    eye = jnp.where(eye, 1.0, 0.0).astype(BF16)
    for u in range(3):
        for v in range(3):
            t = 3 * u + v
            pair = jnp.concatenate([kern_ref[t], kern_ref[3 * v + u]], 0)
            both_ref[channels * t : channels * (t + 1), :] = dot(eye, pair, NT).astype(BF16)
    for t in range(0, TAPS - 1, 2):
        flat_ref[:, channels * t : channels * (t + 2)] = jnp.concatenate(
            [kern_ref[t].astype(F32), kern_ref[t + 1].astype(F32)], 1
        ).astype(BF16)
    flat_ref[:, channels * (TAPS - 1) : channels * TAPS] = kern_ref[TAPS - 1]
    weight = weight_ref[...].astype(F32)
    own = embed_ref[...].astype(F32)
    for r in range(TILE):
        scaled_ref[channels * r : channels * (r + 1), :] = (own[r : r + 1, :] * weight).astype(
            BF16
        )


def unpacked(x):
    return jnp.concatenate([x[:TILE], x[TILE:]], 1)


def forward(
    meta_ref, weight_ref, own_ref, core_ref, chip_ref, dense_ref, scaled_ref,
    part_ref, pair_ref, rolled_ref,
    map_ref,
):
    channels = weight_ref.shape[0]
    width = channels // GROUPS
    weight = weight_ref[...].astype(F32)
    own = own_ref[...].astype(F32)
    after = unpacked(from_below(core_ref, chip_ref, slice(RIM_EMBED, RIM)))
    before = unpacked(from_above(core_ref, chip_ref, slice(RIM_EMBED, RIM)))[TILE - HALO :]
    filler = jnp.zeros((LANES - 2 * TILE - HALO, own.shape[1]), F32)
    columns = jnp.concatenate([own, after, filler, before], 0).astype(BF16)
    lane = lane_ids(channels)
    kept = (
        jnp.logical_or(lane < TILE, lane >= LANES - HALO),
        lane < 2 * TILE,
        within(lane, TILE, 2 * TILE),
    )
    for c in range(6):
        part = 0 if c == 0 else (2 if c == 5 else 1)
        if part == 1:
            scaled = scaled_ref[8 * channels * (c - 1) : 8 * channels * c, :]
        else:
            rim = before if part == 0 else after
            scaled = jnp.concatenate(
                [(rim[i : i + 1, :] * weight).astype(BF16) for i in range(HALO)], 0
            )
        pair = dot(scaled, columns, NT).astype(BF16)
        for i in range(8):
            one = pair[channels * i : channels * (i + 1)]
            if part == 1:
                pair_ref[8 * (c - 1) + i] = one
            map_ref[8 * c + i] = jnp.where(kept[part], jnp.maximum(one.astype(F32), 0.0), 0.0)
    swap = swap_table()

    def gathered(first, per, low, high, move):
        halves = []
        for half in range(2):
            total = None
            for m in range(per):
                piece = jnp.where(within(lane, low, high), map_ref[first + per * half + m], 0.0)
                piece = turn(piece, move(m))
                total = piece if total is None else total + piece
            halves.append(total.astype(BF16))
        return jnp.concatenate(halves, 1)

    above = dot(gathered(0, 4, 0, TILE, lambda m: TILE * m), swap)
    below = dot(gathered(8, 16, TILE, TILE + HALO, lambda m: HALO * m - TILE), swap, NT)
    for r in range(TILE):
        half = LANES * (r // 16)
        side = turn(above[:, half : half + LANES], LANES - HALO - HALO * (r % 16))
        map_ref[HALO + r] += jnp.where(lane >= LANES - HALO, side, 0.0)
    for i in range(HALO):
        half = LANES * (i // 4)
        side = turn(below[:, half : half + LANES], -TILE * (i % 4))
        map_ref[HALO + TILE + i] += jnp.where(lane < TILE, side, 0.0)

    spacing = [meta_ref[g] for g in range(GROUPS)]
    left = lane_ids(width) < 2 * TILE

    def roll_row(i, carry):
        for g in range(GROUPS):
            at = width * g
            x = map_ref[i, at : at + width, :]
            y = turn(map_ref[i + 16, at : at + width, :], 2 * TILE)
            for v, by in enumerate((spacing[g], None, LANES - spacing[g])):
                one, two = (x, y) if by is None else (pltpu.roll(x, by, 1), pltpu.roll(y, by, 1))
                to = channels * v + at
                rolled_ref[i, to : to + width, :] = jnp.where(left, one, two).astype(BF16)
        return carry

    lax.fori_loop(0, TILE, roll_row, 0, unroll=8)

    part_ref[...] = jnp.zeros_like(part_ref)

    def sum_rows(j, carry):
        stack = jnp.concatenate([taps_of(rolled_ref, spacing, 2 * j + m) for m in range(2)], 1)
        grads = jnp.concatenate([dense_ref[2 * j], dense_ref[2 * j + 1]], 1)
        part_ref[...] += dot(grads, stack, NT)
        return carry

    lax.fori_loop(0, 8, sum_rows, 0, unroll=4)


def taps_of(rolled_ref, spacing, r):
    channels = rolled_ref.shape[1] // 3
    width = channels // GROUPS
    pieces = []
    for u in range(3):
        for v in range(3):
            for g in range(GROUPS):
                at = channels * v + width * g
                pieces.append(rolled_ref[r + HALO + (u - 1) * spacing[g], at : at + width, :])
    return jnp.concatenate(pieces, 0)


def respond(
    meta_ref, flat_ref, rolled_ref, pair_ref, core_ref, chip_ref,
    out_ref,
    rows_ref, share_ref,
):
    channels = flat_ref.shape[0]
    spacing = [meta_ref[g] for g in range(GROUPS)]
    lane = lane_ids(channels)
    low = lane < 2 * TILE
    _, even, _, keep = place()
    corner = core_ref[...] * even + chip_ref[...] * ((1.0 - even) * keep)
    corner = jnp.concatenate([corner, turn(corner, 8 * HALO)], 0)
    share = dot(flat_ref[:, channels * (TAPS - 1) :], corner_shift(corner, spacing))
    share_ref[:HALO] = jnp.zeros((HALO, channels, LANES), F32)
    for i in range(HALO):
        share_ref[HALO + i] = jnp.where(
            lane >= LANES - HALO, turn(share, LANES - HALO - HALO * i), 0.0
        )

    def conv_rows(j, carry):
        for h in range(2):
            r = 4 * j + 2 * h
            stack = jnp.concatenate([taps_of(rolled_ref, spacing, r + m) for m in range(2)], 1)
            response = dot(flat_ref[...], stack)
            for m in range(2):
                row = jnp.where(
                    low,
                    pair_ref[r + m].astype(F32),
                    turn(pair_ref[r + m + 16].astype(F32), 2 * TILE),
                )
                row = row + (response[:, LANES * m : LANES * (m + 1)] + share_ref[r + m])
                at = LANES * (2 * h + m)
                to = pl.ds(pl.multiple_of(channels * j, channels), channels)
                rows_ref[to, at : at + LANES] = row.astype(BF16)
        return carry

    lax.fori_loop(0, 4, conv_rows, 0)
    slot = meta_ref[GROUPS]
    chunks = dot(rows_ref[...], spread_table(4), NT)
    for j in range(4):
        chunk = chunks[channels * j : channels * (j + 1)]
        for h in range(2):
            at = slice(LANES * (j + 4 * h), LANES * (j + 4 * h + 1))
            to = 2 * LANES * h
            out_ref[slot, :, at] = chunk[:, to : to + LANES].astype(BF16)
            out_ref[1 - slot, :, at] = (chunk[:, to + LANES : to + 2 * LANES] * keep).astype(BF16)


def adjoint(
    meta_ref, g_ref, core_ref, chip_ref, tail_ref, both_ref, pair_ref,
    grad_ref,
    map_ref, spread_ref,
):
    channels = g_ref.shape[1]
    width = channels // GROUPS
    lane = lane_ids(channels)
    zeros = jnp.zeros((channels, LANES), BF16)

    above = from_above(core_ref, chip_ref, slice(0, RIM_EMBED))
    below = from_below(core_ref, chip_ref, slice(0, RIM_EMBED))

    def moved(rim, at, to, size, per, i):
        at += LANES * (i // per)
        x = turn(rim[:, at : at + LANES], to - size * (i % per))
        return jnp.where(within(lane, to, to + size), x, 0.0)

    for i in range(HALO):
        x = moved(above, 0, 0, TILE, 4, i) + moved(above, RIM_CORNER, LANES - HALO, HALO, 16, i)
        map_ref[i, :channels] = x.astype(BF16)
        map_ref[i, channels:] = zeros
        at = HALO + TILE + i
        x = moved(below, 0, TILE, TILE, 4, i) + moved(below, RIM_CORNER, 2 * TILE, HALO, 16, i)
        map_ref[at, :channels] = x.astype(BF16)
        x = moved(below, RIM_SIDE, 80, TILE, 4, i)
        map_ref[at, channels:] = x.astype(BF16) + tail_ref[i]
    inner = jnp.where(lane < 2 * TILE, 1.0, 0.0).astype(BF16)
    side = jnp.where(within(lane, 72, 80), 1.0, 0.0).astype(BF16)

    def own_rows(r, carry):
        x = g_ref[r]
        map_ref[HALO + r, :channels] = x * inner
        map_ref[HALO + r, channels:] = x * side
        return carry

    lax.fori_loop(0, TILE, own_rows, 0, unroll=8)
    span = 3 * channels

    def spread_rows(i, low, high):
        x = jnp.concatenate([map_ref[2 * i], map_ref[2 * i + 1]], 1)
        y = dot(both_ref[low:high, :], x)
        spread_ref[2 * i, low:high, :] = y[:, :LANES]
        spread_ref[2 * i + 1, low:high, :] = y[:, LANES:]

    for i in range(HALO // 2):
        spread_rows(i, 2 * span, 3 * span)
        spread_rows((HALO + TILE) // 2 + i, 0, span)

    def spread_own(i, carry):
        spread_rows(HALO // 2 + i, 0, 3 * span)
        return carry

    lax.fori_loop(0, TILE // 2, spread_own, 0, unroll=4)
    spacing = [meta_ref[g] for g in range(GROUPS)]
    second = within(lane, TILE, 2 * TILE)

    def gather_row(r, carry):
        pieces = []
        for g in range(GROUPS):
            totals = []
            for v in range(3):
                total = None
                for u in range(3):
                    at = channels * (3 * u + v) + width * g
                    piece = spread_ref[r + HALO - (u - 1) * spacing[g], at : at + width, :]
                    total = piece if total is None else total + piece
                totals.append(total)
            pieces.append(
                totals[1]
                + pltpu.roll(totals[0], LANES - spacing[g], 1)
                + pltpu.roll(totals[2], spacing[g], 1)
            )
        grad = jnp.concatenate(pieces, 0)
        grad = grad + jnp.where(second, turn(grad, -48), 0.0)
        own = g_ref[r].astype(F32)
        own = own + jnp.where(pair_ref[r].astype(F32) > 0, grad, 0.0)
        grad_ref[pl.ds(pl.multiple_of(r * channels, channels), channels), :] = jnp.where(
            lane < 2 * TILE, own, 0.0
        ).astype(BF16)
        return carry

    lax.fori_loop(0, TILE, gather_row, 0, unroll=8)


def project(
    meta_ref, weight_ref, own_ref, core_ref, chip_ref, scaled_ref, grad_ref, part_ref, pair_ref,
    keep_ref, send_ref, side_ref, near_ref,
    sum_ref, kernel_ref,
):
    channels = weight_ref.shape[0]
    weight = weight_ref[...].astype(F32)
    own = own_ref[...].astype(F32)
    columns = jnp.concatenate(
        [own, unpacked(from_below(core_ref, chip_ref, slice(RIM_EMBED, RIM))), jnp.zeros((LANES - 2 * TILE, own.shape[1]), F32)], 0
    ).astype(BF16)
    weight_part = jnp.zeros_like(weight)
    local = []
    for c in range(4):
        at = slice(8 * channels * c, 8 * channels * (c + 1))
        grad_scaled = dot(grad_ref[at, :], columns)
        for i in range(8):
            one = grad_scaled[channels * i : channels * (i + 1)]
            local.append(jnp.sum(one * weight, 0, keepdims=True))
            weight_part = weight_part + one * own[8 * c + i : 8 * c + i + 1, :]
    both = dot(grad_ref[...], scaled_ref[...], TN)
    near_ref[...] = jnp.concatenate(local, 0) + both[:TILE]
    lane = lane_ids(channels)
    rim = from_above(core_ref, chip_ref, slice(0, RIM_SIDE))
    corner, ends = None, None
    for i in range(HALO):
        x = jnp.where(within(lane, TILE, TILE + HALO), pair_ref[i].astype(F32), 0.0)
        x = turn(jnp.maximum(x, 0.0), HALO * i - TILE)
        half = LANES * (i // 4)
        y = turn(rim[:, half : half + LANES], HALO * i - TILE * (i % 4) - (TILE - HALO))
        y = jnp.where(within(lane, HALO * i, HALO * (i + 1)), y, 0.0)
        corner, ends = (x, y) if i == 0 else (corner + x, ends + y)
    spacing = [meta_ref[g] for g in range(GROUPS)]
    share = dot(ends.astype(BF16), corner_shift(corner, spacing), NT)
    last = channels * (TAPS - 1)
    kernel_ref[:, :last] = part_ref[:, :last]
    kernel_ref[:, last:] = part_ref[:, last:] + share
    corner = corner[: channels // 2] + turn(corner[channels // 2 :], 8 * HALO)
    sum_ref[...] = weight_part
    rows = channels // 2
    features = own.shape[1]
    half = lax.axis_index("blk") % 2
    mine = pl.ds(pl.multiple_of(rows * half, rows), rows)
    other = pl.ds(pl.multiple_of(rows * (1 - half), rows), rows)
    keep_ref[:, :features] = sum_ref[mine, :]
    keep_ref[:, features:] = kernel_ref[mine, :]
    side = features + LANES
    for ref in (send_ref, side_ref):
        ref[:, :features] = both[TILE : 2 * TILE]
        ref[:, features:side] = corner
    send_ref[:, side : side + features] = sum_ref[other, :]
    send_ref[:, side + features :] = kernel_ref[other, :]


def finish(
    mine_ref, other_ref, core_ref, chip_ref, near_ref,
    weight_ref, kernel_ref, embed_ref,
):
    index, even, before, _ = place()
    rows = mine_ref.shape[0]
    channels = 2 * rows
    features = weight_ref.shape[1]
    half = index % 2
    for ref, which in ((mine_ref, half), (other_ref, 1 - half)):
        at = pl.ds(pl.multiple_of(rows * which, rows), rows)
        weight_ref[at, :] = ref[:, :features]
        for t in range(TAPS):
            to = features + channels * t
            kernel_ref[t, at, :] = ref[:, to : to + channels]
    carried = core_ref[:, :features] * (1.0 - even) + chip_ref[:, :features] * (even * before)
    embed_ref[...] = near_ref[...] + carried


VMEM = pl.BlockSpec(memory_space=pltpu.VMEM)
SMEM = pl.BlockSpec(memory_space=pltpu.SMEM)
HBM = pl.BlockSpec(memory_space=pltpu.HBM)


def shape(dims, kind):
    return jax.ShapeDtypeStruct(dims, kind)


def call(kernel, outs, scalars, operands, scratch=(), flops=0, moved=0, first=None, room=40):
    specs = [first or SMEM] * scalars + [VMEM] * (len(operands) - scalars)
    return pl.pallas_call(
        kernel,
        out_shape=outs,
        in_specs=specs,
        out_specs=[SMEM if out.dtype == jnp.int32 else VMEM for out in outs],
        scratch_shapes=list(scratch),
        compiler_params=pltpu.CompilerParams(vmem_limit_bytes=room * 1024 * 1024),
        cost_estimate=pl.CostEstimate(flops=flops, bytes_accessed=moved, transcendentals=0),
    )(*operands)


def swap_with(shard, step):
    return lax.ppermute(shard, "blk", [(i, i ^ step) for i in range(lax.axis_size("blk"))])


def swap_stage(shard, even, odd):
    pairs = [(i, i ^ (odd if i % 2 else even)) for i in range(lax.axis_size("blk"))]
    return lax.ppermute(shard, "blk", pairs)


def swap_chips(shard):
    count = lax.axis_size("blk")
    pairs = [(i, (i + (1 if i % 2 else -1)) % count) for i in range(count)]
    return lax.ppermute(shard, "blk", pairs)


def per_device(embed, pair_weight, conv_kernel, dilations, tile_order, cotangent):
    features = embed.shape[1]
    channels = conv_kernel.shape[0]
    count = lax.axis_size("blk")
    weight = pair_weight.T
    taps = jnp.transpose(conv_kernel, (1, 0, 2))
    cot = cotangent.reshape(2, channels, TILE * TILE)
    packed = shape((channels, RIM), BF16)
    body = shape((TILE, channels, LANES), BF16)
    to_core, to_chip = call(
        pack,
        [packed, packed],
        3,
        (tile_order, cot, embed),
        [
            pltpu.SMEM(tile_order.shape, jnp.int32),
            pltpu.VMEM(cot.shape, BF16),
            pltpu.VMEM(embed.shape, BF16),
            pltpu.SemaphoreType.DMA((3,)),
        ],
        flops=10**9,
        moved=10**6,
        first=HBM,
        room=60,
    )
    core = swap_with(to_core, 1)
    chip = swap_chips(to_chip)
    grads, dense, tail, flat, both, scaled, meta = call(
        prepare,
        [
            body,
            shape((TILE // 2, channels, LANES), BF16),
            shape((HALO, channels, LANES), BF16),
            shape((channels, TAPS * channels), BF16),
            shape((TAPS * channels, 2 * channels), BF16),
            shape((TILE * channels, features), BF16),
            shape((2 * GROUPS,), jnp.int32),
        ],
        2,
        (tile_order, dilations, cot, taps, weight, embed),
        flops=2 * 10**8,
        moved=3 * 10**6,
    )
    part, pair, rolled = call(
        forward,
        [
            shape((channels, TAPS * channels), F32),
            body,
            shape((TILE, 3 * channels, LANES), BF16),
        ],
        1,
        (meta, weight, embed, core, chip, dense, scaled),
        [pltpu.VMEM((TILE + 2 * HALO, channels, LANES), F32)],
        flops=8 * 10**8,
        moved=4 * 10**6,
    )
    (grad_pair,) = call(
        adjoint,
        [shape((TILE * channels, LANES), BF16)],
        1,
        (meta, grads, core, chip, tail, both, pair),
        [
            pltpu.VMEM((TILE + 2 * HALO, 2 * channels, LANES), BF16),
            pltpu.VMEM((TILE + 2 * HALO, TAPS * channels, LANES), F32),
        ],
        flops=8 * 10**8,
        moved=4 * 10**6,
    )
    width = features + TAPS * channels
    side = features + LANES
    total, send, sided, near = call(
        project,
        [
            shape((channels // 2, width), F32),
            shape((channels // 2, side + width), F32),
            shape((channels // 2, side), F32),
            shape((TILE, features), F32),
        ],
        1,
        (meta, weight, embed, core, chip, scaled, grad_pair, part, pair),
        [pltpu.VMEM((channels, features), F32), pltpu.VMEM((channels, TAPS * channels), F32)],
        flops=4 * 10**8,
        moved=4 * 10**6,
    )
    by_core = swap_with(send, 1)
    by_chip = swap_chips(sided)
    total = total + by_core[:, side:]
    by_core = by_core[:, :side]
    steps = [1 << b for b in range(1, count.bit_length() - 1)]
    turns = list(zip(steps[1:] + steps[:1], steps))
    for even, odd in turns[:-1]:
        total = total + swap_stage(total, even, odd)
        total, by_chip = lax.optimization_barrier((total, by_chip))
    rolled, total = lax.optimization_barrier((rolled, total))
    last = swap_stage(total, *turns[-1])
    (out,) = call(
        respond,
        [shape((2, channels, TILE * TILE), BF16)],
        1,
        (meta, flat, rolled, pair, by_core[:, features:], by_chip[:, features:]),
        [
            pltpu.VMEM((4 * channels, 4 * LANES), BF16),
            pltpu.VMEM((TILE // 2, channels, LANES), F32),
        ],
        flops=2 * 10**8,
        moved=2 * 10**6,
    )
    out, last = lax.optimization_barrier((out, last))
    total = total + last
    rest = swap_with(total, 1)
    grad_weight, grad_kernel, grad_embed = call(
        finish,
        [
            shape((channels, features), F32),
            shape((TAPS, channels, channels), F32),
            shape((TILE, features), F32),
        ],
        0,
        (total, rest, by_core, by_chip, near),
        moved=10**6,
    )
    return (
        out.reshape(1, 2, channels, TILE * TILE),
        grad_embed,
        grad_weight.T,
        jnp.transpose(grad_kernel, (1, 0, 2)),
    )


def solution(mesh):
    placed = (
        P(("grp", "blk"), None),
        P(),
        P(),
        P(),
        P(("grp", "blk"), None),
        P(("grp", "blk"), None, None, None),
    )
    return jax.shard_map(
        per_device,
        mesh=mesh,
        in_specs=placed,
        out_specs=(
            P(("grp", "blk"), None, None, None),
            P(("grp", "blk"), None),
            P("grp", None),
            P("grp", None, None),
        ),
        check_vma=False,
    )
```

```python
import jax
import jax.numpy as jnp
from jax import lax
from jax.experimental import pallas as pl
from jax.experimental.pallas import tpu as pltpu
from jax.sharding import PartitionSpec as P

GROUPS = 4
HALO = 8
TILE = 32
LANES = 128
TAPS = 9
F32 = jnp.float32
BF16 = jnp.bfloat16
NN = (((1,), (0,)), ((), ()))
NT = (((1,), (1,)), ((), ()))
TN = (((0,), (0,)), ((), ()))


def dot(a, b, dims=NN):
    return lax.dot_general(a, b, dims, preferred_element_type=F32)


def turn(x, by):
    by = by % LANES
    return x if by == 0 else pltpu.roll(x, by, 1)


def lane_ids(rows):
    return lax.broadcasted_iota(jnp.int32, (rows, LANES), 1)


def within(lane, low, high):
    return jnp.logical_and(lane >= low, lane < high)


def one_hot(target, chunks):
    lane = lane_ids(target.shape[0])
    hits = [jnp.where(target == lane + LANES * c, 1.0, 0.0).astype(BF16) for c in range(chunks)]
    return jnp.concatenate(hits, 1)


def row_ids(rows):
    return lax.broadcasted_iota(jnp.int32, (rows, LANES), 0)


def spread_table(chunks):
    x = row_ids(LANES * chunks)
    return one_hot((((x >> 5) & 3) << 7) + ((x >> 7) << 5) + (x & 31), 4)


def swap_table():
    x = row_ids(HALO * TILE)
    return one_hot(((x & 31) << 3) + (x >> 5), 2)


def edge_table():
    x = row_ids(LANES)
    return one_hot(jnp.where((x & 31) < HALO, ((x & 31) << 5) + (x >> 5), -1), 2)


def corner_table(first):
    x = row_ids(HALO * TILE)
    c = (x & 31) - first
    return one_hot(jnp.where(within(c, 0, HALO), ((x >> 5) << 3) + c, -1), 1)


def as_float(flag):
    return jnp.where(flag, 1.0, 0.0).astype(F32)


def place():
    index = lax.axis_index("blk")
    last = lax.axis_size("blk") - 1
    return index, as_float(index % 2 == 0), as_float(index > 0), as_float(index < last)


def corner_shift(flat, spacing):
    width = flat.shape[0] // GROUPS
    lane = lane_ids(width)
    pieces = []
    for g in range(GROUPS):
        d = spacing[g]
        kept = jnp.logical_and(jnp.logical_and(lane < 8 * HALO, (lane >> 3) < d), (lane & 7) < d)
        x = jnp.where(kept, flat[width * g : width * (g + 1)], 0.0)
        pieces.append(pltpu.roll(x, (HALO + 1) * (HALO - d), 1))
    return jnp.concatenate(pieces, 0).astype(BF16)


def tiles_of(order_ref, cot_ref):
    slot = order_ref[0, 0]
    _, _, _, keep = place()
    return cot_ref[slot], (cot_ref[1 - slot].astype(F32) * keep).astype(BF16)


def fetch(sources, targets, sems):
    copies = [
        pltpu.make_async_copy(source, target, sems.at[i])
        for i, (source, target) in enumerate(zip(sources, targets))
    ]
    for copy in copies:
        copy.start()
    for copy in copies:
        copy.wait()


def pack(
    order_hbm, cot_hbm, embed_hbm,
    core_ref, chip_ref,
    order_ref, cot_ref, embed_ref, sems,
):
    fetch((order_hbm, cot_hbm, embed_hbm), (order_ref, cot_ref, embed_ref), sems)
    zero, one = tiles_of(order_ref, cot_ref)
    _, even, _, _ = place()
    channels = zero.shape[0]
    moved = dot(
        jnp.concatenate([zero[:, LANES * j : LANES * (j + 1)] for j in range(8)], 0), edge_table()
    )
    columns = []
    for h in range(2):
        total = None
        for j in range(8):
            piece = moved[channels * j : channels * (j + 1), LANES * h : LANES * (h + 1)]
            piece = turn(piece, 4 * j)
            total = piece if total is None else total + piece
        columns.append(total)
    rim = HALO * TILE
    tail_at = TILE * (TILE - HALO)
    up = [zero[:, :rim].astype(F32)] + columns + [dot(one[:, :rim], corner_table(0))]
    down = [one[:, tail_at:].astype(F32)] + [jnp.zeros_like(x) for x in columns]
    down += [dot(zero[:, tail_at:], corner_table(TILE - HALO))]
    up, down = jnp.concatenate(up, 1), jnp.concatenate(down, 1)
    width = up.shape[1]
    both = jnp.concatenate([embed_ref[:, :LANES], embed_ref[:, LANES:]], 0)
    core_ref[:, :width] = (down * even + up * (1.0 - even)).astype(BF16)
    core_ref[:, width:] = both
    chip_ref[:, :width] = (up * even + down * (1.0 - even)).astype(BF16)
    chip_ref[:, width:] = both


RIM_SIDE, RIM_CORNER, RIM_EMBED, RIM = 256, 512, 640, 768


def from_above(core_ref, chip_ref, at):
    _, even, before, _ = place()
    x = chip_ref[:, at].astype(F32) * (even * before)
    return x + core_ref[:, at].astype(F32) * ((1.0 - even) * before)


def from_below(core_ref, chip_ref, at):
    _, even, _, after = place()
    x = core_ref[:, at].astype(F32) * (even * after)
    return x + chip_ref[:, at].astype(F32) * ((1.0 - even) * after)


def prepare(
    order_ref, dil_ref, cot_ref, kern_ref, weight_ref, embed_ref,
    g_ref, dense_ref, tail_ref, flat_ref, both_ref, scaled_ref, spread_ref, meta_ref,
):
    for g in range(GROUPS):
        meta_ref[g] = jnp.left_shift(jnp.int32(1), dil_ref[g])
    meta_ref[GROUPS] = order_ref[0, 0]
    zero, one = tiles_of(order_ref, cot_ref)
    channels = kern_ref.shape[1]
    swap = swap_table()
    tail_at = TILE * (TILE - HALO)
    y_zero = dot(zero[:, tail_at:], swap)
    y_one = dot(one[:, tail_at:], swap)
    lane = lane_ids(channels)
    own_side = within(lane, 72, 80)
    low = lane < 2 * TILE
    pieces = []
    for j in range(4):
        at = slice(LANES * j, LANES * (j + 1))
        later = slice(LANES * (j + 4), LANES * (j + 5))
        pieces.append(
            jnp.concatenate([zero[:, at], one[:, at], zero[:, later], one[:, later]], 1)
        )
    rows = dot(jnp.concatenate(pieces, 0), spread_table(4))
    for j in range(4):
        for m in range(4):
            row = rows[channels * j : channels * (j + 1), LANES * m : LANES * (m + 1)]
            dense_ref[4 * j + m] = row.astype(BF16)
            for h in range(2):
                r = 16 * h + 4 * j + m
                side = turn(y_zero[:, LANES * h : LANES * (h + 1)], 72 - 8 * (r % 16))
                side = jnp.where(own_side, side, 0.0)
                g_ref[r] = jnp.where(low, turn(row, 64 * h), side).astype(BF16)
    for i in range(HALO):
        rest = turn(y_one[:, :LANES], 72 - 8 * i)
        tail_ref[i] = jnp.where(own_side, rest, 0.0).astype(BF16)
    eye = (
        lax.broadcasted_iota(jnp.int32, (channels, channels), 0)
        == lax.broadcasted_iota(jnp.int32, (channels, channels), 1)
    )
    eye = jnp.where(eye, 1.0, 0.0).astype(BF16)
    for u in range(3):
        for v in range(3):
            t = 3 * u + v
            pair = jnp.concatenate([kern_ref[t], kern_ref[3 * v + u]], 0)
            both_ref[channels * t : channels * (t + 1), :] = dot(eye, pair, NT).astype(BF16)
    for t in range(0, TAPS - 1, 2):
        flat_ref[:, channels * t : channels * (t + 2)] = jnp.concatenate(
            [kern_ref[t].astype(F32), kern_ref[t + 1].astype(F32)], 1
        ).astype(BF16)
    flat_ref[:, channels * (TAPS - 1) : channels * TAPS] = kern_ref[TAPS - 1]
    weight = weight_ref[...].astype(F32)
    own = embed_ref[...].astype(F32)
    for r in range(TILE):
        scaled_ref[channels * r : channels * (r + 1), :] = (own[r : r + 1, :] * weight).astype(
            BF16
        )
    inner = jnp.where(lane < 2 * TILE, 1.0, 0.0).astype(BF16)
    beside = jnp.where(own_side, 1.0, 0.0).astype(BF16)

    def spread_rows(i, carry):
        x = jnp.concatenate([g_ref[2 * i], g_ref[2 * i + 1]], 1)
        y = jnp.concatenate([inner, inner], 1), jnp.concatenate([beside, beside], 1)
        y = dot(both_ref[...], jnp.concatenate([x * y[0], x * y[1]], 0))
        spread_ref[2 * i] = y[:, :LANES]
        spread_ref[2 * i + 1] = y[:, LANES:]
        return carry

    lax.fori_loop(0, TILE // 2, spread_rows, 0, unroll=2)


def unpacked(x):
    return jnp.concatenate([x[:TILE], x[TILE:]], 1)


def forward(
    meta_ref, weight_ref, own_ref, core_ref, chip_ref, dense_ref, scaled_ref,
    part_ref, pair_ref, rolled_ref,
    map_ref,
):
    channels = weight_ref.shape[0]
    width = channels // GROUPS
    weight = weight_ref[...].astype(F32)
    own = own_ref[...].astype(F32)
    after = unpacked(from_below(core_ref, chip_ref, slice(RIM_EMBED, RIM)))
    before = unpacked(from_above(core_ref, chip_ref, slice(RIM_EMBED, RIM)))[TILE - HALO :]
    filler = jnp.zeros((LANES - 2 * TILE - HALO, own.shape[1]), F32)
    columns = jnp.concatenate([own, after, filler, before], 0).astype(BF16)
    lane = lane_ids(channels)
    kept = (
        jnp.logical_or(lane < TILE, lane >= LANES - HALO),
        lane < 2 * TILE,
        within(lane, TILE, 2 * TILE),
    )
    for c in range(6):
        part = 0 if c == 0 else (2 if c == 5 else 1)
        if part == 1:
            scaled = scaled_ref[8 * channels * (c - 1) : 8 * channels * c, :]
        else:
            rim = before if part == 0 else after
            scaled = jnp.concatenate(
                [(rim[i : i + 1, :] * weight).astype(BF16) for i in range(HALO)], 0
            )
        pair = dot(scaled, columns, NT).astype(BF16)
        for i in range(8):
            one = pair[channels * i : channels * (i + 1)]
            if part == 1:
                pair_ref[8 * (c - 1) + i] = one
            map_ref[8 * c + i] = jnp.where(kept[part], jnp.maximum(one.astype(F32), 0.0), 0.0)
    swap = swap_table()

    def gathered(first, per, low, high, move):
        halves = []
        for half in range(2):
            total = None
            for m in range(per):
                piece = jnp.where(within(lane, low, high), map_ref[first + per * half + m], 0.0)
                piece = turn(piece, move(m))
                total = piece if total is None else total + piece
            halves.append(total.astype(BF16))
        return jnp.concatenate(halves, 1)

    above = dot(gathered(0, 4, 0, TILE, lambda m: TILE * m), swap)
    below = dot(gathered(8, 16, TILE, TILE + HALO, lambda m: HALO * m - TILE), swap, NT)
    for r in range(TILE):
        half = LANES * (r // 16)
        side = turn(above[:, half : half + LANES], LANES - HALO - HALO * (r % 16))
        map_ref[HALO + r] += jnp.where(lane >= LANES - HALO, side, 0.0)
    for i in range(HALO):
        half = LANES * (i // 4)
        side = turn(below[:, half : half + LANES], -TILE * (i % 4))
        map_ref[HALO + TILE + i] += jnp.where(lane < TILE, side, 0.0)

    spacing = [meta_ref[g] for g in range(GROUPS)]
    left = lane_ids(width) < 2 * TILE

    def roll_row(i, carry):
        for g in range(GROUPS):
            at = width * g
            x = map_ref[i, at : at + width, :]
            y = turn(map_ref[i + 16, at : at + width, :], 2 * TILE)
            for v, by in enumerate((spacing[g], None, LANES - spacing[g])):
                one, two = (x, y) if by is None else (pltpu.roll(x, by, 1), pltpu.roll(y, by, 1))
                to = channels * v + at
                rolled_ref[i, to : to + width, :] = jnp.where(left, one, two).astype(BF16)
        return carry

    lax.fori_loop(0, TILE, roll_row, 0, unroll=4)

    part_ref[...] = jnp.zeros_like(part_ref)

    def sum_rows(j, carry):
        stack = jnp.concatenate([taps_of(rolled_ref, spacing, 2 * j + m) for m in range(2)], 1)
        grads = jnp.concatenate([dense_ref[2 * j], dense_ref[2 * j + 1]], 1)
        part_ref[...] += dot(grads, stack, NT)
        return carry

    lax.fori_loop(0, 8, sum_rows, 0, unroll=2)


def taps_of(rolled_ref, spacing, r):
    channels = rolled_ref.shape[1] // 3
    width = channels // GROUPS
    pieces = []
    for u in range(3):
        for v in range(3):
            for g in range(GROUPS):
                at = channels * v + width * g
                pieces.append(rolled_ref[r + HALO + (u - 1) * spacing[g], at : at + width, :])
    return jnp.concatenate(pieces, 0)


def respond(
    meta_ref, flat_ref, rolled_ref, pair_ref, core_ref, chip_ref,
    out_ref,
    rows_ref, share_ref,
):
    channels = flat_ref.shape[0]
    spacing = [meta_ref[g] for g in range(GROUPS)]
    lane = lane_ids(channels)
    low = lane < 2 * TILE
    _, even, _, keep = place()
    corner = core_ref[...] * even + chip_ref[...] * ((1.0 - even) * keep)
    corner = jnp.concatenate([corner, turn(corner, 8 * HALO)], 0)
    share = dot(flat_ref[:, channels * (TAPS - 1) :], corner_shift(corner, spacing))
    share_ref[:HALO] = jnp.zeros((HALO, channels, LANES), F32)
    for i in range(HALO):
        share_ref[HALO + i] = jnp.where(
            lane >= LANES - HALO, turn(share, LANES - HALO - HALO * i), 0.0
        )

    def conv_rows(j, carry):
        for h in range(2):
            r = 4 * j + 2 * h
            stack = jnp.concatenate([taps_of(rolled_ref, spacing, r + m) for m in range(2)], 1)
            response = dot(flat_ref[...], stack)
            for m in range(2):
                row = jnp.where(
                    low,
                    pair_ref[r + m].astype(F32),
                    turn(pair_ref[r + m + 16].astype(F32), 2 * TILE),
                )
                row = row + (response[:, LANES * m : LANES * (m + 1)] + share_ref[r + m])
                at = LANES * (2 * h + m)
                to = pl.ds(pl.multiple_of(channels * j, channels), channels)
                rows_ref[to, at : at + LANES] = row.astype(BF16)
        return carry

    lax.fori_loop(0, 4, conv_rows, 0)
    slot = meta_ref[GROUPS]
    chunks = dot(rows_ref[...], spread_table(4), NT)
    for j in range(4):
        chunk = chunks[channels * j : channels * (j + 1)]
        for h in range(2):
            at = slice(LANES * (j + 4 * h), LANES * (j + 4 * h + 1))
            to = 2 * LANES * h
            out_ref[slot, :, at] = chunk[:, to : to + LANES].astype(BF16)
            out_ref[1 - slot, :, at] = (chunk[:, to + LANES : to + 2 * LANES] * keep).astype(BF16)


def adjoint(
    meta_ref, g_ref, core_ref, chip_ref, tail_ref, both_ref, pair_ref, spread_ref,
    grad_ref,
    above_ref, below_ref,
):
    channels = g_ref.shape[1]
    width = channels // GROUPS
    span = 3 * channels
    lane = lane_ids(channels)
    zeros = jnp.zeros((channels, LANES), BF16)
    above = from_above(core_ref, chip_ref, slice(0, RIM_EMBED))
    below = from_below(core_ref, chip_ref, slice(0, RIM_EMBED))

    def moved(rim, at, to, size, per, i):
        at += LANES * (i // per)
        x = turn(rim[:, at : at + LANES], to - size * (i % per))
        return jnp.where(within(lane, to, to + size), x, 0.0)

    for h in range(HALO // 2):
        upper, lower = [], []
        for i in (2 * h, 2 * h + 1):
            x = moved(above, 0, 0, TILE, 4, i)
            x = x + moved(above, RIM_CORNER, LANES - HALO, HALO, 16, i)
            upper.append(jnp.concatenate([x.astype(BF16), zeros], 0))
            x = moved(below, 0, TILE, TILE, 4, i)
            x = x + moved(below, RIM_CORNER, 2 * TILE, HALO, 16, i)
            y = moved(below, RIM_SIDE, 80, TILE, 4, i).astype(BF16) + tail_ref[i]
            lower.append(jnp.concatenate([x.astype(BF16), y], 0))
        x = dot(both_ref[2 * span :, :], jnp.concatenate(upper, 1))
        y = dot(both_ref[:span, :], jnp.concatenate(lower, 1))
        for m in range(2):
            above_ref[2 * h + m] = x[:, LANES * m : LANES * (m + 1)]
            below_ref[2 * h + m] = y[:, LANES * m : LANES * (m + 1)]
    spacing = [meta_ref[g] for g in range(GROUPS)]
    second = within(lane, TILE, 2 * TILE)

    def gather_row(first, edge):
        def body(i, carry):
            r = first + i
            pieces = []
            for g in range(GROUPS):
                totals = []
                for v in range(3):
                    at = channels * v + width * g
                    tap = slice(at, at + width)
                    total = spread_ref[r, span + at : span + at + width, :]
                    up, down = r - spacing[g], r + spacing[g]
                    if edge < 0:
                        x = spread_ref[jnp.maximum(up, 0), 2 * span + at : 2 * span + at + width, :]
                        y = above_ref[jnp.minimum(up + HALO, HALO - 1), tap, :]
                        total = total + jnp.where(up < 0, y, x)
                    else:
                        total = total + spread_ref[up, 2 * span + at : 2 * span + at + width, :]
                    if edge > 0:
                        x = spread_ref[jnp.minimum(down, TILE - 1), tap, :]
                        y = below_ref[jnp.maximum(down - TILE, 0), tap, :]
                        total = total + jnp.where(down >= TILE, y, x)
                    else:
                        total = total + spread_ref[down, tap, :]
                    totals.append(total)
                pieces.append(
                    totals[1]
                    + pltpu.roll(totals[0], LANES - spacing[g], 1)
                    + pltpu.roll(totals[2], spacing[g], 1)
                )
            grad = jnp.concatenate(pieces, 0)
            grad = grad + jnp.where(second, turn(grad, -48), 0.0)
            own = g_ref[r].astype(F32)
            own = own + jnp.where(pair_ref[r].astype(F32) > 0, grad, 0.0)
            grad_ref[pl.ds(pl.multiple_of(r * channels, channels), channels), :] = jnp.where(
                lane < 2 * TILE, own, 0.0
            ).astype(BF16)
            return carry

        return body

    lax.fori_loop(0, HALO, gather_row(0, -1), 0, unroll=4)
    lax.fori_loop(0, TILE - 2 * HALO, gather_row(HALO, 0), 0, unroll=4)
    lax.fori_loop(0, HALO, gather_row(TILE - HALO, 1), 0, unroll=4)


def project(
    meta_ref, weight_ref, own_ref, core_ref, chip_ref, scaled_ref, grad_ref, part_ref, pair_ref,
    keep_ref, send_ref, side_ref, near_ref,
    sum_ref, kernel_ref,
):
    channels = weight_ref.shape[0]
    weight = weight_ref[...].astype(F32)
    own = own_ref[...].astype(F32)
    columns = jnp.concatenate(
        [own, unpacked(from_below(core_ref, chip_ref, slice(RIM_EMBED, RIM))), jnp.zeros((LANES - 2 * TILE, own.shape[1]), F32)], 0
    ).astype(BF16)
    weight_part = jnp.zeros_like(weight)
    local = []
    for c in range(4):
        at = slice(8 * channels * c, 8 * channels * (c + 1))
        grad_scaled = dot(grad_ref[at, :], columns)
        for i in range(8):
            one = grad_scaled[channels * i : channels * (i + 1)]
            local.append(jnp.sum(one * weight, 0, keepdims=True))
            weight_part = weight_part + one * own[8 * c + i : 8 * c + i + 1, :]
    both = dot(grad_ref[...], scaled_ref[...], TN)
    near_ref[...] = jnp.concatenate(local, 0) + both[:TILE]
    lane = lane_ids(channels)
    rim = from_above(core_ref, chip_ref, slice(0, RIM_SIDE))
    corner, ends = None, None
    for i in range(HALO):
        x = jnp.where(within(lane, TILE, TILE + HALO), pair_ref[i].astype(F32), 0.0)
        x = turn(jnp.maximum(x, 0.0), HALO * i - TILE)
        half = LANES * (i // 4)
        y = turn(rim[:, half : half + LANES], HALO * i - TILE * (i % 4) - (TILE - HALO))
        y = jnp.where(within(lane, HALO * i, HALO * (i + 1)), y, 0.0)
        corner, ends = (x, y) if i == 0 else (corner + x, ends + y)
    spacing = [meta_ref[g] for g in range(GROUPS)]
    share = dot(ends.astype(BF16), corner_shift(corner, spacing), NT)
    last = channels * (TAPS - 1)
    kernel_ref[:, :last] = part_ref[:, :last]
    kernel_ref[:, last:] = part_ref[:, last:] + share
    corner = corner[: channels // 2] + turn(corner[channels // 2 :], 8 * HALO)
    sum_ref[...] = weight_part
    rows = channels // 2
    features = own.shape[1]
    half = lax.axis_index("blk") % 2
    mine = pl.ds(pl.multiple_of(rows * half, rows), rows)
    other = pl.ds(pl.multiple_of(rows * (1 - half), rows), rows)
    keep_ref[:, :features] = sum_ref[mine, :]
    keep_ref[:, features:] = kernel_ref[mine, :]
    side = features + LANES
    for ref in (send_ref, side_ref):
        ref[:, :features] = both[TILE : 2 * TILE]
        ref[:, features:side] = corner
    send_ref[:, side : side + features] = sum_ref[other, :]
    send_ref[:, side + features :] = kernel_ref[other, :]


def finish(
    mine_ref, other_ref, core_ref, chip_ref, near_ref,
    weight_ref, kernel_ref, embed_ref,
):
    index, even, before, _ = place()
    rows = mine_ref.shape[0]
    channels = 2 * rows
    features = weight_ref.shape[1]
    half = index % 2
    for ref, which in ((mine_ref, half), (other_ref, 1 - half)):
        at = pl.ds(pl.multiple_of(rows * which, rows), rows)
        weight_ref[at, :] = ref[:, :features]
        for t in range(TAPS):
            to = features + channels * t
            kernel_ref[t, at, :] = ref[:, to : to + channels]
    carried = core_ref[:, :features] * (1.0 - even) + chip_ref[:, :features] * (even * before)
    embed_ref[...] = near_ref[...] + carried


VMEM = pl.BlockSpec(memory_space=pltpu.VMEM)
SMEM = pl.BlockSpec(memory_space=pltpu.SMEM)
HBM = pl.BlockSpec(memory_space=pltpu.HBM)


def shape(dims, kind):
    return jax.ShapeDtypeStruct(dims, kind)


def call(kernel, outs, scalars, operands, scratch=(), flops=0, moved=0, first=None, room=40):
    specs = [first or SMEM] * scalars + [VMEM] * (len(operands) - scalars)
    return pl.pallas_call(
        kernel,
        out_shape=outs,
        in_specs=specs,
        out_specs=[SMEM if out.dtype == jnp.int32 else VMEM for out in outs],
        scratch_shapes=list(scratch),
        compiler_params=pltpu.CompilerParams(vmem_limit_bytes=room * 1024 * 1024),
        cost_estimate=pl.CostEstimate(flops=flops, bytes_accessed=moved, transcendentals=0),
    )(*operands)


def swap_with(shard, step):
    return lax.ppermute(shard, "blk", [(i, i ^ step) for i in range(lax.axis_size("blk"))])


def swap_stage(shard, even, odd):
    pairs = [(i, i ^ (odd if i % 2 else even)) for i in range(lax.axis_size("blk"))]
    return lax.ppermute(shard, "blk", pairs)


def swap_chips(shard):
    count = lax.axis_size("blk")
    pairs = [(i, (i + (1 if i % 2 else -1)) % count) for i in range(count)]
    return lax.ppermute(shard, "blk", pairs)


def per_device(embed, pair_weight, conv_kernel, dilations, tile_order, cotangent):
    features = embed.shape[1]
    channels = conv_kernel.shape[0]
    count = lax.axis_size("blk")
    weight = pair_weight.T
    taps = jnp.transpose(conv_kernel, (1, 0, 2))
    cot = cotangent.reshape(2, channels, TILE * TILE)
    packed = shape((channels, RIM), BF16)
    body = shape((TILE, channels, LANES), BF16)
    to_core, to_chip = call(
        pack,
        [packed, packed],
        3,
        (tile_order, cot, embed),
        [
            pltpu.SMEM(tile_order.shape, jnp.int32),
            pltpu.VMEM(cot.shape, BF16),
            pltpu.VMEM(embed.shape, BF16),
            pltpu.SemaphoreType.DMA((3,)),
        ],
        flops=10**10,
        moved=10**6,
        first=HBM,
        room=60,
    )
    core = swap_with(to_core, 1)
    chip = swap_chips(to_chip)
    grads, dense, tail, flat, both, scaled, spread, meta = call(
        prepare,
        [
            body,
            shape((TILE // 2, channels, LANES), BF16),
            shape((HALO, channels, LANES), BF16),
            shape((channels, TAPS * channels), BF16),
            shape((TAPS * channels, 2 * channels), BF16),
            shape((TILE * channels, features), BF16),
            shape((TILE, TAPS * channels, LANES), F32),
            shape((2 * GROUPS,), jnp.int32),
        ],
        2,
        (tile_order, dilations, cot, taps, weight, embed),
        flops=2 * 10**8,
        moved=3 * 10**6,
    )
    part, pair, rolled = call(
        forward,
        [
            shape((channels, TAPS * channels), F32),
            body,
            shape((TILE, 3 * channels, LANES), BF16),
        ],
        1,
        (meta, weight, embed, core, chip, dense, scaled),
        [pltpu.VMEM((TILE + 2 * HALO, channels, LANES), F32)],
        flops=8 * 10**8,
        moved=4 * 10**6,
    )
    (grad_pair,) = call(
        adjoint,
        [shape((TILE * channels, LANES), BF16)],
        1,
        (meta, grads, core, chip, tail, both, pair, spread),
        [pltpu.VMEM((HALO, 3 * channels, LANES), F32)] * 2,
        flops=8 * 10**8,
        moved=4 * 10**6,
    )
    width = features + TAPS * channels
    side = features + LANES
    total, send, sided, near = call(
        project,
        [
            shape((channels // 2, width), F32),
            shape((channels // 2, side + width), F32),
            shape((channels // 2, side), F32),
            shape((TILE, features), F32),
        ],
        1,
        (meta, weight, embed, core, chip, scaled, grad_pair, part, pair),
        [pltpu.VMEM((channels, features), F32), pltpu.VMEM((channels, TAPS * channels), F32)],
        flops=4 * 10**8,
        moved=4 * 10**6,
    )
    by_core = swap_with(send, 1)
    by_chip = swap_chips(sided)
    total = total + by_core[:, side:]
    by_core = by_core[:, :side]
    steps = [1 << b for b in range(1, count.bit_length() - 1)]
    turns = list(zip(steps[1:] + steps[:1], steps))
    for even, odd in turns[:-1]:
        total = total + swap_stage(total, even, odd)
    rolled, total, by_chip = lax.optimization_barrier((rolled, total, by_chip))
    last = swap_stage(total, *turns[-1])
    (out,) = call(
        respond,
        [shape((2, channels, TILE * TILE), BF16)],
        1,
        (meta, flat, rolled, pair, by_core[:, features:], by_chip[:, features:]),
        [
            pltpu.VMEM((4 * channels, 4 * LANES), BF16),
            pltpu.VMEM((TILE // 2, channels, LANES), F32),
        ],
        flops=2 * 10**8,
        moved=2 * 10**6,
    )
    out, last = lax.optimization_barrier((out, last))
    total = total + last
    rest = swap_with(total, 1)
    grad_weight, grad_kernel, grad_embed = call(
        finish,
        [
            shape((channels, features), F32),
            shape((TAPS, channels, channels), F32),
            shape((TILE, features), F32),
        ],
        0,
        (total, rest, by_core, by_chip, near),
        moved=10**6,
    )
    return (
        out.reshape(1, 2, channels, TILE * TILE),
        grad_embed,
        grad_weight.T,
        jnp.transpose(grad_kernel, (1, 0, 2)),
    )


def solution(mesh):
    placed = (
        P(("grp", "blk"), None),
        P(),
        P(),
        P(),
        P(("grp", "blk"), None),
        P(("grp", "blk"), None, None, None),
    )
    return jax.shard_map(
        per_device,
        mesh=mesh,
        in_specs=placed,
        out_specs=(
            P(("grp", "blk"), None, None, None),
            P(("grp", "blk"), None),
            P("grp", None),
            P("grp", None, None),
        ),
        check_vma=False,
    )
```

```python
import jax
import jax.numpy as jnp
from jax import lax
from jax.experimental import pallas as pl
from jax.experimental.pallas import tpu as pltpu
from jax.sharding import PartitionSpec as P

GROUPS = 4
HALO = 8
TILE = 32
LANES = 128
TAPS = 9
F32 = jnp.float32
BF16 = jnp.bfloat16
NN = (((1,), (0,)), ((), ()))
NT = (((1,), (1,)), ((), ()))
TN = (((0,), (0,)), ((), ()))


def dot(a, b, dims=NN):
    return lax.dot_general(a, b, dims, preferred_element_type=F32)


def turn(x, by):
    by = by % LANES
    return x if by == 0 else pltpu.roll(x, by, 1)


def lane_ids(rows):
    return lax.broadcasted_iota(jnp.int32, (rows, LANES), 1)


def within(lane, low, high):
    return jnp.logical_and(lane >= low, lane < high)


def one_hot(target, chunks):
    lane = lane_ids(target.shape[0])
    hits = [jnp.where(target == lane + LANES * c, 1.0, 0.0).astype(BF16) for c in range(chunks)]
    return jnp.concatenate(hits, 1)


def row_ids(rows):
    return lax.broadcasted_iota(jnp.int32, (rows, LANES), 0)


def spread_table(chunks):
    x = row_ids(LANES * chunks)
    return one_hot((((x >> 5) & 3) << 7) + ((x >> 7) << 5) + (x & 31), 4)


def swap_table():
    x = row_ids(HALO * TILE)
    return one_hot(((x & 31) << 3) + (x >> 5), 2)


def edge_table():
    x = row_ids(LANES)
    return one_hot(jnp.where((x & 31) < HALO, ((x & 31) << 5) + (x >> 5), -1), 2)


def corner_table(first):
    x = row_ids(HALO * TILE)
    c = (x & 31) - first
    return one_hot(jnp.where(within(c, 0, HALO), ((x >> 5) << 3) + c, -1), 1)


def as_float(flag):
    return jnp.where(flag, 1.0, 0.0).astype(F32)


def place():
    index = lax.axis_index("blk")
    last = lax.axis_size("blk") - 1
    return index, as_float(index % 2 == 0), as_float(index > 0), as_float(index < last)


def half_of(index):
    return (index + index // 2) % 2


def corner_shift(flat, spacing):
    width = flat.shape[0] // GROUPS
    lane = lane_ids(width)
    pieces = []
    for g in range(GROUPS):
        d = spacing[g]
        kept = jnp.logical_and(jnp.logical_and(lane < 8 * HALO, (lane >> 3) < d), (lane & 7) < d)
        x = jnp.where(kept, flat[width * g : width * (g + 1)], 0.0)
        pieces.append(pltpu.roll(x, (HALO + 1) * (HALO - d), 1))
    return jnp.concatenate(pieces, 0).astype(BF16)


def tiles_of(order_ref, cot_ref):
    slot = order_ref[0, 0]
    _, _, _, keep = place()
    return cot_ref[slot], (cot_ref[1 - slot].astype(F32) * keep).astype(BF16)


def fetch(sources, targets, sems):
    copies = [
        pltpu.make_async_copy(source, target, sems.at[i])
        for i, (source, target) in enumerate(zip(sources, targets))
    ]
    for copy in copies:
        copy.start()
    for copy in copies:
        copy.wait()


def pack(
    order_hbm, cot_hbm, embed_hbm,
    core_ref, chip_ref,
    order_ref, cot_ref, embed_ref, sems,
):
    fetch((order_hbm, cot_hbm, embed_hbm), (order_ref, cot_ref, embed_ref), sems)
    zero, one = tiles_of(order_ref, cot_ref)
    _, even, _, _ = place()
    channels = zero.shape[0]
    moved = dot(
        jnp.concatenate([zero[:, LANES * j : LANES * (j + 1)] for j in range(8)], 0), edge_table()
    )
    columns = []
    for h in range(2):
        total = None
        for j in range(8):
            piece = moved[channels * j : channels * (j + 1), LANES * h : LANES * (h + 1)]
            piece = turn(piece, 4 * j)
            total = piece if total is None else total + piece
        columns.append(total)
    rim = HALO * TILE
    tail_at = TILE * (TILE - HALO)
    up = [zero[:, :rim].astype(F32)] + columns + [dot(one[:, :rim], corner_table(0))]
    down = [one[:, tail_at:].astype(F32)] + [jnp.zeros_like(x) for x in columns]
    down += [dot(zero[:, tail_at:], corner_table(TILE - HALO))]
    up, down = jnp.concatenate(up, 1), jnp.concatenate(down, 1)
    width = up.shape[1]
    both = jnp.concatenate([embed_ref[:, :LANES], embed_ref[:, LANES:]], 0)
    core_ref[:, :width] = (down * even + up * (1.0 - even)).astype(BF16)
    core_ref[:, width:] = both
    chip_ref[:, :width] = (up * even + down * (1.0 - even)).astype(BF16)
    chip_ref[:, width:] = both


RIM_SIDE, RIM_CORNER, RIM_EMBED, RIM = 256, 512, 640, 768


def from_above(core_ref, chip_ref, at):
    _, even, before, _ = place()
    x = chip_ref[:, at].astype(F32) * (even * before)
    return x + core_ref[:, at].astype(F32) * ((1.0 - even) * before)


def from_below(core_ref, chip_ref, at):
    _, even, _, after = place()
    x = core_ref[:, at].astype(F32) * (even * after)
    return x + chip_ref[:, at].astype(F32) * ((1.0 - even) * after)


def prepare(
    order_ref, dil_ref, cot_ref, kern_ref, weight_ref, embed_ref,
    g_ref, dense_ref, tail_ref, flat_ref, both_ref, scaled_ref, spread_ref, meta_ref,
):
    for g in range(GROUPS):
        meta_ref[g] = jnp.left_shift(jnp.int32(1), dil_ref[g])
    meta_ref[GROUPS] = order_ref[0, 0]
    zero, one = tiles_of(order_ref, cot_ref)
    channels = kern_ref.shape[1]
    swap = swap_table()
    tail_at = TILE * (TILE - HALO)
    y_zero = dot(zero[:, tail_at:], swap)
    y_one = dot(one[:, tail_at:], swap)
    lane = lane_ids(channels)
    own_side = within(lane, 72, 80)
    low = lane < 2 * TILE
    pieces = []
    for j in range(4):
        at = slice(LANES * j, LANES * (j + 1))
        later = slice(LANES * (j + 4), LANES * (j + 5))
        pieces.append(
            jnp.concatenate([zero[:, at], one[:, at], zero[:, later], one[:, later]], 1)
        )
    rows = dot(jnp.concatenate(pieces, 0), spread_table(4))
    for j in range(4):
        for m in range(4):
            row = rows[channels * j : channels * (j + 1), LANES * m : LANES * (m + 1)]
            dense_ref[4 * j + m] = row.astype(BF16)
            for h in range(2):
                r = 16 * h + 4 * j + m
                side = turn(y_zero[:, LANES * h : LANES * (h + 1)], 72 - 8 * (r % 16))
                side = jnp.where(own_side, side, 0.0)
                g_ref[r] = jnp.where(low, turn(row, 64 * h), side).astype(BF16)
    for i in range(HALO):
        rest = turn(y_one[:, :LANES], 72 - 8 * i)
        tail_ref[i] = jnp.where(own_side, rest, 0.0).astype(BF16)
    eye = (
        lax.broadcasted_iota(jnp.int32, (channels, channels), 0)
        == lax.broadcasted_iota(jnp.int32, (channels, channels), 1)
    )
    eye = jnp.where(eye, 1.0, 0.0).astype(BF16)
    for u in range(3):
        for v in range(3):
            t = 3 * u + v
            pair = jnp.concatenate([kern_ref[t], kern_ref[3 * v + u]], 0)
            both_ref[channels * t : channels * (t + 1), :] = dot(eye, pair, NT).astype(BF16)
    for t in range(0, TAPS - 1, 2):
        flat_ref[:, channels * t : channels * (t + 2)] = jnp.concatenate(
            [kern_ref[t].astype(F32), kern_ref[t + 1].astype(F32)], 1
        ).astype(BF16)
    flat_ref[:, channels * (TAPS - 1) : channels * TAPS] = kern_ref[TAPS - 1]
    weight = weight_ref[...].astype(F32)
    own = embed_ref[...].astype(F32)
    for r in range(TILE):
        scaled_ref[channels * r : channels * (r + 1), :] = (own[r : r + 1, :] * weight).astype(
            BF16
        )
    inner = jnp.where(lane < 2 * TILE, 1.0, 0.0).astype(BF16)
    beside = jnp.where(own_side, 1.0, 0.0).astype(BF16)

    def spread_rows(i, carry):
        x = jnp.concatenate([g_ref[2 * i], g_ref[2 * i + 1]], 1)
        y = jnp.concatenate([inner, inner], 1), jnp.concatenate([beside, beside], 1)
        y = dot(both_ref[...], jnp.concatenate([x * y[0], x * y[1]], 0))
        spread_ref[2 * i] = y[:, :LANES]
        spread_ref[2 * i + 1] = y[:, LANES:]
        return carry

    lax.fori_loop(0, TILE // 2, spread_rows, 0)


def unpacked(x):
    return jnp.concatenate([x[:TILE], x[TILE:]], 1)


def forward(
    meta_ref, weight_ref, own_ref, core_ref, chip_ref, dense_ref, scaled_ref,
    part_ref, pair_ref, rolled_ref,
    map_ref,
):
    channels = weight_ref.shape[0]
    width = channels // GROUPS
    weight = weight_ref[...].astype(F32)
    own = own_ref[...].astype(F32)
    after = unpacked(from_below(core_ref, chip_ref, slice(RIM_EMBED, RIM)))
    before = unpacked(from_above(core_ref, chip_ref, slice(RIM_EMBED, RIM)))[TILE - HALO :]
    filler = jnp.zeros((LANES - 2 * TILE - HALO, own.shape[1]), F32)
    columns = jnp.concatenate([own, after, filler, before], 0).astype(BF16)
    lane = lane_ids(channels)
    kept = (
        jnp.logical_or(lane < TILE, lane >= LANES - HALO),
        lane < 2 * TILE,
        within(lane, TILE, 2 * TILE),
    )
    for c in range(6):
        part = 0 if c == 0 else (2 if c == 5 else 1)
        if part == 1:
            scaled = scaled_ref[8 * channels * (c - 1) : 8 * channels * c, :]
        else:
            rim = before if part == 0 else after
            scaled = jnp.concatenate(
                [(rim[i : i + 1, :] * weight).astype(BF16) for i in range(HALO)], 0
            )
        pair = dot(scaled, columns, NT).astype(BF16)
        for i in range(8):
            one = pair[channels * i : channels * (i + 1)]
            if part == 1:
                pair_ref[8 * (c - 1) + i] = one
            map_ref[8 * c + i] = jnp.where(kept[part], jnp.maximum(one.astype(F32), 0.0), 0.0)
    swap = swap_table()

    def gathered(first, per, low, high, move):
        halves = []
        for half in range(2):
            total = None
            for m in range(per):
                piece = jnp.where(within(lane, low, high), map_ref[first + per * half + m], 0.0)
                piece = turn(piece, move(m))
                total = piece if total is None else total + piece
            halves.append(total.astype(BF16))
        return jnp.concatenate(halves, 1)

    above = dot(gathered(0, 4, 0, TILE, lambda m: TILE * m), swap)
    below = dot(gathered(8, 16, TILE, TILE + HALO, lambda m: HALO * m - TILE), swap, NT)
    for r in range(TILE):
        half = LANES * (r // 16)
        side = turn(above[:, half : half + LANES], LANES - HALO - HALO * (r % 16))
        map_ref[HALO + r] += jnp.where(lane >= LANES - HALO, side, 0.0)
    for i in range(HALO):
        half = LANES * (i // 4)
        side = turn(below[:, half : half + LANES], -TILE * (i % 4))
        map_ref[HALO + TILE + i] += jnp.where(lane < TILE, side, 0.0)

    spacing = [meta_ref[g] for g in range(GROUPS)]
    left = lane_ids(width) < 2 * TILE

    def roll_row(i, carry):
        for g in range(GROUPS):
            at = width * g
            x = map_ref[i, at : at + width, :]
            y = turn(map_ref[i + 16, at : at + width, :], 2 * TILE)
            for v, by in enumerate((spacing[g], None, LANES - spacing[g])):
                one, two = (x, y) if by is None else (pltpu.roll(x, by, 1), pltpu.roll(y, by, 1))
                to = channels * v + at
                rolled_ref[i, to : to + width, :] = jnp.where(left, one, two).astype(BF16)
        return carry

    lax.fori_loop(0, TILE, roll_row, 0, unroll=2)

    part_ref[...] = jnp.zeros_like(part_ref)

    def sum_rows(j, carry):
        stack = jnp.concatenate([taps_of(rolled_ref, spacing, 2 * j + m) for m in range(2)], 1)
        grads = jnp.concatenate([dense_ref[2 * j], dense_ref[2 * j + 1]], 1)
        part_ref[...] += dot(grads, stack, NT)
        return carry

    lax.fori_loop(0, 8, sum_rows, 0)


def taps_of(rolled_ref, spacing, r):
    channels = rolled_ref.shape[1] // 3
    width = channels // GROUPS
    pieces = []
    for u in range(3):
        for v in range(3):
            for g in range(GROUPS):
                at = channels * v + width * g
                pieces.append(rolled_ref[r + HALO + (u - 1) * spacing[g], at : at + width, :])
    return jnp.concatenate(pieces, 0)


def respond(
    meta_ref, flat_ref, rolled_ref, pair_ref, core_ref, chip_ref,
    out_ref,
    rows_ref, share_ref,
):
    channels = flat_ref.shape[0]
    spacing = [meta_ref[g] for g in range(GROUPS)]
    lane = lane_ids(channels)
    low = lane < 2 * TILE
    _, even, _, keep = place()
    corner = core_ref[...] * even + chip_ref[...] * ((1.0 - even) * keep)
    corner = jnp.concatenate([corner, turn(corner, 8 * HALO)], 0)
    share = dot(flat_ref[:, channels * (TAPS - 1) :], corner_shift(corner, spacing))
    share_ref[:HALO] = jnp.zeros((HALO, channels, LANES), F32)
    for i in range(HALO):
        share_ref[HALO + i] = jnp.where(
            lane >= LANES - HALO, turn(share, LANES - HALO - HALO * i), 0.0
        )

    def conv_rows(j, carry):
        for h in range(2):
            r = 4 * j + 2 * h
            stack = jnp.concatenate([taps_of(rolled_ref, spacing, r + m) for m in range(2)], 1)
            response = dot(flat_ref[...], stack)
            for m in range(2):
                row = jnp.where(
                    low,
                    pair_ref[r + m].astype(F32),
                    turn(pair_ref[r + m + 16].astype(F32), 2 * TILE),
                )
                row = row + (response[:, LANES * m : LANES * (m + 1)] + share_ref[r + m])
                at = LANES * (2 * h + m)
                to = pl.ds(pl.multiple_of(channels * j, channels), channels)
                rows_ref[to, at : at + LANES] = row.astype(BF16)
        return carry

    lax.fori_loop(0, 4, conv_rows, 0)
    slot = meta_ref[GROUPS]
    chunks = dot(rows_ref[...], spread_table(4), NT)
    for j in range(4):
        chunk = chunks[channels * j : channels * (j + 1)]
        for h in range(2):
            at = slice(LANES * (j + 4 * h), LANES * (j + 4 * h + 1))
            to = 2 * LANES * h
            out_ref[slot, :, at] = chunk[:, to : to + LANES].astype(BF16)
            out_ref[1 - slot, :, at] = (chunk[:, to + LANES : to + 2 * LANES] * keep).astype(BF16)


def adjoint(
    meta_ref, g_ref, core_ref, chip_ref, tail_ref, both_ref, pair_ref, spread_ref,
    grad_ref,
    above_ref, below_ref,
):
    channels = g_ref.shape[1]
    width = channels // GROUPS
    span = 3 * channels
    lane = lane_ids(channels)
    zeros = jnp.zeros((channels, LANES), BF16)
    above = from_above(core_ref, chip_ref, slice(0, RIM_EMBED))
    below = from_below(core_ref, chip_ref, slice(0, RIM_EMBED))

    def moved(rim, at, to, size, per, i):
        at += LANES * (i // per)
        x = turn(rim[:, at : at + LANES], to - size * (i % per))
        return jnp.where(within(lane, to, to + size), x, 0.0)

    for h in range(HALO // 2):
        upper, lower = [], []
        for i in (2 * h, 2 * h + 1):
            x = moved(above, 0, 0, TILE, 4, i)
            x = x + moved(above, RIM_CORNER, LANES - HALO, HALO, 16, i)
            upper.append(jnp.concatenate([x.astype(BF16), zeros], 0))
            x = moved(below, 0, TILE, TILE, 4, i)
            x = x + moved(below, RIM_CORNER, 2 * TILE, HALO, 16, i)
            y = moved(below, RIM_SIDE, 80, TILE, 4, i).astype(BF16) + tail_ref[i]
            lower.append(jnp.concatenate([x.astype(BF16), y], 0))
        x = dot(both_ref[2 * span :, :], jnp.concatenate(upper, 1))
        y = dot(both_ref[:span, :], jnp.concatenate(lower, 1))
        for m in range(2):
            above_ref[2 * h + m] = x[:, LANES * m : LANES * (m + 1)]
            below_ref[2 * h + m] = y[:, LANES * m : LANES * (m + 1)]
    spacing = [meta_ref[g] for g in range(GROUPS)]
    second = within(lane, TILE, 2 * TILE)

    def gather_row(first, edge):
        def body(i, carry):
            r = first + i
            pieces = []
            for g in range(GROUPS):
                totals = []
                for v in range(3):
                    at = channels * v + width * g
                    tap = slice(at, at + width)
                    total = spread_ref[r, span + at : span + at + width, :]
                    up, down = r - spacing[g], r + spacing[g]
                    if edge < 0:
                        x = spread_ref[jnp.maximum(up, 0), 2 * span + at : 2 * span + at + width, :]
                        y = above_ref[jnp.minimum(up + HALO, HALO - 1), tap, :]
                        total = total + jnp.where(up < 0, y, x)
                    else:
                        total = total + spread_ref[up, 2 * span + at : 2 * span + at + width, :]
                    if edge > 0:
                        x = spread_ref[jnp.minimum(down, TILE - 1), tap, :]
                        y = below_ref[jnp.maximum(down - TILE, 0), tap, :]
                        total = total + jnp.where(down >= TILE, y, x)
                    else:
                        total = total + spread_ref[down, tap, :]
                    totals.append(total)
                pieces.append(
                    totals[1]
                    + pltpu.roll(totals[0], LANES - spacing[g], 1)
                    + pltpu.roll(totals[2], spacing[g], 1)
                )
            grad = jnp.concatenate(pieces, 0)
            grad = grad + jnp.where(second, turn(grad, -48), 0.0)
            own = g_ref[r].astype(F32)
            own = own + jnp.where(pair_ref[r].astype(F32) > 0, grad, 0.0)
            grad_ref[pl.ds(pl.multiple_of(r * channels, channels), channels), :] = jnp.where(
                lane < 2 * TILE, own, 0.0
            ).astype(BF16)
            return carry

        return body

    lax.fori_loop(0, HALO, gather_row(0, -1), 0, unroll=2)
    lax.fori_loop(0, TILE - 2 * HALO, gather_row(HALO, 0), 0, unroll=2)
    lax.fori_loop(0, HALO, gather_row(TILE - HALO, 1), 0, unroll=2)


def project(
    meta_ref, weight_ref, own_ref, core_ref, chip_ref, scaled_ref, grad_ref, part_ref, pair_ref,
    keep_ref, send_ref, side_ref, near_ref,
    sum_ref, kernel_ref,
):
    channels = weight_ref.shape[0]
    weight = weight_ref[...].astype(F32)
    own = own_ref[...].astype(F32)
    columns = jnp.concatenate(
        [own, unpacked(from_below(core_ref, chip_ref, slice(RIM_EMBED, RIM))), jnp.zeros((LANES - 2 * TILE, own.shape[1]), F32)], 0
    ).astype(BF16)
    weight_part = jnp.zeros_like(weight)
    local = []
    for c in range(4):
        at = slice(8 * channels * c, 8 * channels * (c + 1))
        grad_scaled = dot(grad_ref[at, :], columns)
        for i in range(8):
            one = grad_scaled[channels * i : channels * (i + 1)]
            local.append(jnp.sum(one * weight, 0, keepdims=True))
            weight_part = weight_part + one * own[8 * c + i : 8 * c + i + 1, :]
    both = dot(grad_ref[...], scaled_ref[...], TN)
    near_ref[...] = jnp.concatenate(local, 0) + both[:TILE]
    lane = lane_ids(channels)
    rim = from_above(core_ref, chip_ref, slice(0, RIM_SIDE))
    corner, ends = None, None
    for i in range(HALO):
        x = jnp.where(within(lane, TILE, TILE + HALO), pair_ref[i].astype(F32), 0.0)
        x = turn(jnp.maximum(x, 0.0), HALO * i - TILE)
        half = LANES * (i // 4)
        y = turn(rim[:, half : half + LANES], HALO * i - TILE * (i % 4) - (TILE - HALO))
        y = jnp.where(within(lane, HALO * i, HALO * (i + 1)), y, 0.0)
        corner, ends = (x, y) if i == 0 else (corner + x, ends + y)
    spacing = [meta_ref[g] for g in range(GROUPS)]
    share = dot(ends.astype(BF16), corner_shift(corner, spacing), NT)
    last = channels * (TAPS - 1)
    kernel_ref[:, :last] = part_ref[:, :last]
    kernel_ref[:, last:] = part_ref[:, last:] + share
    corner = corner[: channels // 2] + turn(corner[channels // 2 :], 8 * HALO)
    sum_ref[...] = weight_part
    rows = channels // 2
    features = own.shape[1]
    half = half_of(lax.axis_index("blk"))
    mine = pl.ds(pl.multiple_of(rows * half, rows), rows)
    other = pl.ds(pl.multiple_of(rows * (1 - half), rows), rows)
    keep_ref[:, :features] = sum_ref[mine, :]
    keep_ref[:, features:] = kernel_ref[mine, :]
    side = features + LANES
    for ref in (send_ref, side_ref):
        ref[:, :features] = both[TILE : 2 * TILE]
        ref[:, features:side] = corner
    send_ref[:, side : side + features] = sum_ref[other, :]
    send_ref[:, side + features :] = kernel_ref[other, :]


def finish(
    mine_ref, other_ref, core_ref, chip_ref, near_ref,
    weight_ref, kernel_ref, embed_ref,
):
    index, even, before, _ = place()
    rows = mine_ref.shape[0]
    channels = 2 * rows
    features = weight_ref.shape[1]
    half = half_of(index)
    for ref, which in ((mine_ref, half), (other_ref, 1 - half)):
        at = pl.ds(pl.multiple_of(rows * which, rows), rows)
        weight_ref[at, :] = ref[:, :features]
        for t in range(TAPS):
            to = features + channels * t
            kernel_ref[t, at, :] = ref[:, to : to + channels]
    carried = core_ref[:, :features] * (1.0 - even) + chip_ref[:, :features] * (even * before)
    embed_ref[...] = near_ref[...] + carried


VMEM = pl.BlockSpec(memory_space=pltpu.VMEM)
SMEM = pl.BlockSpec(memory_space=pltpu.SMEM)
HBM = pl.BlockSpec(memory_space=pltpu.HBM)


def shape(dims, kind):
    return jax.ShapeDtypeStruct(dims, kind)


def call(kernel, outs, scalars, operands, scratch=(), flops=0, moved=0, first=None, room=40):
    specs = [first or SMEM] * scalars + [VMEM] * (len(operands) - scalars)
    return pl.pallas_call(
        kernel,
        out_shape=outs,
        in_specs=specs,
        out_specs=[SMEM if out.dtype == jnp.int32 else VMEM for out in outs],
        scratch_shapes=list(scratch),
        compiler_params=pltpu.CompilerParams(vmem_limit_bytes=room * 1024 * 1024),
        cost_estimate=pl.CostEstimate(flops=flops, bytes_accessed=moved, transcendentals=0),
    )(*operands)


def swap_with(shard, step):
    return lax.ppermute(shard, "blk", [(i, i ^ step) for i in range(lax.axis_size("blk"))])


def swap_stage(shard, first, second):
    pairs = [(i, i ^ (second if half_of(i) else first)) for i in range(lax.axis_size("blk"))]
    return lax.ppermute(shard, "blk", pairs)


def swap_chips(shard):
    count = lax.axis_size("blk")
    pairs = [(i, (i + (1 if i % 2 else -1)) % count) for i in range(count)]
    return lax.ppermute(shard, "blk", pairs)


def per_device(embed, pair_weight, conv_kernel, dilations, tile_order, cotangent):
    features = embed.shape[1]
    channels = conv_kernel.shape[0]
    count = lax.axis_size("blk")
    weight = pair_weight.T
    taps = jnp.transpose(conv_kernel, (1, 0, 2))
    cot = cotangent.reshape(2, channels, TILE * TILE)
    packed = shape((channels, RIM), BF16)
    body = shape((TILE, channels, LANES), BF16)
    to_core, to_chip = call(
        pack,
        [packed, packed],
        3,
        (tile_order, cot, embed),
        [
            pltpu.SMEM(tile_order.shape, jnp.int32),
            pltpu.VMEM(cot.shape, BF16),
            pltpu.VMEM(embed.shape, BF16),
            pltpu.SemaphoreType.DMA((3,)),
        ],
        flops=10**10,
        moved=10**6,
        first=HBM,
        room=60,
    )
    core = swap_with(to_core, 1)
    chip = swap_chips(to_chip)
    grads, dense, tail, flat, both, scaled, spread, meta = call(
        prepare,
        [
            body,
            shape((TILE // 2, channels, LANES), BF16),
            shape((HALO, channels, LANES), BF16),
            shape((channels, TAPS * channels), BF16),
            shape((TAPS * channels, 2 * channels), BF16),
            shape((TILE * channels, features), BF16),
            shape((TILE, TAPS * channels, LANES), F32),
            shape((2 * GROUPS,), jnp.int32),
        ],
        2,
        (tile_order, dilations, cot, taps, weight, embed),
        flops=2 * 10**8,
        moved=3 * 10**6,
    )
    part, pair, rolled = call(
        forward,
        [
            shape((channels, TAPS * channels), F32),
            body,
            shape((TILE, 3 * channels, LANES), BF16),
        ],
        1,
        (meta, weight, embed, core, chip, dense, scaled),
        [pltpu.VMEM((TILE + 2 * HALO, channels, LANES), F32)],
        flops=8 * 10**8,
        moved=4 * 10**6,
    )
    (grad_pair,) = call(
        adjoint,
        [shape((TILE * channels, LANES), BF16)],
        1,
        (meta, grads, core, chip, tail, both, pair, spread),
        [pltpu.VMEM((HALO, 3 * channels, LANES), F32)] * 2,
        flops=8 * 10**8,
        moved=4 * 10**6,
    )
    width = features + TAPS * channels
    side = features + LANES
    total, send, sided, near = call(
        project,
        [
            shape((channels // 2, width), F32),
            shape((channels // 2, side + width), F32),
            shape((channels // 2, side), F32),
            shape((TILE, features), F32),
        ],
        1,
        (meta, weight, embed, core, chip, scaled, grad_pair, part, pair),
        [pltpu.VMEM((channels, features), F32), pltpu.VMEM((channels, TAPS * channels), F32)],
        flops=4 * 10**8,
        moved=4 * 10**6,
    )
    by_core = swap_with(send, 1)
    total = total + by_core[:, side:]
    by_core = by_core[:, :side]
    by_chip = swap_chips(jnp.concatenate([sided, total], 1))
    total = total + by_chip[:, side:]
    by_chip = by_chip[:, :side]
    steps = [1 << b for b in range(2, count.bit_length() - 1)]
    turns = list(zip(steps, steps[1:] + steps[:1]))
    for first, second in turns[:-1]:
        total = total + swap_stage(total, first, second)
    rolled, total = lax.optimization_barrier((rolled, total))
    last = swap_stage(total, *turns[-1])
    (out,) = call(
        respond,
        [shape((2, channels, TILE * TILE), BF16)],
        1,
        (meta, flat, rolled, pair, by_core[:, features:], by_chip[:, features:]),
        [
            pltpu.VMEM((4 * channels, 4 * LANES), BF16),
            pltpu.VMEM((TILE // 2, channels, LANES), F32),
        ],
        flops=2 * 10**8,
        moved=2 * 10**6,
    )
    out, last = lax.optimization_barrier((out, last))
    total = total + last
    rest = swap_with(total, 1)
    grad_weight, grad_kernel, grad_embed = call(
        finish,
        [
            shape((channels, features), F32),
            shape((TAPS, channels, channels), F32),
            shape((TILE, features), F32),
        ],
        0,
        (total, rest, by_core, by_chip, near),
        moved=10**6,
    )
    return (
        out.reshape(1, 2, channels, TILE * TILE),
        grad_embed,
        grad_weight.T,
        jnp.transpose(grad_kernel, (1, 0, 2)),
    )


def solution(mesh):
    placed = (
        P(("grp", "blk"), None),
        P(),
        P(),
        P(),
        P(("grp", "blk"), None),
        P(("grp", "blk"), None, None, None),
    )
    return jax.shard_map(
        per_device,
        mesh=mesh,
        in_specs=placed,
        out_specs=(
            P(("grp", "blk"), None, None, None),
            P(("grp", "blk"), None),
            P("grp", None),
            P("grp", None, None),
        ),
        check_vma=False,
    )
```

```python
import jax
import jax.numpy as jnp
from jax import lax
from jax.experimental import pallas as pl
from jax.experimental.pallas import tpu as pltpu
from jax.sharding import PartitionSpec as P

GROUPS = 4
HALO = 8
TILE = 32
LANES = 128
TAPS = 9
F32 = jnp.float32
BF16 = jnp.bfloat16
NN = (((1,), (0,)), ((), ()))
NT = (((1,), (1,)), ((), ()))
TN = (((0,), (0,)), ((), ()))


def dot(a, b, dims=NN):
    return lax.dot_general(a, b, dims, preferred_element_type=F32)


def turn(x, by):
    by = by % LANES
    return x if by == 0 else pltpu.roll(x, by, 1)


def lane_ids(rows):
    return lax.broadcasted_iota(jnp.int32, (rows, LANES), 1)


def within(lane, low, high):
    return jnp.logical_and(lane >= low, lane < high)


def one_hot(target, chunks):
    lane = lane_ids(target.shape[0])
    hits = [jnp.where(target == lane + LANES * c, 1.0, 0.0).astype(BF16) for c in range(chunks)]
    return jnp.concatenate(hits, 1)


def row_ids(rows):
    return lax.broadcasted_iota(jnp.int32, (rows, LANES), 0)


def spread_table(chunks):
    x = row_ids(LANES * chunks)
    return one_hot((((x >> 5) & 3) << 7) + ((x >> 7) << 5) + (x & 31), 4)


def swap_table():
    x = row_ids(HALO * TILE)
    return one_hot(((x & 31) << 3) + (x >> 5), 2)


def edge_table():
    x = row_ids(LANES)
    return one_hot(jnp.where((x & 31) < HALO, ((x & 31) << 5) + (x >> 5), -1), 2)


def corner_table(first):
    x = row_ids(HALO * TILE)
    c = (x & 31) - first
    return one_hot(jnp.where(within(c, 0, HALO), ((x >> 5) << 3) + c, -1), 1)


def as_float(flag):
    return jnp.where(flag, 1.0, 0.0).astype(F32)


def place():
    index = lax.axis_index("blk")
    last = lax.axis_size("blk") - 1
    return index, as_float(index % 2 == 0), as_float(index > 0), as_float(index < last)


def corner_shift(flat, spacing):
    width = flat.shape[0] // GROUPS
    lane = lane_ids(width)
    pieces = []
    for g in range(GROUPS):
        d = spacing[g]
        kept = jnp.logical_and(jnp.logical_and(lane < 8 * HALO, (lane >> 3) < d), (lane & 7) < d)
        x = jnp.where(kept, flat[width * g : width * (g + 1)], 0.0)
        pieces.append(pltpu.roll(x, (HALO + 1) * (HALO - d), 1))
    return jnp.concatenate(pieces, 0).astype(BF16)


def tiles_of(order_ref, cot_ref):
    slot = order_ref[0, 0]
    _, _, _, keep = place()
    return cot_ref[slot], (cot_ref[1 - slot].astype(F32) * keep).astype(BF16)


def fetch(sources, targets, sems):
    copies = [
        pltpu.make_async_copy(source, target, sems.at[i])
        for i, (source, target) in enumerate(zip(sources, targets))
    ]
    for copy in copies:
        copy.start()
    for copy in copies:
        copy.wait()


def pack(
    order_hbm, cot_hbm, embed_hbm,
    core_ref, chip_ref,
    order_ref, cot_ref, embed_ref, sems,
):
    fetch((order_hbm, cot_hbm, embed_hbm), (order_ref, cot_ref, embed_ref), sems)
    zero, one = tiles_of(order_ref, cot_ref)
    _, even, _, _ = place()
    channels = zero.shape[0]
    moved = dot(
        jnp.concatenate([zero[:, LANES * j : LANES * (j + 1)] for j in range(8)], 0), edge_table()
    )
    columns = []
    for h in range(2):
        total = None
        for j in range(8):
            piece = moved[channels * j : channels * (j + 1), LANES * h : LANES * (h + 1)]
            piece = turn(piece, 4 * j)
            total = piece if total is None else total + piece
        columns.append(total)
    rim = HALO * TILE
    tail_at = TILE * (TILE - HALO)
    up = [zero[:, :rim].astype(F32)] + columns + [dot(one[:, :rim], corner_table(0))]
    down = [one[:, tail_at:].astype(F32)] + [jnp.zeros_like(x) for x in columns]
    down += [dot(zero[:, tail_at:], corner_table(TILE - HALO))]
    up, down = jnp.concatenate(up, 1), jnp.concatenate(down, 1)
    width = up.shape[1]
    both = jnp.concatenate([embed_ref[:, :LANES], embed_ref[:, LANES:]], 0)
    core_ref[:, :width] = (down * even + up * (1.0 - even)).astype(BF16)
    core_ref[:, width:] = both
    chip_ref[:, :width] = (up * even + down * (1.0 - even)).astype(BF16)
    chip_ref[:, width:] = both


RIM_SIDE, RIM_CORNER, RIM_EMBED, RIM = 256, 512, 640, 768


def from_above(core_ref, chip_ref, at):
    _, even, before, _ = place()
    x = chip_ref[:, at].astype(F32) * (even * before)
    return x + core_ref[:, at].astype(F32) * ((1.0 - even) * before)


def from_below(core_ref, chip_ref, at):
    _, even, _, after = place()
    x = core_ref[:, at].astype(F32) * (even * after)
    return x + chip_ref[:, at].astype(F32) * ((1.0 - even) * after)


def prepare(
    order_ref, dil_ref, cot_ref, kern_ref, weight_ref, embed_ref,
    g_ref, dense_ref, tail_ref, flat_ref, both_ref, scaled_ref, spread_ref, meta_ref,
):
    for g in range(GROUPS):
        meta_ref[g] = jnp.left_shift(jnp.int32(1), dil_ref[g])
    meta_ref[GROUPS] = order_ref[0, 0]
    zero, one = tiles_of(order_ref, cot_ref)
    channels = kern_ref.shape[1]
    swap = swap_table()
    tail_at = TILE * (TILE - HALO)
    y_zero = dot(zero[:, tail_at:], swap)
    y_one = dot(one[:, tail_at:], swap)
    lane = lane_ids(channels)
    own_side = within(lane, 72, 80)
    low = lane < 2 * TILE
    pieces = []
    for j in range(4):
        at = slice(LANES * j, LANES * (j + 1))
        later = slice(LANES * (j + 4), LANES * (j + 5))
        pieces.append(
            jnp.concatenate([zero[:, at], one[:, at], zero[:, later], one[:, later]], 1)
        )
    rows = dot(jnp.concatenate(pieces, 0), spread_table(4))
    for j in range(4):
        for m in range(4):
            row = rows[channels * j : channels * (j + 1), LANES * m : LANES * (m + 1)]
            dense_ref[4 * j + m] = row.astype(BF16)
            for h in range(2):
                r = 16 * h + 4 * j + m
                side = turn(y_zero[:, LANES * h : LANES * (h + 1)], 72 - 8 * (r % 16))
                side = jnp.where(own_side, side, 0.0)
                g_ref[r] = jnp.where(low, turn(row, 64 * h), side).astype(BF16)
    for i in range(HALO):
        rest = turn(y_one[:, :LANES], 72 - 8 * i)
        tail_ref[i] = jnp.where(own_side, rest, 0.0).astype(BF16)
    eye = (
        lax.broadcasted_iota(jnp.int32, (channels, channels), 0)
        == lax.broadcasted_iota(jnp.int32, (channels, channels), 1)
    )
    eye = jnp.where(eye, 1.0, 0.0).astype(BF16)
    for u in range(3):
        for v in range(3):
            t = 3 * u + v
            pair = jnp.concatenate([kern_ref[t], kern_ref[3 * v + u]], 0)
            both_ref[channels * t : channels * (t + 1), :] = dot(eye, pair, NT).astype(BF16)
    for t in range(0, TAPS - 1, 2):
        flat_ref[:, channels * t : channels * (t + 2)] = jnp.concatenate(
            [kern_ref[t].astype(F32), kern_ref[t + 1].astype(F32)], 1
        ).astype(BF16)
    flat_ref[:, channels * (TAPS - 1) : channels * TAPS] = kern_ref[TAPS - 1]
    weight = weight_ref[...].astype(F32)
    own = embed_ref[...].astype(F32)
    for r in range(TILE):
        scaled_ref[channels * r : channels * (r + 1), :] = (own[r : r + 1, :] * weight).astype(
            BF16
        )
    inner = jnp.where(lane < 2 * TILE, 1.0, 0.0).astype(BF16)
    beside = jnp.where(own_side, 1.0, 0.0).astype(BF16)

    def spread_rows(i, carry):
        x = jnp.concatenate([g_ref[2 * i], g_ref[2 * i + 1]], 1)
        y = jnp.concatenate([inner, inner], 1), jnp.concatenate([beside, beside], 1)
        y = dot(both_ref[...], jnp.concatenate([x * y[0], x * y[1]], 0))
        spread_ref[2 * i] = y[:, :LANES]
        spread_ref[2 * i + 1] = y[:, LANES:]
        return carry

    lax.fori_loop(0, TILE // 2, spread_rows, 0, unroll=4)


def unpacked(x):
    return jnp.concatenate([x[:TILE], x[TILE:]], 1)


def forward(
    meta_ref, weight_ref, own_ref, core_ref, chip_ref, dense_ref, scaled_ref,
    part_ref, pair_ref, rolled_ref,
    map_ref,
):
    channels = weight_ref.shape[0]
    width = channels // GROUPS
    weight = weight_ref[...].astype(F32)
    own = own_ref[...].astype(F32)
    after = unpacked(from_below(core_ref, chip_ref, slice(RIM_EMBED, RIM)))
    before = unpacked(from_above(core_ref, chip_ref, slice(RIM_EMBED, RIM)))[TILE - HALO :]
    filler = jnp.zeros((LANES - 2 * TILE - HALO, own.shape[1]), F32)
    columns = jnp.concatenate([own, after, filler, before], 0).astype(BF16)
    lane = lane_ids(channels)
    kept = (
        jnp.logical_or(lane < TILE, lane >= LANES - HALO),
        lane < 2 * TILE,
        within(lane, TILE, 2 * TILE),
    )
    for c in range(6):
        part = 0 if c == 0 else (2 if c == 5 else 1)
        if part == 1:
            scaled = scaled_ref[8 * channels * (c - 1) : 8 * channels * c, :]
        else:
            rim = before if part == 0 else after
            scaled = jnp.concatenate(
                [(rim[i : i + 1, :] * weight).astype(BF16) for i in range(HALO)], 0
            )
        pair = dot(scaled, columns, NT).astype(BF16)
        for i in range(8):
            one = pair[channels * i : channels * (i + 1)]
            if part == 1:
                pair_ref[8 * (c - 1) + i] = one
            map_ref[8 * c + i] = jnp.where(kept[part], jnp.maximum(one.astype(F32), 0.0), 0.0)
    swap = swap_table()

    def gathered(first, per, low, high, move):
        halves = []
        for half in range(2):
            total = None
            for m in range(per):
                piece = jnp.where(within(lane, low, high), map_ref[first + per * half + m], 0.0)
                piece = turn(piece, move(m))
                total = piece if total is None else total + piece
            halves.append(total.astype(BF16))
        return jnp.concatenate(halves, 1)

    above = dot(gathered(0, 4, 0, TILE, lambda m: TILE * m), swap)
    below = dot(gathered(8, 16, TILE, TILE + HALO, lambda m: HALO * m - TILE), swap, NT)
    for r in range(TILE):
        half = LANES * (r // 16)
        side = turn(above[:, half : half + LANES], LANES - HALO - HALO * (r % 16))
        map_ref[HALO + r] += jnp.where(lane >= LANES - HALO, side, 0.0)
    for i in range(HALO):
        half = LANES * (i // 4)
        side = turn(below[:, half : half + LANES], -TILE * (i % 4))
        map_ref[HALO + TILE + i] += jnp.where(lane < TILE, side, 0.0)

    spacing = [meta_ref[g] for g in range(GROUPS)]
    left = lane_ids(width) < 2 * TILE

    def roll_row(i, carry):
        for g in range(GROUPS):
            at = width * g
            x = map_ref[i, at : at + width, :]
            y = turn(map_ref[i + 16, at : at + width, :], 2 * TILE)
            for v, by in enumerate((spacing[g], None, LANES - spacing[g])):
                one, two = (x, y) if by is None else (pltpu.roll(x, by, 1), pltpu.roll(y, by, 1))
                to = channels * v + at
                rolled_ref[i, to : to + width, :] = jnp.where(left, one, two).astype(BF16)
        return carry

    lax.fori_loop(0, TILE, roll_row, 0, unroll=8)

    part_ref[...] = jnp.zeros_like(part_ref)

    def sum_rows(j, carry):
        stack = jnp.concatenate([taps_of(rolled_ref, spacing, 2 * j + m) for m in range(2)], 1)
        grads = jnp.concatenate([dense_ref[2 * j], dense_ref[2 * j + 1]], 1)
        part_ref[...] += dot(grads, stack, NT)
        return carry

    lax.fori_loop(0, 8, sum_rows, 0, unroll=2)


def taps_of(rolled_ref, spacing, r):
    channels = rolled_ref.shape[1] // 3
    width = channels // GROUPS
    pieces = []
    for u in range(3):
        for v in range(3):
            for g in range(GROUPS):
                at = channels * v + width * g
                pieces.append(rolled_ref[r + HALO + (u - 1) * spacing[g], at : at + width, :])
    return jnp.concatenate(pieces, 0)


def respond(
    meta_ref, flat_ref, rolled_ref, pair_ref, core_ref, chip_ref,
    out_ref,
    rows_ref, share_ref,
):
    channels = flat_ref.shape[0]
    spacing = [meta_ref[g] for g in range(GROUPS)]
    lane = lane_ids(channels)
    low = lane < 2 * TILE
    _, even, _, keep = place()
    corner = core_ref[...] * even + chip_ref[...] * ((1.0 - even) * keep)
    corner = jnp.concatenate([corner, turn(corner, 8 * HALO)], 0)
    share = dot(flat_ref[:, channels * (TAPS - 1) :], corner_shift(corner, spacing))
    share_ref[:HALO] = jnp.zeros((HALO, channels, LANES), F32)
    for i in range(HALO):
        share_ref[HALO + i] = jnp.where(
            lane >= LANES - HALO, turn(share, LANES - HALO - HALO * i), 0.0
        )

    def conv_rows(j, carry):
        for h in range(2):
            r = 4 * j + 2 * h
            stack = jnp.concatenate([taps_of(rolled_ref, spacing, r + m) for m in range(2)], 1)
            response = dot(flat_ref[...], stack)
            for m in range(2):
                row = jnp.where(
                    low,
                    pair_ref[r + m].astype(F32),
                    turn(pair_ref[r + m + 16].astype(F32), 2 * TILE),
                )
                row = row + (response[:, LANES * m : LANES * (m + 1)] + share_ref[r + m])
                at = LANES * (2 * h + m)
                to = pl.ds(pl.multiple_of(channels * j, channels), channels)
                rows_ref[to, at : at + LANES] = row.astype(BF16)
        return carry

    lax.fori_loop(0, 4, conv_rows, 0)
    slot = meta_ref[GROUPS]
    chunks = dot(rows_ref[...], spread_table(4), NT)
    for j in range(4):
        chunk = chunks[channels * j : channels * (j + 1)]
        for h in range(2):
            at = slice(LANES * (j + 4 * h), LANES * (j + 4 * h + 1))
            to = 2 * LANES * h
            out_ref[slot, :, at] = chunk[:, to : to + LANES].astype(BF16)
            out_ref[1 - slot, :, at] = (chunk[:, to + LANES : to + 2 * LANES] * keep).astype(BF16)


def adjoint(
    meta_ref, g_ref, core_ref, chip_ref, tail_ref, both_ref, pair_ref, spread_ref,
    grad_ref,
    above_ref, below_ref,
):
    channels = g_ref.shape[1]
    width = channels // GROUPS
    span = 3 * channels
    lane = lane_ids(channels)
    zeros = jnp.zeros((channels, LANES), BF16)
    above = from_above(core_ref, chip_ref, slice(0, RIM_EMBED))
    below = from_below(core_ref, chip_ref, slice(0, RIM_EMBED))

    def moved(rim, at, to, size, per, i):
        at += LANES * (i // per)
        x = turn(rim[:, at : at + LANES], to - size * (i % per))
        return jnp.where(within(lane, to, to + size), x, 0.0)

    for h in range(HALO // 2):
        upper, lower = [], []
        for i in (2 * h, 2 * h + 1):
            x = moved(above, 0, 0, TILE, 4, i)
            x = x + moved(above, RIM_CORNER, LANES - HALO, HALO, 16, i)
            upper.append(jnp.concatenate([x.astype(BF16), zeros], 0))
            x = moved(below, 0, TILE, TILE, 4, i)
            x = x + moved(below, RIM_CORNER, 2 * TILE, HALO, 16, i)
            y = moved(below, RIM_SIDE, 80, TILE, 4, i).astype(BF16) + tail_ref[i]
            lower.append(jnp.concatenate([x.astype(BF16), y], 0))
        x = dot(both_ref[2 * span :, :], jnp.concatenate(upper, 1))
        y = dot(both_ref[:span, :], jnp.concatenate(lower, 1))
        for m in range(2):
            above_ref[2 * h + m] = x[:, LANES * m : LANES * (m + 1)]
            below_ref[2 * h + m] = y[:, LANES * m : LANES * (m + 1)]
    spacing = [meta_ref[g] for g in range(GROUPS)]
    second = within(lane, TILE, 2 * TILE)

    def gather_row(first, edge):
        def body(i, carry):
            r = first + i
            pieces = []
            for g in range(GROUPS):
                totals = []
                for v in range(3):
                    at = channels * v + width * g
                    tap = slice(at, at + width)
                    total = spread_ref[r, span + at : span + at + width, :]
                    up, down = r - spacing[g], r + spacing[g]
                    if edge < 0:
                        x = spread_ref[jnp.maximum(up, 0), 2 * span + at : 2 * span + at + width, :]
                        y = above_ref[jnp.minimum(up + HALO, HALO - 1), tap, :]
                        total = total + jnp.where(up < 0, y, x)
                    else:
                        total = total + spread_ref[up, 2 * span + at : 2 * span + at + width, :]
                    if edge > 0:
                        x = spread_ref[jnp.minimum(down, TILE - 1), tap, :]
                        y = below_ref[jnp.maximum(down - TILE, 0), tap, :]
                        total = total + jnp.where(down >= TILE, y, x)
                    else:
                        total = total + spread_ref[down, tap, :]
                    totals.append(total)
                pieces.append(
                    totals[1]
                    + pltpu.roll(totals[0], LANES - spacing[g], 1)
                    + pltpu.roll(totals[2], spacing[g], 1)
                )
            grad = jnp.concatenate(pieces, 0)
            grad = grad + jnp.where(second, turn(grad, -48), 0.0)
            own = g_ref[r].astype(F32)
            own = own + jnp.where(pair_ref[r].astype(F32) > 0, grad, 0.0)
            grad_ref[pl.ds(pl.multiple_of(r * channels, channels), channels), :] = jnp.where(
                lane < 2 * TILE, own, 0.0
            ).astype(BF16)
            return carry

        return body

    lax.fori_loop(0, HALO, gather_row(0, -1), 0, unroll=8)
    lax.fori_loop(0, TILE - 2 * HALO, gather_row(HALO, 0), 0, unroll=8)
    lax.fori_loop(0, HALO, gather_row(TILE - HALO, 1), 0, unroll=8)


def project(
    meta_ref, weight_ref, own_ref, core_ref, chip_ref, scaled_ref, grad_ref, part_ref, pair_ref,
    keep_ref, send_ref, side_ref, near_ref,
    sum_ref, kernel_ref,
):
    channels = weight_ref.shape[0]
    weight = weight_ref[...].astype(F32)
    own = own_ref[...].astype(F32)
    columns = jnp.concatenate(
        [own, unpacked(from_below(core_ref, chip_ref, slice(RIM_EMBED, RIM))), jnp.zeros((LANES - 2 * TILE, own.shape[1]), F32)], 0
    ).astype(BF16)
    weight_part = jnp.zeros_like(weight)
    local = []
    for c in range(4):
        at = slice(8 * channels * c, 8 * channels * (c + 1))
        grad_scaled = dot(grad_ref[at, :], columns)
        for i in range(8):
            one = grad_scaled[channels * i : channels * (i + 1)]
            local.append(jnp.sum(one * weight, 0, keepdims=True))
            weight_part = weight_part + one * own[8 * c + i : 8 * c + i + 1, :]
    both = dot(grad_ref[...], scaled_ref[...], TN)
    near_ref[...] = jnp.concatenate(local, 0) + both[:TILE]
    lane = lane_ids(channels)
    rim = from_above(core_ref, chip_ref, slice(0, RIM_SIDE))
    corner, ends = None, None
    for i in range(HALO):
        x = jnp.where(within(lane, TILE, TILE + HALO), pair_ref[i].astype(F32), 0.0)
        x = turn(jnp.maximum(x, 0.0), HALO * i - TILE)
        half = LANES * (i // 4)
        y = turn(rim[:, half : half + LANES], HALO * i - TILE * (i % 4) - (TILE - HALO))
        y = jnp.where(within(lane, HALO * i, HALO * (i + 1)), y, 0.0)
        corner, ends = (x, y) if i == 0 else (corner + x, ends + y)
    spacing = [meta_ref[g] for g in range(GROUPS)]
    share = dot(ends.astype(BF16), corner_shift(corner, spacing), NT)
    last = channels * (TAPS - 1)
    kernel_ref[:, :last] = part_ref[:, :last]
    kernel_ref[:, last:] = part_ref[:, last:] + share
    corner = corner[: channels // 2] + turn(corner[channels // 2 :], 8 * HALO)
    sum_ref[...] = weight_part
    rows = channels // 2
    features = own.shape[1]
    half = lax.axis_index("blk") % 2
    mine = pl.ds(pl.multiple_of(rows * half, rows), rows)
    other = pl.ds(pl.multiple_of(rows * (1 - half), rows), rows)
    keep_ref[:, :features] = sum_ref[mine, :]
    keep_ref[:, features:] = kernel_ref[mine, :]
    side = features + LANES
    for ref in (send_ref, side_ref):
        ref[:, :features] = both[TILE : 2 * TILE]
        ref[:, features:side] = corner
    send_ref[:, side : side + features] = sum_ref[other, :]
    send_ref[:, side + features :] = kernel_ref[other, :]


def finish(
    mine_ref, other_ref, core_ref, chip_ref, near_ref,
    weight_ref, kernel_ref, embed_ref,
):
    index, even, before, _ = place()
    rows = mine_ref.shape[0]
    channels = 2 * rows
    features = weight_ref.shape[1]
    half = index % 2
    for ref, which in ((mine_ref, half), (other_ref, 1 - half)):
        at = pl.ds(pl.multiple_of(rows * which, rows), rows)
        weight_ref[at, :] = ref[:, :features]
        for t in range(TAPS):
            to = features + channels * t
            kernel_ref[t, at, :] = ref[:, to : to + channels]
    carried = core_ref[:, :features] * (1.0 - even) + chip_ref[:, :features] * (even * before)
    embed_ref[...] = near_ref[...] + carried


VMEM = pl.BlockSpec(memory_space=pltpu.VMEM)
SMEM = pl.BlockSpec(memory_space=pltpu.SMEM)
HBM = pl.BlockSpec(memory_space=pltpu.HBM)


def shape(dims, kind):
    return jax.ShapeDtypeStruct(dims, kind)


def call(kernel, outs, scalars, operands, scratch=(), flops=0, moved=0, first=None, room=40):
    specs = [first or SMEM] * scalars + [VMEM] * (len(operands) - scalars)
    return pl.pallas_call(
        kernel,
        out_shape=outs,
        in_specs=specs,
        out_specs=[SMEM if out.dtype == jnp.int32 else VMEM for out in outs],
        scratch_shapes=list(scratch),
        compiler_params=pltpu.CompilerParams(vmem_limit_bytes=room * 1024 * 1024),
        cost_estimate=pl.CostEstimate(flops=flops, bytes_accessed=moved, transcendentals=0),
    )(*operands)


def swap_with(shard, step):
    return lax.ppermute(shard, "blk", [(i, i ^ step) for i in range(lax.axis_size("blk"))])


def swap_stage(shard, even, odd):
    pairs = [(i, i ^ (odd if i % 2 else even)) for i in range(lax.axis_size("blk"))]
    return lax.ppermute(shard, "blk", pairs)


def swap_chips(shard):
    count = lax.axis_size("blk")
    pairs = [(i, (i + (1 if i % 2 else -1)) % count) for i in range(count)]
    return lax.ppermute(shard, "blk", pairs)


def per_device(embed, pair_weight, conv_kernel, dilations, tile_order, cotangent):
    features = embed.shape[1]
    channels = conv_kernel.shape[0]
    count = lax.axis_size("blk")
    weight = pair_weight.T
    taps = jnp.transpose(conv_kernel, (1, 0, 2))
    cot = cotangent.reshape(2, channels, TILE * TILE)
    packed = shape((channels, RIM), BF16)
    body = shape((TILE, channels, LANES), BF16)
    to_core, to_chip = call(
        pack,
        [packed, packed],
        3,
        (tile_order, cot, embed),
        [
            pltpu.SMEM(tile_order.shape, jnp.int32),
            pltpu.VMEM(cot.shape, BF16),
            pltpu.VMEM(embed.shape, BF16),
            pltpu.SemaphoreType.DMA((3,)),
        ],
        flops=10**10,
        moved=10**6,
        first=HBM,
        room=60,
    )
    core = swap_with(to_core, 1)
    chip = swap_chips(to_chip)
    grads, dense, tail, flat, both, scaled, spread, meta = call(
        prepare,
        [
            body,
            shape((TILE // 2, channels, LANES), BF16),
            shape((HALO, channels, LANES), BF16),
            shape((channels, TAPS * channels), BF16),
            shape((TAPS * channels, 2 * channels), BF16),
            shape((TILE * channels, features), BF16),
            shape((TILE, TAPS * channels, LANES), F32),
            shape((2 * GROUPS,), jnp.int32),
        ],
        2,
        (tile_order, dilations, cot, taps, weight, embed),
        flops=2 * 10**8,
        moved=3 * 10**6,
    )
    part, pair, rolled = call(
        forward,
        [
            shape((channels, TAPS * channels), F32),
            body,
            shape((TILE, 3 * channels, LANES), BF16),
        ],
        1,
        (meta, weight, embed, core, chip, dense, scaled),
        [pltpu.VMEM((TILE + 2 * HALO, channels, LANES), F32)],
        flops=8 * 10**8,
        moved=4 * 10**6,
    )
    (grad_pair,) = call(
        adjoint,
        [shape((TILE * channels, LANES), BF16)],
        1,
        (meta, grads, core, chip, tail, both, pair, spread),
        [pltpu.VMEM((HALO, 3 * channels, LANES), F32)] * 2,
        flops=8 * 10**8,
        moved=4 * 10**6,
    )
    width = features + TAPS * channels
    side = features + LANES
    total, send, sided, near = call(
        project,
        [
            shape((channels // 2, width), F32),
            shape((channels // 2, side + width), F32),
            shape((channels // 2, side), F32),
            shape((TILE, features), F32),
        ],
        1,
        (meta, weight, embed, core, chip, scaled, grad_pair, part, pair),
        [pltpu.VMEM((channels, features), F32), pltpu.VMEM((channels, TAPS * channels), F32)],
        flops=4 * 10**8,
        moved=4 * 10**6,
    )
    by_core = swap_with(send, 1)
    by_chip = swap_chips(sided)
    total = total + by_core[:, side:]
    by_core = by_core[:, :side]
    steps = [1 << b for b in range(1, count.bit_length() - 1)]
    turns = list(zip(steps[1:] + steps[:1], steps))
    for even, odd in turns[:-1]:
        total = total + swap_stage(total, even, odd)
    rolled, total, by_chip = lax.optimization_barrier((rolled, total, by_chip))
    last = swap_stage(total, *turns[-1])
    (out,) = call(
        respond,
        [shape((2, channels, TILE * TILE), BF16)],
        1,
        (meta, flat, rolled, pair, by_core[:, features:], by_chip[:, features:]),
        [
            pltpu.VMEM((4 * channels, 4 * LANES), BF16),
            pltpu.VMEM((TILE // 2, channels, LANES), F32),
        ],
        flops=2 * 10**8,
        moved=2 * 10**6,
    )
    out, last = lax.optimization_barrier((out, last))
    total = total + last
    rest = swap_with(total, 1)
    grad_weight, grad_kernel, grad_embed = call(
        finish,
        [
            shape((channels, features), F32),
            shape((TAPS, channels, channels), F32),
            shape((TILE, features), F32),
        ],
        0,
        (total, rest, by_core, by_chip, near),
        moved=10**6,
    )
    return (
        out.reshape(1, 2, channels, TILE * TILE),
        grad_embed,
        grad_weight.T,
        jnp.transpose(grad_kernel, (1, 0, 2)),
    )


def solution(mesh):
    placed = (
        P(("grp", "blk"), None),
        P(),
        P(),
        P(),
        P(("grp", "blk"), None),
        P(("grp", "blk"), None, None, None),
    )
    return jax.shard_map(
        per_device,
        mesh=mesh,
        in_specs=placed,
        out_specs=(
            P(("grp", "blk"), None, None, None),
            P(("grp", "blk"), None),
            P("grp", None),
            P("grp", None, None),
        ),
        check_vma=False,
    )
```

```python
import jax
import jax.numpy as jnp
from jax import lax
from jax.experimental import pallas as pl
from jax.experimental.pallas import tpu as pltpu
from jax.sharding import PartitionSpec as P

GROUPS = 4
HALO = 8
TILE = 32
LANES = 128
TAPS = 9
F32 = jnp.float32
BF16 = jnp.bfloat16
NN = (((1,), (0,)), ((), ()))
NT = (((1,), (1,)), ((), ()))
TN = (((0,), (0,)), ((), ()))


def dot(a, b, dims=NN):
    return lax.dot_general(a, b, dims, preferred_element_type=F32)


def turn(x, by):
    by = by % LANES
    return x if by == 0 else pltpu.roll(x, by, 1)


def lane_ids(rows):
    return lax.broadcasted_iota(jnp.int32, (rows, LANES), 1)


def within(lane, low, high):
    return jnp.logical_and(lane >= low, lane < high)


def one_hot(target, chunks):
    lane = lane_ids(target.shape[0])
    hits = [jnp.where(target == lane + LANES * c, 1.0, 0.0).astype(BF16) for c in range(chunks)]
    return jnp.concatenate(hits, 1)


def row_ids(rows):
    return lax.broadcasted_iota(jnp.int32, (rows, LANES), 0)


def spread_table(chunks):
    x = row_ids(LANES * chunks)
    return one_hot((((x >> 5) & 3) << 7) + ((x >> 7) << 5) + (x & 31), 4)


def swap_table():
    x = row_ids(HALO * TILE)
    return one_hot(((x & 31) << 3) + (x >> 5), 2)


def edge_table():
    x = row_ids(LANES)
    return one_hot(jnp.where((x & 31) < HALO, ((x & 31) << 5) + (x >> 5), -1), 2)


def corner_table(first):
    x = row_ids(HALO * TILE)
    c = (x & 31) - first
    return one_hot(jnp.where(within(c, 0, HALO), ((x >> 5) << 3) + c, -1), 1)


def as_float(flag):
    return jnp.where(flag, 1.0, 0.0).astype(F32)


def place():
    index = lax.axis_index("blk")
    last = lax.axis_size("blk") - 1
    return index, as_float(index % 2 == 0), as_float(index > 0), as_float(index < last)


def corner_shift(flat, spacing):
    width = flat.shape[0] // GROUPS
    lane = lane_ids(width)
    pieces = []
    for g in range(GROUPS):
        d = spacing[g]
        kept = jnp.logical_and(jnp.logical_and(lane < 8 * HALO, (lane >> 3) < d), (lane & 7) < d)
        x = jnp.where(kept, flat[width * g : width * (g + 1)], 0.0)
        pieces.append(pltpu.roll(x, (HALO + 1) * (HALO - d), 1))
    return jnp.concatenate(pieces, 0).astype(BF16)


def tiles_of(order_ref, cot_ref):
    slot = order_ref[0, 0]
    _, _, _, keep = place()
    return cot_ref[slot], (cot_ref[1 - slot].astype(F32) * keep).astype(BF16)


def fetch(sources, targets, sems):
    copies = [
        pltpu.make_async_copy(source, target, sems.at[i])
        for i, (source, target) in enumerate(zip(sources, targets))
    ]
    for copy in copies:
        copy.start()
    for copy in copies:
        copy.wait()


def pack(
    order_hbm, cot_hbm, embed_hbm,
    core_ref, chip_ref,
    order_ref, cot_ref, embed_ref, sems,
):
    fetch((order_hbm, cot_hbm, embed_hbm), (order_ref, cot_ref, embed_ref), sems)
    zero, one = tiles_of(order_ref, cot_ref)
    _, even, _, _ = place()
    channels = zero.shape[0]
    moved = dot(
        jnp.concatenate([zero[:, LANES * j : LANES * (j + 1)] for j in range(8)], 0), edge_table()
    )
    columns = []
    for h in range(2):
        total = None
        for j in range(8):
            piece = moved[channels * j : channels * (j + 1), LANES * h : LANES * (h + 1)]
            piece = turn(piece, 4 * j)
            total = piece if total is None else total + piece
        columns.append(total)
    rim = HALO * TILE
    tail_at = TILE * (TILE - HALO)
    up = [zero[:, :rim].astype(F32)] + columns + [dot(one[:, :rim], corner_table(0))]
    down = [one[:, tail_at:].astype(F32)] + [jnp.zeros_like(x) for x in columns]
    down += [dot(zero[:, tail_at:], corner_table(TILE - HALO))]
    up, down = jnp.concatenate(up, 1), jnp.concatenate(down, 1)
    width = up.shape[1]
    both = jnp.concatenate([embed_ref[:, :LANES], embed_ref[:, LANES:]], 0)
    core_ref[:, :width] = (down * even + up * (1.0 - even)).astype(BF16)
    core_ref[:, width:] = both
    chip_ref[:, :width] = (up * even + down * (1.0 - even)).astype(BF16)
    chip_ref[:, width:] = both


RIM_SIDE, RIM_CORNER, RIM_EMBED, RIM = 256, 512, 640, 768


def from_above(core_ref, chip_ref, at):
    _, even, before, _ = place()
    x = chip_ref[:, at].astype(F32) * (even * before)
    return x + core_ref[:, at].astype(F32) * ((1.0 - even) * before)


def from_below(core_ref, chip_ref, at):
    _, even, _, after = place()
    x = core_ref[:, at].astype(F32) * (even * after)
    return x + chip_ref[:, at].astype(F32) * ((1.0 - even) * after)


def prepare(
    order_ref, dil_ref, cot_ref, kern_ref, weight_ref, embed_ref,
    g_ref, dense_ref, tail_ref, flat_ref, both_ref, scaled_ref, spread_ref, meta_ref,
):
    for g in range(GROUPS):
        meta_ref[g] = jnp.left_shift(jnp.int32(1), dil_ref[g])
    meta_ref[GROUPS] = order_ref[0, 0]
    zero, one = tiles_of(order_ref, cot_ref)
    channels = kern_ref.shape[1]
    swap = swap_table()
    tail_at = TILE * (TILE - HALO)
    y_zero = dot(zero[:, tail_at:], swap)
    y_one = dot(one[:, tail_at:], swap)
    lane = lane_ids(channels)
    own_side = within(lane, 72, 80)
    low = lane < 2 * TILE
    pieces = []
    for j in range(4):
        at = slice(LANES * j, LANES * (j + 1))
        later = slice(LANES * (j + 4), LANES * (j + 5))
        pieces.append(
            jnp.concatenate([zero[:, at], one[:, at], zero[:, later], one[:, later]], 1)
        )
    rows = dot(jnp.concatenate(pieces, 0), spread_table(4))
    for j in range(4):
        for m in range(4):
            row = rows[channels * j : channels * (j + 1), LANES * m : LANES * (m + 1)]
            dense_ref[4 * j + m] = row.astype(BF16)
            for h in range(2):
                r = 16 * h + 4 * j + m
                side = turn(y_zero[:, LANES * h : LANES * (h + 1)], 72 - 8 * (r % 16))
                side = jnp.where(own_side, side, 0.0)
                g_ref[r] = jnp.where(low, turn(row, 64 * h), side).astype(BF16)
    for i in range(HALO):
        rest = turn(y_one[:, :LANES], 72 - 8 * i)
        tail_ref[i] = jnp.where(own_side, rest, 0.0).astype(BF16)
    eye = (
        lax.broadcasted_iota(jnp.int32, (channels, channels), 0)
        == lax.broadcasted_iota(jnp.int32, (channels, channels), 1)
    )
    eye = jnp.where(eye, 1.0, 0.0).astype(BF16)
    for u in range(3):
        for v in range(3):
            t = 3 * u + v
            pair = jnp.concatenate([kern_ref[t], kern_ref[3 * v + u]], 0)
            both_ref[channels * t : channels * (t + 1), :] = dot(eye, pair, NT).astype(BF16)
    for t in range(0, TAPS - 1, 2):
        flat_ref[:, channels * t : channels * (t + 2)] = jnp.concatenate(
            [kern_ref[t].astype(F32), kern_ref[t + 1].astype(F32)], 1
        ).astype(BF16)
    flat_ref[:, channels * (TAPS - 1) : channels * TAPS] = kern_ref[TAPS - 1]
    weight = weight_ref[...].astype(F32)
    own = embed_ref[...].astype(F32)
    for r in range(TILE):
        scaled_ref[channels * r : channels * (r + 1), :] = (own[r : r + 1, :] * weight).astype(
            BF16
        )
    inner = jnp.where(lane < 2 * TILE, 1.0, 0.0).astype(BF16)
    beside = jnp.where(own_side, 1.0, 0.0).astype(BF16)

    def spread_rows(i, carry):
        x = jnp.concatenate([g_ref[2 * i], g_ref[2 * i + 1]], 1)
        y = jnp.concatenate([inner, inner], 1), jnp.concatenate([beside, beside], 1)
        y = dot(both_ref[...], jnp.concatenate([x * y[0], x * y[1]], 0))
        spread_ref[2 * i] = y[:, :LANES]
        spread_ref[2 * i + 1] = y[:, LANES:]
        return carry

    lax.fori_loop(0, TILE // 2, spread_rows, 0, unroll=4)


def unpacked(x):
    return jnp.concatenate([x[:TILE], x[TILE:]], 1)


def forward(
    meta_ref, weight_ref, own_ref, core_ref, chip_ref, dense_ref, scaled_ref,
    part_ref, pair_ref, rolled_ref,
    map_ref,
):
    channels = weight_ref.shape[0]
    width = channels // GROUPS
    weight = weight_ref[...].astype(F32)
    own = own_ref[...].astype(F32)
    after = unpacked(from_below(core_ref, chip_ref, slice(RIM_EMBED, RIM)))
    before = unpacked(from_above(core_ref, chip_ref, slice(RIM_EMBED, RIM)))[TILE - HALO :]
    filler = jnp.zeros((LANES - 2 * TILE - HALO, own.shape[1]), F32)
    columns = jnp.concatenate([own, after, filler, before], 0).astype(BF16)
    lane = lane_ids(channels)
    kept = (
        jnp.logical_or(lane < TILE, lane >= LANES - HALO),
        lane < 2 * TILE,
        within(lane, TILE, 2 * TILE),
    )
    for c in range(6):
        part = 0 if c == 0 else (2 if c == 5 else 1)
        if part == 1:
            scaled = scaled_ref[8 * channels * (c - 1) : 8 * channels * c, :]
        else:
            rim = before if part == 0 else after
            scaled = jnp.concatenate(
                [(rim[i : i + 1, :] * weight).astype(BF16) for i in range(HALO)], 0
            )
        pair = dot(scaled, columns, NT).astype(BF16)
        for i in range(8):
            one = pair[channels * i : channels * (i + 1)]
            if part == 1:
                pair_ref[8 * (c - 1) + i] = one
            map_ref[8 * c + i] = jnp.where(kept[part], jnp.maximum(one.astype(F32), 0.0), 0.0)
    swap = swap_table()

    def gathered(first, per, low, high, move):
        halves = []
        for half in range(2):
            total = None
            for m in range(per):
                piece = jnp.where(within(lane, low, high), map_ref[first + per * half + m], 0.0)
                piece = turn(piece, move(m))
                total = piece if total is None else total + piece
            halves.append(total.astype(BF16))
        return jnp.concatenate(halves, 1)

    above = dot(gathered(0, 4, 0, TILE, lambda m: TILE * m), swap)
    below = dot(gathered(8, 16, TILE, TILE + HALO, lambda m: HALO * m - TILE), swap, NT)
    for r in range(TILE):
        half = LANES * (r // 16)
        side = turn(above[:, half : half + LANES], LANES - HALO - HALO * (r % 16))
        map_ref[HALO + r] += jnp.where(lane >= LANES - HALO, side, 0.0)
    for i in range(HALO):
        half = LANES * (i // 4)
        side = turn(below[:, half : half + LANES], -TILE * (i % 4))
        map_ref[HALO + TILE + i] += jnp.where(lane < TILE, side, 0.0)

    spacing = [meta_ref[g] for g in range(GROUPS)]
    left = lane_ids(width) < 2 * TILE

    def roll_row(i, carry):
        for g in range(GROUPS):
            at = width * g
            x = map_ref[i, at : at + width, :]
            y = turn(map_ref[i + 16, at : at + width, :], 2 * TILE)
            for v, by in enumerate((spacing[g], None, LANES - spacing[g])):
                one, two = (x, y) if by is None else (pltpu.roll(x, by, 1), pltpu.roll(y, by, 1))
                to = channels * v + at
                rolled_ref[i, to : to + width, :] = jnp.where(left, one, two).astype(BF16)
        return carry

    lax.fori_loop(0, TILE, roll_row, 0, unroll=4)

    part_ref[...] = jnp.zeros_like(part_ref)

    def sum_rows(j, carry):
        stack = jnp.concatenate([taps_of(rolled_ref, spacing, 2 * j + m) for m in range(2)], 1)
        grads = jnp.concatenate([dense_ref[2 * j], dense_ref[2 * j + 1]], 1)
        part_ref[...] += dot(grads, stack, NT)
        return carry

    lax.fori_loop(0, 8, sum_rows, 0, unroll=4)


def taps_of(rolled_ref, spacing, r):
    channels = rolled_ref.shape[1] // 3
    width = channels // GROUPS
    pieces = []
    for u in range(3):
        for v in range(3):
            for g in range(GROUPS):
                at = channels * v + width * g
                pieces.append(rolled_ref[r + HALO + (u - 1) * spacing[g], at : at + width, :])
    return jnp.concatenate(pieces, 0)


def respond(
    meta_ref, flat_ref, rolled_ref, pair_ref, core_ref, chip_ref,
    out_ref,
    rows_ref, share_ref,
):
    channels = flat_ref.shape[0]
    spacing = [meta_ref[g] for g in range(GROUPS)]
    lane = lane_ids(channels)
    low = lane < 2 * TILE
    _, even, _, keep = place()
    corner = core_ref[...] * even + chip_ref[...].astype(F32) * ((1.0 - even) * keep)
    corner = jnp.concatenate([corner, turn(corner, 8 * HALO)], 0)
    share = dot(flat_ref[:, channels * (TAPS - 1) :], corner_shift(corner, spacing))
    share_ref[:HALO] = jnp.zeros((HALO, channels, LANES), F32)
    for i in range(HALO):
        share_ref[HALO + i] = jnp.where(
            lane >= LANES - HALO, turn(share, LANES - HALO - HALO * i), 0.0
        )

    def conv_rows(j, carry):
        for h in range(2):
            r = 4 * j + 2 * h
            stack = jnp.concatenate([taps_of(rolled_ref, spacing, r + m) for m in range(2)], 1)
            response = dot(flat_ref[...], stack)
            for m in range(2):
                row = jnp.where(
                    low,
                    pair_ref[r + m].astype(F32),
                    turn(pair_ref[r + m + 16].astype(F32), 2 * TILE),
                )
                row = row + (response[:, LANES * m : LANES * (m + 1)] + share_ref[r + m])
                at = LANES * (2 * h + m)
                to = pl.ds(pl.multiple_of(channels * j, channels), channels)
                rows_ref[to, at : at + LANES] = row.astype(BF16)
        return carry

    lax.fori_loop(0, 4, conv_rows, 0)
    slot = meta_ref[GROUPS]
    chunks = dot(rows_ref[...], spread_table(4), NT)
    for j in range(4):
        chunk = chunks[channels * j : channels * (j + 1)]
        for h in range(2):
            at = slice(LANES * (j + 4 * h), LANES * (j + 4 * h + 1))
            to = 2 * LANES * h
            out_ref[slot, :, at] = chunk[:, to : to + LANES].astype(BF16)
            out_ref[1 - slot, :, at] = (chunk[:, to + LANES : to + 2 * LANES] * keep).astype(BF16)


def adjoint(
    meta_ref, g_ref, core_ref, chip_ref, tail_ref, both_ref, pair_ref, spread_ref,
    grad_ref,
    above_ref, below_ref,
):
    channels = g_ref.shape[1]
    width = channels // GROUPS
    span = 3 * channels
    lane = lane_ids(channels)
    zeros = jnp.zeros((channels, LANES), BF16)
    above = from_above(core_ref, chip_ref, slice(0, RIM_EMBED))
    below = from_below(core_ref, chip_ref, slice(0, RIM_EMBED))

    def moved(rim, at, to, size, per, i):
        at += LANES * (i // per)
        x = turn(rim[:, at : at + LANES], to - size * (i % per))
        return jnp.where(within(lane, to, to + size), x, 0.0)

    for h in range(HALO // 2):
        upper, lower = [], []
        for i in (2 * h, 2 * h + 1):
            x = moved(above, 0, 0, TILE, 4, i)
            x = x + moved(above, RIM_CORNER, LANES - HALO, HALO, 16, i)
            upper.append(jnp.concatenate([x.astype(BF16), zeros], 0))
            x = moved(below, 0, TILE, TILE, 4, i)
            x = x + moved(below, RIM_CORNER, 2 * TILE, HALO, 16, i)
            y = moved(below, RIM_SIDE, 80, TILE, 4, i).astype(BF16) + tail_ref[i]
            lower.append(jnp.concatenate([x.astype(BF16), y], 0))
        x = dot(both_ref[2 * span :, :], jnp.concatenate(upper, 1))
        y = dot(both_ref[:span, :], jnp.concatenate(lower, 1))
        for m in range(2):
            above_ref[2 * h + m] = x[:, LANES * m : LANES * (m + 1)]
            below_ref[2 * h + m] = y[:, LANES * m : LANES * (m + 1)]
    spacing = [meta_ref[g] for g in range(GROUPS)]
    second = within(lane, TILE, 2 * TILE)

    def gather_row(first, edge):
        def body(i, carry):
            r = first + i
            pieces = []
            for g in range(GROUPS):
                totals = []
                for v in range(3):
                    at = channels * v + width * g
                    tap = slice(at, at + width)
                    total = spread_ref[r, span + at : span + at + width, :]
                    up, down = r - spacing[g], r + spacing[g]
                    if edge < 0:
                        x = spread_ref[jnp.maximum(up, 0), 2 * span + at : 2 * span + at + width, :]
                        y = above_ref[jnp.minimum(up + HALO, HALO - 1), tap, :]
                        total = total + jnp.where(up < 0, y, x)
                    else:
                        total = total + spread_ref[up, 2 * span + at : 2 * span + at + width, :]
                    if edge > 0:
                        x = spread_ref[jnp.minimum(down, TILE - 1), tap, :]
                        y = below_ref[jnp.maximum(down - TILE, 0), tap, :]
                        total = total + jnp.where(down >= TILE, y, x)
                    else:
                        total = total + spread_ref[down, tap, :]
                    totals.append(total)
                pieces.append(
                    totals[1]
                    + pltpu.roll(totals[0], LANES - spacing[g], 1)
                    + pltpu.roll(totals[2], spacing[g], 1)
                )
            grad = jnp.concatenate(pieces, 0)
            grad = grad + jnp.where(second, turn(grad, -48), 0.0)
            own = g_ref[r].astype(F32)
            own = own + jnp.where(pair_ref[r].astype(F32) > 0, grad, 0.0)
            grad_ref[pl.ds(pl.multiple_of(r * channels, channels), channels), :] = jnp.where(
                lane < 2 * TILE, own, 0.0
            ).astype(BF16)
            return carry

        return body

    lax.fori_loop(0, HALO, gather_row(0, -1), 0, unroll=8)
    lax.fori_loop(0, TILE - 2 * HALO, gather_row(HALO, 0), 0, unroll=8)
    lax.fori_loop(0, HALO, gather_row(TILE - HALO, 1), 0, unroll=8)


def project(
    meta_ref, weight_ref, own_ref, core_ref, chip_ref, scaled_ref, grad_ref, part_ref, pair_ref,
    keep_ref, send_ref, side_ref, near_ref,
    sum_ref, kernel_ref,
):
    channels = weight_ref.shape[0]
    weight = weight_ref[...].astype(F32)
    own = own_ref[...].astype(F32)
    columns = jnp.concatenate(
        [own, unpacked(from_below(core_ref, chip_ref, slice(RIM_EMBED, RIM))), jnp.zeros((LANES - 2 * TILE, own.shape[1]), F32)], 0
    ).astype(BF16)
    weight_part = jnp.zeros_like(weight)
    local = []
    for c in range(4):
        at = slice(8 * channels * c, 8 * channels * (c + 1))
        grad_scaled = dot(grad_ref[at, :], columns)
        for i in range(8):
            one = grad_scaled[channels * i : channels * (i + 1)]
            local.append(jnp.sum(one * weight, 0, keepdims=True))
            weight_part = weight_part + one * own[8 * c + i : 8 * c + i + 1, :]
    both = dot(grad_ref[...], scaled_ref[...], TN)
    near_ref[...] = jnp.concatenate(local, 0) + both[:TILE]
    lane = lane_ids(channels)
    rim = from_above(core_ref, chip_ref, slice(0, RIM_SIDE))
    corner, ends = None, None
    for i in range(HALO):
        x = jnp.where(within(lane, TILE, TILE + HALO), pair_ref[i].astype(F32), 0.0)
        x = turn(jnp.maximum(x, 0.0), HALO * i - TILE)
        half = LANES * (i // 4)
        y = turn(rim[:, half : half + LANES], HALO * i - TILE * (i % 4) - (TILE - HALO))
        y = jnp.where(within(lane, HALO * i, HALO * (i + 1)), y, 0.0)
        corner, ends = (x, y) if i == 0 else (corner + x, ends + y)
    spacing = [meta_ref[g] for g in range(GROUPS)]
    share = dot(ends.astype(BF16), corner_shift(corner, spacing), NT)
    last = channels * (TAPS - 1)
    kernel_ref[:, :last] = part_ref[:, :last]
    kernel_ref[:, last:] = part_ref[:, last:] + share
    corner = corner[: channels // 2] + turn(corner[channels // 2 :], 8 * HALO)
    sum_ref[...] = weight_part
    rows = channels // 2
    features = own.shape[1]
    half = lax.axis_index("blk") % 2
    mine = pl.ds(pl.multiple_of(rows * half, rows), rows)
    other = pl.ds(pl.multiple_of(rows * (1 - half), rows), rows)
    keep_ref[:, :features] = sum_ref[mine, :]
    keep_ref[:, features:] = kernel_ref[mine, :]
    side = features + LANES
    for ref in (send_ref, side_ref):
        ref[:, :features] = both[TILE : 2 * TILE].astype(ref.dtype)
        ref[:, features:side] = corner.astype(ref.dtype)
    send_ref[:, side : side + features] = sum_ref[other, :]
    send_ref[:, side + features :] = kernel_ref[other, :]


def finish(
    mine_ref, other_ref, core_ref, chip_ref, near_ref,
    weight_ref, kernel_ref, embed_ref,
):
    index, even, before, _ = place()
    rows = mine_ref.shape[0]
    channels = 2 * rows
    features = weight_ref.shape[1]
    half = index % 2
    for ref, which in ((mine_ref, half), (other_ref, 1 - half)):
        at = pl.ds(pl.multiple_of(rows * which, rows), rows)
        weight_ref[at, :] = ref[:, :features]
        for t in range(TAPS):
            to = features + channels * t
            kernel_ref[t, at, :] = ref[:, to : to + channels]
    carried = core_ref[:, :features] * (1.0 - even) + chip_ref[:, :features].astype(F32) * (even * before)
    embed_ref[...] = near_ref[...] + carried


VMEM = pl.BlockSpec(memory_space=pltpu.VMEM)
SMEM = pl.BlockSpec(memory_space=pltpu.SMEM)
HBM = pl.BlockSpec(memory_space=pltpu.HBM)


def shape(dims, kind):
    return jax.ShapeDtypeStruct(dims, kind)


def call(kernel, outs, scalars, operands, scratch=(), flops=0, moved=0, first=None, room=40):
    specs = [first or SMEM] * scalars + [VMEM] * (len(operands) - scalars)
    return pl.pallas_call(
        kernel,
        out_shape=outs,
        in_specs=specs,
        out_specs=[SMEM if out.dtype == jnp.int32 else VMEM for out in outs],
        scratch_shapes=list(scratch),
        compiler_params=pltpu.CompilerParams(vmem_limit_bytes=room * 1024 * 1024),
        cost_estimate=pl.CostEstimate(flops=flops, bytes_accessed=moved, transcendentals=0),
    )(*operands)


def swap_with(shard, step):
    return lax.ppermute(shard, "blk", [(i, i ^ step) for i in range(lax.axis_size("blk"))])


def swap_stage(shard, even, odd):
    pairs = [(i, i ^ (odd if i % 2 else even)) for i in range(lax.axis_size("blk"))]
    return lax.ppermute(shard, "blk", pairs)


def swap_chips(shard):
    count = lax.axis_size("blk")
    pairs = [(i, (i + (1 if i % 2 else -1)) % count) for i in range(count)]
    return lax.ppermute(shard, "blk", pairs)


def per_device(embed, pair_weight, conv_kernel, dilations, tile_order, cotangent):
    features = embed.shape[1]
    channels = conv_kernel.shape[0]
    count = lax.axis_size("blk")
    weight = pair_weight.T
    taps = jnp.transpose(conv_kernel, (1, 0, 2))
    cot = cotangent.reshape(2, channels, TILE * TILE)
    packed = shape((channels, RIM), BF16)
    body = shape((TILE, channels, LANES), BF16)
    to_core, to_chip = call(
        pack,
        [packed, packed],
        3,
        (tile_order, cot, embed),
        [
            pltpu.SMEM(tile_order.shape, jnp.int32),
            pltpu.VMEM(cot.shape, BF16),
            pltpu.VMEM(embed.shape, BF16),
            pltpu.SemaphoreType.DMA((3,)),
        ],
        flops=10**10,
        moved=10**6,
        first=HBM,
        room=60,
    )
    core = swap_with(to_core, 1)
    chip = swap_chips(to_chip)
    grads, dense, tail, flat, both, scaled, spread, meta = call(
        prepare,
        [
            body,
            shape((TILE // 2, channels, LANES), BF16),
            shape((HALO, channels, LANES), BF16),
            shape((channels, TAPS * channels), BF16),
            shape((TAPS * channels, 2 * channels), BF16),
            shape((TILE * channels, features), BF16),
            shape((TILE, TAPS * channels, LANES), F32),
            shape((2 * GROUPS,), jnp.int32),
        ],
        2,
        (tile_order, dilations, cot, taps, weight, embed),
        flops=2 * 10**8,
        moved=3 * 10**6,
    )
    part, pair, rolled = call(
        forward,
        [
            shape((channels, TAPS * channels), F32),
            body,
            shape((TILE, 3 * channels, LANES), BF16),
        ],
        1,
        (meta, weight, embed, core, chip, dense, scaled),
        [pltpu.VMEM((TILE + 2 * HALO, channels, LANES), F32)],
        flops=8 * 10**8,
        moved=4 * 10**6,
    )
    (grad_pair,) = call(
        adjoint,
        [shape((TILE * channels, LANES), BF16)],
        1,
        (meta, grads, core, chip, tail, both, pair, spread),
        [pltpu.VMEM((HALO, 3 * channels, LANES), F32)] * 2,
        flops=8 * 10**8,
        moved=4 * 10**6,
    )
    width = features + TAPS * channels
    side = features + LANES
    total, send, sided, near = call(
        project,
        [
            shape((channels // 2, width), F32),
            shape((channels // 2, side + width), F32),
            shape((channels // 2, side), BF16),
            shape((TILE, features), F32),
        ],
        1,
        (meta, weight, embed, core, chip, scaled, grad_pair, part, pair),
        [pltpu.VMEM((channels, features), F32), pltpu.VMEM((channels, TAPS * channels), F32)],
        flops=4 * 10**8,
        moved=4 * 10**6,
    )
    by_core = swap_with(send, 1)
    by_chip = swap_chips(sided)
    total = total + by_core[:, side:]
    by_core = by_core[:, :side]
    steps = [1 << b for b in range(1, count.bit_length() - 1)]
    turns = list(zip(steps[1:] + steps[:1], steps))
    for s, (even, odd) in enumerate(turns[:-1]):
        parts = jnp.split(total, 2) if s == 0 else [total]
        parts = [part + swap_stage(part, even, odd) for part in parts]
        total = jnp.concatenate(parts) if s == 0 else parts[0]
    rolled, total, by_chip = lax.optimization_barrier((rolled, total, by_chip))
    last = swap_stage(total, *turns[-1])
    (out,) = call(
        respond,
        [shape((2, channels, TILE * TILE), BF16)],
        1,
        (meta, flat, rolled, pair, by_core[:, features:], by_chip[:, features:]),
        [
            pltpu.VMEM((4 * channels, 4 * LANES), BF16),
            pltpu.VMEM((TILE // 2, channels, LANES), F32),
        ],
        flops=2 * 10**8,
        moved=2 * 10**6,
    )
    out, last = lax.optimization_barrier((out, last))
    total = total + last
    rest = swap_with(total, 1)
    grad_weight, grad_kernel, grad_embed = call(
        finish,
        [
            shape((channels, features), F32),
            shape((TAPS, channels, channels), F32),
            shape((TILE, features), F32),
        ],
        0,
        (total, rest, by_core, by_chip, near),
        moved=10**6,
    )
    return (
        out.reshape(1, 2, channels, TILE * TILE),
        grad_embed,
        grad_weight.T,
        jnp.transpose(grad_kernel, (1, 0, 2)),
    )


def solution(mesh):
    placed = (
        P(("grp", "blk"), None),
        P(),
        P(),
        P(),
        P(("grp", "blk"), None),
        P(("grp", "blk"), None, None, None),
    )
    return jax.shard_map(
        per_device,
        mesh=mesh,
        in_specs=placed,
        out_specs=(
            P(("grp", "blk"), None, None, None),
            P(("grp", "blk"), None),
            P("grp", None),
            P("grp", None, None),
        ),
        check_vma=False,
    )
```

```python
import jax
import jax.numpy as jnp
from jax import lax
from jax.experimental import pallas as pl
from jax.experimental.pallas import tpu as pltpu
from jax.sharding import PartitionSpec as P

GROUPS = 4
HALO = 8
TILE = 32
LANES = 128
TAPS = 9
F32 = jnp.float32
BF16 = jnp.bfloat16
NN = (((1,), (0,)), ((), ()))
NT = (((1,), (1,)), ((), ()))
TN = (((0,), (0,)), ((), ()))


def dot(a, b, dims=NN):
    return lax.dot_general(a, b, dims, preferred_element_type=F32)


def turn(x, by):
    by = by % LANES
    return x if by == 0 else pltpu.roll(x, by, 1)


def lane_ids(rows):
    return lax.broadcasted_iota(jnp.int32, (rows, LANES), 1)


def within(lane, low, high):
    return jnp.logical_and(lane >= low, lane < high)


def one_hot(target, chunks):
    lane = lane_ids(target.shape[0])
    hits = [jnp.where(target == lane + LANES * c, 1.0, 0.0).astype(BF16) for c in range(chunks)]
    return jnp.concatenate(hits, 1)


def row_ids(rows):
    return lax.broadcasted_iota(jnp.int32, (rows, LANES), 0)


def spread_table(chunks):
    x = row_ids(LANES * chunks)
    return one_hot((((x >> 5) & 3) << 7) + ((x >> 7) << 5) + (x & 31), 4)


def swap_table():
    x = row_ids(HALO * TILE)
    return one_hot(((x & 31) << 3) + (x >> 5), 2)


def edge_table():
    x = row_ids(LANES)
    return one_hot(jnp.where((x & 31) < HALO, ((x & 31) << 5) + (x >> 5), -1), 2)


def corner_table(first):
    x = row_ids(HALO * TILE)
    c = (x & 31) - first
    return one_hot(jnp.where(within(c, 0, HALO), ((x >> 5) << 3) + c, -1), 1)


def as_float(flag):
    return jnp.where(flag, 1.0, 0.0).astype(F32)


def place():
    index = lax.axis_index("blk")
    last = lax.axis_size("blk") - 1
    return index, as_float(index % 2 == 0), as_float(index > 0), as_float(index < last)


def corner_shift(flat, spacing):
    width = flat.shape[0] // GROUPS
    lane = lane_ids(width)
    pieces = []
    for g in range(GROUPS):
        d = spacing[g]
        kept = jnp.logical_and(jnp.logical_and(lane < 8 * HALO, (lane >> 3) < d), (lane & 7) < d)
        x = jnp.where(kept, flat[width * g : width * (g + 1)], 0.0)
        pieces.append(pltpu.roll(x, (HALO + 1) * (HALO - d), 1))
    return jnp.concatenate(pieces, 0).astype(BF16)


def tiles_of(order_ref, cot_ref):
    slot = order_ref[0, 0]
    _, _, _, keep = place()
    return cot_ref[slot], (cot_ref[1 - slot].astype(F32) * keep).astype(BF16)


def fetch(sources, targets, sems):
    copies = [
        pltpu.make_async_copy(source, target, sems.at[i])
        for i, (source, target) in enumerate(zip(sources, targets))
    ]
    for copy in copies:
        copy.start()
    return copies


def pack(
    order_hbm, cot_hbm, embed_hbm,
    chip_ref, core_ref,
    order_ref, cot_ref, embed_ref, sems,
):
    copies = fetch((order_hbm, cot_hbm, embed_hbm), (order_ref, cot_ref, embed_ref), sems)
    edge, head, tail = edge_table(), corner_table(0), corner_table(TILE - HALO)
    for copy in copies:
        copy.wait()
    zero, one = tiles_of(order_ref, cot_ref)
    _, even, _, _ = place()
    channels = zero.shape[0]
    moved = dot(
        jnp.concatenate([zero[:, LANES * j : LANES * (j + 1)] for j in range(8)], 0), edge
    )
    columns = []
    for h in range(2):
        total = None
        for j in range(8):
            piece = moved[channels * j : channels * (j + 1), LANES * h : LANES * (h + 1)]
            piece = turn(piece, 4 * j)
            total = piece if total is None else total + piece
        columns.append(total)
    rim = HALO * TILE
    tail_at = TILE * (TILE - HALO)
    up = [zero[:, :rim].astype(F32)] + columns + [dot(one[:, :rim], head)]
    down = [one[:, tail_at:].astype(F32)] + [jnp.zeros_like(x) for x in columns]
    down += [dot(zero[:, tail_at:], tail)]
    up, down = jnp.concatenate(up, 1), jnp.concatenate(down, 1)
    width = up.shape[1]
    both = jnp.concatenate([embed_ref[:, :LANES], embed_ref[:, LANES:]], 0)
    core_ref[:, :width] = (down * even + up * (1.0 - even)).astype(BF16)
    core_ref[:, width:] = both
    chip_ref[:, :width] = (up * even + down * (1.0 - even)).astype(BF16)
    chip_ref[:, width:] = both


RIM_SIDE, RIM_CORNER, RIM_EMBED, RIM = 256, 512, 640, 768


def from_above(core_ref, chip_ref, at):
    _, even, before, _ = place()
    x = chip_ref[:, at].astype(F32) * (even * before)
    return x + core_ref[:, at].astype(F32) * ((1.0 - even) * before)


def from_below(core_ref, chip_ref, at):
    _, even, _, after = place()
    x = core_ref[:, at].astype(F32) * (even * after)
    return x + chip_ref[:, at].astype(F32) * ((1.0 - even) * after)


def prepare(
    order_ref, dil_ref, cot_ref, kern_ref, weight_ref, embed_ref,
    g_ref, dense_ref, tail_ref, flat_ref, both_ref, scaled_ref, spread_ref, meta_ref,
):
    for g in range(GROUPS):
        meta_ref[g] = jnp.left_shift(jnp.int32(1), dil_ref[g])
    meta_ref[GROUPS] = order_ref[0, 0]
    zero, one = tiles_of(order_ref, cot_ref)
    channels = kern_ref.shape[1]
    swap = swap_table()
    tail_at = TILE * (TILE - HALO)
    y_zero = dot(zero[:, tail_at:], swap)
    y_one = dot(one[:, tail_at:], swap)
    lane = lane_ids(channels)
    own_side = within(lane, 72, 80)
    low = lane < 2 * TILE
    pieces = []
    for j in range(4):
        at = slice(LANES * j, LANES * (j + 1))
        later = slice(LANES * (j + 4), LANES * (j + 5))
        pieces.append(
            jnp.concatenate([zero[:, at], one[:, at], zero[:, later], one[:, later]], 1)
        )
    rows = dot(jnp.concatenate(pieces, 0), spread_table(4))
    for j in range(4):
        for m in range(4):
            row = rows[channels * j : channels * (j + 1), LANES * m : LANES * (m + 1)]
            dense_ref[4 * j + m] = row.astype(BF16)
            for h in range(2):
                r = 16 * h + 4 * j + m
                side = turn(y_zero[:, LANES * h : LANES * (h + 1)], 72 - 8 * (r % 16))
                side = jnp.where(own_side, side, 0.0)
                g_ref[r] = jnp.where(low, turn(row, 64 * h), side).astype(BF16)
    for i in range(HALO):
        rest = turn(y_one[:, :LANES], 72 - 8 * i)
        tail_ref[i] = jnp.where(own_side, rest, 0.0).astype(BF16)
    eye = (
        lax.broadcasted_iota(jnp.int32, (channels, channels), 0)
        == lax.broadcasted_iota(jnp.int32, (channels, channels), 1)
    )
    eye = jnp.where(eye, 1.0, 0.0).astype(BF16)
    for u in range(3):
        for v in range(3):
            t = 3 * u + v
            pair = jnp.concatenate([kern_ref[t], kern_ref[3 * v + u]], 0)
            both_ref[channels * t : channels * (t + 1), :] = dot(eye, pair, NT).astype(BF16)
    for t in range(0, TAPS - 1, 2):
        flat_ref[:, channels * t : channels * (t + 2)] = jnp.concatenate(
            [kern_ref[t].astype(F32), kern_ref[t + 1].astype(F32)], 1
        ).astype(BF16)
    flat_ref[:, channels * (TAPS - 1) : channels * TAPS] = kern_ref[TAPS - 1]
    weight = weight_ref[...].astype(F32)
    own = embed_ref[...].astype(F32)
    for r in range(TILE):
        scaled_ref[channels * r : channels * (r + 1), :] = (own[r : r + 1, :] * weight).astype(
            BF16
        )
    inner = jnp.where(lane < 2 * TILE, 1.0, 0.0).astype(BF16)
    beside = jnp.where(own_side, 1.0, 0.0).astype(BF16)

    def spread_rows(i, carry):
        x = jnp.concatenate([g_ref[2 * i], g_ref[2 * i + 1]], 1)
        y = jnp.concatenate([inner, inner], 1), jnp.concatenate([beside, beside], 1)
        y = dot(both_ref[...], jnp.concatenate([x * y[0], x * y[1]], 0))
        spread_ref[2 * i] = y[:, :LANES]
        spread_ref[2 * i + 1] = y[:, LANES:]
        return carry

    lax.fori_loop(0, TILE // 2, spread_rows, 0, unroll=4)


def unpacked(x):
    return jnp.concatenate([x[:TILE], x[TILE:]], 1)


def forward(
    meta_ref, weight_ref, own_ref, chip_ref, core_ref, dense_ref, scaled_ref,
    part_ref, pair_ref, rolled_ref,
    map_ref,
):
    channels = weight_ref.shape[0]
    width = channels // GROUPS
    weight = weight_ref[...].astype(F32)
    own = own_ref[...].astype(F32)
    after = unpacked(from_below(core_ref, chip_ref, slice(RIM_EMBED, RIM)))
    before = unpacked(from_above(core_ref, chip_ref, slice(RIM_EMBED, RIM)))[TILE - HALO :]
    filler = jnp.zeros((LANES - 2 * TILE - HALO, own.shape[1]), F32)
    columns = jnp.concatenate([own, after, filler, before], 0).astype(BF16)
    lane = lane_ids(channels)
    kept = (
        jnp.logical_or(lane < TILE, lane >= LANES - HALO),
        lane < 2 * TILE,
        within(lane, TILE, 2 * TILE),
    )
    for c in range(6):
        part = 0 if c == 0 else (2 if c == 5 else 1)
        if part == 1:
            scaled = scaled_ref[8 * channels * (c - 1) : 8 * channels * c, :]
        else:
            rim = before if part == 0 else after
            scaled = jnp.concatenate(
                [(rim[i : i + 1, :] * weight).astype(BF16) for i in range(HALO)], 0
            )
        pair = dot(scaled, columns, NT).astype(BF16)
        for i in range(8):
            one = pair[channels * i : channels * (i + 1)]
            if part == 1:
                pair_ref[8 * (c - 1) + i] = one
            x = jnp.where(kept[part], jnp.maximum(one.astype(F32), 0.0), 0.0)
            map_ref[8 * c + i] = x.astype(BF16)
    swap = swap_table()

    def gathered(first, per, low, high, move):
        halves = []
        for half in range(2):
            total = None
            for m in range(per):
                piece = map_ref[first + per * half + m].astype(F32)
                piece = jnp.where(within(lane, low, high), piece, 0.0)
                piece = turn(piece, move(m))
                total = piece if total is None else total + piece
            halves.append(total.astype(BF16))
        return jnp.concatenate(halves, 1)

    above = dot(gathered(0, 4, 0, TILE, lambda m: TILE * m), swap)
    below = dot(gathered(8, 16, TILE, TILE + HALO, lambda m: HALO * m - TILE), swap, NT)
    for r in range(TILE):
        half = LANES * (r // 16)
        side = turn(above[:, half : half + LANES], LANES - HALO - HALO * (r % 16))
        map_ref[HALO + r] += jnp.where(lane >= LANES - HALO, side, 0.0).astype(BF16)
    for i in range(HALO):
        half = LANES * (i // 4)
        side = turn(below[:, half : half + LANES], -TILE * (i % 4))
        map_ref[HALO + TILE + i] += jnp.where(lane < TILE, side, 0.0).astype(BF16)

    spacing = [meta_ref[g] for g in range(GROUPS)]
    source = row_ids(LANES)
    to = lane_ids(LANES)
    for g in range(GROUPS):
        tables = []
        for h in range(2):
            half = within(to, 2 * TILE * h, 2 * TILE * (h + 1))
            offset = jnp.where(half, (source - (to - 2 * TILE * h)) & (LANES - 1), LANES)
            hits = [
                jnp.where(offset == (v * spacing[g]) & (LANES - 1), 1.0, 0.0).astype(BF16)
                for v in (-1, 0, 1)
            ]
            tables.append(jnp.concatenate(hits, 1))
        table = jnp.concatenate(tables, 0)
        at = width * g
        for part in range(2):
            low = [map_ref[16 * part + i, at : at + width, :] for i in range(16)]
            high = [map_ref[16 * part + i + 16, at : at + width, :] for i in range(16)]
            x = jnp.concatenate([jnp.concatenate(low, 0), jnp.concatenate(high, 0)], 1)
            y = dot(x, table).astype(BF16)
            for i in range(16):
                for v in range(3):
                    to_row = channels * v + at
                    rolled_ref[16 * part + i, to_row : to_row + width, :] = y[
                        width * i : width * (i + 1), LANES * v : LANES * (v + 1)
                    ]
    part_ref[...] = jnp.zeros_like(part_ref)

    def sum_rows(j, carry):
        stack = jnp.concatenate([taps_of(rolled_ref, spacing, 2 * j + m) for m in range(2)], 1)
        grads = jnp.concatenate([dense_ref[2 * j], dense_ref[2 * j + 1]], 1)
        part_ref[...] += dot(grads, stack, NT)
        return carry

    lax.fori_loop(0, 8, sum_rows, 0, unroll=4)


def taps_of(rolled_ref, spacing, r):
    channels = rolled_ref.shape[1] // 3
    width = channels // GROUPS
    pieces = []
    for u in range(3):
        for v in range(3):
            for g in range(GROUPS):
                at = channels * v + width * g
                pieces.append(rolled_ref[r + HALO + (u - 1) * spacing[g], at : at + width, :])
    return jnp.concatenate(pieces, 0)


def respond(
    meta_ref, flat_ref, rolled_ref, pair_ref, core_ref, chip_ref,
    out_ref,
    rows_ref, share_ref,
):
    channels = flat_ref.shape[0]
    spacing = [meta_ref[g] for g in range(GROUPS)]
    lane = lane_ids(channels)
    low = lane < 2 * TILE
    _, even, _, keep = place()
    corner = core_ref[...] * even + chip_ref[...].astype(F32) * ((1.0 - even) * keep)
    corner = jnp.concatenate([corner, turn(corner, 8 * HALO)], 0)
    share = dot(flat_ref[:, channels * (TAPS - 1) :], corner_shift(corner, spacing))
    share_ref[:HALO] = jnp.zeros((HALO, channels, LANES), F32)
    for i in range(HALO):
        share_ref[HALO + i] = jnp.where(
            lane >= LANES - HALO, turn(share, LANES - HALO - HALO * i), 0.0
        )

    def conv_rows(j, carry):
        for h in range(2):
            r = 4 * j + 2 * h
            stack = jnp.concatenate([taps_of(rolled_ref, spacing, r + m) for m in range(2)], 1)
            response = dot(flat_ref[...], stack)
            for m in range(2):
                row = jnp.where(
                    low,
                    pair_ref[r + m].astype(F32),
                    turn(pair_ref[r + m + 16].astype(F32), 2 * TILE),
                )
                row = row + (response[:, LANES * m : LANES * (m + 1)] + share_ref[r + m])
                at = LANES * (2 * h + m)
                to = pl.ds(pl.multiple_of(channels * j, channels), channels)
                rows_ref[to, at : at + LANES] = row.astype(BF16)
        return carry

    lax.fori_loop(0, 4, conv_rows, 0)
    slot = meta_ref[GROUPS]
    chunks = dot(rows_ref[...], spread_table(4), NT)
    for j in range(4):
        chunk = chunks[channels * j : channels * (j + 1)]
        for h in range(2):
            at = slice(LANES * (j + 4 * h), LANES * (j + 4 * h + 1))
            to = 2 * LANES * h
            out_ref[slot, :, at] = chunk[:, to : to + LANES].astype(BF16)
            out_ref[1 - slot, :, at] = (chunk[:, to + LANES : to + 2 * LANES] * keep).astype(BF16)


def adjoint(
    meta_ref, g_ref, core_ref, chip_ref, tail_ref, both_ref, pair_ref, spread_ref,
    grad_ref,
    above_ref, below_ref,
):
    channels = g_ref.shape[1]
    width = channels // GROUPS
    span = 3 * channels
    lane = lane_ids(channels)
    zeros = jnp.zeros((channels, LANES), BF16)
    above = from_above(core_ref, chip_ref, slice(0, RIM_EMBED))
    below = from_below(core_ref, chip_ref, slice(0, RIM_EMBED))

    def moved(rim, at, to, size, per, i):
        at += LANES * (i // per)
        x = turn(rim[:, at : at + LANES], to - size * (i % per))
        return jnp.where(within(lane, to, to + size), x, 0.0)

    for h in range(HALO // 2):
        upper, lower = [], []
        for i in (2 * h, 2 * h + 1):
            x = moved(above, 0, 0, TILE, 4, i)
            x = x + moved(above, RIM_CORNER, LANES - HALO, HALO, 16, i)
            upper.append(jnp.concatenate([x.astype(BF16), zeros], 0))
            x = moved(below, 0, TILE, TILE, 4, i)
            x = x + moved(below, RIM_CORNER, 2 * TILE, HALO, 16, i)
            y = moved(below, RIM_SIDE, 80, TILE, 4, i).astype(BF16) + tail_ref[i]
            lower.append(jnp.concatenate([x.astype(BF16), y], 0))
        x = dot(both_ref[2 * span :, :], jnp.concatenate(upper, 1))
        y = dot(both_ref[:span, :], jnp.concatenate(lower, 1))
        for m in range(2):
            above_ref[2 * h + m] = x[:, LANES * m : LANES * (m + 1)]
            below_ref[2 * h + m] = y[:, LANES * m : LANES * (m + 1)]
    spacing = [meta_ref[g] for g in range(GROUPS)]
    second = within(lane, TILE, 2 * TILE)

    def gather_row(first, edge):
        def body(i, carry):
            r = first + i
            pieces = []
            for g in range(GROUPS):
                totals = []
                for v in range(3):
                    at = channels * v + width * g
                    tap = slice(at, at + width)
                    total = spread_ref[r, span + at : span + at + width, :]
                    up, down = r - spacing[g], r + spacing[g]
                    if edge < 0:
                        x = spread_ref[jnp.maximum(up, 0), 2 * span + at : 2 * span + at + width, :]
                        y = above_ref[jnp.minimum(up + HALO, HALO - 1), tap, :]
                        total = total + jnp.where(up < 0, y, x)
                    else:
                        total = total + spread_ref[up, 2 * span + at : 2 * span + at + width, :]
                    if edge > 0:
                        x = spread_ref[jnp.minimum(down, TILE - 1), tap, :]
                        y = below_ref[jnp.maximum(down - TILE, 0), tap, :]
                        total = total + jnp.where(down >= TILE, y, x)
                    else:
                        total = total + spread_ref[down, tap, :]
                    totals.append(total)
                pieces.append(
                    totals[1]
                    + pltpu.roll(totals[0], LANES - spacing[g], 1)
                    + pltpu.roll(totals[2], spacing[g], 1)
                )
            grad = jnp.concatenate(pieces, 0)
            grad = grad + jnp.where(second, turn(grad, -48), 0.0)
            own = g_ref[r].astype(F32)
            own = own + jnp.where(pair_ref[r].astype(F32) > 0, grad, 0.0)
            grad_ref[pl.ds(pl.multiple_of(r * channels, channels), channels), :] = jnp.where(
                lane < 2 * TILE, own, 0.0
            ).astype(BF16)
            return carry

        return body

    lax.fori_loop(0, HALO, gather_row(0, -1), 0, unroll=8)
    lax.fori_loop(0, TILE - 2 * HALO, gather_row(HALO, 0), 0, unroll=8)
    lax.fori_loop(0, HALO, gather_row(TILE - HALO, 1), 0, unroll=8)


def project(
    meta_ref, weight_ref, own_ref, core_ref, chip_ref, scaled_ref, grad_ref, part_ref, pair_ref,
    keep_ref, send_ref, side_ref, near_ref,
    sum_ref, kernel_ref,
):
    channels = weight_ref.shape[0]
    weight = weight_ref[...].astype(F32)
    own = own_ref[...].astype(F32)
    columns = jnp.concatenate(
        [own, unpacked(from_below(core_ref, chip_ref, slice(RIM_EMBED, RIM))), jnp.zeros((LANES - 2 * TILE, own.shape[1]), F32)], 0
    ).astype(BF16)
    weight_part = jnp.zeros_like(weight)
    local = []
    for c in range(4):
        at = slice(8 * channels * c, 8 * channels * (c + 1))
        grad_scaled = dot(grad_ref[at, :], columns)
        for i in range(8):
            one = grad_scaled[channels * i : channels * (i + 1)]
            local.append(jnp.sum(one * weight, 0, keepdims=True))
            weight_part = weight_part + one * own[8 * c + i : 8 * c + i + 1, :]
    both = dot(grad_ref[...], scaled_ref[...], TN)
    near_ref[...] = jnp.concatenate(local, 0) + both[:TILE]
    lane = lane_ids(channels)
    rim = from_above(core_ref, chip_ref, slice(0, RIM_SIDE))
    corner, ends = None, None
    for i in range(HALO):
        x = jnp.where(within(lane, TILE, TILE + HALO), pair_ref[i].astype(F32), 0.0)
        x = turn(jnp.maximum(x, 0.0), HALO * i - TILE)
        half = LANES * (i // 4)
        y = turn(rim[:, half : half + LANES], HALO * i - TILE * (i % 4) - (TILE - HALO))
        y = jnp.where(within(lane, HALO * i, HALO * (i + 1)), y, 0.0)
        corner, ends = (x, y) if i == 0 else (corner + x, ends + y)
    spacing = [meta_ref[g] for g in range(GROUPS)]
    share = dot(ends.astype(BF16), corner_shift(corner, spacing), NT)
    last = channels * (TAPS - 1)
    kernel_ref[:, :last] = part_ref[:, :last]
    kernel_ref[:, last:] = part_ref[:, last:] + share
    corner = corner[: channels // 2] + turn(corner[channels // 2 :], 8 * HALO)
    sum_ref[...] = weight_part
    rows = channels // 2
    features = own.shape[1]
    half = lax.axis_index("blk") % 2
    mine = pl.ds(pl.multiple_of(rows * half, rows), rows)
    other = pl.ds(pl.multiple_of(rows * (1 - half), rows), rows)
    keep_ref[:, :features] = sum_ref[mine, :]
    keep_ref[:, features:] = kernel_ref[mine, :]
    side = features + LANES
    for ref in (send_ref, side_ref):
        ref[:, :features] = both[TILE : 2 * TILE].astype(ref.dtype)
        ref[:, features:side] = corner.astype(ref.dtype)
    send_ref[:, side : side + features] = sum_ref[other, :]
    send_ref[:, side + features :] = kernel_ref[other, :]


def finish(
    mine_ref, other_ref, core_ref, chip_ref, near_ref,
    weight_ref, kernel_ref, embed_ref,
):
    index, even, before, _ = place()
    rows = mine_ref.shape[0]
    channels = 2 * rows
    features = weight_ref.shape[1]
    half = index % 2
    for ref, which in ((mine_ref, half), (other_ref, 1 - half)):
        at = pl.ds(pl.multiple_of(rows * which, rows), rows)
        weight_ref[at, :] = ref[:, :features]
        for t in range(TAPS):
            to = features + channels * t
            kernel_ref[t, at, :] = ref[:, to : to + channels]
    carried = core_ref[:, :features] * (1.0 - even) + chip_ref[:, :features].astype(F32) * (even * before)
    embed_ref[...] = near_ref[...] + carried


VMEM = pl.BlockSpec(memory_space=pltpu.VMEM)
SMEM = pl.BlockSpec(memory_space=pltpu.SMEM)
HBM = pl.BlockSpec(memory_space=pltpu.HBM)


def shape(dims, kind):
    return jax.ShapeDtypeStruct(dims, kind)


def call(kernel, outs, scalars, operands, scratch=(), flops=0, moved=0, first=None, room=40):
    specs = [first or SMEM] * scalars + [VMEM] * (len(operands) - scalars)
    return pl.pallas_call(
        kernel,
        out_shape=outs,
        in_specs=specs,
        out_specs=[SMEM if out.dtype == jnp.int32 else VMEM for out in outs],
        scratch_shapes=list(scratch),
        compiler_params=pltpu.CompilerParams(vmem_limit_bytes=room * 1024 * 1024),
        cost_estimate=pl.CostEstimate(flops=flops, bytes_accessed=moved, transcendentals=0),
    )(*operands)


def swap_with(shard, step):
    return lax.ppermute(shard, "blk", [(i, i ^ step) for i in range(lax.axis_size("blk"))])


def swap_stage(shard, even, odd):
    pairs = [(i, i ^ (odd if i % 2 else even)) for i in range(lax.axis_size("blk"))]
    return lax.ppermute(shard, "blk", pairs)


def swap_chips(shard):
    count = lax.axis_size("blk")
    pairs = [(i, (i + (1 if i % 2 else -1)) % count) for i in range(count)]
    return lax.ppermute(shard, "blk", pairs)


def per_device(embed, pair_weight, conv_kernel, dilations, tile_order, cotangent):
    features = embed.shape[1]
    channels = conv_kernel.shape[0]
    count = lax.axis_size("blk")
    weight = pair_weight.T
    taps = jnp.transpose(conv_kernel, (1, 0, 2))
    cot = cotangent.reshape(2, channels, TILE * TILE)
    packed = shape((channels, RIM), BF16)
    body = shape((TILE, channels, LANES), BF16)
    to_chip, to_core = call(
        pack,
        [packed, packed],
        3,
        (tile_order, cot, embed),
        [
            pltpu.SMEM(tile_order.shape, jnp.int32),
            pltpu.VMEM(cot.shape, BF16),
            pltpu.VMEM(embed.shape, BF16),
            pltpu.SemaphoreType.DMA((3,)),
        ],
        flops=10**10,
        moved=10**6,
        first=HBM,
        room=60,
    )
    chip = swap_chips(to_chip)
    core = swap_with(to_core, 1)
    grads, dense, tail, flat, both, scaled, spread, meta = call(
        prepare,
        [
            body,
            shape((TILE // 2, channels, LANES), BF16),
            shape((HALO, channels, LANES), BF16),
            shape((channels, TAPS * channels), BF16),
            shape((TAPS * channels, 2 * channels), BF16),
            shape((TILE * channels, features), BF16),
            shape((TILE, TAPS * channels, LANES), F32),
            shape((2 * GROUPS,), jnp.int32),
        ],
        2,
        (tile_order, dilations, cot, taps, weight, embed),
        flops=2 * 10**8,
        moved=3 * 10**6,
    )
    part, pair, rolled = call(
        forward,
        [
            shape((channels, TAPS * channels), F32),
            body,
            shape((TILE, 3 * channels, LANES), BF16),
        ],
        1,
        (meta, weight, embed, chip, core, dense, scaled),
        [pltpu.VMEM((TILE + 2 * HALO, channels, LANES), BF16)],
        flops=8 * 10**8,
        moved=4 * 10**6,
    )
    (grad_pair,) = call(
        adjoint,
        [shape((TILE * channels, LANES), BF16)],
        1,
        (meta, grads, core, chip, tail, both, pair, spread),
        [pltpu.VMEM((HALO, 3 * channels, LANES), F32)] * 2,
        flops=8 * 10**8,
        moved=4 * 10**6,
    )
    width = features + TAPS * channels
    side = features + LANES
    total, send, sided, near = call(
        project,
        [
            shape((channels // 2, width), F32),
            shape((channels // 2, side + width), F32),
            shape((channels // 2, side), BF16),
            shape((TILE, features), F32),
        ],
        1,
        (meta, weight, embed, core, chip, scaled, grad_pair, part, pair),
        [pltpu.VMEM((channels, features), F32), pltpu.VMEM((channels, TAPS * channels), F32)],
        flops=4 * 10**8,
        moved=4 * 10**6,
    )
    by_core = swap_with(send, 1)
    by_chip = swap_chips(sided)
    total = total + by_core[:, side:]
    by_core = by_core[:, :side]
    steps = [1 << b for b in range(1, count.bit_length() - 1)]
    turns = list(zip(steps[1:] + steps[:1], steps))
    for even, odd in turns[:-1]:
        total = total + swap_stage(total, even, odd)
    rolled, total, by_chip = lax.optimization_barrier((rolled, total, by_chip))
    last = swap_stage(total, *turns[-1])
    (out,) = call(
        respond,
        [shape((2, channels, TILE * TILE), BF16)],
        1,
        (meta, flat, rolled, pair, by_core[:, features:], by_chip[:, features:]),
        [
            pltpu.VMEM((4 * channels, 4 * LANES), BF16),
            pltpu.VMEM((TILE // 2, channels, LANES), F32),
        ],
        flops=2 * 10**8,
        moved=2 * 10**6,
    )
    out, last = lax.optimization_barrier((out, last))
    total = total + last
    rest = swap_with(total, 1)
    grad_weight, grad_kernel, grad_embed = call(
        finish,
        [
            shape((channels, features), F32),
            shape((TAPS, channels, channels), F32),
            shape((TILE, features), F32),
        ],
        0,
        (total, rest, by_core, by_chip, near),
        moved=10**6,
    )
    return (
        out.reshape(1, 2, channels, TILE * TILE),
        grad_embed,
        grad_weight.T,
        jnp.transpose(grad_kernel, (1, 0, 2)),
    )


def solution(mesh):
    placed = (
        P(("grp", "blk"), None),
        P(),
        P(),
        P(),
        P(("grp", "blk"), None),
        P(("grp", "blk"), None, None, None),
    )
    return jax.shard_map(
        per_device,
        mesh=mesh,
        in_specs=placed,
        out_specs=(
            P(("grp", "blk"), None, None, None),
            P(("grp", "blk"), None),
            P("grp", None),
            P("grp", None, None),
        ),
        check_vma=False,
    )
```

```python
import jax
import jax.numpy as jnp
from jax import lax
from jax.experimental import pallas as pl
from jax.experimental.pallas import tpu as pltpu
from jax.sharding import PartitionSpec as P

GROUPS = 4
HALO = 8
TILE = 32
LANES = 128
TAPS = 9
F32 = jnp.float32
BF16 = jnp.bfloat16
NN = (((1,), (0,)), ((), ()))
NT = (((1,), (1,)), ((), ()))
TN = (((0,), (0,)), ((), ()))


def dot(a, b, dims=NN):
    return lax.dot_general(a, b, dims, preferred_element_type=F32)


def turn(x, by):
    by = by % LANES
    return x if by == 0 else pltpu.roll(x, by, 1)


def lane_ids(rows):
    return lax.broadcasted_iota(jnp.int32, (rows, LANES), 1)


def within(lane, low, high):
    return jnp.logical_and(lane >= low, lane < high)


def one_hot(target, chunks):
    lane = lane_ids(target.shape[0])
    hits = [jnp.where(target == lane + LANES * c, 1.0, 0.0).astype(BF16) for c in range(chunks)]
    return jnp.concatenate(hits, 1)


def row_ids(rows):
    return lax.broadcasted_iota(jnp.int32, (rows, LANES), 0)


def spread_table(chunks):
    x = row_ids(LANES * chunks)
    return one_hot((((x >> 5) & 3) << 7) + ((x >> 7) << 5) + (x & 31), 4)


def swap_table():
    x = row_ids(HALO * TILE)
    return one_hot(((x & 31) << 3) + (x >> 5), 2)


def edge_table():
    x = row_ids(LANES)
    return one_hot(jnp.where((x & 31) < HALO, ((x & 31) << 5) + (x >> 5), -1), 2)


def corner_table(first):
    x = row_ids(HALO * TILE)
    c = (x & 31) - first
    return one_hot(jnp.where(within(c, 0, HALO), ((x >> 5) << 3) + c, -1), 1)


def as_float(flag):
    return jnp.where(flag, 1.0, 0.0).astype(F32)


def place():
    index = lax.axis_index("blk")
    last = lax.axis_size("blk") - 1
    return index, as_float(index % 2 == 0), as_float(index > 0), as_float(index < last)


def corner_shift(flat, spacing):
    width = flat.shape[0] // GROUPS
    lane = lane_ids(width)
    pieces = []
    for g in range(GROUPS):
        d = spacing[g]
        kept = jnp.logical_and(jnp.logical_and(lane < 8 * HALO, (lane >> 3) < d), (lane & 7) < d)
        x = jnp.where(kept, flat[width * g : width * (g + 1)], 0.0)
        pieces.append(pltpu.roll(x, (HALO + 1) * (HALO - d), 1))
    return jnp.concatenate(pieces, 0).astype(BF16)


def tiles_of(order_ref, cot_ref):
    slot = order_ref[0, 0]
    _, _, _, keep = place()
    return cot_ref[slot], (cot_ref[1 - slot].astype(F32) * keep).astype(BF16)


def fetch(sources, targets, sems):
    copies = [
        pltpu.make_async_copy(source, target, sems.at[i])
        for i, (source, target) in enumerate(zip(sources, targets))
    ]
    for copy in copies:
        copy.start()
    return copies


def pack(
    order_hbm, cot_hbm, embed_hbm,
    chip_ref, core_ref,
    order_ref, cot_ref, embed_ref, sems,
):
    copies = fetch((order_hbm, cot_hbm, embed_hbm), (order_ref, cot_ref, embed_ref), sems)
    edge, head, tail = edge_table(), corner_table(0), corner_table(TILE - HALO)
    for copy in copies:
        copy.wait()
    zero, one = tiles_of(order_ref, cot_ref)
    _, even, _, _ = place()
    channels = zero.shape[0]
    moved = dot(
        jnp.concatenate([zero[:, LANES * j : LANES * (j + 1)] for j in range(8)], 0), edge
    )
    columns = []
    for h in range(2):
        total = None
        for j in range(8):
            piece = moved[channels * j : channels * (j + 1), LANES * h : LANES * (h + 1)]
            piece = turn(piece, 4 * j)
            total = piece if total is None else total + piece
        columns.append(total)
    rim = HALO * TILE
    tail_at = TILE * (TILE - HALO)
    up = [zero[:, :rim].astype(F32)] + columns + [dot(one[:, :rim], head)]
    down = [one[:, tail_at:].astype(F32)] + [jnp.zeros_like(x) for x in columns]
    down += [dot(zero[:, tail_at:], tail)]
    up, down = jnp.concatenate(up, 1), jnp.concatenate(down, 1)
    width = up.shape[1]
    both = jnp.concatenate([embed_ref[:, :LANES], embed_ref[:, LANES:]], 0)
    core_ref[:, :width] = (down * even + up * (1.0 - even)).astype(BF16)
    core_ref[:, width:] = both
    chip_ref[:, :width] = (up * even + down * (1.0 - even)).astype(BF16)
    chip_ref[:, width:] = both


RIM_SIDE, RIM_CORNER, RIM_EMBED, RIM = 256, 512, 640, 768


def from_above(core_ref, chip_ref, at):
    _, even, before, _ = place()
    x = chip_ref[:, at].astype(F32) * (even * before)
    return x + core_ref[:, at].astype(F32) * ((1.0 - even) * before)


def from_below(core_ref, chip_ref, at):
    _, even, _, after = place()
    x = core_ref[:, at].astype(F32) * (even * after)
    return x + chip_ref[:, at].astype(F32) * ((1.0 - even) * after)


def prepare(
    order_ref, dil_ref, cot_ref, kern_ref, weight_ref, embed_ref,
    g_ref, dense_ref, tail_ref, flat_ref, both_ref, scaled_ref, spread_ref, meta_ref,
):
    for g in range(GROUPS):
        meta_ref[g] = jnp.left_shift(jnp.int32(1), dil_ref[g])
    meta_ref[GROUPS] = order_ref[0, 0]
    zero, one = tiles_of(order_ref, cot_ref)
    channels = kern_ref.shape[1]
    swap = swap_table()
    tail_at = TILE * (TILE - HALO)
    y_zero = dot(zero[:, tail_at:], swap)
    y_one = dot(one[:, tail_at:], swap)
    lane = lane_ids(channels)
    own_side = within(lane, 72, 80)
    low = lane < 2 * TILE
    pieces = []
    for j in range(4):
        at = slice(LANES * j, LANES * (j + 1))
        later = slice(LANES * (j + 4), LANES * (j + 5))
        pieces.append(
            jnp.concatenate([zero[:, at], one[:, at], zero[:, later], one[:, later]], 1)
        )
    rows = dot(jnp.concatenate(pieces, 0), spread_table(4))
    for j in range(4):
        for m in range(4):
            row = rows[channels * j : channels * (j + 1), LANES * m : LANES * (m + 1)]
            dense_ref[4 * j + m] = row.astype(BF16)
            for h in range(2):
                r = 16 * h + 4 * j + m
                side = turn(y_zero[:, LANES * h : LANES * (h + 1)], 72 - 8 * (r % 16))
                side = jnp.where(own_side, side, 0.0)
                g_ref[r] = jnp.where(low, turn(row, 64 * h), side).astype(BF16)
    for i in range(HALO):
        rest = turn(y_one[:, :LANES], 72 - 8 * i)
        tail_ref[i] = jnp.where(own_side, rest, 0.0).astype(BF16)
    eye = (
        lax.broadcasted_iota(jnp.int32, (channels, channels), 0)
        == lax.broadcasted_iota(jnp.int32, (channels, channels), 1)
    )
    eye = jnp.where(eye, 1.0, 0.0).astype(BF16)
    for u in range(3):
        for v in range(3):
            t = 3 * u + v
            pair = jnp.concatenate([kern_ref[t], kern_ref[3 * v + u]], 0)
            both_ref[channels * t : channels * (t + 1), :] = dot(eye, pair, NT).astype(BF16)
    for t in range(0, TAPS - 1, 2):
        flat_ref[:, channels * t : channels * (t + 2)] = jnp.concatenate(
            [kern_ref[t].astype(F32), kern_ref[t + 1].astype(F32)], 1
        ).astype(BF16)
    flat_ref[:, channels * (TAPS - 1) : channels * TAPS] = kern_ref[TAPS - 1]
    weight = weight_ref[...].astype(F32)
    own = embed_ref[...].astype(F32)
    for r in range(TILE):
        scaled_ref[channels * r : channels * (r + 1), :] = (own[r : r + 1, :] * weight).astype(
            BF16
        )
    inner = jnp.where(lane < 2 * TILE, 1.0, 0.0).astype(BF16)
    beside = jnp.where(own_side, 1.0, 0.0).astype(BF16)

    def spread_rows(i, carry):
        x = jnp.concatenate([g_ref[2 * i], g_ref[2 * i + 1]], 1)
        y = jnp.concatenate([inner, inner], 1), jnp.concatenate([beside, beside], 1)
        y = dot(both_ref[...], jnp.concatenate([x * y[0], x * y[1]], 0))
        spread_ref[2 * i] = y[:, :LANES]
        spread_ref[2 * i + 1] = y[:, LANES:]
        return carry

    lax.fori_loop(0, TILE // 2, spread_rows, 0, unroll=4)


def unpacked(x):
    return jnp.concatenate([x[:TILE], x[TILE:]], 1)


def forward(
    meta_ref, weight_ref, own_ref, chip_ref, core_ref, dense_ref, scaled_ref,
    part_ref, pair_ref, rolled_ref,
    map_ref,
):
    channels = weight_ref.shape[0]
    width = channels // GROUPS
    weight = weight_ref[...].astype(F32)
    own = own_ref[...].astype(F32)
    after = unpacked(from_below(core_ref, chip_ref, slice(RIM_EMBED, RIM)))
    before = unpacked(from_above(core_ref, chip_ref, slice(RIM_EMBED, RIM)))[TILE - HALO :]
    filler = jnp.zeros((LANES - 2 * TILE - HALO, own.shape[1]), F32)
    columns = jnp.concatenate([own, after, filler, before], 0).astype(BF16)
    lane = lane_ids(channels)
    kept = (
        jnp.logical_or(lane < TILE, lane >= LANES - HALO),
        lane < 2 * TILE,
        within(lane, TILE, 2 * TILE),
    )
    for c in range(6):
        part = 0 if c == 0 else (2 if c == 5 else 1)
        if part == 1:
            scaled = scaled_ref[8 * channels * (c - 1) : 8 * channels * c, :]
        else:
            rim = before if part == 0 else after
            scaled = jnp.concatenate(
                [(rim[i : i + 1, :] * weight).astype(BF16) for i in range(HALO)], 0
            )
        pair = dot(scaled, columns, NT).astype(BF16)
        for i in range(8):
            one = pair[channels * i : channels * (i + 1)]
            if part == 1:
                pair_ref[8 * (c - 1) + i] = one
            x = jnp.where(kept[part], jnp.maximum(one.astype(F32), 0.0), 0.0)
            map_ref[8 * c + i] = x.astype(BF16)
    swap = swap_table()

    def gathered(first, per, low, high, move):
        halves = []
        for half in range(2):
            total = None
            for m in range(per):
                piece = map_ref[first + per * half + m].astype(F32)
                piece = jnp.where(within(lane, low, high), piece, 0.0)
                piece = turn(piece, move(m))
                total = piece if total is None else total + piece
            halves.append(total.astype(BF16))
        return jnp.concatenate(halves, 1)

    above = dot(gathered(0, 4, 0, TILE, lambda m: TILE * m), swap)
    below = dot(gathered(8, 16, TILE, TILE + HALO, lambda m: HALO * m - TILE), swap, NT)
    for r in range(TILE):
        half = LANES * (r // 16)
        side = turn(above[:, half : half + LANES], LANES - HALO - HALO * (r % 16))
        map_ref[HALO + r] += jnp.where(lane >= LANES - HALO, side, 0.0).astype(BF16)
    for i in range(HALO):
        half = LANES * (i // 4)
        side = turn(below[:, half : half + LANES], -TILE * (i % 4))
        map_ref[HALO + TILE + i] += jnp.where(lane < TILE, side, 0.0).astype(BF16)

    spacing = [meta_ref[g] for g in range(GROUPS)]
    source = row_ids(LANES)
    to = lane_ids(LANES)
    for g in range(GROUPS):
        tables = []
        for h in range(2):
            half = within(to, 2 * TILE * h, 2 * TILE * (h + 1))
            offset = jnp.where(half, (source - (to - 2 * TILE * h)) & (LANES - 1), LANES)
            hits = [
                jnp.where(offset == (v * spacing[g]) & (LANES - 1), 1.0, 0.0).astype(BF16)
                for v in (-1, 0, 1)
            ]
            tables.append(jnp.concatenate(hits, 1))
        table = jnp.concatenate(tables, 0)
        at = width * g
        for part in range(2):
            low = [map_ref[16 * part + i, at : at + width, :] for i in range(16)]
            high = [map_ref[16 * part + i + 16, at : at + width, :] for i in range(16)]
            x = jnp.concatenate([jnp.concatenate(low, 0), jnp.concatenate(high, 0)], 1)
            y = dot(x, table).astype(BF16)
            for i in range(16):
                for v in range(3):
                    to_row = channels * v + at
                    rolled_ref[16 * part + i, to_row : to_row + width, :] = y[
                        width * i : width * (i + 1), LANES * v : LANES * (v + 1)
                    ]
    part_ref[...] = jnp.zeros_like(part_ref)

    def sum_rows(j, carry):
        stack = jnp.concatenate([taps_of(rolled_ref, spacing, 2 * j + m) for m in range(2)], 1)
        grads = jnp.concatenate([dense_ref[2 * j], dense_ref[2 * j + 1]], 1)
        part_ref[...] += dot(grads, stack, NT)
        return carry

    lax.fori_loop(0, 8, sum_rows, 0, unroll=4)


def taps_of(rolled_ref, spacing, r):
    channels = rolled_ref.shape[1] // 3
    width = channels // GROUPS
    pieces = []
    for u in range(3):
        for v in range(3):
            for g in range(GROUPS):
                at = channels * v + width * g
                pieces.append(rolled_ref[r + HALO + (u - 1) * spacing[g], at : at + width, :])
    return jnp.concatenate(pieces, 0)


def respond(
    meta_ref, flat_ref, rolled_ref, pair_ref, core_ref, chip_ref,
    out_ref,
    rows_ref, share_ref,
):
    channels = flat_ref.shape[0]
    spacing = [meta_ref[g] for g in range(GROUPS)]
    lane = lane_ids(channels)
    low = lane < 2 * TILE
    _, even, _, keep = place()
    corner = core_ref[...] * even + chip_ref[...].astype(F32) * ((1.0 - even) * keep)
    corner = jnp.concatenate([corner, turn(corner, 8 * HALO)], 0)
    share = dot(flat_ref[:, channels * (TAPS - 1) :], corner_shift(corner, spacing))
    share_ref[:HALO] = jnp.zeros((HALO, channels, LANES), F32)
    for i in range(HALO):
        share_ref[HALO + i] = jnp.where(
            lane >= LANES - HALO, turn(share, LANES - HALO - HALO * i), 0.0
        )

    def conv_rows(j, carry):
        for h in range(2):
            r = 4 * j + 2 * h
            stack = jnp.concatenate([taps_of(rolled_ref, spacing, r + m) for m in range(2)], 1)
            response = dot(flat_ref[...], stack)
            for m in range(2):
                row = jnp.where(
                    low,
                    pair_ref[r + m].astype(F32),
                    turn(pair_ref[r + m + 16].astype(F32), 2 * TILE),
                )
                row = row + (response[:, LANES * m : LANES * (m + 1)] + share_ref[r + m])
                at = LANES * (2 * h + m)
                to = pl.ds(pl.multiple_of(channels * j, channels), channels)
                rows_ref[to, at : at + LANES] = row.astype(BF16)
        return carry

    lax.fori_loop(0, 4, conv_rows, 0)
    slot = meta_ref[GROUPS]
    chunks = dot(rows_ref[...], spread_table(4), NT)
    for j in range(4):
        chunk = chunks[channels * j : channels * (j + 1)]
        for h in range(2):
            at = slice(LANES * (j + 4 * h), LANES * (j + 4 * h + 1))
            to = 2 * LANES * h
            out_ref[slot, :, at] = chunk[:, to : to + LANES].astype(BF16)
            out_ref[1 - slot, :, at] = (chunk[:, to + LANES : to + 2 * LANES] * keep).astype(BF16)


def adjoint(
    meta_ref, g_ref, core_ref, chip_ref, tail_ref, both_ref, pair_ref, spread_ref,
    grad_ref,
    above_ref, below_ref,
):
    channels = g_ref.shape[1]
    width = channels // GROUPS
    span = 3 * channels
    lane = lane_ids(channels)
    zeros = jnp.zeros((channels, LANES), BF16)
    above = from_above(core_ref, chip_ref, slice(0, RIM_EMBED))
    below = from_below(core_ref, chip_ref, slice(0, RIM_EMBED))

    def moved(rim, at, to, size, per, i):
        at += LANES * (i // per)
        x = turn(rim[:, at : at + LANES], to - size * (i % per))
        return jnp.where(within(lane, to, to + size), x, 0.0)

    for h in range(HALO // 2):
        upper, lower = [], []
        for i in (2 * h, 2 * h + 1):
            x = moved(above, 0, 0, TILE, 4, i)
            x = x + moved(above, RIM_CORNER, LANES - HALO, HALO, 16, i)
            upper.append(jnp.concatenate([x.astype(BF16), zeros], 0))
            x = moved(below, 0, TILE, TILE, 4, i)
            x = x + moved(below, RIM_CORNER, 2 * TILE, HALO, 16, i)
            y = moved(below, RIM_SIDE, 80, TILE, 4, i).astype(BF16) + tail_ref[i]
            lower.append(jnp.concatenate([x.astype(BF16), y], 0))
        x = dot(both_ref[2 * span :, :], jnp.concatenate(upper, 1))
        y = dot(both_ref[:span, :], jnp.concatenate(lower, 1))
        for m in range(2):
            above_ref[2 * h + m] = x[:, LANES * m : LANES * (m + 1)]
            below_ref[2 * h + m] = y[:, LANES * m : LANES * (m + 1)]
    spacing = [meta_ref[g] for g in range(GROUPS)]
    second = within(lane, TILE, 2 * TILE)

    def gather_row(first, edge):
        def body(i, carry):
            r = first + i
            pieces = []
            for g in range(GROUPS):
                totals = []
                for v in range(3):
                    at = channels * v + width * g
                    tap = slice(at, at + width)
                    total = spread_ref[r, span + at : span + at + width, :]
                    up, down = r - spacing[g], r + spacing[g]
                    if edge < 0:
                        x = spread_ref[jnp.maximum(up, 0), 2 * span + at : 2 * span + at + width, :]
                        y = above_ref[jnp.minimum(up + HALO, HALO - 1), tap, :]
                        total = total + jnp.where(up < 0, y, x)
                    else:
                        total = total + spread_ref[up, 2 * span + at : 2 * span + at + width, :]
                    if edge > 0:
                        x = spread_ref[jnp.minimum(down, TILE - 1), tap, :]
                        y = below_ref[jnp.maximum(down - TILE, 0), tap, :]
                        total = total + jnp.where(down >= TILE, y, x)
                    else:
                        total = total + spread_ref[down, tap, :]
                    totals.append(total)
                pieces.append(
                    totals[1]
                    + pltpu.roll(totals[0], LANES - spacing[g], 1)
                    + pltpu.roll(totals[2], spacing[g], 1)
                )
            grad = jnp.concatenate(pieces, 0)
            grad = grad + jnp.where(second, turn(grad, -48), 0.0)
            own = g_ref[r].astype(F32)
            own = own + jnp.where(pair_ref[r].astype(F32) > 0, grad, 0.0)
            grad_ref[pl.ds(pl.multiple_of(r * channels, channels), channels), :] = jnp.where(
                lane < 2 * TILE, own, 0.0
            ).astype(BF16)
            return carry

        return body

    lax.fori_loop(0, HALO, gather_row(0, -1), 0, unroll=8)
    lax.fori_loop(0, TILE - 2 * HALO, gather_row(HALO, 0), 0, unroll=8)
    lax.fori_loop(0, HALO, gather_row(TILE - HALO, 1), 0, unroll=8)


def project(
    meta_ref, weight_ref, own_ref, core_ref, chip_ref, grad_ref, part_ref, pair_ref,
    keep_ref, send_ref, corner_ref, local_ref,
    sum_ref, kernel_ref,
):
    channels = weight_ref.shape[0]
    weight = weight_ref[...].astype(F32)
    own = own_ref[...].astype(F32)
    columns = jnp.concatenate(
        [own, unpacked(from_below(core_ref, chip_ref, slice(RIM_EMBED, RIM))), jnp.zeros((LANES - 2 * TILE, own.shape[1]), F32)], 0
    ).astype(BF16)
    weight_part = jnp.zeros_like(weight)
    local = []
    for c in range(4):
        at = slice(8 * channels * c, 8 * channels * (c + 1))
        grad_scaled = dot(grad_ref[at, :], columns)
        for i in range(8):
            one = grad_scaled[channels * i : channels * (i + 1)]
            local.append(jnp.sum(one * weight, 0, keepdims=True))
            weight_part = weight_part + one * own[8 * c + i : 8 * c + i + 1, :]
    local_ref[...] = jnp.concatenate(local, 0)
    lane = lane_ids(channels)
    rim = from_above(core_ref, chip_ref, slice(0, RIM_SIDE))
    corner, ends = None, None
    for i in range(HALO):
        x = jnp.where(within(lane, TILE, TILE + HALO), pair_ref[i].astype(F32), 0.0)
        x = turn(jnp.maximum(x, 0.0), HALO * i - TILE)
        half = LANES * (i // 4)
        y = turn(rim[:, half : half + LANES], HALO * i - TILE * (i % 4) - (TILE - HALO))
        y = jnp.where(within(lane, HALO * i, HALO * (i + 1)), y, 0.0)
        corner, ends = (x, y) if i == 0 else (corner + x, ends + y)
    spacing = [meta_ref[g] for g in range(GROUPS)]
    share = dot(ends.astype(BF16), corner_shift(corner, spacing), NT)
    last = channels * (TAPS - 1)
    kernel_ref[:, :last] = part_ref[:, :last]
    kernel_ref[:, last:] = part_ref[:, last:] + share
    corner = corner[: channels // 2] + turn(corner[channels // 2 :], 8 * HALO)
    sum_ref[...] = weight_part
    rows = channels // 2
    features = own.shape[1]
    half = lax.axis_index("blk") % 2
    mine = pl.ds(pl.multiple_of(rows * half, rows), rows)
    other = pl.ds(pl.multiple_of(rows * (1 - half), rows), rows)
    keep_ref[:, :features] = sum_ref[mine, :]
    keep_ref[:, features:] = kernel_ref[mine, :]
    corner_ref[...] = corner
    send_ref[:, :LANES] = corner
    send_ref[:, LANES : LANES + features] = sum_ref[other, :]
    send_ref[:, LANES + features :] = kernel_ref[other, :]


def embed_terms(grad_ref, scaled_ref, local_ref, corner_ref, near_ref, far_ref, side_ref):
    both = dot(grad_ref[...], scaled_ref[...], TN)
    features = both.shape[1]
    far = both[TILE : 2 * TILE]
    near_ref[...] = local_ref[...] + both[:TILE]
    far_ref[...] = far
    side_ref[:, :features] = far.astype(BF16)
    side_ref[:, features:] = corner_ref[...].astype(BF16)


def finish(
    mine_ref, other_ref, chip_ref, near_ref,
    weight_ref, kernel_ref, embed_ref,
):
    index, even, before, _ = place()
    rows = mine_ref.shape[0]
    channels = 2 * rows
    features = weight_ref.shape[1]
    half = index % 2
    for ref, which in ((mine_ref, half), (other_ref, 1 - half)):
        at = pl.ds(pl.multiple_of(rows * which, rows), rows)
        weight_ref[at, :] = ref[:, :features]
        for t in range(TAPS):
            to = features + channels * t
            kernel_ref[t, at, :] = ref[:, to : to + channels]
    at = features + TAPS * channels
    carried = other_ref[:, at:] * (1.0 - even) + chip_ref[:, :features].astype(F32) * (even * before)
    embed_ref[...] = near_ref[...] + carried


VMEM = pl.BlockSpec(memory_space=pltpu.VMEM)
SMEM = pl.BlockSpec(memory_space=pltpu.SMEM)
HBM = pl.BlockSpec(memory_space=pltpu.HBM)


def shape(dims, kind):
    return jax.ShapeDtypeStruct(dims, kind)


def call(kernel, outs, scalars, operands, scratch=(), flops=0, moved=0, first=None, room=40):
    specs = [first or SMEM] * scalars + [VMEM] * (len(operands) - scalars)
    return pl.pallas_call(
        kernel,
        out_shape=outs,
        in_specs=specs,
        out_specs=[SMEM if out.dtype == jnp.int32 else VMEM for out in outs],
        scratch_shapes=list(scratch),
        compiler_params=pltpu.CompilerParams(vmem_limit_bytes=room * 1024 * 1024),
        cost_estimate=pl.CostEstimate(flops=flops, bytes_accessed=moved, transcendentals=0),
    )(*operands)


def swap_with(shard, step):
    return lax.ppermute(shard, "blk", [(i, i ^ step) for i in range(lax.axis_size("blk"))])


def swap_stage(shard, even, odd):
    pairs = [(i, i ^ (odd if i % 2 else even)) for i in range(lax.axis_size("blk"))]
    return lax.ppermute(shard, "blk", pairs)


def swap_chips(shard):
    count = lax.axis_size("blk")
    pairs = [(i, (i + (1 if i % 2 else -1)) % count) for i in range(count)]
    return lax.ppermute(shard, "blk", pairs)


def per_device(embed, pair_weight, conv_kernel, dilations, tile_order, cotangent):
    features = embed.shape[1]
    channels = conv_kernel.shape[0]
    count = lax.axis_size("blk")
    weight = pair_weight.T
    taps = jnp.transpose(conv_kernel, (1, 0, 2))
    cot = cotangent.reshape(2, channels, TILE * TILE)
    packed = shape((channels, RIM), BF16)
    body = shape((TILE, channels, LANES), BF16)
    to_chip, to_core = call(
        pack,
        [packed, packed],
        3,
        (tile_order, cot, embed),
        [
            pltpu.SMEM(tile_order.shape, jnp.int32),
            pltpu.VMEM(cot.shape, BF16),
            pltpu.VMEM(embed.shape, BF16),
            pltpu.SemaphoreType.DMA((3,)),
        ],
        flops=10**10,
        moved=10**6,
        first=HBM,
        room=60,
    )
    chip = swap_chips(to_chip)
    core = swap_with(to_core, 1)
    grads, dense, tail, flat, both, scaled, spread, meta = call(
        prepare,
        [
            body,
            shape((TILE // 2, channels, LANES), BF16),
            shape((HALO, channels, LANES), BF16),
            shape((channels, TAPS * channels), BF16),
            shape((TAPS * channels, 2 * channels), BF16),
            shape((TILE * channels, features), BF16),
            shape((TILE, TAPS * channels, LANES), F32),
            shape((2 * GROUPS,), jnp.int32),
        ],
        2,
        (tile_order, dilations, cot, taps, weight, embed),
        flops=2 * 10**8,
        moved=3 * 10**6,
    )
    part, pair, rolled = call(
        forward,
        [
            shape((channels, TAPS * channels), F32),
            body,
            shape((TILE, 3 * channels, LANES), BF16),
        ],
        1,
        (meta, weight, embed, chip, core, dense, scaled),
        [pltpu.VMEM((TILE + 2 * HALO, channels, LANES), BF16)],
        flops=8 * 10**8,
        moved=4 * 10**6,
    )
    (grad_pair,) = call(
        adjoint,
        [shape((TILE * channels, LANES), BF16)],
        1,
        (meta, grads, core, chip, tail, both, pair, spread),
        [pltpu.VMEM((HALO, 3 * channels, LANES), F32)] * 2,
        flops=8 * 10**8,
        moved=4 * 10**6,
    )
    width = features + TAPS * channels
    total, send, corner, local = call(
        project,
        [
            shape((channels // 2, width), F32),
            shape((channels // 2, LANES + width), F32),
            shape((channels // 2, LANES), F32),
            shape((TILE, features), F32),
        ],
        1,
        (meta, weight, embed, core, chip, grad_pair, part, pair),
        [pltpu.VMEM((channels, features), F32), pltpu.VMEM((channels, TAPS * channels), F32)],
        flops=4 * 10**8,
        moved=4 * 10**6,
    )
    by_core = swap_with(send, 1)
    near, far, sided = call(
        embed_terms,
        [
            shape((TILE, features), F32),
            shape((TILE, features), F32),
            shape((TILE, features + LANES), BF16),
        ],
        0,
        (grad_pair, scaled, local, corner),
        flops=2 * 10**8,
        moved=2 * 10**6,
    )
    by_chip = swap_chips(sided)
    by_core, sided = lax.optimization_barrier((by_core, sided))
    total = total + by_core[:, LANES:]
    by_core = by_core[:, :LANES]
    steps = [1 << b for b in range(1, count.bit_length() - 1)]
    turns = list(zip(steps, steps[1:] + steps[:1]))
    for even, odd in turns[:-1]:
        total = total + swap_stage(total, even, odd)
    rolled, total, by_chip = lax.optimization_barrier((rolled, total, by_chip))
    last = swap_stage(total, *turns[-1])
    (out,) = call(
        respond,
        [shape((2, channels, TILE * TILE), BF16)],
        1,
        (meta, flat, rolled, pair, by_core, by_chip[:, features:]),
        [
            pltpu.VMEM((4 * channels, 4 * LANES), BF16),
            pltpu.VMEM((TILE // 2, channels, LANES), F32),
        ],
        flops=2 * 10**8,
        moved=2 * 10**6,
    )
    out, last = lax.optimization_barrier((out, last))
    total = total + last
    rest = swap_with(jnp.concatenate([total, far], 1), 1)
    grad_weight, grad_kernel, grad_embed = call(
        finish,
        [
            shape((channels, features), F32),
            shape((TAPS, channels, channels), F32),
            shape((TILE, features), F32),
        ],
        0,
        (total, rest, by_chip, near),
        moved=10**6,
    )
    return (
        out.reshape(1, 2, channels, TILE * TILE),
        grad_embed,
        grad_weight.T,
        jnp.transpose(grad_kernel, (1, 0, 2)),
    )


def solution(mesh):
    placed = (
        P(("grp", "blk"), None),
        P(),
        P(),
        P(),
        P(("grp", "blk"), None),
        P(("grp", "blk"), None, None, None),
    )
    return jax.shard_map(
        per_device,
        mesh=mesh,
        in_specs=placed,
        out_specs=(
            P(("grp", "blk"), None, None, None),
            P(("grp", "blk"), None),
            P("grp", None),
            P("grp", None, None),
        ),
        check_vma=False,
    )
```

```python
import jax
import jax.numpy as jnp
from jax import lax
from jax.experimental import pallas as pl
from jax.experimental.pallas import tpu as pltpu
from jax.sharding import PartitionSpec as P

GROUPS = 4
HALO = 8
TILE = 32
LANES = 128
TAPS = 9
F32 = jnp.float32
BF16 = jnp.bfloat16
NN = (((1,), (0,)), ((), ()))
NT = (((1,), (1,)), ((), ()))
TN = (((0,), (0,)), ((), ()))


def dot(a, b, dims=NN):
    return lax.dot_general(a, b, dims, preferred_element_type=F32)


def turn(x, by):
    by = by % LANES
    return x if by == 0 else pltpu.roll(x, by, 1)


def lane_ids(rows):
    return lax.broadcasted_iota(jnp.int32, (rows, LANES), 1)


def within(lane, low, high):
    return jnp.logical_and(lane >= low, lane < high)


def one_hot(target, chunks):
    lane = lane_ids(target.shape[0])
    hits = [jnp.where(target == lane + LANES * c, 1.0, 0.0).astype(BF16) for c in range(chunks)]
    return jnp.concatenate(hits, 1)


def row_ids(rows):
    return lax.broadcasted_iota(jnp.int32, (rows, LANES), 0)


def spread_table(chunks):
    x = row_ids(LANES * chunks)
    return one_hot((((x >> 5) & 3) << 7) + ((x >> 7) << 5) + (x & 31), 4)


def swap_table():
    x = row_ids(HALO * TILE)
    return one_hot(((x & 31) << 3) + (x >> 5), 2)


def edge_table():
    x = row_ids(LANES)
    return one_hot(jnp.where((x & 31) < HALO, ((x & 31) << 5) + (x >> 5), -1), 2)


def corner_table(first):
    x = row_ids(HALO * TILE)
    c = (x & 31) - first
    return one_hot(jnp.where(within(c, 0, HALO), ((x >> 5) << 3) + c, -1), 1)


def as_float(flag):
    return jnp.where(flag, 1.0, 0.0).astype(F32)


def place():
    index = lax.axis_index("blk")
    last = lax.axis_size("blk") - 1
    return index, as_float(index % 2 == 0), as_float(index > 0), as_float(index < last)


def half_of(index):
    for by in (8, 4, 2, 1):
        index = index ^ (index >> by)
    return index & 1


def corner_shift(flat, spacing):
    width = flat.shape[0] // GROUPS
    lane = lane_ids(width)
    pieces = []
    for g in range(GROUPS):
        d = spacing[g]
        kept = jnp.logical_and(jnp.logical_and(lane < 8 * HALO, (lane >> 3) < d), (lane & 7) < d)
        x = jnp.where(kept, flat[width * g : width * (g + 1)], 0.0)
        pieces.append(pltpu.roll(x, (HALO + 1) * (HALO - d), 1))
    return jnp.concatenate(pieces, 0).astype(BF16)


def tiles_of(order_ref, cot_ref):
    slot = order_ref[0, 0]
    _, _, _, keep = place()
    return cot_ref[slot], (cot_ref[1 - slot].astype(F32) * keep).astype(BF16)


def fetch(sources, targets, sems):
    copies = [
        pltpu.make_async_copy(source, target, sems.at[i])
        for i, (source, target) in enumerate(zip(sources, targets))
    ]
    for copy in copies:
        copy.start()
    return copies


def pack(
    order_hbm, cot_hbm, embed_hbm,
    chip_ref, core_ref,
    order_ref, cot_ref, embed_ref, sems,
):
    copies = fetch((order_hbm, cot_hbm, embed_hbm), (order_ref, cot_ref, embed_ref), sems)
    edge, head, tail = edge_table(), corner_table(0), corner_table(TILE - HALO)
    for copy in copies:
        copy.wait()
    zero, one = tiles_of(order_ref, cot_ref)
    _, even, _, _ = place()
    channels = zero.shape[0]
    moved = dot(
        jnp.concatenate([zero[:, LANES * j : LANES * (j + 1)] for j in range(8)], 0), edge
    )
    columns = []
    for h in range(2):
        total = None
        for j in range(8):
            piece = moved[channels * j : channels * (j + 1), LANES * h : LANES * (h + 1)]
            piece = turn(piece, 4 * j)
            total = piece if total is None else total + piece
        columns.append(total)
    rim = HALO * TILE
    tail_at = TILE * (TILE - HALO)
    up = [zero[:, :rim].astype(F32)] + columns + [dot(one[:, :rim], head)]
    down = [one[:, tail_at:].astype(F32)] + [jnp.zeros_like(x) for x in columns]
    down += [dot(zero[:, tail_at:], tail)]
    up, down = jnp.concatenate(up, 1), jnp.concatenate(down, 1)
    width = up.shape[1]
    both = jnp.concatenate([embed_ref[:, :LANES], embed_ref[:, LANES:]], 0)
    core_ref[:, :width] = (down * even + up * (1.0 - even)).astype(BF16)
    core_ref[:, width:] = both
    chip_ref[:, :width] = (up * even + down * (1.0 - even)).astype(BF16)
    chip_ref[:, width:] = both


RIM_SIDE, RIM_CORNER, RIM_EMBED, RIM = 256, 512, 640, 768


def from_above(core_ref, chip_ref, at):
    _, even, before, _ = place()
    x = chip_ref[:, at].astype(F32) * (even * before)
    return x + core_ref[:, at].astype(F32) * ((1.0 - even) * before)


def from_below(core_ref, chip_ref, at):
    _, even, _, after = place()
    x = core_ref[:, at].astype(F32) * (even * after)
    return x + chip_ref[:, at].astype(F32) * ((1.0 - even) * after)


def prepare(
    order_ref, dil_ref, cot_ref, kern_ref, weight_ref, embed_ref,
    g_ref, dense_ref, tail_ref, flat_ref, both_ref, scaled_ref, spread_ref, meta_ref,
):
    for g in range(GROUPS):
        meta_ref[g] = jnp.left_shift(jnp.int32(1), dil_ref[g])
    meta_ref[GROUPS] = order_ref[0, 0]
    zero, one = tiles_of(order_ref, cot_ref)
    channels = kern_ref.shape[1]
    swap = swap_table()
    tail_at = TILE * (TILE - HALO)
    y_zero = dot(zero[:, tail_at:], swap)
    y_one = dot(one[:, tail_at:], swap)
    lane = lane_ids(channels)
    own_side = within(lane, 72, 80)
    low = lane < 2 * TILE
    pieces = []
    for j in range(4):
        at = slice(LANES * j, LANES * (j + 1))
        later = slice(LANES * (j + 4), LANES * (j + 5))
        pieces.append(
            jnp.concatenate([zero[:, at], one[:, at], zero[:, later], one[:, later]], 1)
        )
    rows = dot(jnp.concatenate(pieces, 0), spread_table(4))
    for j in range(4):
        for m in range(4):
            row = rows[channels * j : channels * (j + 1), LANES * m : LANES * (m + 1)]
            dense_ref[4 * j + m] = row.astype(BF16)
            for h in range(2):
                r = 16 * h + 4 * j + m
                side = turn(y_zero[:, LANES * h : LANES * (h + 1)], 72 - 8 * (r % 16))
                side = jnp.where(own_side, side, 0.0)
                g_ref[r] = jnp.where(low, turn(row, 64 * h), side).astype(BF16)
    for i in range(HALO):
        rest = turn(y_one[:, :LANES], 72 - 8 * i)
        tail_ref[i] = jnp.where(own_side, rest, 0.0).astype(BF16)
    eye = (
        lax.broadcasted_iota(jnp.int32, (channels, channels), 0)
        == lax.broadcasted_iota(jnp.int32, (channels, channels), 1)
    )
    eye = jnp.where(eye, 1.0, 0.0).astype(BF16)
    for u in range(3):
        for v in range(3):
            t = 3 * u + v
            pair = jnp.concatenate([kern_ref[t], kern_ref[3 * v + u]], 0)
            both_ref[channels * t : channels * (t + 1), :] = dot(eye, pair, NT).astype(BF16)
    for t in range(0, TAPS - 1, 2):
        flat_ref[:, channels * t : channels * (t + 2)] = jnp.concatenate(
            [kern_ref[t].astype(F32), kern_ref[t + 1].astype(F32)], 1
        ).astype(BF16)
    flat_ref[:, channels * (TAPS - 1) : channels * TAPS] = kern_ref[TAPS - 1]
    weight = weight_ref[...].astype(F32)
    own = embed_ref[...].astype(F32)
    for r in range(TILE):
        scaled_ref[channels * r : channels * (r + 1), :] = (own[r : r + 1, :] * weight).astype(
            BF16
        )
    inner = jnp.where(lane < 2 * TILE, 1.0, 0.0).astype(BF16)
    beside = jnp.where(own_side, 1.0, 0.0).astype(BF16)

    def spread_rows(i, carry):
        x = jnp.concatenate([g_ref[2 * i], g_ref[2 * i + 1]], 1)
        y = jnp.concatenate([inner, inner], 1), jnp.concatenate([beside, beside], 1)
        y = dot(both_ref[...], jnp.concatenate([x * y[0], x * y[1]], 0))
        spread_ref[2 * i] = y[:, :LANES]
        spread_ref[2 * i + 1] = y[:, LANES:]
        return carry

    lax.fori_loop(0, TILE // 2, spread_rows, 0, unroll=4)


def unpacked(x):
    return jnp.concatenate([x[:TILE], x[TILE:]], 1)


def forward(
    meta_ref, weight_ref, own_ref, chip_ref, core_ref, dense_ref, scaled_ref,
    part_ref, pair_ref, rolled_ref,
    map_ref,
):
    channels = weight_ref.shape[0]
    width = channels // GROUPS
    weight = weight_ref[...].astype(F32)
    own = own_ref[...].astype(F32)
    after = unpacked(from_below(core_ref, chip_ref, slice(RIM_EMBED, RIM)))
    before = unpacked(from_above(core_ref, chip_ref, slice(RIM_EMBED, RIM)))[TILE - HALO :]
    filler = jnp.zeros((LANES - 2 * TILE - HALO, own.shape[1]), F32)
    columns = jnp.concatenate([own, after, filler, before], 0).astype(BF16)
    lane = lane_ids(channels)
    kept = (
        jnp.logical_or(lane < TILE, lane >= LANES - HALO),
        lane < 2 * TILE,
        within(lane, TILE, 2 * TILE),
    )
    for c in range(6):
        part = 0 if c == 0 else (2 if c == 5 else 1)
        if part == 1:
            scaled = scaled_ref[8 * channels * (c - 1) : 8 * channels * c, :]
        else:
            rim = before if part == 0 else after
            scaled = jnp.concatenate(
                [(rim[i : i + 1, :] * weight).astype(BF16) for i in range(HALO)], 0
            )
        pair = dot(scaled, columns, NT).astype(BF16)
        for i in range(8):
            one = pair[channels * i : channels * (i + 1)]
            if part == 1:
                pair_ref[8 * (c - 1) + i] = one
            x = jnp.where(kept[part], jnp.maximum(one.astype(F32), 0.0), 0.0)
            map_ref[8 * c + i] = x.astype(BF16)
    swap = swap_table()

    def gathered(first, per, low, high, move):
        halves = []
        for half in range(2):
            total = None
            for m in range(per):
                piece = map_ref[first + per * half + m].astype(F32)
                piece = jnp.where(within(lane, low, high), piece, 0.0)
                piece = turn(piece, move(m))
                total = piece if total is None else total + piece
            halves.append(total.astype(BF16))
        return jnp.concatenate(halves, 1)

    above = dot(gathered(0, 4, 0, TILE, lambda m: TILE * m), swap)
    below = dot(gathered(8, 16, TILE, TILE + HALO, lambda m: HALO * m - TILE), swap, NT)
    for r in range(TILE):
        half = LANES * (r // 16)
        side = turn(above[:, half : half + LANES], LANES - HALO - HALO * (r % 16))
        map_ref[HALO + r] += jnp.where(lane >= LANES - HALO, side, 0.0).astype(BF16)
    for i in range(HALO):
        half = LANES * (i // 4)
        side = turn(below[:, half : half + LANES], -TILE * (i % 4))
        map_ref[HALO + TILE + i] += jnp.where(lane < TILE, side, 0.0).astype(BF16)

    spacing = [meta_ref[g] for g in range(GROUPS)]
    source = row_ids(LANES)
    to = lane_ids(LANES)
    for g in range(GROUPS):
        tables = []
        for h in range(2):
            half = within(to, 2 * TILE * h, 2 * TILE * (h + 1))
            offset = jnp.where(half, (source - (to - 2 * TILE * h)) & (LANES - 1), LANES)
            hits = [
                jnp.where(offset == (v * spacing[g]) & (LANES - 1), 1.0, 0.0).astype(BF16)
                for v in (-1, 0, 1)
            ]
            tables.append(jnp.concatenate(hits, 1))
        table = jnp.concatenate(tables, 0)
        at = width * g
        for part in range(2):
            low = [map_ref[16 * part + i, at : at + width, :] for i in range(16)]
            high = [map_ref[16 * part + i + 16, at : at + width, :] for i in range(16)]
            x = jnp.concatenate([jnp.concatenate(low, 0), jnp.concatenate(high, 0)], 1)
            y = dot(x, table).astype(BF16)
            for i in range(16):
                for v in range(3):
                    to_row = channels * v + at
                    rolled_ref[16 * part + i, to_row : to_row + width, :] = y[
                        width * i : width * (i + 1), LANES * v : LANES * (v + 1)
                    ]
    part_ref[...] = jnp.zeros_like(part_ref)

    def sum_rows(j, carry):
        stack = jnp.concatenate([taps_of(rolled_ref, spacing, 2 * j + m) for m in range(2)], 1)
        grads = jnp.concatenate([dense_ref[2 * j], dense_ref[2 * j + 1]], 1)
        part_ref[...] += dot(grads, stack, NT)
        return carry

    lax.fori_loop(0, 8, sum_rows, 0, unroll=4)


def taps_of(rolled_ref, spacing, r):
    channels = rolled_ref.shape[1] // 3
    width = channels // GROUPS
    pieces = []
    for u in range(3):
        for v in range(3):
            for g in range(GROUPS):
                at = channels * v + width * g
                pieces.append(rolled_ref[r + HALO + (u - 1) * spacing[g], at : at + width, :])
    return jnp.concatenate(pieces, 0)


def respond(
    meta_ref, flat_ref, rolled_ref, pair_ref, core_ref, chip_ref,
    out_ref,
    rows_ref, share_ref,
):
    channels = flat_ref.shape[0]
    spacing = [meta_ref[g] for g in range(GROUPS)]
    lane = lane_ids(channels)
    low = lane < 2 * TILE
    _, even, _, keep = place()
    corner = core_ref[...] * even + chip_ref[...].astype(F32) * ((1.0 - even) * keep)
    corner = jnp.concatenate([corner, turn(corner, 8 * HALO)], 0)
    share = dot(flat_ref[:, channels * (TAPS - 1) :], corner_shift(corner, spacing))
    share_ref[:HALO] = jnp.zeros((HALO, channels, LANES), F32)
    for i in range(HALO):
        share_ref[HALO + i] = jnp.where(
            lane >= LANES - HALO, turn(share, LANES - HALO - HALO * i), 0.0
        )

    def conv_rows(j, carry):
        for h in range(2):
            r = 4 * j + 2 * h
            stack = jnp.concatenate([taps_of(rolled_ref, spacing, r + m) for m in range(2)], 1)
            response = dot(flat_ref[...], stack)
            for m in range(2):
                row = jnp.where(
                    low,
                    pair_ref[r + m].astype(F32),
                    turn(pair_ref[r + m + 16].astype(F32), 2 * TILE),
                )
                row = row + (response[:, LANES * m : LANES * (m + 1)] + share_ref[r + m])
                at = LANES * (2 * h + m)
                to = pl.ds(pl.multiple_of(channels * j, channels), channels)
                rows_ref[to, at : at + LANES] = row.astype(BF16)
        return carry

    lax.fori_loop(0, 4, conv_rows, 0)
    slot = meta_ref[GROUPS]
    chunks = dot(rows_ref[...], spread_table(4), NT)
    for j in range(4):
        chunk = chunks[channels * j : channels * (j + 1)]
        for h in range(2):
            at = slice(LANES * (j + 4 * h), LANES * (j + 4 * h + 1))
            to = 2 * LANES * h
            out_ref[slot, :, at] = chunk[:, to : to + LANES].astype(BF16)
            out_ref[1 - slot, :, at] = (chunk[:, to + LANES : to + 2 * LANES] * keep).astype(BF16)


def adjoint(
    meta_ref, g_ref, core_ref, chip_ref, tail_ref, both_ref, pair_ref, spread_ref,
    grad_ref,
    above_ref, below_ref,
):
    channels = g_ref.shape[1]
    width = channels // GROUPS
    span = 3 * channels
    lane = lane_ids(channels)
    zeros = jnp.zeros((channels, LANES), BF16)
    above = from_above(core_ref, chip_ref, slice(0, RIM_EMBED))
    below = from_below(core_ref, chip_ref, slice(0, RIM_EMBED))

    def moved(rim, at, to, size, per, i):
        at += LANES * (i // per)
        x = turn(rim[:, at : at + LANES], to - size * (i % per))
        return jnp.where(within(lane, to, to + size), x, 0.0)

    for h in range(HALO // 2):
        upper, lower = [], []
        for i in (2 * h, 2 * h + 1):
            x = moved(above, 0, 0, TILE, 4, i)
            x = x + moved(above, RIM_CORNER, LANES - HALO, HALO, 16, i)
            upper.append(jnp.concatenate([x.astype(BF16), zeros], 0))
            x = moved(below, 0, TILE, TILE, 4, i)
            x = x + moved(below, RIM_CORNER, 2 * TILE, HALO, 16, i)
            y = moved(below, RIM_SIDE, 80, TILE, 4, i).astype(BF16) + tail_ref[i]
            lower.append(jnp.concatenate([x.astype(BF16), y], 0))
        x = dot(both_ref[2 * span :, :], jnp.concatenate(upper, 1))
        y = dot(both_ref[:span, :], jnp.concatenate(lower, 1))
        for m in range(2):
            above_ref[2 * h + m] = x[:, LANES * m : LANES * (m + 1)]
            below_ref[2 * h + m] = y[:, LANES * m : LANES * (m + 1)]
    spacing = [meta_ref[g] for g in range(GROUPS)]
    second = within(lane, TILE, 2 * TILE)

    def gather_row(first, edge):
        def body(i, carry):
            r = first + i
            pieces = []
            for g in range(GROUPS):
                totals = []
                for v in range(3):
                    at = channels * v + width * g
                    tap = slice(at, at + width)
                    total = spread_ref[r, span + at : span + at + width, :]
                    up, down = r - spacing[g], r + spacing[g]
                    if edge < 0:
                        x = spread_ref[jnp.maximum(up, 0), 2 * span + at : 2 * span + at + width, :]
                        y = above_ref[jnp.minimum(up + HALO, HALO - 1), tap, :]
                        total = total + jnp.where(up < 0, y, x)
                    else:
                        total = total + spread_ref[up, 2 * span + at : 2 * span + at + width, :]
                    if edge > 0:
                        x = spread_ref[jnp.minimum(down, TILE - 1), tap, :]
                        y = below_ref[jnp.maximum(down - TILE, 0), tap, :]
                        total = total + jnp.where(down >= TILE, y, x)
                    else:
                        total = total + spread_ref[down, tap, :]
                    totals.append(total)
                pieces.append(
                    totals[1]
                    + pltpu.roll(totals[0], LANES - spacing[g], 1)
                    + pltpu.roll(totals[2], spacing[g], 1)
                )
            grad = jnp.concatenate(pieces, 0)
            grad = grad + jnp.where(second, turn(grad, -48), 0.0)
            own = g_ref[r].astype(F32)
            own = own + jnp.where(pair_ref[r].astype(F32) > 0, grad, 0.0)
            grad_ref[pl.ds(pl.multiple_of(r * channels, channels), channels), :] = jnp.where(
                lane < 2 * TILE, own, 0.0
            ).astype(BF16)
            return carry

        return body

    lax.fori_loop(0, HALO, gather_row(0, -1), 0, unroll=8)
    lax.fori_loop(0, TILE - 2 * HALO, gather_row(HALO, 0), 0, unroll=8)
    lax.fori_loop(0, HALO, gather_row(TILE - HALO, 1), 0, unroll=8)


def project(
    meta_ref, weight_ref, own_ref, core_ref, chip_ref, grad_ref, part_ref, pair_ref,
    keep_ref, send_ref, corner_ref, local_ref,
    sum_ref, kernel_ref,
):
    channels = weight_ref.shape[0]
    weight = weight_ref[...].astype(F32)
    own = own_ref[...].astype(F32)
    columns = jnp.concatenate(
        [own, unpacked(from_below(core_ref, chip_ref, slice(RIM_EMBED, RIM))), jnp.zeros((LANES - 2 * TILE, own.shape[1]), F32)], 0
    ).astype(BF16)
    weight_part = jnp.zeros_like(weight)
    local = []
    for c in range(4):
        at = slice(8 * channels * c, 8 * channels * (c + 1))
        grad_scaled = dot(grad_ref[at, :], columns)
        for i in range(8):
            one = grad_scaled[channels * i : channels * (i + 1)]
            local.append(jnp.sum(one * weight, 0, keepdims=True))
            weight_part = weight_part + one * own[8 * c + i : 8 * c + i + 1, :]
    local_ref[...] = jnp.concatenate(local, 0)
    lane = lane_ids(channels)
    rim = from_above(core_ref, chip_ref, slice(0, RIM_SIDE))
    corner, ends = None, None
    for i in range(HALO):
        x = jnp.where(within(lane, TILE, TILE + HALO), pair_ref[i].astype(F32), 0.0)
        x = turn(jnp.maximum(x, 0.0), HALO * i - TILE)
        half = LANES * (i // 4)
        y = turn(rim[:, half : half + LANES], HALO * i - TILE * (i % 4) - (TILE - HALO))
        y = jnp.where(within(lane, HALO * i, HALO * (i + 1)), y, 0.0)
        corner, ends = (x, y) if i == 0 else (corner + x, ends + y)
    spacing = [meta_ref[g] for g in range(GROUPS)]
    share = dot(ends.astype(BF16), corner_shift(corner, spacing), NT)
    last = channels * (TAPS - 1)
    kernel_ref[:, :last] = part_ref[:, :last]
    kernel_ref[:, last:] = part_ref[:, last:] + share
    corner = corner[: channels // 2] + turn(corner[channels // 2 :], 8 * HALO)
    sum_ref[...] = weight_part
    rows = channels // 2
    features = own.shape[1]
    half = half_of(lax.axis_index("blk"))
    mine = pl.ds(pl.multiple_of(rows * half, rows), rows)
    other = pl.ds(pl.multiple_of(rows * (1 - half), rows), rows)
    keep_ref[:, :features] = sum_ref[mine, :]
    keep_ref[:, features:] = kernel_ref[mine, :]
    corner_ref[...] = corner
    send_ref[:, :LANES] = corner
    send_ref[:, LANES : LANES + features] = sum_ref[other, :]
    send_ref[:, LANES + features :] = kernel_ref[other, :]


def embed_terms(grad_ref, scaled_ref, local_ref, corner_ref, near_ref, far_ref, side_ref):
    both = dot(grad_ref[...], scaled_ref[...], TN)
    features = both.shape[1]
    far = both[TILE : 2 * TILE]
    near_ref[...] = local_ref[...] + both[:TILE]
    far_ref[...] = far
    side_ref[:, :features] = far.astype(BF16)
    side_ref[:, features:] = corner_ref[...].astype(BF16)


def finish(
    mine_ref, other_ref, chip_ref, near_ref,
    weight_ref, kernel_ref, embed_ref,
):
    index, even, before, _ = place()
    rows = mine_ref.shape[0]
    channels = 2 * rows
    features = weight_ref.shape[1]
    half = half_of(index)
    for ref, which in ((mine_ref, half), (other_ref, 1 - half)):
        at = pl.ds(pl.multiple_of(rows * which, rows), rows)
        weight_ref[at, :] = ref[:, :features]
        for t in range(TAPS):
            to = features + channels * t
            kernel_ref[t, at, :] = ref[:, to : to + channels]
    at = features + TAPS * channels
    carried = other_ref[:, at:] * (1.0 - even) + chip_ref[:, :features].astype(F32) * (even * before)
    embed_ref[...] = near_ref[...] + carried


VMEM = pl.BlockSpec(memory_space=pltpu.VMEM)
SMEM = pl.BlockSpec(memory_space=pltpu.SMEM)
HBM = pl.BlockSpec(memory_space=pltpu.HBM)


def shape(dims, kind):
    return jax.ShapeDtypeStruct(dims, kind)


def call(kernel, outs, scalars, operands, scratch=(), flops=0, moved=0, first=None, room=40):
    specs = [first or SMEM] * scalars + [VMEM] * (len(operands) - scalars)
    return pl.pallas_call(
        kernel,
        out_shape=outs,
        in_specs=specs,
        out_specs=[SMEM if out.dtype == jnp.int32 else VMEM for out in outs],
        scratch_shapes=list(scratch),
        compiler_params=pltpu.CompilerParams(vmem_limit_bytes=room * 1024 * 1024),
        cost_estimate=pl.CostEstimate(flops=flops, bytes_accessed=moved, transcendentals=0),
    )(*operands)


def swap_with(shard, step):
    return lax.ppermute(shard, "blk", [(i, i ^ step) for i in range(lax.axis_size("blk"))])


def swap_stage(shard, first, second):
    pairs = [(i, i ^ (second if half_of(i) else first)) for i in range(lax.axis_size("blk"))]
    return lax.ppermute(shard, "blk", pairs)


def swap_chips(shard):
    count = lax.axis_size("blk")
    pairs = [(i, (i + (1 if i % 2 else -1)) % count) for i in range(count)]
    return lax.ppermute(shard, "blk", pairs)


def per_device(embed, pair_weight, conv_kernel, dilations, tile_order, cotangent):
    features = embed.shape[1]
    channels = conv_kernel.shape[0]
    count = lax.axis_size("blk")
    weight = pair_weight.T
    taps = jnp.transpose(conv_kernel, (1, 0, 2))
    cot = cotangent.reshape(2, channels, TILE * TILE)
    packed = shape((channels, RIM), BF16)
    body = shape((TILE, channels, LANES), BF16)
    to_chip, to_core = call(
        pack,
        [packed, packed],
        3,
        (tile_order, cot, embed),
        [
            pltpu.SMEM(tile_order.shape, jnp.int32),
            pltpu.VMEM(cot.shape, BF16),
            pltpu.VMEM(embed.shape, BF16),
            pltpu.SemaphoreType.DMA((3,)),
        ],
        flops=10**10,
        moved=10**6,
        first=HBM,
        room=60,
    )
    chip = swap_chips(to_chip)
    core = swap_with(to_core, 1)
    grads, dense, tail, flat, both, scaled, spread, meta = call(
        prepare,
        [
            body,
            shape((TILE // 2, channels, LANES), BF16),
            shape((HALO, channels, LANES), BF16),
            shape((channels, TAPS * channels), BF16),
            shape((TAPS * channels, 2 * channels), BF16),
            shape((TILE * channels, features), BF16),
            shape((TILE, TAPS * channels, LANES), F32),
            shape((2 * GROUPS,), jnp.int32),
        ],
        2,
        (tile_order, dilations, cot, taps, weight, embed),
        flops=2 * 10**8,
        moved=3 * 10**6,
    )
    part, pair, rolled = call(
        forward,
        [
            shape((channels, TAPS * channels), F32),
            body,
            shape((TILE, 3 * channels, LANES), BF16),
        ],
        1,
        (meta, weight, embed, chip, core, dense, scaled),
        [pltpu.VMEM((TILE + 2 * HALO, channels, LANES), BF16)],
        flops=8 * 10**8,
        moved=4 * 10**6,
    )
    (grad_pair,) = call(
        adjoint,
        [shape((TILE * channels, LANES), BF16)],
        1,
        (meta, grads, core, chip, tail, both, pair, spread),
        [pltpu.VMEM((HALO, 3 * channels, LANES), F32)] * 2,
        flops=8 * 10**8,
        moved=4 * 10**6,
    )
    width = features + TAPS * channels
    total, send, corner, local = call(
        project,
        [
            shape((channels // 2, width), F32),
            shape((channels // 2, LANES + width), F32),
            shape((channels // 2, LANES), F32),
            shape((TILE, features), F32),
        ],
        1,
        (meta, weight, embed, core, chip, grad_pair, part, pair),
        [pltpu.VMEM((channels, features), F32), pltpu.VMEM((channels, TAPS * channels), F32)],
        flops=4 * 10**8,
        moved=4 * 10**6,
    )
    by_core = swap_with(send, 1)
    near, far, sided = call(
        embed_terms,
        [
            shape((TILE, features), F32),
            shape((TILE, features), F32),
            shape((TILE, features + LANES), BF16),
        ],
        0,
        (grad_pair, scaled, local, corner),
        flops=2 * 10**8,
        moved=2 * 10**6,
    )
    by_chip = swap_chips(sided)
    by_core, sided = lax.optimization_barrier((by_core, sided))
    total = total + by_core[:, LANES:]
    by_core = by_core[:, :LANES]
    steps = [1 | 1 << b for b in range(1, count.bit_length() - 1)]
    turns = list(zip(steps, steps[1:] + steps[:1]))
    for first, second in turns[:-1]:
        total = total + swap_stage(total, first, second)
    rolled, total, by_chip = lax.optimization_barrier((rolled, total, by_chip))
    last = swap_stage(total, *turns[-1])
    (out,) = call(
        respond,
        [shape((2, channels, TILE * TILE), BF16)],
        1,
        (meta, flat, rolled, pair, by_core, by_chip[:, features:]),
        [
            pltpu.VMEM((4 * channels, 4 * LANES), BF16),
            pltpu.VMEM((TILE // 2, channels, LANES), F32),
        ],
        flops=2 * 10**8,
        moved=2 * 10**6,
    )
    out, last = lax.optimization_barrier((out, last))
    total = total + last
    rest = swap_with(jnp.concatenate([total, far], 1), 1)
    grad_weight, grad_kernel, grad_embed = call(
        finish,
        [
            shape((channels, features), F32),
            shape((TAPS, channels, channels), F32),
            shape((TILE, features), F32),
        ],
        0,
        (total, rest, by_chip, near),
        moved=10**6,
    )
    return (
        out.reshape(1, 2, channels, TILE * TILE),
        grad_embed,
        grad_weight.T,
        jnp.transpose(grad_kernel, (1, 0, 2)),
    )


def solution(mesh):
    placed = (
        P(("grp", "blk"), None),
        P(),
        P(),
        P(),
        P(("grp", "blk"), None),
        P(("grp", "blk"), None, None, None),
    )
    return jax.shard_map(
        per_device,
        mesh=mesh,
        in_specs=placed,
        out_specs=(
            P(("grp", "blk"), None, None, None),
            P(("grp", "blk"), None),
            P("grp", None),
            P("grp", None, None),
        ),
        check_vma=False,
    )
```

```python
import jax
import jax.numpy as jnp
from jax import lax
from jax.experimental import pallas as pl
from jax.experimental.pallas import tpu as pltpu
from jax.sharding import PartitionSpec as P

GROUPS = 4
HALO = 8
TILE = 32
LANES = 128
TAPS = 9
F32 = jnp.float32
BF16 = jnp.bfloat16
NN = (((1,), (0,)), ((), ()))
NT = (((1,), (1,)), ((), ()))
TN = (((0,), (0,)), ((), ()))


def dot(a, b, dims=NN):
    return lax.dot_general(a, b, dims, preferred_element_type=F32)


def turn(x, by):
    by = by % LANES
    return x if by == 0 else pltpu.roll(x, by, 1)


def lane_ids(rows):
    return lax.broadcasted_iota(jnp.int32, (rows, LANES), 1)


def within(lane, low, high):
    return jnp.logical_and(lane >= low, lane < high)


def one_hot(target, chunks):
    lane = lane_ids(target.shape[0])
    hits = [jnp.where(target == lane + LANES * c, 1.0, 0.0).astype(BF16) for c in range(chunks)]
    return jnp.concatenate(hits, 1)


def row_ids(rows):
    return lax.broadcasted_iota(jnp.int32, (rows, LANES), 0)


def spread_table(chunks):
    x = row_ids(LANES * chunks)
    return one_hot((((x >> 5) & 3) << 7) + ((x >> 7) << 5) + (x & 31), 4)


def swap_table():
    x = row_ids(HALO * TILE)
    return one_hot(((x & 31) << 3) + (x >> 5), 2)


def edge_table():
    x = row_ids(LANES)
    return one_hot(jnp.where((x & 31) < HALO, ((x & 31) << 5) + (x >> 5), -1), 2)


def corner_table(first):
    x = row_ids(HALO * TILE)
    c = (x & 31) - first
    return one_hot(jnp.where(within(c, 0, HALO), ((x >> 5) << 3) + c, -1), 1)


def as_float(flag):
    return jnp.where(flag, 1.0, 0.0).astype(F32)


def place():
    index = lax.axis_index("blk")
    last = lax.axis_size("blk") - 1
    return index, as_float(index % 2 == 0), as_float(index > 0), as_float(index < last)


def half_of(index):
    for by in (8, 4, 2, 1):
        index = index ^ (index >> by)
    return index & 1


def corner_shift(flat, spacing):
    width = flat.shape[0] // GROUPS
    lane = lane_ids(width)
    pieces = []
    for g in range(GROUPS):
        d = spacing[g]
        kept = jnp.logical_and(jnp.logical_and(lane < 8 * HALO, (lane >> 3) < d), (lane & 7) < d)
        x = jnp.where(kept, flat[width * g : width * (g + 1)], 0.0)
        pieces.append(pltpu.roll(x, (HALO + 1) * (HALO - d), 1))
    return jnp.concatenate(pieces, 0).astype(BF16)


def tiles_of(order_ref, cot_ref):
    slot = order_ref[0, 0]
    _, _, _, keep = place()
    return cot_ref[slot], (cot_ref[1 - slot].astype(F32) * keep).astype(BF16)


def fetch(sources, targets, sems):
    copies = [
        pltpu.make_async_copy(source, target, sems.at[i])
        for i, (source, target) in enumerate(zip(sources, targets))
    ]
    for copy in copies:
        copy.start()
    return copies


def pack(
    order_hbm, cot_hbm, embed_hbm,
    chip_ref, core_ref,
    order_ref, cot_ref, embed_ref, sems,
):
    copies = fetch((order_hbm, cot_hbm, embed_hbm), (order_ref, cot_ref, embed_ref), sems)
    edge, head, tail = edge_table(), corner_table(0), corner_table(TILE - HALO)
    for copy in copies:
        copy.wait()
    zero, one = tiles_of(order_ref, cot_ref)
    _, even, _, _ = place()
    channels = zero.shape[0]
    moved = dot(
        jnp.concatenate([zero[:, LANES * j : LANES * (j + 1)] for j in range(8)], 0), edge
    )
    columns = []
    for h in range(2):
        total = None
        for j in range(8):
            piece = moved[channels * j : channels * (j + 1), LANES * h : LANES * (h + 1)]
            piece = turn(piece, 4 * j)
            total = piece if total is None else total + piece
        columns.append(total)
    rim = HALO * TILE
    tail_at = TILE * (TILE - HALO)
    up = [zero[:, :rim].astype(F32)] + columns + [dot(one[:, :rim], head)]
    down = [one[:, tail_at:].astype(F32)] + [jnp.zeros_like(x) for x in columns]
    down += [dot(zero[:, tail_at:], tail)]
    up, down = jnp.concatenate(up, 1), jnp.concatenate(down, 1)
    width = up.shape[1]
    both = jnp.concatenate([embed_ref[:, :LANES], embed_ref[:, LANES:]], 0)
    core_ref[:, :width] = (down * even + up * (1.0 - even)).astype(BF16)
    core_ref[:, width:] = both
    chip_ref[:, :width] = (up * even + down * (1.0 - even)).astype(BF16)
    chip_ref[:, width:] = both


RIM_SIDE, RIM_CORNER, RIM_EMBED, RIM = 256, 512, 640, 768


def from_above(core_ref, chip_ref, at):
    _, even, before, _ = place()
    x = chip_ref[:, at].astype(F32) * (even * before)
    return x + core_ref[:, at].astype(F32) * ((1.0 - even) * before)


def from_below(core_ref, chip_ref, at):
    _, even, _, after = place()
    x = core_ref[:, at].astype(F32) * (even * after)
    return x + chip_ref[:, at].astype(F32) * ((1.0 - even) * after)


def prepare(
    order_ref, dil_ref, cot_ref, kern_ref, weight_ref, embed_ref,
    g_ref, dense_ref, tail_ref, flat_ref, both_ref, scaled_ref, spread_ref, meta_ref,
):
    for g in range(GROUPS):
        meta_ref[g] = jnp.left_shift(jnp.int32(1), dil_ref[g])
    meta_ref[GROUPS] = order_ref[0, 0]
    zero, one = tiles_of(order_ref, cot_ref)
    channels = kern_ref.shape[1]
    swap = swap_table()
    tail_at = TILE * (TILE - HALO)
    y_zero = dot(zero[:, tail_at:], swap)
    y_one = dot(one[:, tail_at:], swap)
    lane = lane_ids(channels)
    own_side = within(lane, 72, 80)
    low = lane < 2 * TILE
    pieces = []
    for j in range(4):
        at = slice(LANES * j, LANES * (j + 1))
        later = slice(LANES * (j + 4), LANES * (j + 5))
        pieces.append(
            jnp.concatenate([zero[:, at], one[:, at], zero[:, later], one[:, later]], 1)
        )
    rows = dot(jnp.concatenate(pieces, 0), spread_table(4))
    for j in range(4):
        for m in range(4):
            row = rows[channels * j : channels * (j + 1), LANES * m : LANES * (m + 1)]
            dense_ref[4 * j + m] = row.astype(BF16)
            for h in range(2):
                r = 16 * h + 4 * j + m
                side = turn(y_zero[:, LANES * h : LANES * (h + 1)], 72 - 8 * (r % 16))
                side = jnp.where(own_side, side, 0.0)
                g_ref[r] = jnp.where(low, turn(row, 64 * h), side).astype(BF16)
    for i in range(HALO):
        rest = turn(y_one[:, :LANES], 72 - 8 * i)
        tail_ref[i] = jnp.where(own_side, rest, 0.0).astype(BF16)
    eye = (
        lax.broadcasted_iota(jnp.int32, (channels, channels), 0)
        == lax.broadcasted_iota(jnp.int32, (channels, channels), 1)
    )
    eye = jnp.where(eye, 1.0, 0.0).astype(BF16)
    for u in range(3):
        for v in range(3):
            t = 3 * u + v
            pair = jnp.concatenate([kern_ref[t], kern_ref[3 * v + u]], 0)
            both_ref[channels * t : channels * (t + 1), :] = dot(eye, pair, NT).astype(BF16)
    for t in range(0, TAPS - 1, 2):
        flat_ref[:, channels * t : channels * (t + 2)] = jnp.concatenate(
            [kern_ref[t].astype(F32), kern_ref[t + 1].astype(F32)], 1
        ).astype(BF16)
    flat_ref[:, channels * (TAPS - 1) : channels * TAPS] = kern_ref[TAPS - 1]
    weight = weight_ref[...].astype(F32)
    own = embed_ref[...].astype(F32)
    for r in range(TILE):
        scaled_ref[channels * r : channels * (r + 1), :] = (own[r : r + 1, :] * weight).astype(
            BF16
        )
    inner = jnp.where(lane < 2 * TILE, 1.0, 0.0).astype(BF16)
    beside = jnp.where(own_side, 1.0, 0.0).astype(BF16)

    def spread_rows(i, carry):
        x = jnp.concatenate([g_ref[2 * i], g_ref[2 * i + 1]], 1)
        y = jnp.concatenate([inner, inner], 1), jnp.concatenate([beside, beside], 1)
        y = dot(both_ref[...], jnp.concatenate([x * y[0], x * y[1]], 0))
        spread_ref[2 * i] = y[:, :LANES]
        spread_ref[2 * i + 1] = y[:, LANES:]
        return carry

    lax.fori_loop(0, TILE // 2, spread_rows, 0, unroll=4)


def unpacked(x):
    return jnp.concatenate([x[:TILE], x[TILE:]], 1)


def forward(
    meta_ref, weight_ref, own_ref, chip_ref, core_ref, dense_ref, scaled_ref,
    part_ref, pair_ref, rolled_ref, map_ref,
):
    channels = weight_ref.shape[0]
    width = channels // GROUPS
    weight = weight_ref[...].astype(F32)
    own = own_ref[...].astype(F32)
    after = unpacked(from_below(core_ref, chip_ref, slice(RIM_EMBED, RIM)))
    before = unpacked(from_above(core_ref, chip_ref, slice(RIM_EMBED, RIM)))[TILE - HALO :]
    filler = jnp.zeros((LANES - 2 * TILE - HALO, own.shape[1]), F32)
    columns = jnp.concatenate([own, after, filler, before], 0).astype(BF16)
    lane = lane_ids(channels)
    kept = (
        jnp.logical_or(lane < TILE, lane >= LANES - HALO),
        lane < 2 * TILE,
        within(lane, TILE, 2 * TILE),
    )
    for c in range(6):
        part = 0 if c == 0 else (2 if c == 5 else 1)
        if part == 1:
            scaled = scaled_ref[8 * channels * (c - 1) : 8 * channels * c, :]
        else:
            rim = before if part == 0 else after
            scaled = jnp.concatenate(
                [(rim[i : i + 1, :] * weight).astype(BF16) for i in range(HALO)], 0
            )
        pair = dot(scaled, columns, NT).astype(BF16)
        for i in range(8):
            one = pair[channels * i : channels * (i + 1)]
            if part == 1:
                pair_ref[8 * (c - 1) + i] = one
            x = jnp.where(kept[part], jnp.maximum(one.astype(F32), 0.0), 0.0)
            map_ref[8 * c + i] = x.astype(BF16)
    swap = swap_table()

    def gathered(first, per, low, high, move):
        halves = []
        for half in range(2):
            total = None
            for m in range(per):
                piece = map_ref[first + per * half + m].astype(F32)
                piece = jnp.where(within(lane, low, high), piece, 0.0)
                piece = turn(piece, move(m))
                total = piece if total is None else total + piece
            halves.append(total.astype(BF16))
        return jnp.concatenate(halves, 1)

    above = dot(gathered(0, 4, 0, TILE, lambda m: TILE * m), swap)
    below = dot(gathered(8, 16, TILE, TILE + HALO, lambda m: HALO * m - TILE), swap, NT)
    for r in range(TILE):
        half = LANES * (r // 16)
        side = turn(above[:, half : half + LANES], LANES - HALO - HALO * (r % 16))
        map_ref[HALO + r] += jnp.where(lane >= LANES - HALO, side, 0.0).astype(BF16)
    for i in range(HALO):
        half = LANES * (i // 4)
        side = turn(below[:, half : half + LANES], -TILE * (i % 4))
        map_ref[HALO + TILE + i] += jnp.where(lane < TILE, side, 0.0).astype(BF16)

    spacing = [meta_ref[g] for g in range(GROUPS)]
    source = row_ids(LANES)
    to = lane_ids(LANES)
    for g in range(GROUPS):
        tables = []
        for h in range(2):
            half = within(to, 2 * TILE * h, 2 * TILE * (h + 1))
            offset = jnp.where(half, (source - (to - 2 * TILE * h)) & (LANES - 1), LANES)
            hits = [
                jnp.where(offset == (v * spacing[g]) & (LANES - 1), 1.0, 0.0).astype(BF16)
                for v in (-1, 0, 1)
            ]
            tables.append(jnp.concatenate(hits, 1))
        table = jnp.concatenate(tables, 0)
        at = width * g
        for part in range(2):
            low = [map_ref[16 * part + i, at : at + width, :] for i in range(16)]
            high = [map_ref[16 * part + i + 16, at : at + width, :] for i in range(16)]
            x = jnp.concatenate([jnp.concatenate(low, 0), jnp.concatenate(high, 0)], 1)
            y = dot(x, table).astype(BF16)
            for i in range(16):
                for v in range(3):
                    to_row = channels * v + at
                    rolled_ref[16 * part + i, to_row : to_row + width, :] = y[
                        width * i : width * (i + 1), LANES * v : LANES * (v + 1)
                    ]
    part_ref[...] = jnp.zeros_like(part_ref)

    def sum_rows(j, carry):
        stack = jnp.concatenate([taps_of(rolled_ref, spacing, 2 * j + m) for m in range(2)], 1)
        grads = jnp.concatenate([dense_ref[2 * j], dense_ref[2 * j + 1]], 1)
        part_ref[...] += dot(grads, stack, NT)
        return carry

    lax.fori_loop(0, 8, sum_rows, 0, unroll=4)


def taps_of(rolled_ref, spacing, r):
    channels = rolled_ref.shape[1] // 3
    width = channels // GROUPS
    pieces = []
    for u in range(3):
        for v in range(3):
            for g in range(GROUPS):
                at = channels * v + width * g
                pieces.append(rolled_ref[r + HALO + (u - 1) * spacing[g], at : at + width, :])
    return jnp.concatenate(pieces, 0)


def respond(
    meta_ref, flat_ref, rolled_ref, pair_ref, core_ref, chip_ref,
    out_ref,
    rows_ref, share_ref,
):
    channels = flat_ref.shape[0]
    spacing = [meta_ref[g] for g in range(GROUPS)]
    lane = lane_ids(channels)
    low = lane < 2 * TILE
    _, even, _, keep = place()
    corner = core_ref[...] * even + chip_ref[...].astype(F32) * ((1.0 - even) * keep)
    low_side, high_side = corner[:, :LANES], corner[:, LANES:]
    corner = jnp.concatenate(
        [low_side, turn(low_side, 64), high_side, turn(high_side, 64)], 0
    )
    share = dot(flat_ref[:, channels * (TAPS - 1) :], corner_shift(corner, spacing))
    share_ref[:HALO] = jnp.zeros((HALO, channels, LANES), F32)
    for i in range(HALO):
        share_ref[HALO + i] = jnp.where(
            lane >= LANES - HALO, turn(share, LANES - HALO - HALO * i), 0.0
        )

    def conv_rows(j, carry):
        for h in range(2):
            r = 4 * j + 2 * h
            stack = jnp.concatenate([taps_of(rolled_ref, spacing, r + m) for m in range(2)], 1)
            response = dot(flat_ref[...], stack)
            for m in range(2):
                row = jnp.where(
                    low,
                    pair_ref[r + m].astype(F32),
                    turn(pair_ref[r + m + 16].astype(F32), 2 * TILE),
                )
                row = row + (response[:, LANES * m : LANES * (m + 1)] + share_ref[r + m])
                at = LANES * (2 * h + m)
                to = pl.ds(pl.multiple_of(channels * j, channels), channels)
                rows_ref[to, at : at + LANES] = row.astype(BF16)
        return carry

    lax.fori_loop(0, 4, conv_rows, 0)
    slot = meta_ref[GROUPS]
    chunks = dot(rows_ref[...], spread_table(4), NT)
    for j in range(4):
        chunk = chunks[channels * j : channels * (j + 1)]
        for h in range(2):
            at = slice(LANES * (j + 4 * h), LANES * (j + 4 * h + 1))
            to = 2 * LANES * h
            out_ref[slot, :, at] = chunk[:, to : to + LANES].astype(BF16)
            out_ref[1 - slot, :, at] = (chunk[:, to + LANES : to + 2 * LANES] * keep).astype(BF16)


def adjoint(
    meta_ref, g_ref, core_ref, chip_ref, tail_ref, both_ref, pair_ref, spread_ref,
    grad_ref, above_ref, below_ref,
):
    channels = g_ref.shape[1]
    width = channels // GROUPS
    span = 3 * channels
    lane = lane_ids(channels)
    zeros = jnp.zeros((channels, LANES), BF16)
    above = from_above(core_ref, chip_ref, slice(0, RIM_EMBED))
    below = from_below(core_ref, chip_ref, slice(0, RIM_EMBED))

    def moved(rim, at, to, size, per, i):
        at += LANES * (i // per)
        x = turn(rim[:, at : at + LANES], to - size * (i % per))
        return jnp.where(within(lane, to, to + size), x, 0.0)

    for h in range(HALO // 2):
        upper, lower = [], []
        for i in (2 * h, 2 * h + 1):
            x = moved(above, 0, 0, TILE, 4, i)
            x = x + moved(above, RIM_CORNER, LANES - HALO, HALO, 16, i)
            upper.append(jnp.concatenate([x.astype(BF16), zeros], 0))
            x = moved(below, 0, TILE, TILE, 4, i)
            x = x + moved(below, RIM_CORNER, 2 * TILE, HALO, 16, i)
            y = moved(below, RIM_SIDE, 80, TILE, 4, i).astype(BF16) + tail_ref[i]
            lower.append(jnp.concatenate([x.astype(BF16), y], 0))
        x = dot(both_ref[2 * span :, :], jnp.concatenate(upper, 1))
        y = dot(both_ref[:span, :], jnp.concatenate(lower, 1))
        for m in range(2):
            above_ref[2 * h + m] = x[:, LANES * m : LANES * (m + 1)]
            below_ref[2 * h + m] = y[:, LANES * m : LANES * (m + 1)]
    spacing = [meta_ref[g] for g in range(GROUPS)]
    second = within(lane, TILE, 2 * TILE)

    def gather_row(first, edge):
        def body(i, carry):
            r = first + i
            pieces = []
            for g in range(GROUPS):
                totals = []
                for v in range(3):
                    at = channels * v + width * g
                    tap = slice(at, at + width)
                    total = spread_ref[r, span + at : span + at + width, :]
                    up, down = r - spacing[g], r + spacing[g]
                    if edge < 0:
                        x = spread_ref[jnp.maximum(up, 0), 2 * span + at : 2 * span + at + width, :]
                        y = above_ref[jnp.minimum(up + HALO, HALO - 1), tap, :]
                        total = total + jnp.where(up < 0, y, x)
                    else:
                        total = total + spread_ref[up, 2 * span + at : 2 * span + at + width, :]
                    if edge > 0:
                        x = spread_ref[jnp.minimum(down, TILE - 1), tap, :]
                        y = below_ref[jnp.maximum(down - TILE, 0), tap, :]
                        total = total + jnp.where(down >= TILE, y, x)
                    else:
                        total = total + spread_ref[down, tap, :]
                    totals.append(total)
                pieces.append(
                    totals[1]
                    + pltpu.roll(totals[0], LANES - spacing[g], 1)
                    + pltpu.roll(totals[2], spacing[g], 1)
                )
            grad = jnp.concatenate(pieces, 0)
            grad = grad + jnp.where(second, turn(grad, -48), 0.0)
            own = g_ref[r].astype(F32)
            own = own + jnp.where(pair_ref[r].astype(F32) > 0, grad, 0.0)
            grad_ref[pl.ds(pl.multiple_of(r * channels, channels), channels), :] = jnp.where(
                lane < 2 * TILE, own, 0.0
            ).astype(BF16)
            return carry

        return body

    lax.fori_loop(0, HALO, gather_row(0, -1), 0, unroll=8)
    lax.fori_loop(0, TILE - 2 * HALO, gather_row(HALO, 0), 0, unroll=8)
    lax.fori_loop(0, HALO, gather_row(TILE - HALO, 1), 0, unroll=8)


def project(
    meta_ref, weight_ref, own_ref, core_ref, chip_ref, grad_ref, part_ref, pair_ref,
    keep_ref, send_ref, corner_ref, local_ref, sum_ref, kernel_ref,
):
    channels = weight_ref.shape[0]
    weight = weight_ref[...].astype(F32)
    own = own_ref[...].astype(F32)
    columns = jnp.concatenate(
        [own, unpacked(from_below(core_ref, chip_ref, slice(RIM_EMBED, RIM))), jnp.zeros((LANES - 2 * TILE, own.shape[1]), F32)], 0
    ).astype(BF16)
    weight_part = jnp.zeros_like(weight)
    local = []
    for c in range(4):
        at = slice(8 * channels * c, 8 * channels * (c + 1))
        grad_scaled = dot(grad_ref[at, :], columns)
        for i in range(8):
            one = grad_scaled[channels * i : channels * (i + 1)]
            local.append(jnp.sum(one * weight, 0, keepdims=True))
            weight_part = weight_part + one * own[8 * c + i : 8 * c + i + 1, :]
    local_ref[...] = jnp.concatenate(local, 0)
    lane = lane_ids(channels)
    rim = from_above(core_ref, chip_ref, slice(0, RIM_SIDE))
    corner, ends = None, None
    for i in range(HALO):
        x = jnp.where(within(lane, TILE, TILE + HALO), pair_ref[i].astype(F32), 0.0)
        x = turn(jnp.maximum(x, 0.0), HALO * i - TILE)
        half = LANES * (i // 4)
        y = turn(rim[:, half : half + LANES], HALO * i - TILE * (i % 4) - (TILE - HALO))
        y = jnp.where(within(lane, HALO * i, HALO * (i + 1)), y, 0.0)
        corner, ends = (x, y) if i == 0 else (corner + x, ends + y)
    spacing = [meta_ref[g] for g in range(GROUPS)]
    share = dot(ends.astype(BF16), corner_shift(corner, spacing), NT)
    last = channels * (TAPS - 1)
    kernel_ref[:, :last] = part_ref[:, :last]
    kernel_ref[:, last:] = part_ref[:, last:] + share
    quarter = channels // 4
    corner = [corner[quarter * q : quarter * (q + 1)] for q in range(4)]
    corner = jnp.concatenate(
        [corner[0] + turn(corner[1], 64), corner[2] + turn(corner[3], 64)], 1
    )
    corner_ref[...] = corner
    sum_ref[...] = weight_part
    rows = channels // 2
    half = half_of(lax.axis_index("blk"))
    send_ref[:quarter] = corner
    for ref, which, first in ((keep_ref, half, 0), (send_ref, 1 - half, quarter)):
        at = pl.multiple_of(rows * which, rows)
        ref[first : first + rows] = sum_ref[pl.ds(at, rows), :]
        for q in range(2):
            to = first + rows * (q + 1)
            ref[to : to + rows] = kernel_ref[pl.ds(at, rows), 256 * q : 256 * (q + 1)]
        ref[first + 3 * rows :] = jnp.concatenate(
            [kernel_ref[pl.ds(at + 8 * q, 8), 512:] for q in range(4)], 1
        )


def middle(
    meta_ref, weight_ref, own_ref, chip_ref, core_ref, dense_ref, scaled_ref, g_ref, tail_ref,
    both_ref, spread_ref,
    keep_ref, send_ref, corner_ref, local_ref, grad_ref, pair_ref, rolled_ref,
    map_ref, part_ref, above_ref, below_ref, sum_ref, kernel_ref,
):
    forward(
        meta_ref, weight_ref, own_ref, chip_ref, core_ref, dense_ref, scaled_ref,
        part_ref, pair_ref, rolled_ref, map_ref,
    )
    adjoint(
        meta_ref, g_ref, core_ref, chip_ref, tail_ref, both_ref, pair_ref, spread_ref,
        grad_ref, above_ref, below_ref,
    )
    project(
        meta_ref, weight_ref, own_ref, core_ref, chip_ref, grad_ref, part_ref, pair_ref,
        keep_ref, send_ref, corner_ref, local_ref, sum_ref, kernel_ref,
    )


def embed_terms(grad_ref, scaled_ref, local_ref, corner_ref, near_ref, far_ref, side_ref):
    both = dot(grad_ref[...], scaled_ref[...], TN)
    far = both[TILE : 2 * TILE]
    near_ref[...] = local_ref[...] + both[:TILE]
    far_ref[...] = far
    side_ref[:TILE] = far.astype(BF16)
    side_ref[TILE:] = corner_ref[...].astype(BF16)


def finish(
    mine_ref, other_ref, chip_ref, near_ref,
    weight_ref, kernel_ref, embed_ref,
):
    index, even, before, _ = place()
    channels = kernel_ref.shape[1]
    rows = channels // 2
    half = half_of(index)
    for ref, which in ((mine_ref, half), (other_ref, 1 - half)):
        at = pl.multiple_of(rows * which, rows)
        weight_ref[pl.ds(at, rows), :] = ref[:rows]
        for t in range(TAPS - 1):
            first = rows * (1 + t // 4)
            to = channels * (t % 4)
            kernel_ref[t, pl.ds(at, rows), :] = ref[first : first + rows, to : to + channels]
        for q in range(4):
            kernel_ref[TAPS - 1, pl.ds(at + 8 * q, 8), :] = ref[
                3 * rows : 3 * rows + 8, channels * q : channels * (q + 1)
            ]
    carried = other_ref[3 * rows + 8 :] * (1.0 - even)
    carried = carried + chip_ref[...].astype(F32) * (even * before)
    embed_ref[...] = near_ref[...] + carried


VMEM = pl.BlockSpec(memory_space=pltpu.VMEM)
SMEM = pl.BlockSpec(memory_space=pltpu.SMEM)
HBM = pl.BlockSpec(memory_space=pltpu.HBM)


def shape(dims, kind):
    return jax.ShapeDtypeStruct(dims, kind)


def call(kernel, outs, scalars, operands, scratch=(), flops=0, moved=0, first=None, room=32):
    specs = [first or SMEM] * scalars + [VMEM] * (len(operands) - scalars)
    return pl.pallas_call(
        kernel,
        out_shape=outs,
        in_specs=specs,
        out_specs=[SMEM if out.dtype == jnp.int32 else VMEM for out in outs],
        scratch_shapes=list(scratch),
        compiler_params=pltpu.CompilerParams(vmem_limit_bytes=room * 1024 * 1024),
        cost_estimate=pl.CostEstimate(flops=flops, bytes_accessed=moved, transcendentals=0),
    )(*operands)


def swap_with(shard, step):
    return lax.ppermute(shard, "blk", [(i, i ^ step) for i in range(lax.axis_size("blk"))])


def swap_stage(shard, first, second):
    pairs = [(i, i ^ (second if half_of(i) else first)) for i in range(lax.axis_size("blk"))]
    return lax.ppermute(shard, "blk", pairs)


def swap_chips(shard):
    count = lax.axis_size("blk")
    pairs = [(i, (i + (1 if i % 2 else -1)) % count) for i in range(count)]
    return lax.ppermute(shard, "blk", pairs)


def per_device(embed, pair_weight, conv_kernel, dilations, tile_order, cotangent):
    features = embed.shape[1]
    channels = conv_kernel.shape[0]
    count = lax.axis_size("blk")
    weight = pair_weight.T
    taps = jnp.transpose(conv_kernel, (1, 0, 2))
    cot = cotangent.reshape(2, channels, TILE * TILE)
    packed = shape((channels, RIM), BF16)
    body = shape((TILE, channels, LANES), BF16)
    to_chip, to_core = call(
        pack,
        [packed, packed],
        3,
        (tile_order, cot, embed),
        [
            pltpu.SMEM(tile_order.shape, jnp.int32),
            pltpu.VMEM(cot.shape, BF16),
            pltpu.VMEM(embed.shape, BF16),
            pltpu.SemaphoreType.DMA((3,)),
        ],
        flops=10**10,
        moved=10**6,
        first=HBM,
        room=60,
    )
    chip = swap_chips(to_chip)
    core = swap_with(to_core, 1)
    grads, dense, tail, flat, both, scaled, spread, meta = call(
        prepare,
        [
            body,
            shape((TILE // 2, channels, LANES), BF16),
            shape((HALO, channels, LANES), BF16),
            shape((channels, TAPS * channels), BF16),
            shape((TAPS * channels, 2 * channels), BF16),
            shape((TILE * channels, features), BF16),
            shape((TILE, TAPS * channels, LANES), F32),
            shape((2 * GROUPS,), jnp.int32),
        ],
        2,
        (tile_order, dilations, cot, taps, weight, embed),
        flops=2 * 10**8,
        moved=3 * 10**6,
    )
    rows = channels // 2
    sums = 3 * rows + rows * channels // features
    total, send, corner, local, grad_pair, pair, rolled = call(
        middle,
        [
            shape((sums, features), F32),
            shape((channels // 4 + sums, features), F32),
            shape((channels // 4, features), F32),
            shape((TILE, features), F32),
            shape((TILE * channels, LANES), BF16),
            body,
            shape((TILE, 3 * channels, LANES), BF16),
        ],
        1,
        (meta, weight, embed, chip, core, dense, scaled, grads, tail, both, spread),
        [
            pltpu.VMEM((TILE + 2 * HALO, channels, LANES), BF16),
            pltpu.VMEM((channels, TAPS * channels), F32),
            pltpu.VMEM((HALO, 3 * channels, LANES), F32),
            pltpu.VMEM((HALO, 3 * channels, LANES), F32),
            pltpu.VMEM((channels, features), F32),
            pltpu.VMEM((channels, TAPS * channels), F32),
        ],
        flops=2 * 10**9,
        moved=8 * 10**6,
        room=24,
    )
    by_core = swap_with(send, 1)
    near, far, sided = call(
        embed_terms,
        [
            shape((TILE, features), F32),
            shape((TILE, features), F32),
            shape((TILE + channels // 4, features), BF16),
        ],
        0,
        (grad_pair, scaled, local, corner),
        flops=2 * 10**8,
        moved=2 * 10**6,
    )
    by_chip = swap_chips(sided)
    by_core, sided = lax.optimization_barrier((by_core, sided))
    total = total + by_core[channels // 4 :]
    by_core = by_core[: channels // 4]
    steps = [1 | 1 << b for b in range(1, count.bit_length() - 1)]
    turns = list(zip(steps, steps[1:] + steps[:1]))
    for first, second in turns[:-1]:
        total = total + swap_stage(total, first, second)
    rolled, total, by_chip = lax.optimization_barrier((rolled, total, by_chip))
    last = swap_stage(total, *turns[-1])
    (out,) = call(
        respond,
        [shape((2, channels, TILE * TILE), BF16)],
        1,
        (meta, flat, rolled, pair, by_core, by_chip[TILE:]),
        [
            pltpu.VMEM((4 * channels, 4 * LANES), BF16),
            pltpu.VMEM((TILE // 2, channels, LANES), F32),
        ],
        flops=2 * 10**8,
        moved=2 * 10**6,
    )
    out, last = lax.optimization_barrier((out, last))
    total = total + last
    rest = swap_with(jnp.concatenate([total, far]), 1)
    grad_weight, grad_kernel, grad_embed = call(
        finish,
        [
            shape((channels, features), F32),
            shape((TAPS, channels, channels), F32),
            shape((TILE, features), F32),
        ],
        0,
        (total, rest, by_chip[:TILE], near),
        moved=10**6,
    )
    return (
        out.reshape(1, 2, channels, TILE * TILE),
        grad_embed,
        grad_weight.T,
        jnp.transpose(grad_kernel, (1, 0, 2)),
    )


def solution(mesh):
    placed = (
        P(("grp", "blk"), None),
        P(),
        P(),
        P(),
        P(("grp", "blk"), None),
        P(("grp", "blk"), None, None, None),
    )
    return jax.shard_map(
        per_device,
        mesh=mesh,
        in_specs=placed,
        out_specs=(
            P(("grp", "blk"), None, None, None),
            P(("grp", "blk"), None),
            P("grp", None),
            P("grp", None, None),
        ),
        check_vma=False,
    )
```

```python
import jax
import jax.numpy as jnp
from jax import lax
from jax.experimental import pallas as pl
from jax.experimental.pallas import tpu as pltpu
from jax.sharding import PartitionSpec as P

GROUPS = 4
HALO = 8
TILE = 32
LANES = 128
TAPS = 9
F32 = jnp.float32
BF16 = jnp.bfloat16
NN = (((1,), (0,)), ((), ()))
NT = (((1,), (1,)), ((), ()))
TN = (((0,), (0,)), ((), ()))


def dot(a, b, dims=NN):
    return lax.dot_general(a, b, dims, preferred_element_type=F32)


def turn(x, by):
    by = by % LANES
    return x if by == 0 else pltpu.roll(x, by, 1)


def lane_ids(rows):
    return lax.broadcasted_iota(jnp.int32, (rows, LANES), 1)


def within(lane, low, high):
    return jnp.logical_and(lane >= low, lane < high)


def one_hot(target, chunks):
    lane = lane_ids(target.shape[0])
    hits = [jnp.where(target == lane + LANES * c, 1.0, 0.0).astype(BF16) for c in range(chunks)]
    return jnp.concatenate(hits, 1)


def row_ids(rows):
    return lax.broadcasted_iota(jnp.int32, (rows, LANES), 0)


def spread_table(chunks):
    x = row_ids(LANES * chunks)
    return one_hot((((x >> 5) & 3) << 7) + ((x >> 7) << 5) + (x & 31), 4)


def swap_table():
    x = row_ids(HALO * TILE)
    return one_hot(((x & 31) << 3) + (x >> 5), 2)


def edge_table():
    x = row_ids(LANES)
    return one_hot(jnp.where((x & 31) < HALO, ((x & 31) << 5) + (x >> 5), -1), 2)


def corner_table(first):
    x = row_ids(HALO * TILE)
    c = (x & 31) - first
    return one_hot(jnp.where(within(c, 0, HALO), ((x >> 5) << 3) + c, -1), 1)


def as_float(flag):
    return jnp.where(flag, 1.0, 0.0).astype(F32)


def place():
    index = lax.axis_index("blk")
    last = lax.axis_size("blk") - 1
    return index, as_float(index % 2 == 0), as_float(index > 0), as_float(index < last)


def half_of(index):
    for by in (8, 4, 2, 1):
        index = index ^ (index >> by)
    return index & 1


def corner_shift(flat, spacing):
    width = flat.shape[0] // GROUPS
    lane = lane_ids(width)
    pieces = []
    for g in range(GROUPS):
        d = spacing[g]
        kept = jnp.logical_and(jnp.logical_and(lane < 8 * HALO, (lane >> 3) < d), (lane & 7) < d)
        x = jnp.where(kept, flat[width * g : width * (g + 1)], 0.0)
        pieces.append(pltpu.roll(x, (HALO + 1) * (HALO - d), 1))
    return jnp.concatenate(pieces, 0).astype(BF16)


def tiles_of(order_ref, cot_ref):
    slot = order_ref[0, 0]
    _, _, _, keep = place()
    return cot_ref[slot], (cot_ref[1 - slot].astype(F32) * keep).astype(BF16)


def fetch(sources, targets, sems):
    copies = [
        pltpu.make_async_copy(source, target, sems.at[i])
        for i, (source, target) in enumerate(zip(sources, targets))
    ]
    for copy in copies:
        copy.start()
    return copies


def pack(
    order_hbm, cot_hbm, embed_hbm,
    chip_ref, core_ref,
    order_ref, cot_ref, embed_ref, sems,
):
    half = cot_ref.shape[1] // 2
    pieces = [(t, pl.ds(half * h, half)) for t in range(2) for h in range(2)]
    copies = fetch(
        [order_hbm, embed_hbm] + [cot_hbm.at[piece] for piece in pieces],
        [order_ref, embed_ref] + [cot_ref.at[piece] for piece in pieces],
        sems,
    )
    edge, head, tail = edge_table(), corner_table(0), corner_table(TILE - HALO)
    for copy in copies:
        copy.wait()
    zero, one = tiles_of(order_ref, cot_ref)
    _, even, _, _ = place()
    channels = zero.shape[0]
    moved = dot(
        jnp.concatenate([zero[:, LANES * j : LANES * (j + 1)] for j in range(8)], 0), edge
    )
    columns = []
    for h in range(2):
        total = None
        for j in range(8):
            piece = moved[channels * j : channels * (j + 1), LANES * h : LANES * (h + 1)]
            piece = turn(piece, 4 * j)
            total = piece if total is None else total + piece
        columns.append(total)
    rim = HALO * TILE
    tail_at = TILE * (TILE - HALO)
    up = [zero[:, :rim].astype(F32)] + columns + [dot(one[:, :rim], head)]
    down = [one[:, tail_at:].astype(F32)] + [jnp.zeros_like(x) for x in columns]
    down += [dot(zero[:, tail_at:], tail)]
    up, down = jnp.concatenate(up, 1), jnp.concatenate(down, 1)
    width = up.shape[1]
    both = jnp.concatenate([embed_ref[:, :LANES], embed_ref[:, LANES:]], 0)
    core_ref[:, :width] = (down * even + up * (1.0 - even)).astype(BF16)
    core_ref[:, width:] = both
    chip_ref[:, :width] = (up * even + down * (1.0 - even)).astype(BF16)
    chip_ref[:, width:] = both


RIM_SIDE, RIM_CORNER, RIM_EMBED, RIM = 256, 512, 640, 768


def from_above(core_ref, chip_ref, at):
    _, even, before, _ = place()
    x = chip_ref[:, at].astype(F32) * (even * before)
    return x + core_ref[:, at].astype(F32) * ((1.0 - even) * before)


def from_below(core_ref, chip_ref, at):
    _, even, _, after = place()
    x = core_ref[:, at].astype(F32) * (even * after)
    return x + chip_ref[:, at].astype(F32) * ((1.0 - even) * after)


def prepare(
    order_ref, dil_ref, cot_ref, kern_ref, weight_ref, embed_ref,
    g_ref, dense_ref, tail_ref, flat_ref, both_ref, scaled_ref, spread_ref, meta_ref,
):
    for g in range(GROUPS):
        meta_ref[g] = jnp.left_shift(jnp.int32(1), dil_ref[g])
    meta_ref[GROUPS] = order_ref[0, 0]
    zero, one = tiles_of(order_ref, cot_ref)
    channels = kern_ref.shape[1]
    swap = swap_table()
    tail_at = TILE * (TILE - HALO)
    y_zero = dot(zero[:, tail_at:], swap)
    y_one = dot(one[:, tail_at:], swap)
    lane = lane_ids(channels)
    own_side = within(lane, 72, 80)
    low = lane < 2 * TILE
    pieces = []
    for j in range(4):
        at = slice(LANES * j, LANES * (j + 1))
        later = slice(LANES * (j + 4), LANES * (j + 5))
        pieces.append(
            jnp.concatenate([zero[:, at], one[:, at], zero[:, later], one[:, later]], 1)
        )
    rows = dot(jnp.concatenate(pieces, 0), spread_table(4))
    for j in range(4):
        for m in range(4):
            row = rows[channels * j : channels * (j + 1), LANES * m : LANES * (m + 1)]
            dense_ref[4 * j + m] = row.astype(BF16)
            for h in range(2):
                r = 16 * h + 4 * j + m
                side = turn(y_zero[:, LANES * h : LANES * (h + 1)], 72 - 8 * (r % 16))
                side = jnp.where(own_side, side, 0.0)
                g_ref[r] = jnp.where(low, turn(row, 64 * h), side).astype(BF16)
    for i in range(HALO):
        rest = turn(y_one[:, :LANES], 72 - 8 * i)
        tail_ref[i] = jnp.where(own_side, rest, 0.0).astype(BF16)
    eye = (
        lax.broadcasted_iota(jnp.int32, (channels, channels), 0)
        == lax.broadcasted_iota(jnp.int32, (channels, channels), 1)
    )
    eye = jnp.where(eye, 1.0, 0.0).astype(BF16)
    for u in range(3):
        for v in range(3):
            t = 3 * u + v
            pair = jnp.concatenate([kern_ref[t], kern_ref[3 * v + u]], 0)
            both_ref[channels * t : channels * (t + 1), :] = dot(eye, pair, NT).astype(BF16)
    for t in range(0, TAPS - 1, 2):
        flat_ref[:, channels * t : channels * (t + 2)] = jnp.concatenate(
            [kern_ref[t].astype(F32), kern_ref[t + 1].astype(F32)], 1
        ).astype(BF16)
    flat_ref[:, channels * (TAPS - 1) : channels * TAPS] = kern_ref[TAPS - 1]
    weight = weight_ref[...].astype(F32)
    own = embed_ref[...].astype(F32)
    for r in range(TILE):
        scaled_ref[channels * r : channels * (r + 1), :] = (own[r : r + 1, :] * weight).astype(
            BF16
        )
    inner = jnp.where(lane < 2 * TILE, 1.0, 0.0).astype(BF16)
    beside = jnp.where(own_side, 1.0, 0.0).astype(BF16)

    def spread_rows(i, carry):
        x = jnp.concatenate([g_ref[2 * i], g_ref[2 * i + 1]], 1)
        y = jnp.concatenate([inner, inner], 1), jnp.concatenate([beside, beside], 1)
        y = dot(both_ref[...], jnp.concatenate([x * y[0], x * y[1]], 0))
        spread_ref[2 * i] = y[:, :LANES]
        spread_ref[2 * i + 1] = y[:, LANES:]
        return carry

    lax.fori_loop(0, TILE // 2, spread_rows, 0, unroll=4)


def unpacked(x):
    return jnp.concatenate([x[:TILE], x[TILE:]], 1)


def forward(
    meta_ref, weight_ref, own_ref, chip_ref, core_ref, dense_ref, scaled_ref,
    part_ref, pair_ref, rolled_ref, map_ref,
):
    channels = weight_ref.shape[0]
    width = channels // GROUPS
    weight = weight_ref[...].astype(F32)
    own = own_ref[...].astype(F32)
    after = unpacked(from_below(core_ref, chip_ref, slice(RIM_EMBED, RIM)))
    before = unpacked(from_above(core_ref, chip_ref, slice(RIM_EMBED, RIM)))[TILE - HALO :]
    filler = jnp.zeros((LANES - 2 * TILE - HALO, own.shape[1]), F32)
    columns = jnp.concatenate([own, after, filler, before], 0).astype(BF16)
    lane = lane_ids(channels)
    kept = (
        jnp.logical_or(lane < TILE, lane >= LANES - HALO),
        lane < 2 * TILE,
        within(lane, TILE, 2 * TILE),
    )
    for c in range(6):
        part = 0 if c == 0 else (2 if c == 5 else 1)
        if part == 1:
            scaled = scaled_ref[8 * channels * (c - 1) : 8 * channels * c, :]
        else:
            rim = before if part == 0 else after
            scaled = jnp.concatenate(
                [(rim[i : i + 1, :] * weight).astype(BF16) for i in range(HALO)], 0
            )
        pair = dot(scaled, columns, NT).astype(BF16)
        for i in range(8):
            one = pair[channels * i : channels * (i + 1)]
            if part == 1:
                pair_ref[8 * (c - 1) + i] = one
            x = jnp.where(kept[part], jnp.maximum(one.astype(F32), 0.0), 0.0)
            map_ref[8 * c + i] = x.astype(BF16)
    swap = swap_table()

    def gathered(first, per, low, high, move):
        halves = []
        for half in range(2):
            total = None
            for m in range(per):
                piece = map_ref[first + per * half + m].astype(F32)
                piece = jnp.where(within(lane, low, high), piece, 0.0)
                piece = turn(piece, move(m))
                total = piece if total is None else total + piece
            halves.append(total.astype(BF16))
        return jnp.concatenate(halves, 1)

    above = dot(gathered(0, 4, 0, TILE, lambda m: TILE * m), swap)
    below = dot(gathered(8, 16, TILE, TILE + HALO, lambda m: HALO * m - TILE), swap, NT)
    for r in range(TILE):
        half = LANES * (r // 16)
        side = turn(above[:, half : half + LANES], LANES - HALO - HALO * (r % 16))
        map_ref[HALO + r] += jnp.where(lane >= LANES - HALO, side, 0.0).astype(BF16)
    for i in range(HALO):
        half = LANES * (i // 4)
        side = turn(below[:, half : half + LANES], -TILE * (i % 4))
        map_ref[HALO + TILE + i] += jnp.where(lane < TILE, side, 0.0).astype(BF16)

    spacing = [meta_ref[g] for g in range(GROUPS)]
    source = row_ids(LANES)
    to = lane_ids(LANES)
    for g in range(GROUPS):
        tables = []
        for h in range(2):
            half = within(to, 2 * TILE * h, 2 * TILE * (h + 1))
            offset = jnp.where(half, (source - (to - 2 * TILE * h)) & (LANES - 1), LANES)
            hits = [
                jnp.where(offset == (v * spacing[g]) & (LANES - 1), 1.0, 0.0).astype(BF16)
                for v in (-1, 0, 1)
            ]
            tables.append(jnp.concatenate(hits, 1))
        table = jnp.concatenate(tables, 0)
        at = width * g
        for part in range(2):
            low = [map_ref[16 * part + i, at : at + width, :] for i in range(16)]
            high = [map_ref[16 * part + i + 16, at : at + width, :] for i in range(16)]
            x = jnp.concatenate([jnp.concatenate(low, 0), jnp.concatenate(high, 0)], 1)
            y = dot(x, table).astype(BF16)
            for i in range(16):
                for v in range(3):
                    to_row = channels * v + at
                    rolled_ref[16 * part + i, to_row : to_row + width, :] = y[
                        width * i : width * (i + 1), LANES * v : LANES * (v + 1)
                    ]
    part_ref[...] = jnp.zeros_like(part_ref)

    def sum_rows(j, carry):
        stack = jnp.concatenate([taps_of(rolled_ref, spacing, 2 * j + m) for m in range(2)], 1)
        grads = jnp.concatenate([dense_ref[2 * j], dense_ref[2 * j + 1]], 1)
        part_ref[...] += dot(stack, grads, NT)
        return carry

    lax.fori_loop(0, 8, sum_rows, 0, unroll=4)


def taps_of(rolled_ref, spacing, r):
    channels = rolled_ref.shape[1] // 3
    width = channels // GROUPS
    pieces = []
    for u in range(3):
        for v in range(3):
            for g in range(GROUPS):
                at = channels * v + width * g
                pieces.append(rolled_ref[r + HALO + (u - 1) * spacing[g], at : at + width, :])
    return jnp.concatenate(pieces, 0)


def respond(
    meta_ref, flat_ref, rolled_ref, pair_ref, core_ref, chip_ref,
    out_ref,
    rows_ref, share_ref,
):
    channels = flat_ref.shape[0]
    spacing = [meta_ref[g] for g in range(GROUPS)]
    lane = lane_ids(channels)
    low = lane < 2 * TILE
    _, even, _, keep = place()
    corner = core_ref[...] * even + chip_ref[...].astype(F32) * ((1.0 - even) * keep)
    low_side, high_side = corner[:, :LANES], corner[:, LANES:]
    corner = jnp.concatenate(
        [low_side, turn(low_side, 64), high_side, turn(high_side, 64)], 0
    )
    share = dot(flat_ref[:, channels * (TAPS - 1) :], corner_shift(corner, spacing))
    share_ref[:HALO] = jnp.zeros((HALO, channels, LANES), F32)
    for i in range(HALO):
        share_ref[HALO + i] = jnp.where(
            lane >= LANES - HALO, turn(share, LANES - HALO - HALO * i), 0.0
        )

    def conv_rows(j, carry):
        for h in range(2):
            r = 4 * j + 2 * h
            stack = jnp.concatenate([taps_of(rolled_ref, spacing, r + m) for m in range(2)], 1)
            response = dot(flat_ref[...], stack)
            for m in range(2):
                row = jnp.where(
                    low,
                    pair_ref[r + m].astype(F32),
                    turn(pair_ref[r + m + 16].astype(F32), 2 * TILE),
                )
                row = row + (response[:, LANES * m : LANES * (m + 1)] + share_ref[r + m])
                at = LANES * (2 * h + m)
                to = pl.ds(pl.multiple_of(channels * j, channels), channels)
                rows_ref[to, at : at + LANES] = row.astype(BF16)
        return carry

    lax.fori_loop(0, 4, conv_rows, 0)
    slot = meta_ref[GROUPS]
    chunks = dot(rows_ref[...], spread_table(4), NT)
    for j in range(4):
        chunk = chunks[channels * j : channels * (j + 1)]
        for h in range(2):
            at = slice(LANES * (j + 4 * h), LANES * (j + 4 * h + 1))
            to = 2 * LANES * h
            out_ref[slot, :, at] = chunk[:, to : to + LANES].astype(BF16)
            out_ref[1 - slot, :, at] = (chunk[:, to + LANES : to + 2 * LANES] * keep).astype(BF16)


def adjoint(
    meta_ref, g_ref, core_ref, chip_ref, tail_ref, both_ref, pair_ref, spread_ref,
    grad_ref, above_ref, below_ref,
):
    channels = g_ref.shape[1]
    width = channels // GROUPS
    span = 3 * channels
    lane = lane_ids(channels)
    zeros = jnp.zeros((channels, LANES), BF16)
    above = from_above(core_ref, chip_ref, slice(0, RIM_EMBED))
    below = from_below(core_ref, chip_ref, slice(0, RIM_EMBED))

    def moved(rim, at, to, size, per, i):
        at += LANES * (i // per)
        x = turn(rim[:, at : at + LANES], to - size * (i % per))
        return jnp.where(within(lane, to, to + size), x, 0.0)

    for h in range(HALO // 2):
        upper, lower = [], []
        for i in (2 * h, 2 * h + 1):
            x = moved(above, 0, 0, TILE, 4, i)
            x = x + moved(above, RIM_CORNER, LANES - HALO, HALO, 16, i)
            upper.append(jnp.concatenate([x.astype(BF16), zeros], 0))
            x = moved(below, 0, TILE, TILE, 4, i)
            x = x + moved(below, RIM_CORNER, 2 * TILE, HALO, 16, i)
            y = moved(below, RIM_SIDE, 80, TILE, 4, i).astype(BF16) + tail_ref[i]
            lower.append(jnp.concatenate([x.astype(BF16), y], 0))
        x = dot(both_ref[2 * span :, :], jnp.concatenate(upper, 1))
        y = dot(both_ref[:span, :], jnp.concatenate(lower, 1))
        for m in range(2):
            above_ref[2 * h + m] = x[:, LANES * m : LANES * (m + 1)]
            below_ref[2 * h + m] = y[:, LANES * m : LANES * (m + 1)]
    spacing = [meta_ref[g] for g in range(GROUPS)]
    second = within(lane, TILE, 2 * TILE)

    def gather_row(first, edge):
        def body(i, carry):
            r = first + i
            pieces = []
            for g in range(GROUPS):
                totals = []
                for v in range(3):
                    at = channels * v + width * g
                    tap = slice(at, at + width)
                    total = spread_ref[r, span + at : span + at + width, :]
                    up, down = r - spacing[g], r + spacing[g]
                    if edge < 0:
                        x = spread_ref[jnp.maximum(up, 0), 2 * span + at : 2 * span + at + width, :]
                        y = above_ref[jnp.minimum(up + HALO, HALO - 1), tap, :]
                        total = total + jnp.where(up < 0, y, x)
                    else:
                        total = total + spread_ref[up, 2 * span + at : 2 * span + at + width, :]
                    if edge > 0:
                        x = spread_ref[jnp.minimum(down, TILE - 1), tap, :]
                        y = below_ref[jnp.maximum(down - TILE, 0), tap, :]
                        total = total + jnp.where(down >= TILE, y, x)
                    else:
                        total = total + spread_ref[down, tap, :]
                    totals.append(total)
                pieces.append(
                    totals[1]
                    + pltpu.roll(totals[0], LANES - spacing[g], 1)
                    + pltpu.roll(totals[2], spacing[g], 1)
                )
            grad = jnp.concatenate(pieces, 0)
            grad = grad + jnp.where(second, turn(grad, -48), 0.0)
            own = g_ref[r].astype(F32)
            own = own + jnp.where(pair_ref[r].astype(F32) > 0, grad, 0.0)
            grad_ref[pl.ds(pl.multiple_of(r * channels, channels), channels), :] = jnp.where(
                lane < 2 * TILE, own, 0.0
            ).astype(BF16)
            return carry

        return body

    lax.fori_loop(0, HALO, gather_row(0, -1), 0, unroll=8)
    lax.fori_loop(0, TILE - 2 * HALO, gather_row(HALO, 0), 0, unroll=8)
    lax.fori_loop(0, HALO, gather_row(TILE - HALO, 1), 0, unroll=8)


def project(
    meta_ref, weight_ref, own_ref, core_ref, chip_ref, grad_ref, part_ref, pair_ref,
    keep_ref, send_ref, corner_ref, local_ref, sum_ref, kernel_ref,
):
    channels = weight_ref.shape[0]
    weight = weight_ref[...].astype(F32)
    own = own_ref[...].astype(F32)
    columns = jnp.concatenate(
        [own, unpacked(from_below(core_ref, chip_ref, slice(RIM_EMBED, RIM))), jnp.zeros((LANES - 2 * TILE, own.shape[1]), F32)], 0
    ).astype(BF16)
    weight_part = jnp.zeros_like(weight)
    local = []
    for c in range(4):
        at = slice(8 * channels * c, 8 * channels * (c + 1))
        grad_scaled = dot(grad_ref[at, :], columns)
        for i in range(8):
            one = grad_scaled[channels * i : channels * (i + 1)]
            local.append(jnp.sum(one * weight, 0, keepdims=True))
            weight_part = weight_part + one * own[8 * c + i : 8 * c + i + 1, :]
    local_ref[...] = jnp.concatenate(local, 0)
    lane = lane_ids(channels)
    rim = from_above(core_ref, chip_ref, slice(0, RIM_SIDE))
    corner, ends = None, None
    for i in range(HALO):
        x = jnp.where(within(lane, TILE, TILE + HALO), pair_ref[i].astype(F32), 0.0)
        x = turn(jnp.maximum(x, 0.0), HALO * i - TILE)
        half = LANES * (i // 4)
        y = turn(rim[:, half : half + LANES], HALO * i - TILE * (i % 4) - (TILE - HALO))
        y = jnp.where(within(lane, HALO * i, HALO * (i + 1)), y, 0.0)
        corner, ends = (x, y) if i == 0 else (corner + x, ends + y)
    spacing = [meta_ref[g] for g in range(GROUPS)]
    share = dot(ends.astype(BF16), corner_shift(corner, spacing), NT)
    for t in range(TAPS):
        at = slice(channels * t, channels * (t + 1))
        turned = part_ref[at, :].T
        kernel_ref[:, at] = turned if t < TAPS - 1 else turned + share
    quarter = channels // 4
    corner = [corner[quarter * q : quarter * (q + 1)] for q in range(4)]
    corner = jnp.concatenate(
        [corner[0] + turn(corner[1], 64), corner[2] + turn(corner[3], 64)], 1
    )
    corner_ref[...] = corner
    sum_ref[...] = weight_part
    rows = channels // 2
    half = half_of(lax.axis_index("blk"))
    send_ref[:quarter] = corner
    for ref, which, first in ((keep_ref, half, 0), (send_ref, 1 - half, quarter)):
        at = pl.multiple_of(rows * which, rows)
        ref[first : first + rows] = sum_ref[pl.ds(at, rows), :]
        for q in range(2):
            to = first + rows * (q + 1)
            ref[to : to + rows] = kernel_ref[pl.ds(at, rows), 256 * q : 256 * (q + 1)]
        ref[first + 3 * rows :] = jnp.concatenate(
            [kernel_ref[pl.ds(at + 8 * q, 8), 512:] for q in range(4)], 1
        )


def middle(
    meta_ref, weight_ref, own_ref, chip_ref, core_ref, dense_ref, scaled_ref, g_ref, tail_ref,
    both_ref, spread_ref,
    keep_ref, send_ref, corner_ref, local_ref, grad_ref, pair_ref, rolled_ref,
    map_ref, part_ref, above_ref, below_ref, sum_ref, kernel_ref,
):
    forward(
        meta_ref, weight_ref, own_ref, chip_ref, core_ref, dense_ref, scaled_ref,
        part_ref, pair_ref, rolled_ref, map_ref,
    )
    adjoint(
        meta_ref, g_ref, core_ref, chip_ref, tail_ref, both_ref, pair_ref, spread_ref,
        grad_ref, above_ref, below_ref,
    )
    project(
        meta_ref, weight_ref, own_ref, core_ref, chip_ref, grad_ref, part_ref, pair_ref,
        keep_ref, send_ref, corner_ref, local_ref, sum_ref, kernel_ref,
    )


def embed_terms(grad_ref, scaled_ref, local_ref, corner_ref, near_ref, far_ref, side_ref):
    both = dot(grad_ref[...], scaled_ref[...], TN)
    far = both[TILE : 2 * TILE]
    near_ref[...] = local_ref[...] + both[:TILE]
    far_ref[...] = far
    side_ref[:TILE] = far.astype(BF16)
    side_ref[TILE:] = corner_ref[...].astype(BF16)


def finish(
    mine_ref, other_ref, chip_ref, near_ref,
    weight_ref, kernel_ref, embed_ref,
):
    index, even, before, _ = place()
    channels = kernel_ref.shape[1]
    rows = channels // 2
    half = half_of(index)
    for ref, which in ((mine_ref, half), (other_ref, 1 - half)):
        at = pl.multiple_of(rows * which, rows)
        weight_ref[pl.ds(at, rows), :] = ref[:rows]
        for t in range(TAPS - 1):
            first = rows * (1 + t // 4)
            to = channels * (t % 4)
            kernel_ref[t, pl.ds(at, rows), :] = ref[first : first + rows, to : to + channels]
        for q in range(4):
            kernel_ref[TAPS - 1, pl.ds(at + 8 * q, 8), :] = ref[
                3 * rows : 3 * rows + 8, channels * q : channels * (q + 1)
            ]
    carried = other_ref[3 * rows + 8 :] * (1.0 - even)
    carried = carried + chip_ref[...].astype(F32) * (even * before)
    embed_ref[...] = near_ref[...] + carried


VMEM = pl.BlockSpec(memory_space=pltpu.VMEM)
SMEM = pl.BlockSpec(memory_space=pltpu.SMEM)
HBM = pl.BlockSpec(memory_space=pltpu.HBM)


def shape(dims, kind):
    return jax.ShapeDtypeStruct(dims, kind)


def call(kernel, outs, scalars, operands, scratch=(), flops=0, moved=0, first=None, room=32):
    specs = [first or SMEM] * scalars + [VMEM] * (len(operands) - scalars)
    return pl.pallas_call(
        kernel,
        out_shape=outs,
        in_specs=specs,
        out_specs=[SMEM if out.dtype == jnp.int32 else VMEM for out in outs],
        scratch_shapes=list(scratch),
        compiler_params=pltpu.CompilerParams(vmem_limit_bytes=room * 1024 * 1024),
        cost_estimate=pl.CostEstimate(flops=flops, bytes_accessed=moved, transcendentals=0),
    )(*operands)


def swap_with(shard, step):
    return lax.ppermute(shard, "blk", [(i, i ^ step) for i in range(lax.axis_size("blk"))])


def swap_stage(shard, first, second):
    pairs = [(i, i ^ (second if half_of(i) else first)) for i in range(lax.axis_size("blk"))]
    return lax.ppermute(shard, "blk", pairs)


def swap_chips(shard):
    count = lax.axis_size("blk")
    pairs = [(i, (i + (1 if i % 2 else -1)) % count) for i in range(count)]
    return lax.ppermute(shard, "blk", pairs)


def per_device(embed, pair_weight, conv_kernel, dilations, tile_order, cotangent):
    features = embed.shape[1]
    channels = conv_kernel.shape[0]
    count = lax.axis_size("blk")
    weight = pair_weight.T
    taps = jnp.transpose(conv_kernel, (1, 0, 2))
    cot = cotangent.reshape(2, channels, TILE * TILE)
    packed = shape((channels, RIM), BF16)
    body = shape((TILE, channels, LANES), BF16)
    to_chip, to_core = call(
        pack,
        [packed, packed],
        3,
        (tile_order, cot, embed),
        [
            pltpu.SMEM(tile_order.shape, jnp.int32),
            pltpu.VMEM(cot.shape, BF16),
            pltpu.VMEM(embed.shape, BF16),
            pltpu.SemaphoreType.DMA((6,)),
        ],
        flops=10**10,
        moved=10**6,
        first=HBM,
        room=60,
    )
    chip = swap_chips(to_chip)
    core = swap_with(to_core, 1)
    grads, dense, tail, flat, both, scaled, spread, meta = call(
        prepare,
        [
            body,
            shape((TILE // 2, channels, LANES), BF16),
            shape((HALO, channels, LANES), BF16),
            shape((channels, TAPS * channels), BF16),
            shape((TAPS * channels, 2 * channels), BF16),
            shape((TILE * channels, features), BF16),
            shape((TILE, TAPS * channels, LANES), F32),
            shape((2 * GROUPS,), jnp.int32),
        ],
        2,
        (tile_order, dilations, cot, taps, weight, embed),
        flops=2 * 10**8,
        moved=3 * 10**6,
    )
    rows = channels // 2
    sums = 3 * rows + rows * channels // features
    total, send, corner, local, grad_pair, pair, rolled = call(
        middle,
        [
            shape((sums, features), F32),
            shape((channels // 4 + sums, features), F32),
            shape((channels // 4, features), F32),
            shape((TILE, features), F32),
            shape((TILE * channels, LANES), BF16),
            body,
            shape((TILE, 3 * channels, LANES), BF16),
        ],
        1,
        (meta, weight, embed, chip, core, dense, scaled, grads, tail, both, spread),
        [
            pltpu.VMEM((TILE + 2 * HALO, channels, LANES), BF16),
            pltpu.VMEM((TAPS * channels, channels), F32),
            pltpu.VMEM((HALO, 3 * channels, LANES), F32),
            pltpu.VMEM((HALO, 3 * channels, LANES), F32),
            pltpu.VMEM((channels, features), F32),
            pltpu.VMEM((channels, TAPS * channels), F32),
        ],
        flops=2 * 10**9,
        moved=8 * 10**6,
        room=24,
    )
    by_core = swap_with(send, 1)
    near, far, sided = call(
        embed_terms,
        [
            shape((TILE, features), F32),
            shape((TILE, features), F32),
            shape((TILE + channels // 4, features), BF16),
        ],
        0,
        (grad_pair, scaled, local, corner),
        flops=2 * 10**8,
        moved=2 * 10**6,
    )
    by_chip = swap_chips(sided)
    by_core, sided = lax.optimization_barrier((by_core, sided))
    total = total + by_core[channels // 4 :]
    by_core = by_core[: channels // 4]
    steps = [1 | 1 << b for b in range(1, count.bit_length() - 1)]
    turns = list(zip(steps, steps[1:] + steps[:1]))
    for first, second in turns[:-1]:
        total = total + swap_stage(total, first, second)
    rolled, total, by_chip = lax.optimization_barrier((rolled, total, by_chip))
    last = swap_stage(total, *turns[-1])
    (out,) = call(
        respond,
        [shape((2, channels, TILE * TILE), BF16)],
        1,
        (meta, flat, rolled, pair, by_core, by_chip[TILE:]),
        [
            pltpu.VMEM((4 * channels, 4 * LANES), BF16),
            pltpu.VMEM((TILE // 2, channels, LANES), F32),
        ],
        flops=2 * 10**8,
        moved=2 * 10**6,
    )
    out, last = lax.optimization_barrier((out, last))
    total = total + last
    rest = swap_with(jnp.concatenate([total, far]), 1)
    grad_weight, grad_kernel, grad_embed = call(
        finish,
        [
            shape((channels, features), F32),
            shape((TAPS, channels, channels), F32),
            shape((TILE, features), F32),
        ],
        0,
        (total, rest, by_chip[:TILE], near),
        moved=10**6,
    )
    return (
        out.reshape(1, 2, channels, TILE * TILE),
        grad_embed,
        grad_weight.T,
        jnp.transpose(grad_kernel, (1, 0, 2)),
    )


def solution(mesh):
    placed = (
        P(("grp", "blk"), None),
        P(),
        P(),
        P(),
        P(("grp", "blk"), None),
        P(("grp", "blk"), None, None, None),
    )
    return jax.shard_map(
        per_device,
        mesh=mesh,
        in_specs=placed,
        out_specs=(
            P(("grp", "blk"), None, None, None),
            P(("grp", "blk"), None),
            P("grp", None),
            P("grp", None, None),
        ),
        check_vma=False,
    )
```

```python
import jax
import jax.numpy as jnp
from jax import lax
from jax.experimental import pallas as pl
from jax.experimental.pallas import tpu as pltpu
from jax.sharding import PartitionSpec as P

GROUPS = 4
HALO = 8
TILE = 32
LANES = 128
TAPS = 9
F32 = jnp.float32
BF16 = jnp.bfloat16
NN = (((1,), (0,)), ((), ()))
NT = (((1,), (1,)), ((), ()))
TN = (((0,), (0,)), ((), ()))


def dot(a, b, dims=NN):
    return lax.dot_general(a, b, dims, preferred_element_type=F32)


def turn(x, by):
    by = by % LANES
    return x if by == 0 else pltpu.roll(x, by, 1)


def lane_ids(rows):
    return lax.broadcasted_iota(jnp.int32, (rows, LANES), 1)


def within(lane, low, high):
    return jnp.logical_and(lane >= low, lane < high)


def one_hot(target, chunks):
    lane = lane_ids(target.shape[0])
    hits = [jnp.where(target == lane + LANES * c, 1.0, 0.0).astype(BF16) for c in range(chunks)]
    return jnp.concatenate(hits, 1)


def row_ids(rows):
    return lax.broadcasted_iota(jnp.int32, (rows, LANES), 0)


def spread_table(chunks):
    x = row_ids(LANES * chunks)
    return one_hot((((x >> 5) & 3) << 7) + ((x >> 7) << 5) + (x & 31), 4)


def swap_table():
    x = row_ids(HALO * TILE)
    return one_hot(((x & 31) << 3) + (x >> 5), 2)


def edge_table():
    x = row_ids(LANES)
    return one_hot(jnp.where((x & 31) < HALO, ((x & 31) << 5) + (x >> 5), -1), 2)


def corner_table(first):
    x = row_ids(HALO * TILE)
    c = (x & 31) - first
    return one_hot(jnp.where(within(c, 0, HALO), ((x >> 5) << 3) + c, -1), 1)


def as_float(flag):
    return jnp.where(flag, 1.0, 0.0).astype(F32)


def place():
    index = lax.axis_index("blk")
    last = lax.axis_size("blk") - 1
    return index, as_float(index % 2 == 0), as_float(index > 0), as_float(index < last)


def half_of(index):
    for by in (8, 4, 2, 1):
        index = index ^ (index >> by)
    return index & 1


def corner_shift(flat, spacing):
    width = flat.shape[0] // GROUPS
    lane = lane_ids(width)
    pieces = []
    for g in range(GROUPS):
        d = spacing[g]
        kept = jnp.logical_and(jnp.logical_and(lane < 8 * HALO, (lane >> 3) < d), (lane & 7) < d)
        x = jnp.where(kept, flat[width * g : width * (g + 1)], 0.0)
        pieces.append(pltpu.roll(x, (HALO + 1) * (HALO - d), 1))
    return jnp.concatenate(pieces, 0).astype(BF16)


def tiles_of(order_ref, cot_ref):
    slot = order_ref[0, 0]
    _, _, _, keep = place()
    return cot_ref[slot], (cot_ref[1 - slot].astype(F32) * keep).astype(BF16)


def fetch(sources, targets, sems):
    copies = [
        pltpu.make_async_copy(source, target, sems.at[i])
        for i, (source, target) in enumerate(zip(sources, targets))
    ]
    for copy in copies:
        copy.start()
    return copies


def pack(
    order_hbm, cot_hbm, embed_hbm,
    chip_ref, core_ref,
    order_ref, cot_ref, embed_ref, sems,
):
    copies = fetch((order_hbm, cot_hbm, embed_hbm), (order_ref, cot_ref, embed_ref), sems)
    edge, head, tail = edge_table(), corner_table(0), corner_table(TILE - HALO)
    for copy in copies:
        copy.wait()
    zero, one = tiles_of(order_ref, cot_ref)
    _, even, _, _ = place()
    channels = zero.shape[0]
    moved = dot(
        jnp.concatenate([zero[:, LANES * j : LANES * (j + 1)] for j in range(8)], 0), edge
    )
    columns = []
    for h in range(2):
        total = None
        for j in range(8):
            piece = moved[channels * j : channels * (j + 1), LANES * h : LANES * (h + 1)]
            piece = turn(piece, 4 * j)
            total = piece if total is None else total + piece
        columns.append(total)
    rim = HALO * TILE
    tail_at = TILE * (TILE - HALO)
    up = [zero[:, :rim].astype(F32)] + columns + [dot(one[:, :rim], head)]
    down = [one[:, tail_at:].astype(F32)] + [jnp.zeros_like(x) for x in columns]
    down += [dot(zero[:, tail_at:], tail)]
    up, down = jnp.concatenate(up, 1), jnp.concatenate(down, 1)
    width = up.shape[1]
    both = jnp.concatenate([embed_ref[:, :LANES], embed_ref[:, LANES:]], 0)
    core_ref[:, :width] = (down * even + up * (1.0 - even)).astype(BF16)
    core_ref[:, width:] = both
    chip_ref[:, :width] = (up * even + down * (1.0 - even)).astype(BF16)
    chip_ref[:, width:] = both


RIM_SIDE, RIM_CORNER, RIM_EMBED, RIM = 256, 512, 640, 768


def from_above(core_ref, chip_ref, at):
    _, even, before, _ = place()
    x = chip_ref[:, at].astype(F32) * (even * before)
    return x + core_ref[:, at].astype(F32) * ((1.0 - even) * before)


def from_below(core_ref, chip_ref, at):
    _, even, _, after = place()
    x = core_ref[:, at].astype(F32) * (even * after)
    return x + chip_ref[:, at].astype(F32) * ((1.0 - even) * after)


def prepare(
    order_ref, dil_ref, cot_ref, kern_ref, weight_ref, embed_ref,
    g_ref, dense_ref, tail_ref, flat_ref, both_ref, scaled_ref, spread_ref, meta_ref,
):
    for g in range(GROUPS):
        meta_ref[g] = jnp.left_shift(jnp.int32(1), dil_ref[g])
    meta_ref[GROUPS] = order_ref[0, 0]
    zero, one = tiles_of(order_ref, cot_ref)
    channels = kern_ref.shape[1]
    swap = swap_table()
    tail_at = TILE * (TILE - HALO)
    y_zero = dot(zero[:, tail_at:], swap)
    y_one = dot(one[:, tail_at:], swap)
    lane = lane_ids(channels)
    own_side = within(lane, 72, 80)
    low = lane < 2 * TILE
    pieces = []
    for j in range(4):
        at = slice(LANES * j, LANES * (j + 1))
        later = slice(LANES * (j + 4), LANES * (j + 5))
        pieces.append(
            jnp.concatenate([zero[:, at], one[:, at], zero[:, later], one[:, later]], 1)
        )
    rows = dot(jnp.concatenate(pieces, 0), spread_table(4))
    for j in range(4):
        for m in range(4):
            row = rows[channels * j : channels * (j + 1), LANES * m : LANES * (m + 1)]
            dense_ref[4 * j + m] = row.astype(BF16)
            for h in range(2):
                r = 16 * h + 4 * j + m
                side = turn(y_zero[:, LANES * h : LANES * (h + 1)], 72 - 8 * (r % 16))
                side = jnp.where(own_side, side, 0.0)
                g_ref[r] = jnp.where(low, turn(row, 64 * h), side).astype(BF16)
    for i in range(HALO):
        rest = turn(y_one[:, :LANES], 72 - 8 * i)
        tail_ref[i] = jnp.where(own_side, rest, 0.0).astype(BF16)
    eye = (
        lax.broadcasted_iota(jnp.int32, (channels, channels), 0)
        == lax.broadcasted_iota(jnp.int32, (channels, channels), 1)
    )
    eye = jnp.where(eye, 1.0, 0.0).astype(BF16)
    for u in range(3):
        for v in range(3):
            t = 3 * u + v
            pair = jnp.concatenate([kern_ref[t], kern_ref[3 * v + u]], 0)
            both_ref[channels * t : channels * (t + 1), :] = dot(eye, pair, NT).astype(BF16)
    for t in range(0, TAPS - 1, 2):
        flat_ref[:, channels * t : channels * (t + 2)] = jnp.concatenate(
            [kern_ref[t].astype(F32), kern_ref[t + 1].astype(F32)], 1
        ).astype(BF16)
    flat_ref[:, channels * (TAPS - 1) : channels * TAPS] = kern_ref[TAPS - 1]
    weight = weight_ref[...].astype(F32)
    own = embed_ref[...].astype(F32)
    for r in range(TILE):
        scaled_ref[channels * r : channels * (r + 1), :] = (own[r : r + 1, :] * weight).astype(
            BF16
        )
    inner = jnp.where(lane < 2 * TILE, 1.0, 0.0).astype(BF16)
    beside = jnp.where(own_side, 1.0, 0.0).astype(BF16)

    def spread_rows(i, carry):
        x = jnp.concatenate([g_ref[2 * i], g_ref[2 * i + 1]], 1)
        y = jnp.concatenate([inner, inner], 1), jnp.concatenate([beside, beside], 1)
        y = dot(both_ref[...], jnp.concatenate([x * y[0], x * y[1]], 0))
        spread_ref[2 * i] = y[:, :LANES]
        spread_ref[2 * i + 1] = y[:, LANES:]
        return carry

    lax.fori_loop(0, TILE // 2, spread_rows, 0, unroll=4)


def unpacked(x):
    return jnp.concatenate([x[:TILE], x[TILE:]], 1)


def forward(
    meta_ref, weight_ref, own_ref, chip_ref, core_ref, dense_ref, scaled_ref,
    part_ref, pair_ref, rolled_ref, map_ref,
):
    channels = weight_ref.shape[0]
    width = channels // GROUPS
    weight = weight_ref[...].astype(F32)
    own = own_ref[...].astype(F32)
    after = unpacked(from_below(core_ref, chip_ref, slice(RIM_EMBED, RIM)))
    before = unpacked(from_above(core_ref, chip_ref, slice(RIM_EMBED, RIM)))[TILE - HALO :]
    filler = jnp.zeros((LANES - 2 * TILE - HALO, own.shape[1]), F32)
    columns = jnp.concatenate([own, after, filler, before], 0).astype(BF16)
    lane = lane_ids(channels)
    kept = (
        jnp.logical_or(lane < TILE, lane >= LANES - HALO),
        lane < 2 * TILE,
        within(lane, TILE, 2 * TILE),
    )
    for c in range(6):
        part = 0 if c == 0 else (2 if c == 5 else 1)
        if part == 1:
            scaled = scaled_ref[8 * channels * (c - 1) : 8 * channels * c, :]
        else:
            rim = before if part == 0 else after
            scaled = jnp.concatenate(
                [(rim[i : i + 1, :] * weight).astype(BF16) for i in range(HALO)], 0
            )
        pair = dot(scaled, columns, NT).astype(BF16)
        for i in range(8):
            one = pair[channels * i : channels * (i + 1)]
            if part == 1:
                pair_ref[8 * (c - 1) + i] = one
            x = jnp.where(kept[part], jnp.maximum(one.astype(F32), 0.0), 0.0)
            map_ref[8 * c + i] = x.astype(BF16)
    swap = swap_table()

    def gathered(first, per, low, high, move):
        halves = []
        for half in range(2):
            total = None
            for m in range(per):
                piece = map_ref[first + per * half + m].astype(F32)
                piece = jnp.where(within(lane, low, high), piece, 0.0)
                piece = turn(piece, move(m))
                total = piece if total is None else total + piece
            halves.append(total.astype(BF16))
        return jnp.concatenate(halves, 1)

    above = dot(gathered(0, 4, 0, TILE, lambda m: TILE * m), swap)
    below = dot(gathered(8, 16, TILE, TILE + HALO, lambda m: HALO * m - TILE), swap, NT)
    for r in range(TILE):
        half = LANES * (r // 16)
        side = turn(above[:, half : half + LANES], LANES - HALO - HALO * (r % 16))
        map_ref[HALO + r] += jnp.where(lane >= LANES - HALO, side, 0.0).astype(BF16)
    for i in range(HALO):
        half = LANES * (i // 4)
        side = turn(below[:, half : half + LANES], -TILE * (i % 4))
        map_ref[HALO + TILE + i] += jnp.where(lane < TILE, side, 0.0).astype(BF16)

    spacing = [meta_ref[g] for g in range(GROUPS)]
    source = row_ids(LANES)
    to = lane_ids(LANES)
    for g in range(GROUPS):
        tables = []
        for h in range(2):
            half = within(to, 2 * TILE * h, 2 * TILE * (h + 1))
            offset = jnp.where(half, (source - (to - 2 * TILE * h)) & (LANES - 1), LANES)
            hits = [
                jnp.where(offset == (v * spacing[g]) & (LANES - 1), 1.0, 0.0).astype(BF16)
                for v in (-1, 0, 1)
            ]
            tables.append(jnp.concatenate(hits, 1))
        table = jnp.concatenate(tables, 0)
        at = width * g
        for part in range(2):
            low = [map_ref[16 * part + i, at : at + width, :] for i in range(16)]
            high = [map_ref[16 * part + i + 16, at : at + width, :] for i in range(16)]
            x = jnp.concatenate([jnp.concatenate(low, 0), jnp.concatenate(high, 0)], 1)
            y = dot(x, table).astype(BF16)
            for i in range(16):
                for v in range(3):
                    to_row = channels * v + at
                    rolled_ref[16 * part + i, to_row : to_row + width, :] = y[
                        width * i : width * (i + 1), LANES * v : LANES * (v + 1)
                    ]
    total = None
    for j in range(4):
        rows = range(4 * j, 4 * (j + 1))
        stack = jnp.concatenate([taps_of(rolled_ref, spacing, r) for r in rows], 1)
        share = dot(jnp.concatenate([dense_ref[r] for r in rows], 1), stack, NT)
        total = share if total is None else total + share
    part_ref[...] = total


def taps_of(rolled_ref, spacing, r):
    channels = rolled_ref.shape[1] // 3
    width = channels // GROUPS
    pieces = []
    for u in range(3):
        for v in range(3):
            for g in range(GROUPS):
                at = channels * v + width * g
                pieces.append(rolled_ref[r + HALO + (u - 1) * spacing[g], at : at + width, :])
    return jnp.concatenate(pieces, 0)


def respond(
    meta_ref, flat_ref, rolled_ref, pair_ref, core_ref, chip_ref,
    out_ref,
    rows_ref, share_ref,
):
    channels = flat_ref.shape[0]
    spacing = [meta_ref[g] for g in range(GROUPS)]
    lane = lane_ids(channels)
    low = lane < 2 * TILE
    _, even, _, keep = place()
    corner = core_ref[...] * even + chip_ref[...].astype(F32) * ((1.0 - even) * keep)
    low_side, high_side = corner[:, :LANES], corner[:, LANES:]
    corner = jnp.concatenate(
        [low_side, turn(low_side, 64), high_side, turn(high_side, 64)], 0
    )
    share = dot(flat_ref[:, channels * (TAPS - 1) :], corner_shift(corner, spacing))
    share_ref[:HALO] = jnp.zeros((HALO, channels, LANES), F32)
    for i in range(HALO):
        share_ref[HALO + i] = jnp.where(
            lane >= LANES - HALO, turn(share, LANES - HALO - HALO * i), 0.0
        )

    def conv_rows(j, carry):
        for h in range(2):
            r = 4 * j + 2 * h
            stack = jnp.concatenate([taps_of(rolled_ref, spacing, r + m) for m in range(2)], 1)
            response = dot(flat_ref[...], stack)
            for m in range(2):
                row = jnp.where(
                    low,
                    pair_ref[r + m].astype(F32),
                    turn(pair_ref[r + m + 16].astype(F32), 2 * TILE),
                )
                row = row + (response[:, LANES * m : LANES * (m + 1)] + share_ref[r + m])
                at = LANES * (2 * h + m)
                to = pl.ds(pl.multiple_of(channels * j, channels), channels)
                rows_ref[to, at : at + LANES] = row.astype(BF16)
        return carry

    lax.fori_loop(0, 4, conv_rows, 0)
    slot = meta_ref[GROUPS]
    chunks = dot(rows_ref[...], spread_table(4), NT)
    for j in range(4):
        chunk = chunks[channels * j : channels * (j + 1)]
        for h in range(2):
            at = slice(LANES * (j + 4 * h), LANES * (j + 4 * h + 1))
            to = 2 * LANES * h
            out_ref[slot, :, at] = chunk[:, to : to + LANES].astype(BF16)
            out_ref[1 - slot, :, at] = (chunk[:, to + LANES : to + 2 * LANES] * keep).astype(BF16)


def adjoint(
    meta_ref, g_ref, core_ref, chip_ref, tail_ref, both_ref, pair_ref, spread_ref,
    grad_ref, above_ref, below_ref,
):
    channels = g_ref.shape[1]
    width = channels // GROUPS
    span = 3 * channels
    lane = lane_ids(channels)
    zeros = jnp.zeros((channels, LANES), BF16)
    above = from_above(core_ref, chip_ref, slice(0, RIM_EMBED))
    below = from_below(core_ref, chip_ref, slice(0, RIM_EMBED))

    def moved(rim, at, to, size, per, i):
        at += LANES * (i // per)
        x = turn(rim[:, at : at + LANES], to - size * (i % per))
        return jnp.where(within(lane, to, to + size), x, 0.0)

    for h in range(HALO // 2):
        upper, lower = [], []
        for i in (2 * h, 2 * h + 1):
            x = moved(above, 0, 0, TILE, 4, i)
            x = x + moved(above, RIM_CORNER, LANES - HALO, HALO, 16, i)
            upper.append(jnp.concatenate([x.astype(BF16), zeros], 0))
            x = moved(below, 0, TILE, TILE, 4, i)
            x = x + moved(below, RIM_CORNER, 2 * TILE, HALO, 16, i)
            y = moved(below, RIM_SIDE, 80, TILE, 4, i).astype(BF16) + tail_ref[i]
            lower.append(jnp.concatenate([x.astype(BF16), y], 0))
        x = dot(both_ref[2 * span :, :], jnp.concatenate(upper, 1))
        y = dot(both_ref[:span, :], jnp.concatenate(lower, 1))
        for m in range(2):
            above_ref[2 * h + m] = x[:, LANES * m : LANES * (m + 1)]
            below_ref[2 * h + m] = y[:, LANES * m : LANES * (m + 1)]
    spacing = [meta_ref[g] for g in range(GROUPS)]
    second = within(lane, TILE, 2 * TILE)

    def gather_row(first, edge):
        def body(i, carry):
            r = first + i
            pieces = []
            for g in range(GROUPS):
                totals = []
                for v in range(3):
                    at = channels * v + width * g
                    tap = slice(at, at + width)
                    total = spread_ref[r, span + at : span + at + width, :]
                    up, down = r - spacing[g], r + spacing[g]
                    if edge < 0:
                        x = spread_ref[jnp.maximum(up, 0), 2 * span + at : 2 * span + at + width, :]
                        y = above_ref[jnp.minimum(up + HALO, HALO - 1), tap, :]
                        total = total + jnp.where(up < 0, y, x)
                    else:
                        total = total + spread_ref[up, 2 * span + at : 2 * span + at + width, :]
                    if edge > 0:
                        x = spread_ref[jnp.minimum(down, TILE - 1), tap, :]
                        y = below_ref[jnp.maximum(down - TILE, 0), tap, :]
                        total = total + jnp.where(down >= TILE, y, x)
                    else:
                        total = total + spread_ref[down, tap, :]
                    totals.append(total)
                pieces.append(
                    totals[1]
                    + pltpu.roll(totals[0], LANES - spacing[g], 1)
                    + pltpu.roll(totals[2], spacing[g], 1)
                )
            grad = jnp.concatenate(pieces, 0)
            grad = grad + jnp.where(second, turn(grad, -48), 0.0)
            own = g_ref[r].astype(F32)
            own = own + jnp.where(pair_ref[r].astype(F32) > 0, grad, 0.0)
            grad_ref[pl.ds(pl.multiple_of(r * channels, channels), channels), :] = jnp.where(
                lane < 2 * TILE, own, 0.0
            ).astype(BF16)
            return carry

        return body

    lax.fori_loop(0, HALO, gather_row(0, -1), 0, unroll=8)
    lax.fori_loop(0, TILE - 2 * HALO, gather_row(HALO, 0), 0, unroll=8)
    lax.fori_loop(0, HALO, gather_row(TILE - HALO, 1), 0, unroll=8)


def project(
    meta_ref, weight_ref, own_ref, core_ref, chip_ref, grad_ref, part_ref, pair_ref,
    keep_ref, send_ref, corner_ref, local_ref, sum_ref, kernel_ref,
):
    channels = weight_ref.shape[0]
    weight = weight_ref[...].astype(F32)
    own = own_ref[...].astype(F32)
    columns = jnp.concatenate(
        [own, unpacked(from_below(core_ref, chip_ref, slice(RIM_EMBED, RIM))), jnp.zeros((LANES - 2 * TILE, own.shape[1]), F32)], 0
    ).astype(BF16)
    weight_part = jnp.zeros_like(weight)
    local = []
    for c in range(4):
        at = slice(8 * channels * c, 8 * channels * (c + 1))
        grad_scaled = dot(grad_ref[at, :], columns)
        for i in range(8):
            one = grad_scaled[channels * i : channels * (i + 1)]
            local.append(jnp.sum(one * weight, 0, keepdims=True))
            weight_part = weight_part + one * own[8 * c + i : 8 * c + i + 1, :]
    local_ref[...] = jnp.concatenate(local, 0)
    lane = lane_ids(channels)
    rim = from_above(core_ref, chip_ref, slice(0, RIM_SIDE))
    corner, ends = None, None
    for i in range(HALO):
        x = jnp.where(within(lane, TILE, TILE + HALO), pair_ref[i].astype(F32), 0.0)
        x = turn(jnp.maximum(x, 0.0), HALO * i - TILE)
        half = LANES * (i // 4)
        y = turn(rim[:, half : half + LANES], HALO * i - TILE * (i % 4) - (TILE - HALO))
        y = jnp.where(within(lane, HALO * i, HALO * (i + 1)), y, 0.0)
        corner, ends = (x, y) if i == 0 else (corner + x, ends + y)
    spacing = [meta_ref[g] for g in range(GROUPS)]
    share = dot(ends.astype(BF16), corner_shift(corner, spacing), NT)
    last = channels * (TAPS - 1)
    kernel_ref[:, :last] = part_ref[:, :last]
    kernel_ref[:, last:] = part_ref[:, last:] + share
    quarter = channels // 4
    corner = [corner[quarter * q : quarter * (q + 1)] for q in range(4)]
    corner = jnp.concatenate(
        [corner[0] + turn(corner[1], 64), corner[2] + turn(corner[3], 64)], 1
    )
    corner_ref[...] = corner
    sum_ref[...] = weight_part
    rows = channels // 2
    half = half_of(lax.axis_index("blk"))
    send_ref[:quarter] = corner
    for ref, which, first in ((keep_ref, half, 0), (send_ref, 1 - half, quarter)):
        at = pl.multiple_of(rows * which, rows)
        ref[first : first + rows] = sum_ref[pl.ds(at, rows), :]
        for q in range(2):
            to = first + rows * (q + 1)
            ref[to : to + rows] = kernel_ref[pl.ds(at, rows), 256 * q : 256 * (q + 1)]
        ref[first + 3 * rows :] = jnp.concatenate(
            [kernel_ref[pl.ds(at + 8 * q, 8), 512:] for q in range(4)], 1
        )


def middle(
    meta_ref, weight_ref, own_ref, chip_ref, core_ref, dense_ref, scaled_ref, g_ref, tail_ref,
    both_ref, spread_ref,
    keep_ref, send_ref, corner_ref, local_ref, grad_ref, pair_ref, rolled_ref,
    map_ref, part_ref, above_ref, below_ref, sum_ref, kernel_ref,
):
    forward(
        meta_ref, weight_ref, own_ref, chip_ref, core_ref, dense_ref, scaled_ref,
        part_ref, pair_ref, rolled_ref, map_ref,
    )
    adjoint(
        meta_ref, g_ref, core_ref, chip_ref, tail_ref, both_ref, pair_ref, spread_ref,
        grad_ref, above_ref, below_ref,
    )
    project(
        meta_ref, weight_ref, own_ref, core_ref, chip_ref, grad_ref, part_ref, pair_ref,
        keep_ref, send_ref, corner_ref, local_ref, sum_ref, kernel_ref,
    )


def embed_terms(grad_ref, scaled_ref, local_ref, corner_ref, near_ref, far_ref, side_ref):
    both = dot(grad_ref[...], scaled_ref[...], TN)
    far = both[TILE : 2 * TILE]
    near_ref[...] = local_ref[...] + both[:TILE]
    far_ref[...] = far
    side_ref[:TILE] = far.astype(BF16)
    side_ref[TILE:] = corner_ref[...].astype(BF16)


def finish(
    mine_ref, other_ref, chip_ref, near_ref,
    weight_ref, kernel_ref, embed_ref,
):
    index, even, before, _ = place()
    channels = kernel_ref.shape[1]
    rows = channels // 2
    half = half_of(index)
    for ref, which in ((mine_ref, half), (other_ref, 1 - half)):
        at = pl.multiple_of(rows * which, rows)
        weight_ref[pl.ds(at, rows), :] = ref[:rows]
        for t in range(TAPS - 1):
            first = rows * (1 + t // 4)
            to = channels * (t % 4)
            kernel_ref[t, pl.ds(at, rows), :] = ref[first : first + rows, to : to + channels]
        for q in range(4):
            kernel_ref[TAPS - 1, pl.ds(at + 8 * q, 8), :] = ref[
                3 * rows : 3 * rows + 8, channels * q : channels * (q + 1)
            ]
    carried = other_ref[3 * rows + 8 :] * (1.0 - even)
    carried = carried + chip_ref[...].astype(F32) * (even * before)
    embed_ref[...] = near_ref[...] + carried


VMEM = pl.BlockSpec(memory_space=pltpu.VMEM)
SMEM = pl.BlockSpec(memory_space=pltpu.SMEM)
HBM = pl.BlockSpec(memory_space=pltpu.HBM)


def shape(dims, kind):
    return jax.ShapeDtypeStruct(dims, kind)


def call(kernel, outs, scalars, operands, scratch=(), flops=0, moved=0, first=None, room=32):
    specs = [first or SMEM] * scalars + [VMEM] * (len(operands) - scalars)
    return pl.pallas_call(
        kernel,
        out_shape=outs,
        in_specs=specs,
        out_specs=[SMEM if out.dtype == jnp.int32 else VMEM for out in outs],
        scratch_shapes=list(scratch),
        compiler_params=pltpu.CompilerParams(vmem_limit_bytes=room * 1024 * 1024),
        cost_estimate=pl.CostEstimate(flops=flops, bytes_accessed=moved, transcendentals=0),
    )(*operands)


def swap_with(shard, step):
    return lax.ppermute(shard, "blk", [(i, i ^ step) for i in range(lax.axis_size("blk"))])


def swap_stage(shard, first, second):
    pairs = [(i, i ^ (second if half_of(i) else first)) for i in range(lax.axis_size("blk"))]
    return lax.ppermute(shard, "blk", pairs)


def swap_chips(shard):
    count = lax.axis_size("blk")
    pairs = [(i, (i + (1 if i % 2 else -1)) % count) for i in range(count)]
    return lax.ppermute(shard, "blk", pairs)


def per_device(embed, pair_weight, conv_kernel, dilations, tile_order, cotangent):
    features = embed.shape[1]
    channels = conv_kernel.shape[0]
    count = lax.axis_size("blk")
    weight = pair_weight.T
    taps = jnp.transpose(conv_kernel, (1, 0, 2))
    cot = cotangent.reshape(2, channels, TILE * TILE)
    packed = shape((channels, RIM), BF16)
    body = shape((TILE, channels, LANES), BF16)
    to_chip, to_core = call(
        pack,
        [packed, packed],
        3,
        (tile_order, cot, embed),
        [
            pltpu.SMEM(tile_order.shape, jnp.int32),
            pltpu.VMEM(cot.shape, BF16),
            pltpu.VMEM(embed.shape, BF16),
            pltpu.SemaphoreType.DMA((3,)),
        ],
        flops=10**10,
        moved=10**6,
        first=HBM,
        room=60,
    )
    chip = swap_chips(to_chip)
    core = swap_with(to_core, 1)
    grads, dense, tail, flat, both, scaled, spread, meta = call(
        prepare,
        [
            body,
            shape((TILE // 2, channels, LANES), BF16),
            shape((HALO, channels, LANES), BF16),
            shape((channels, TAPS * channels), BF16),
            shape((TAPS * channels, 2 * channels), BF16),
            shape((TILE * channels, features), BF16),
            shape((TILE, TAPS * channels, LANES), F32),
            shape((2 * GROUPS,), jnp.int32),
        ],
        2,
        (tile_order, dilations, cot, taps, weight, embed),
        flops=2 * 10**8,
        moved=3 * 10**6,
    )
    rows = channels // 2
    sums = 3 * rows + rows * channels // features
    total, send, corner, local, grad_pair, pair, rolled = call(
        middle,
        [
            shape((sums, features), F32),
            shape((channels // 4 + sums, features), F32),
            shape((channels // 4, features), F32),
            shape((TILE, features), F32),
            shape((TILE * channels, LANES), BF16),
            body,
            shape((TILE, 3 * channels, LANES), BF16),
        ],
        1,
        (meta, weight, embed, chip, core, dense, scaled, grads, tail, both, spread),
        [
            pltpu.VMEM((TILE + 2 * HALO, channels, LANES), BF16),
            pltpu.VMEM((channels, TAPS * channels), F32),
            pltpu.VMEM((HALO, 3 * channels, LANES), F32),
            pltpu.VMEM((HALO, 3 * channels, LANES), F32),
            pltpu.VMEM((channels, features), F32),
            pltpu.VMEM((channels, TAPS * channels), F32),
        ],
        flops=2 * 10**9,
        moved=8 * 10**6,
        room=24,
    )
    by_core = swap_with(send, 1)
    near, far, sided = call(
        embed_terms,
        [
            shape((TILE, features), F32),
            shape((TILE, features), F32),
            shape((TILE + channels // 4, features), BF16),
        ],
        0,
        (grad_pair, scaled, local, corner),
        flops=2 * 10**8,
        moved=2 * 10**6,
    )
    by_chip = swap_chips(sided)
    by_core, sided = lax.optimization_barrier((by_core, sided))
    total = total + by_core[channels // 4 :]
    by_core = by_core[: channels // 4]
    steps = [1 | 1 << b for b in range(1, count.bit_length() - 1)]
    turns = list(zip(steps, steps[1:] + steps[:1]))
    for first, second in turns[:-1]:
        total = total + swap_stage(total, first, second)
    rolled, total, by_chip = lax.optimization_barrier((rolled, total, by_chip))
    last = swap_stage(total, *turns[-1])
    (out,) = call(
        respond,
        [shape((2, channels, TILE * TILE), BF16)],
        1,
        (meta, flat, rolled, pair, by_core, by_chip[TILE:]),
        [
            pltpu.VMEM((4 * channels, 4 * LANES), BF16),
            pltpu.VMEM((TILE // 2, channels, LANES), F32),
        ],
        flops=2 * 10**8,
        moved=2 * 10**6,
    )
    out, last = lax.optimization_barrier((out, last))
    total = total + last
    rest = swap_with(jnp.concatenate([total, far]), 1)
    grad_weight, grad_kernel, grad_embed = call(
        finish,
        [
            shape((channels, features), F32),
            shape((TAPS, channels, channels), F32),
            shape((TILE, features), F32),
        ],
        0,
        (total, rest, by_chip[:TILE], near),
        moved=10**6,
    )
    return (
        out.reshape(1, 2, channels, TILE * TILE),
        grad_embed,
        grad_weight.T,
        jnp.transpose(grad_kernel, (1, 0, 2)),
    )


def solution(mesh):
    placed = (
        P(("grp", "blk"), None),
        P(),
        P(),
        P(),
        P(("grp", "blk"), None),
        P(("grp", "blk"), None, None, None),
    )
    return jax.shard_map(
        per_device,
        mesh=mesh,
        in_specs=placed,
        out_specs=(
            P(("grp", "blk"), None, None, None),
            P(("grp", "blk"), None),
            P("grp", None),
            P("grp", None, None),
        ),
        check_vma=False,
    )
```

```python
import jax
import jax.numpy as jnp
from jax import lax
from jax.experimental import pallas as pl
from jax.experimental.pallas import tpu as pltpu
from jax.sharding import PartitionSpec as P

GROUPS = 4
HALO = 8
TILE = 32
LANES = 128
TAPS = 9
F32 = jnp.float32
BF16 = jnp.bfloat16
NN = (((1,), (0,)), ((), ()))
NT = (((1,), (1,)), ((), ()))
TN = (((0,), (0,)), ((), ()))


def dot(a, b, dims=NN):
    return lax.dot_general(a, b, dims, preferred_element_type=F32)


def turn(x, by):
    by = by % LANES
    return x if by == 0 else pltpu.roll(x, by, 1)


def lane_ids(rows):
    return lax.broadcasted_iota(jnp.int32, (rows, LANES), 1)


def within(lane, low, high):
    return jnp.logical_and(lane >= low, lane < high)


def one_hot(target, chunks):
    lane = lane_ids(target.shape[0])
    hits = [jnp.where(target == lane + LANES * c, 1.0, 0.0).astype(BF16) for c in range(chunks)]
    return jnp.concatenate(hits, 1)


def row_ids(rows):
    return lax.broadcasted_iota(jnp.int32, (rows, LANES), 0)


def spread_table(chunks):
    x = row_ids(LANES * chunks)
    return one_hot((((x >> 5) & 3) << 7) + ((x >> 7) << 5) + (x & 31), 4)


def swap_table():
    x = row_ids(HALO * TILE)
    return one_hot(((x & 31) << 3) + (x >> 5), 2)


def edge_table():
    x = row_ids(LANES)
    return one_hot(jnp.where((x & 31) < HALO, ((x & 31) << 5) + (x >> 5), -1), 2)


def corner_table(first):
    x = row_ids(HALO * TILE)
    c = (x & 31) - first
    return one_hot(jnp.where(within(c, 0, HALO), ((x >> 5) << 3) + c, -1), 1)


def as_float(flag):
    return jnp.where(flag, 1.0, 0.0).astype(F32)


def place():
    index = lax.axis_index("blk")
    last = lax.axis_size("blk") - 1
    return index, as_float(index % 2 == 0), as_float(index > 0), as_float(index < last)


def half_of(index):
    for by in (8, 4, 2, 1):
        index = index ^ (index >> by)
    return index & 1


def corner_shift(flat, spacing):
    width = flat.shape[0] // GROUPS
    lane = lane_ids(width)
    pieces = []
    for g in range(GROUPS):
        d = spacing[g]
        kept = jnp.logical_and(jnp.logical_and(lane < 8 * HALO, (lane >> 3) < d), (lane & 7) < d)
        x = jnp.where(kept, flat[width * g : width * (g + 1)], 0.0)
        pieces.append(pltpu.roll(x, (HALO + 1) * (HALO - d), 1))
    return jnp.concatenate(pieces, 0).astype(BF16)


def tiles_of(order_ref, cot_ref):
    slot = order_ref[0, 0]
    _, _, _, keep = place()
    return cot_ref[slot], (cot_ref[1 - slot].astype(F32) * keep).astype(BF16)


def fetch(sources, targets, sems):
    copies = [
        pltpu.make_async_copy(source, target, sems.at[i])
        for i, (source, target) in enumerate(zip(sources, targets))
    ]
    for copy in copies:
        copy.start()
    return copies


def pack(
    order_hbm, cot_hbm, embed_hbm,
    chip_ref, core_ref,
    order_ref, cot_ref, embed_ref, sems,
):
    copies = fetch((order_hbm, cot_hbm, embed_hbm), (order_ref, cot_ref, embed_ref), sems)
    edge, head, tail = edge_table(), corner_table(0), corner_table(TILE - HALO)
    for copy in copies:
        copy.wait()
    zero, one = tiles_of(order_ref, cot_ref)
    _, even, _, _ = place()
    channels = zero.shape[0]
    moved = dot(
        jnp.concatenate([zero[:, LANES * j : LANES * (j + 1)] for j in range(8)], 0), edge
    )
    columns = []
    for h in range(2):
        total = None
        for j in range(8):
            piece = moved[channels * j : channels * (j + 1), LANES * h : LANES * (h + 1)]
            piece = turn(piece, 4 * j)
            total = piece if total is None else total + piece
        columns.append(total)
    rim = HALO * TILE
    tail_at = TILE * (TILE - HALO)
    up = [zero[:, :rim].astype(F32)] + columns + [dot(one[:, :rim], head)]
    down = [one[:, tail_at:].astype(F32)] + [jnp.zeros_like(x) for x in columns]
    down += [dot(zero[:, tail_at:], tail)]
    up, down = jnp.concatenate(up, 1), jnp.concatenate(down, 1)
    width = up.shape[1]
    both = jnp.concatenate([embed_ref[:, :LANES], embed_ref[:, LANES:]], 0)
    core_ref[:, :width] = (down * even + up * (1.0 - even)).astype(BF16)
    core_ref[:, width:] = both
    chip_ref[:, :width] = (up * even + down * (1.0 - even)).astype(BF16)
    chip_ref[:, width:] = both


RIM_SIDE, RIM_CORNER, RIM_EMBED, RIM = 256, 512, 640, 768


def from_above(core_ref, chip_ref, at):
    _, even, before, _ = place()
    x = chip_ref[:, at].astype(F32) * (even * before)
    return x + core_ref[:, at].astype(F32) * ((1.0 - even) * before)


def from_below(core_ref, chip_ref, at):
    _, even, _, after = place()
    x = core_ref[:, at].astype(F32) * (even * after)
    return x + chip_ref[:, at].astype(F32) * ((1.0 - even) * after)


def prepare(
    order_ref, dil_ref, cot_ref, kern_ref, weight_ref, embed_ref,
    g_ref, dense_ref, tail_ref, flat_ref, both_ref, scaled_ref, spread_ref, meta_ref,
):
    for g in range(GROUPS):
        meta_ref[g] = jnp.left_shift(jnp.int32(1), dil_ref[g])
    meta_ref[GROUPS] = order_ref[0, 0]
    zero, one = tiles_of(order_ref, cot_ref)
    channels = kern_ref.shape[1]
    swap = swap_table()
    tail_at = TILE * (TILE - HALO)
    y_zero = dot(zero[:, tail_at:], swap)
    y_one = dot(one[:, tail_at:], swap)
    lane = lane_ids(channels)
    own_side = within(lane, 72, 80)
    low = lane < 2 * TILE
    pieces = []
    for j in range(4):
        at = slice(LANES * j, LANES * (j + 1))
        later = slice(LANES * (j + 4), LANES * (j + 5))
        pieces.append(
            jnp.concatenate([zero[:, at], one[:, at], zero[:, later], one[:, later]], 1)
        )
    rows = dot(jnp.concatenate(pieces, 0), spread_table(4))
    for j in range(4):
        for m in range(4):
            row = rows[channels * j : channels * (j + 1), LANES * m : LANES * (m + 1)]
            dense_ref[4 * j + m] = row.astype(BF16)
            for h in range(2):
                r = 16 * h + 4 * j + m
                side = turn(y_zero[:, LANES * h : LANES * (h + 1)], 72 - 8 * (r % 16))
                side = jnp.where(own_side, side, 0.0)
                g_ref[r] = jnp.where(low, turn(row, 64 * h), side).astype(BF16)
    for i in range(HALO):
        rest = turn(y_one[:, :LANES], 72 - 8 * i)
        tail_ref[i] = jnp.where(own_side, rest, 0.0).astype(BF16)
    eye = (
        lax.broadcasted_iota(jnp.int32, (channels, channels), 0)
        == lax.broadcasted_iota(jnp.int32, (channels, channels), 1)
    )
    eye = jnp.where(eye, 1.0, 0.0).astype(BF16)
    for u in range(3):
        for v in range(3):
            t = 3 * u + v
            pair = jnp.concatenate([kern_ref[t], kern_ref[3 * v + u]], 0)
            both_ref[channels * t : channels * (t + 1), :] = dot(eye, pair, NT).astype(BF16)
    for t in range(0, TAPS - 1, 2):
        flat_ref[:, channels * t : channels * (t + 2)] = jnp.concatenate(
            [kern_ref[t].astype(F32), kern_ref[t + 1].astype(F32)], 1
        ).astype(BF16)
    flat_ref[:, channels * (TAPS - 1) : channels * TAPS] = kern_ref[TAPS - 1]
    weight = weight_ref[...].astype(F32)
    own = embed_ref[...].astype(F32)
    for r in range(TILE):
        scaled_ref[channels * r : channels * (r + 1), :] = (own[r : r + 1, :] * weight).astype(
            BF16
        )
    inner = jnp.where(lane < 2 * TILE, 1.0, 0.0).astype(BF16)
    beside = jnp.where(own_side, 1.0, 0.0).astype(BF16)

    def spread_rows(i, carry):
        x = jnp.concatenate([g_ref[2 * i], g_ref[2 * i + 1]], 1)
        y = jnp.concatenate([inner, inner], 1), jnp.concatenate([beside, beside], 1)
        y = dot(both_ref[...], jnp.concatenate([x * y[0], x * y[1]], 0))
        spread_ref[2 * i] = y[:, :LANES]
        spread_ref[2 * i + 1] = y[:, LANES:]
        return carry

    lax.fori_loop(0, TILE // 2, spread_rows, 0, unroll=4)


def unpacked(x):
    return jnp.concatenate([x[:TILE], x[TILE:]], 1)


def forward(
    meta_ref, weight_ref, own_ref, chip_ref, core_ref, dense_ref, scaled_ref,
    part_ref, pair_ref, rolled_ref, map_ref,
):
    channels = weight_ref.shape[0]
    width = channels // GROUPS
    weight = weight_ref[...].astype(F32)
    own = own_ref[...].astype(F32)
    after = unpacked(from_below(core_ref, chip_ref, slice(RIM_EMBED, RIM)))
    before = unpacked(from_above(core_ref, chip_ref, slice(RIM_EMBED, RIM)))[TILE - HALO :]
    filler = jnp.zeros((LANES - 2 * TILE - HALO, own.shape[1]), F32)
    columns = jnp.concatenate([own, after, filler, before], 0).astype(BF16)
    lane = lane_ids(channels)
    kept = (
        jnp.logical_or(lane < TILE, lane >= LANES - HALO),
        lane < 2 * TILE,
        within(lane, TILE, 2 * TILE),
    )
    for c in range(6):
        part = 0 if c == 0 else (2 if c == 5 else 1)
        if part == 1:
            scaled = scaled_ref[8 * channels * (c - 1) : 8 * channels * c, :]
        else:
            rim = before if part == 0 else after
            scaled = jnp.concatenate(
                [(rim[i : i + 1, :] * weight).astype(BF16) for i in range(HALO)], 0
            )
        pair = dot(scaled, columns, NT).astype(BF16)
        for i in range(8):
            one = pair[channels * i : channels * (i + 1)]
            if part == 1:
                pair_ref[8 * (c - 1) + i] = one
            x = jnp.where(kept[part], jnp.maximum(one.astype(F32), 0.0), 0.0)
            map_ref[8 * c + i] = x.astype(BF16)
    swap = swap_table()

    def gathered(first, per, low, high, move):
        halves = []
        for half in range(2):
            total = None
            for m in range(per):
                piece = map_ref[first + per * half + m].astype(F32)
                piece = jnp.where(within(lane, low, high), piece, 0.0)
                piece = turn(piece, move(m))
                total = piece if total is None else total + piece
            halves.append(total.astype(BF16))
        return jnp.concatenate(halves, 1)

    above = dot(gathered(0, 4, 0, TILE, lambda m: TILE * m), swap)
    below = dot(gathered(8, 16, TILE, TILE + HALO, lambda m: HALO * m - TILE), swap, NT)
    for r in range(TILE):
        half = LANES * (r // 16)
        side = turn(above[:, half : half + LANES], LANES - HALO - HALO * (r % 16))
        map_ref[HALO + r] += jnp.where(lane >= LANES - HALO, side, 0.0).astype(BF16)
    for i in range(HALO):
        half = LANES * (i // 4)
        side = turn(below[:, half : half + LANES], -TILE * (i % 4))
        map_ref[HALO + TILE + i] += jnp.where(lane < TILE, side, 0.0).astype(BF16)

    spacing = [meta_ref[g] for g in range(GROUPS)]
    source = row_ids(LANES)
    to = lane_ids(LANES)
    for g in range(GROUPS):
        tables = []
        for h in range(2):
            half = within(to, 2 * TILE * h, 2 * TILE * (h + 1))
            offset = jnp.where(half, (source - (to - 2 * TILE * h)) & (LANES - 1), LANES)
            hits = [
                jnp.where(offset == (v * spacing[g]) & (LANES - 1), 1.0, 0.0).astype(BF16)
                for v in (-1, 0, 1)
            ]
            tables.append(jnp.concatenate(hits, 1))
        table = jnp.concatenate(tables, 0)
        at = width * g
        for part in range(2):
            low = [map_ref[16 * part + i, at : at + width, :] for i in range(16)]
            high = [map_ref[16 * part + i + 16, at : at + width, :] for i in range(16)]
            x = jnp.concatenate([jnp.concatenate(low, 0), jnp.concatenate(high, 0)], 1)
            y = dot(x, table).astype(BF16)
            for i in range(16):
                for v in range(3):
                    to_row = channels * v + at
                    rolled_ref[16 * part + i, to_row : to_row + width, :] = y[
                        width * i : width * (i + 1), LANES * v : LANES * (v + 1)
                    ]
    total = None
    for j in range(4):
        rows = range(4 * j, 4 * (j + 1))
        stack = jnp.concatenate([taps_of(rolled_ref, spacing, r) for r in rows], 1)
        share = dot(jnp.concatenate([dense_ref[r] for r in rows], 1), stack, NT)
        total = share if total is None else total + share
    part_ref[...] = total


def taps_of(rolled_ref, spacing, r):
    channels = rolled_ref.shape[1] // 3
    width = channels // GROUPS
    pieces = []
    for u in range(3):
        for v in range(3):
            for g in range(GROUPS):
                at = channels * v + width * g
                pieces.append(rolled_ref[r + HALO + (u - 1) * spacing[g], at : at + width, :])
    return jnp.concatenate(pieces, 0)


def respond(
    meta_ref, flat_ref, rolled_ref, pair_ref, core_ref, chip_ref,
    out_ref,
    rows_ref, share_ref,
):
    channels = flat_ref.shape[0]
    spacing = [meta_ref[g] for g in range(GROUPS)]
    lane = lane_ids(channels)
    low = lane < 2 * TILE
    _, even, _, keep = place()
    corner = core_ref[...] * even + chip_ref[...].astype(F32) * ((1.0 - even) * keep)
    low_side, high_side = corner[:, :LANES], corner[:, LANES:]
    corner = jnp.concatenate(
        [low_side, turn(low_side, 64), high_side, turn(high_side, 64)], 0
    )
    share = dot(flat_ref[:, channels * (TAPS - 1) :], corner_shift(corner, spacing))
    share_ref[:HALO] = jnp.zeros((HALO, channels, LANES), F32)
    for i in range(HALO):
        share_ref[HALO + i] = jnp.where(
            lane >= LANES - HALO, turn(share, LANES - HALO - HALO * i), 0.0
        )

    def conv_rows(j, carry):
        for h in range(2):
            r = 4 * j + 2 * h
            stack = jnp.concatenate([taps_of(rolled_ref, spacing, r + m) for m in range(2)], 1)
            response = dot(flat_ref[...], stack)
            for m in range(2):
                row = jnp.where(
                    low,
                    pair_ref[r + m].astype(F32),
                    turn(pair_ref[r + m + 16].astype(F32), 2 * TILE),
                )
                row = row + (response[:, LANES * m : LANES * (m + 1)] + share_ref[r + m])
                at = LANES * (2 * h + m)
                to = pl.ds(pl.multiple_of(channels * j, channels), channels)
                rows_ref[to, at : at + LANES] = row.astype(BF16)
        return carry

    lax.fori_loop(0, 4, conv_rows, 0)
    slot = meta_ref[GROUPS]
    chunks = dot(rows_ref[...], spread_table(4), NT)
    for j in range(4):
        chunk = chunks[channels * j : channels * (j + 1)]
        for h in range(2):
            at = slice(LANES * (j + 4 * h), LANES * (j + 4 * h + 1))
            to = 2 * LANES * h
            out_ref[slot, :, at] = chunk[:, to : to + LANES].astype(BF16)
            out_ref[1 - slot, :, at] = (chunk[:, to + LANES : to + 2 * LANES] * keep).astype(BF16)


def adjoint(
    meta_ref, weight_ref, own_ref, g_ref, core_ref, chip_ref, tail_ref, both_ref, pair_ref,
    spread_ref,
    grad_ref, local_ref, sum_ref, above_ref, below_ref,
):
    channels = g_ref.shape[1]
    width = channels // GROUPS
    span = 3 * channels
    lane = lane_ids(channels)
    zeros = jnp.zeros((channels, LANES), BF16)
    above = from_above(core_ref, chip_ref, slice(0, RIM_EMBED))
    below = from_below(core_ref, chip_ref, slice(0, RIM_EMBED))

    def moved(rim, at, to, size, per, i):
        at += LANES * (i // per)
        x = turn(rim[:, at : at + LANES], to - size * (i % per))
        return jnp.where(within(lane, to, to + size), x, 0.0)

    for h in range(HALO // 2):
        upper, lower = [], []
        for i in (2 * h, 2 * h + 1):
            x = moved(above, 0, 0, TILE, 4, i)
            x = x + moved(above, RIM_CORNER, LANES - HALO, HALO, 16, i)
            upper.append(jnp.concatenate([x.astype(BF16), zeros], 0))
            x = moved(below, 0, TILE, TILE, 4, i)
            x = x + moved(below, RIM_CORNER, 2 * TILE, HALO, 16, i)
            y = moved(below, RIM_SIDE, 80, TILE, 4, i).astype(BF16) + tail_ref[i]
            lower.append(jnp.concatenate([x.astype(BF16), y], 0))
        x = dot(both_ref[2 * span :, :], jnp.concatenate(upper, 1))
        y = dot(both_ref[:span, :], jnp.concatenate(lower, 1))
        for m in range(2):
            above_ref[2 * h + m] = x[:, LANES * m : LANES * (m + 1)]
            below_ref[2 * h + m] = y[:, LANES * m : LANES * (m + 1)]
    spacing = [meta_ref[g] for g in range(GROUPS)]
    second = within(lane, TILE, 2 * TILE)

    def gathered(r):
        pieces = []
        for g in range(GROUPS):
            totals = []
            up, down = r - spacing[g], r + spacing[g]
            for v in range(3):
                at = channels * v + width * g
                tap = slice(at, at + width)
                total = spread_ref[r, span + at : span + at + width, :]
                last = slice(2 * span + at, 2 * span + at + width)
                if r < HALO:
                    x = spread_ref[jnp.maximum(up, 0), last, :]
                    y = above_ref[jnp.minimum(up + HALO, HALO - 1), tap, :]
                    total = total + jnp.where(up < 0, y, x)
                else:
                    total = total + spread_ref[up, last, :]
                if r >= TILE - HALO:
                    x = spread_ref[jnp.minimum(down, TILE - 1), tap, :]
                    y = below_ref[jnp.maximum(down - TILE, 0), tap, :]
                    total = total + jnp.where(down >= TILE, y, x)
                else:
                    total = total + spread_ref[down, tap, :]
                totals.append(total)
            pieces.append(
                totals[1]
                + pltpu.roll(totals[0], LANES - spacing[g], 1)
                + pltpu.roll(totals[2], spacing[g], 1)
            )
        grad = jnp.concatenate(pieces, 0)
        grad = grad + jnp.where(second, turn(grad, -48), 0.0)
        own = g_ref[r].astype(F32)
        own = own + jnp.where(pair_ref[r].astype(F32) > 0, grad, 0.0)
        return jnp.where(lane < 2 * TILE, own, 0.0).astype(BF16)

    weight = weight_ref[...].astype(F32)
    own = own_ref[...].astype(F32)
    after = unpacked(from_below(core_ref, chip_ref, slice(RIM_EMBED, RIM)))
    columns = jnp.concatenate(
        [own, after, jnp.zeros((LANES - 2 * TILE, own.shape[1]), F32)], 0
    ).astype(BF16)
    weight_part = jnp.zeros_like(weight)
    local = []
    for c in range(TILE // 8):
        rows = jnp.concatenate([gathered(8 * c + i) for i in range(8)], 0)
        grad_ref[8 * channels * c : 8 * channels * (c + 1), :] = rows
        grad_scaled = dot(rows, columns)
        for i in range(8):
            one = grad_scaled[channels * i : channels * (i + 1)]
            local.append(jnp.sum(one * weight, 0, keepdims=True))
            weight_part = weight_part + one * own[8 * c + i : 8 * c + i + 1, :]
    local_ref[...] = jnp.concatenate(local, 0)
    sum_ref[...] = weight_part


def deliver(
    meta_ref, core_ref, chip_ref, part_ref, pair_ref,
    keep_ref, send_ref, corner_ref, sum_ref, kernel_ref,
):
    channels = part_ref.shape[0]
    lane = lane_ids(channels)
    rim = from_above(core_ref, chip_ref, slice(0, RIM_SIDE))
    corner, ends = None, None
    for i in range(HALO):
        x = jnp.where(within(lane, TILE, TILE + HALO), pair_ref[i].astype(F32), 0.0)
        x = turn(jnp.maximum(x, 0.0), HALO * i - TILE)
        half = LANES * (i // 4)
        y = turn(rim[:, half : half + LANES], HALO * i - TILE * (i % 4) - (TILE - HALO))
        y = jnp.where(within(lane, HALO * i, HALO * (i + 1)), y, 0.0)
        corner, ends = (x, y) if i == 0 else (corner + x, ends + y)
    spacing = [meta_ref[g] for g in range(GROUPS)]
    share = dot(ends.astype(BF16), corner_shift(corner, spacing), NT)
    last = channels * (TAPS - 1)
    kernel_ref[:, :last] = part_ref[:, :last]
    kernel_ref[:, last:] = part_ref[:, last:] + share
    quarter = channels // 4
    corner = [corner[quarter * q : quarter * (q + 1)] for q in range(4)]
    corner = jnp.concatenate(
        [corner[0] + turn(corner[1], 64), corner[2] + turn(corner[3], 64)], 1
    )
    corner_ref[...] = corner
    rows = channels // 2
    half = half_of(lax.axis_index("blk"))
    send_ref[:quarter] = corner
    for ref, which, first in ((keep_ref, half, 0), (send_ref, 1 - half, quarter)):
        at = pl.multiple_of(rows * which, rows)
        ref[first : first + rows] = sum_ref[pl.ds(at, rows), :]
        for q in range(2):
            to = first + rows * (q + 1)
            ref[to : to + rows] = kernel_ref[pl.ds(at, rows), 256 * q : 256 * (q + 1)]
        ref[first + 3 * rows :] = jnp.concatenate(
            [kernel_ref[pl.ds(at + 8 * q, 8), 512:] for q in range(4)], 1
        )


def middle(
    meta_ref, weight_ref, own_ref, chip_ref, core_ref, dense_ref, scaled_ref, g_ref, tail_ref,
    both_ref, spread_ref,
    keep_ref, send_ref, corner_ref, local_ref, grad_ref, pair_ref, rolled_ref,
    map_ref, part_ref, above_ref, below_ref, sum_ref, kernel_ref,
):
    forward(
        meta_ref, weight_ref, own_ref, chip_ref, core_ref, dense_ref, scaled_ref,
        part_ref, pair_ref, rolled_ref, map_ref,
    )
    adjoint(
        meta_ref, weight_ref, own_ref, g_ref, core_ref, chip_ref, tail_ref, both_ref, pair_ref,
        spread_ref,
        grad_ref, local_ref, sum_ref, above_ref, below_ref,
    )
    deliver(
        meta_ref, core_ref, chip_ref, part_ref, pair_ref,
        keep_ref, send_ref, corner_ref, sum_ref, kernel_ref,
    )


def embed_terms(grad_ref, scaled_ref, local_ref, corner_ref, near_ref, far_ref, side_ref):
    both = dot(grad_ref[...], scaled_ref[...], TN)
    far = both[TILE : 2 * TILE]
    near_ref[...] = local_ref[...] + both[:TILE]
    far_ref[...] = far
    side_ref[:TILE] = far.astype(BF16)
    side_ref[TILE:] = corner_ref[...].astype(BF16)


def finish(
    mine_ref, other_ref, chip_ref, near_ref,
    weight_ref, kernel_ref, embed_ref,
):
    index, even, before, _ = place()
    channels = kernel_ref.shape[1]
    rows = channels // 2
    half = half_of(index)
    for ref, which in ((mine_ref, half), (other_ref, 1 - half)):
        at = pl.multiple_of(rows * which, rows)
        weight_ref[pl.ds(at, rows), :] = ref[:rows]
        for t in range(TAPS - 1):
            first = rows * (1 + t // 4)
            to = channels * (t % 4)
            kernel_ref[t, pl.ds(at, rows), :] = ref[first : first + rows, to : to + channels]
        for q in range(4):
            kernel_ref[TAPS - 1, pl.ds(at + 8 * q, 8), :] = ref[
                3 * rows : 3 * rows + 8, channels * q : channels * (q + 1)
            ]
    carried = other_ref[3 * rows + 8 :] * (1.0 - even)
    carried = carried + chip_ref[...].astype(F32) * (even * before)
    embed_ref[...] = near_ref[...] + carried


VMEM = pl.BlockSpec(memory_space=pltpu.VMEM)
SMEM = pl.BlockSpec(memory_space=pltpu.SMEM)
HBM = pl.BlockSpec(memory_space=pltpu.HBM)


def shape(dims, kind):
    return jax.ShapeDtypeStruct(dims, kind)


def call(kernel, outs, scalars, operands, scratch=(), flops=0, moved=0, first=None, room=32):
    specs = [first or SMEM] * scalars + [VMEM] * (len(operands) - scalars)
    return pl.pallas_call(
        kernel,
        out_shape=outs,
        in_specs=specs,
        out_specs=[SMEM if out.dtype == jnp.int32 else VMEM for out in outs],
        scratch_shapes=list(scratch),
        compiler_params=pltpu.CompilerParams(vmem_limit_bytes=room * 1024 * 1024),
        cost_estimate=pl.CostEstimate(flops=flops, bytes_accessed=moved, transcendentals=0),
    )(*operands)


def swap_with(shard, step):
    return lax.ppermute(shard, "blk", [(i, i ^ step) for i in range(lax.axis_size("blk"))])


def swap_stage(shard, first, second):
    pairs = [(i, i ^ (second if half_of(i) else first)) for i in range(lax.axis_size("blk"))]
    return lax.ppermute(shard, "blk", pairs)


def swap_chips(shard):
    count = lax.axis_size("blk")
    pairs = [(i, (i + (1 if i % 2 else -1)) % count) for i in range(count)]
    return lax.ppermute(shard, "blk", pairs)


def per_device(embed, pair_weight, conv_kernel, dilations, tile_order, cotangent):
    features = embed.shape[1]
    channels = conv_kernel.shape[0]
    count = lax.axis_size("blk")
    weight = pair_weight.T
    taps = jnp.transpose(conv_kernel, (1, 0, 2))
    cot = cotangent.reshape(2, channels, TILE * TILE)
    packed = shape((channels, RIM), BF16)
    body = shape((TILE, channels, LANES), BF16)
    to_chip, to_core = call(
        pack,
        [packed, packed],
        3,
        (tile_order, cot, embed),
        [
            pltpu.SMEM(tile_order.shape, jnp.int32),
            pltpu.VMEM(cot.shape, BF16),
            pltpu.VMEM(embed.shape, BF16),
            pltpu.SemaphoreType.DMA((3,)),
        ],
        flops=10**10,
        moved=10**6,
        first=HBM,
        room=60,
    )
    chip = swap_chips(to_chip)
    core = swap_with(to_core, 1)
    grads, dense, tail, flat, both, scaled, spread, meta = call(
        prepare,
        [
            body,
            shape((TILE // 2, channels, LANES), BF16),
            shape((HALO, channels, LANES), BF16),
            shape((channels, TAPS * channels), BF16),
            shape((TAPS * channels, 2 * channels), BF16),
            shape((TILE * channels, features), BF16),
            shape((TILE, TAPS * channels, LANES), F32),
            shape((2 * GROUPS,), jnp.int32),
        ],
        2,
        (tile_order, dilations, cot, taps, weight, embed),
        flops=2 * 10**8,
        moved=3 * 10**6,
    )
    rows = channels // 2
    sums = 3 * rows + rows * channels // features
    total, send, corner, local, grad_pair, pair, rolled = call(
        middle,
        [
            shape((sums, features), F32),
            shape((channels // 4 + sums, features), F32),
            shape((channels // 4, features), F32),
            shape((TILE, features), F32),
            shape((TILE * channels, LANES), BF16),
            body,
            shape((TILE, 3 * channels, LANES), BF16),
        ],
        1,
        (meta, weight, embed, chip, core, dense, scaled, grads, tail, both, spread),
        [
            pltpu.VMEM((TILE + 2 * HALO, channels, LANES), BF16),
            pltpu.VMEM((channels, TAPS * channels), F32),
            pltpu.VMEM((HALO, 3 * channels, LANES), F32),
            pltpu.VMEM((HALO, 3 * channels, LANES), F32),
            pltpu.VMEM((channels, features), F32),
            pltpu.VMEM((channels, TAPS * channels), F32),
        ],
        flops=2 * 10**9,
        moved=8 * 10**6,
        room=24,
    )
    by_core = swap_with(send, 1)
    near, far, sided = call(
        embed_terms,
        [
            shape((TILE, features), F32),
            shape((TILE, features), F32),
            shape((TILE + channels // 4, features), BF16),
        ],
        0,
        (grad_pair, scaled, local, corner),
        flops=2 * 10**8,
        moved=2 * 10**6,
    )
    by_chip = swap_chips(sided)
    by_core, sided = lax.optimization_barrier((by_core, sided))
    total = total + by_core[channels // 4 :]
    by_core = by_core[: channels // 4]
    steps = [1 | 1 << b for b in range(1, count.bit_length() - 1)]
    turns = list(zip(steps, steps[1:] + steps[:1]))
    for first, second in turns[:-1]:
        total = total + swap_stage(total, first, second)
    rolled, total, by_chip = lax.optimization_barrier((rolled, total, by_chip))
    last = swap_stage(total, *turns[-1])
    (out,) = call(
        respond,
        [shape((2, channels, TILE * TILE), BF16)],
        1,
        (meta, flat, rolled, pair, by_core, by_chip[TILE:]),
        [
            pltpu.VMEM((4 * channels, 4 * LANES), BF16),
            pltpu.VMEM((TILE // 2, channels, LANES), F32),
        ],
        flops=2 * 10**8,
        moved=2 * 10**6,
    )
    out, last = lax.optimization_barrier((out, last))
    total = total + last
    rest = swap_with(jnp.concatenate([total, far]), 1)
    grad_weight, grad_kernel, grad_embed = call(
        finish,
        [
            shape((channels, features), F32),
            shape((TAPS, channels, channels), F32),
            shape((TILE, features), F32),
        ],
        0,
        (total, rest, by_chip[:TILE], near),
        moved=10**6,
    )
    return (
        out.reshape(1, 2, channels, TILE * TILE),
        grad_embed,
        grad_weight.T,
        jnp.transpose(grad_kernel, (1, 0, 2)),
    )


def solution(mesh):
    placed = (
        P(("grp", "blk"), None),
        P(),
        P(),
        P(),
        P(("grp", "blk"), None),
        P(("grp", "blk"), None, None, None),
    )
    return jax.shard_map(
        per_device,
        mesh=mesh,
        in_specs=placed,
        out_specs=(
            P(("grp", "blk"), None, None, None),
            P(("grp", "blk"), None),
            P("grp", None),
            P("grp", None, None),
        ),
        check_vma=False,
    )
```

```python
import jax
import jax.numpy as jnp
from jax import lax
from jax.experimental import pallas as pl
from jax.experimental.pallas import tpu as pltpu
from jax.sharding import PartitionSpec as P

GROUPS = 4
HALO = 8
TILE = 32
LANES = 128
TAPS = 9
F32 = jnp.float32
BF16 = jnp.bfloat16
NN = (((1,), (0,)), ((), ()))
NT = (((1,), (1,)), ((), ()))
TN = (((0,), (0,)), ((), ()))


def dot(a, b, dims=NN):
    return lax.dot_general(a, b, dims, preferred_element_type=F32)


def turn(x, by):
    by = by % LANES
    return x if by == 0 else pltpu.roll(x, by, 1)


def lane_ids(rows):
    return lax.broadcasted_iota(jnp.int32, (rows, LANES), 1)


def within(lane, low, high):
    return jnp.logical_and(lane >= low, lane < high)


def one_hot(target, chunks):
    lane = lane_ids(target.shape[0])
    hits = [jnp.where(target == lane + LANES * c, 1.0, 0.0).astype(BF16) for c in range(chunks)]
    return jnp.concatenate(hits, 1)


def row_ids(rows):
    return lax.broadcasted_iota(jnp.int32, (rows, LANES), 0)


def spread_table(chunks):
    x = row_ids(LANES * chunks)
    return one_hot((((x >> 5) & 3) << 7) + ((x >> 7) << 5) + (x & 31), 4)


def swap_table():
    x = row_ids(HALO * TILE)
    return one_hot(((x & 31) << 3) + (x >> 5), 2)


def edge_table():
    x = row_ids(LANES)
    return one_hot(jnp.where((x & 31) < HALO, ((x & 31) << 5) + (x >> 5), -1), 2)


def corner_table(first):
    x = row_ids(HALO * TILE)
    c = (x & 31) - first
    return one_hot(jnp.where(within(c, 0, HALO), ((x >> 5) << 3) + c, -1), 1)


def as_float(flag):
    return jnp.where(flag, 1.0, 0.0).astype(F32)


def place():
    index = lax.axis_index("blk")
    last = lax.axis_size("blk") - 1
    return index, as_float(index % 2 == 0), as_float(index > 0), as_float(index < last)


def half_of(index):
    for by in (8, 4, 2, 1):
        index = index ^ (index >> by)
    return index & 1


def corner_shift(flat, spacing):
    width = flat.shape[0] // GROUPS
    lane = lane_ids(width)
    pieces = []
    for g in range(GROUPS):
        d = spacing[g]
        kept = jnp.logical_and(jnp.logical_and(lane < 8 * HALO, (lane >> 3) < d), (lane & 7) < d)
        x = jnp.where(kept, flat[width * g : width * (g + 1)], 0.0)
        pieces.append(pltpu.roll(x, (HALO + 1) * (HALO - d), 1))
    return jnp.concatenate(pieces, 0).astype(BF16)


def tiles_of(order_ref, cot_ref):
    slot = order_ref[0, 0]
    _, _, _, keep = place()
    return cot_ref[slot], (cot_ref[1 - slot].astype(F32) * keep).astype(BF16)


def fetch(sources, targets, sems):
    copies = [
        pltpu.make_async_copy(source, target, sems.at[i])
        for i, (source, target) in enumerate(zip(sources, targets))
    ]
    for copy in copies:
        copy.start()
    return copies


def pack(
    order_hbm, cot_hbm, embed_hbm,
    chip_ref, core_ref,
    order_ref, cot_ref, embed_ref, sems,
):
    copies = fetch((order_hbm, cot_hbm, embed_hbm), (order_ref, cot_ref, embed_ref), sems)
    edge, head, tail = edge_table(), corner_table(0), corner_table(TILE - HALO)
    for copy in copies:
        copy.wait()
    zero, one = tiles_of(order_ref, cot_ref)
    _, even, _, _ = place()
    channels = zero.shape[0]
    moved = dot(
        jnp.concatenate([zero[:, LANES * j : LANES * (j + 1)] for j in range(8)], 0), edge
    )
    columns = []
    for h in range(2):
        total = None
        for j in range(8):
            piece = moved[channels * j : channels * (j + 1), LANES * h : LANES * (h + 1)]
            piece = turn(piece, 4 * j)
            total = piece if total is None else total + piece
        columns.append(total)
    rim = HALO * TILE
    tail_at = TILE * (TILE - HALO)
    up = [zero[:, :rim].astype(F32)] + columns + [dot(one[:, :rim], head)]
    down = [one[:, tail_at:].astype(F32)] + [jnp.zeros_like(x) for x in columns]
    down += [dot(zero[:, tail_at:], tail)]
    up, down = jnp.concatenate(up, 1), jnp.concatenate(down, 1)
    width = up.shape[1]
    both = jnp.concatenate([embed_ref[:, :LANES], embed_ref[:, LANES:]], 0)
    core_ref[:, :width] = (down * even + up * (1.0 - even)).astype(BF16)
    core_ref[:, width:] = both
    chip_ref[:, :width] = (up * even + down * (1.0 - even)).astype(BF16)
    chip_ref[:, width:] = both


RIM_SIDE, RIM_CORNER, RIM_EMBED, RIM = 256, 512, 640, 768


def from_above(core_ref, chip_ref, at):
    _, even, before, _ = place()
    x = chip_ref[:, at].astype(F32) * (even * before)
    return x + core_ref[:, at].astype(F32) * ((1.0 - even) * before)


def from_below(core_ref, chip_ref, at):
    _, even, _, after = place()
    x = core_ref[:, at].astype(F32) * (even * after)
    return x + chip_ref[:, at].astype(F32) * ((1.0 - even) * after)


def prepare(
    order_ref, dil_ref, cot_ref, kern_ref, weight_ref, embed_ref,
    g_ref, dense_ref, tail_ref, flat_ref, both_ref, scaled_ref, spread_ref, meta_ref,
):
    for g in range(GROUPS):
        meta_ref[g] = jnp.left_shift(jnp.int32(1), dil_ref[g])
    meta_ref[GROUPS] = order_ref[0, 0]
    zero, one = tiles_of(order_ref, cot_ref)
    channels = kern_ref.shape[1]
    swap = swap_table()
    tail_at = TILE * (TILE - HALO)
    y_zero = dot(zero[:, tail_at:], swap)
    y_one = dot(one[:, tail_at:], swap)
    lane = lane_ids(channels)
    own_side = within(lane, 72, 80)
    low = lane < 2 * TILE
    pieces = []
    for j in range(4):
        at = slice(LANES * j, LANES * (j + 1))
        later = slice(LANES * (j + 4), LANES * (j + 5))
        pieces.append(
            jnp.concatenate([zero[:, at], one[:, at], zero[:, later], one[:, later]], 1)
        )
    rows = dot(jnp.concatenate(pieces, 0), spread_table(4))
    for j in range(4):
        for m in range(4):
            row = rows[channels * j : channels * (j + 1), LANES * m : LANES * (m + 1)]
            dense_ref[4 * j + m] = row.astype(BF16)
            for h in range(2):
                r = 16 * h + 4 * j + m
                side = turn(y_zero[:, LANES * h : LANES * (h + 1)], 72 - 8 * (r % 16))
                side = jnp.where(own_side, side, 0.0)
                g_ref[r] = jnp.where(low, turn(row, 64 * h), side).astype(BF16)
    for i in range(HALO):
        rest = turn(y_one[:, :LANES], 72 - 8 * i)
        tail_ref[i] = jnp.where(own_side, rest, 0.0).astype(BF16)
    eye = (
        lax.broadcasted_iota(jnp.int32, (channels, channels), 0)
        == lax.broadcasted_iota(jnp.int32, (channels, channels), 1)
    )
    eye = jnp.where(eye, 1.0, 0.0).astype(BF16)
    for u in range(3):
        for v in range(3):
            t = 3 * u + v
            pair = jnp.concatenate([kern_ref[t], kern_ref[3 * v + u]], 0)
            both_ref[channels * t : channels * (t + 1), :] = dot(eye, pair, NT).astype(BF16)
    for t in range(0, TAPS - 1, 2):
        flat_ref[:, channels * t : channels * (t + 2)] = jnp.concatenate(
            [kern_ref[t].astype(F32), kern_ref[t + 1].astype(F32)], 1
        ).astype(BF16)
    flat_ref[:, channels * (TAPS - 1) : channels * TAPS] = kern_ref[TAPS - 1]
    weight = weight_ref[...].astype(F32)
    own = embed_ref[...].astype(F32)
    for r in range(TILE):
        scaled_ref[channels * r : channels * (r + 1), :] = (own[r : r + 1, :] * weight).astype(
            BF16
        )
    inner = jnp.where(lane < 2 * TILE, 1.0, 0.0).astype(BF16)
    beside = jnp.where(own_side, 1.0, 0.0).astype(BF16)

    def spread_rows(i, carry):
        x = jnp.concatenate([g_ref[2 * i], g_ref[2 * i + 1]], 1)
        y = jnp.concatenate([inner, inner], 1), jnp.concatenate([beside, beside], 1)
        y = dot(both_ref[...], jnp.concatenate([x * y[0], x * y[1]], 0))
        spread_ref[2 * i] = y[:, :LANES]
        spread_ref[2 * i + 1] = y[:, LANES:]
        return carry

    lax.fori_loop(0, TILE // 2, spread_rows, 0, unroll=4)


def unpacked(x):
    return jnp.concatenate([x[:TILE], x[TILE:]], 1)


def forward(
    meta_ref, weight_ref, own_ref, chip_ref, core_ref, dense_ref, scaled_ref,
    part_ref, pair_ref, rolled_ref, map_ref,
):
    channels = weight_ref.shape[0]
    width = channels // GROUPS
    weight = weight_ref[...].astype(F32)
    own = own_ref[...].astype(F32)
    after = unpacked(from_below(core_ref, chip_ref, slice(RIM_EMBED, RIM)))
    before = unpacked(from_above(core_ref, chip_ref, slice(RIM_EMBED, RIM)))[TILE - HALO :]
    filler = jnp.zeros((LANES - 2 * TILE - HALO, own.shape[1]), F32)
    columns = jnp.concatenate([own, after, filler, before], 0).astype(BF16)
    lane = lane_ids(channels)
    kept = (
        jnp.logical_or(lane < TILE, lane >= LANES - HALO),
        lane < 2 * TILE,
        within(lane, TILE, 2 * TILE),
    )
    for c in range(6):
        part = 0 if c == 0 else (2 if c == 5 else 1)
        if part == 1:
            scaled = scaled_ref[8 * channels * (c - 1) : 8 * channels * c, :]
        else:
            rim = before if part == 0 else after
            scaled = jnp.concatenate(
                [(rim[i : i + 1, :] * weight).astype(BF16) for i in range(HALO)], 0
            )
        pair = dot(scaled, columns, NT).astype(BF16)
        for i in range(8):
            one = pair[channels * i : channels * (i + 1)]
            if part == 1:
                pair_ref[8 * (c - 1) + i] = one
            x = jnp.where(kept[part], jnp.maximum(one.astype(F32), 0.0), 0.0)
            map_ref[8 * c + i] = x.astype(BF16)
    swap = swap_table()

    def gathered(first, per, low, high, move):
        halves = []
        for half in range(2):
            total = None
            for m in range(per):
                piece = map_ref[first + per * half + m].astype(F32)
                piece = jnp.where(within(lane, low, high), piece, 0.0)
                piece = turn(piece, move(m))
                total = piece if total is None else total + piece
            halves.append(total.astype(BF16))
        return jnp.concatenate(halves, 1)

    above = dot(gathered(0, 4, 0, TILE, lambda m: TILE * m), swap)
    below = dot(gathered(8, 16, TILE, TILE + HALO, lambda m: HALO * m - TILE), swap, NT)
    for r in range(TILE):
        half = LANES * (r // 16)
        side = turn(above[:, half : half + LANES], LANES - HALO - HALO * (r % 16))
        map_ref[HALO + r] += jnp.where(lane >= LANES - HALO, side, 0.0).astype(BF16)
    for i in range(HALO):
        half = LANES * (i // 4)
        side = turn(below[:, half : half + LANES], -TILE * (i % 4))
        map_ref[HALO + TILE + i] += jnp.where(lane < TILE, side, 0.0).astype(BF16)

    spacing = [meta_ref[g] for g in range(GROUPS)]
    source = row_ids(LANES)
    to = lane_ids(LANES)
    for g in range(GROUPS):
        tables = []
        for h in range(2):
            half = within(to, 2 * TILE * h, 2 * TILE * (h + 1))
            offset = jnp.where(half, (source - (to - 2 * TILE * h)) & (LANES - 1), LANES)
            hits = [
                jnp.where(offset == (v * spacing[g]) & (LANES - 1), 1.0, 0.0).astype(BF16)
                for v in (-1, 0, 1)
            ]
            tables.append(jnp.concatenate(hits, 1))
        table = jnp.concatenate(tables, 0)
        at = width * g
        for part in range(2):
            low = [map_ref[16 * part + i, at : at + width, :] for i in range(16)]
            high = [map_ref[16 * part + i + 16, at : at + width, :] for i in range(16)]
            x = jnp.concatenate([jnp.concatenate(low, 0), jnp.concatenate(high, 0)], 1)
            y = dot(x, table).astype(BF16)
            for i in range(16):
                for v in range(3):
                    to_row = channels * v + at
                    rolled_ref[16 * part + i, to_row : to_row + width, :] = y[
                        width * i : width * (i + 1), LANES * v : LANES * (v + 1)
                    ]
    total = None
    for j in range(4):
        rows = range(4 * j, 4 * (j + 1))
        stack = jnp.concatenate([taps_of(rolled_ref, spacing, r) for r in rows], 1)
        share = dot(jnp.concatenate([dense_ref[r] for r in rows], 1), stack, NT)
        total = share if total is None else total + share
    part_ref[...] = total


def taps_of(rolled_ref, spacing, r):
    channels = rolled_ref.shape[1] // 3
    width = channels // GROUPS
    pieces = []
    for u in range(3):
        for v in range(3):
            for g in range(GROUPS):
                at = channels * v + width * g
                pieces.append(rolled_ref[r + HALO + (u - 1) * spacing[g], at : at + width, :])
    return jnp.concatenate(pieces, 0)


def respond(
    meta_ref, flat_ref, rolled_ref, pair_ref, core_ref, chip_ref,
    out_ref,
    rows_ref,
):
    channels = flat_ref.shape[0]
    spacing = [meta_ref[g] for g in range(GROUPS)]
    lane = lane_ids(channels)
    low = lane < 2 * TILE
    _, even, _, keep = place()
    corner = core_ref[...] * even + chip_ref[...].astype(F32) * ((1.0 - even) * keep)
    low_side, high_side = corner[:, :LANES], corner[:, LANES:]
    corner = jnp.concatenate(
        [low_side, turn(low_side, 64), high_side, turn(high_side, 64)], 0
    )
    share = dot(flat_ref[:, channels * (TAPS - 1) :], corner_shift(corner, spacing))
    for j in range(4):
        rows = range(4 * j, 4 * (j + 1))
        stack = jnp.concatenate([taps_of(rolled_ref, spacing, r) for r in rows], 1)
        response = dot(flat_ref[...], stack)
        for m, r in enumerate(rows):
            row = response[:, LANES * m : LANES * (m + 1)]
            if r >= HALO:
                at = LANES - HALO
                row = row + jnp.where(lane >= at, turn(share, at - HALO * (r - HALO)), 0.0)
            near = pair_ref[r].astype(F32)
            far = turn(pair_ref[r + 16].astype(F32), 2 * TILE)
            row = jnp.where(low, near, far) + row
            rows_ref[channels * j : channels * (j + 1), LANES * m : LANES * (m + 1)] = row.astype(
                BF16
            )
    slot = meta_ref[GROUPS]
    chunks = dot(rows_ref[...], spread_table(4), NT)
    for j in range(4):
        chunk = chunks[channels * j : channels * (j + 1)]
        for h in range(2):
            at = slice(LANES * (j + 4 * h), LANES * (j + 4 * h + 1))
            to = 2 * LANES * h
            out_ref[slot, :, at] = chunk[:, to : to + LANES].astype(BF16)
            out_ref[1 - slot, :, at] = (chunk[:, to + LANES : to + 2 * LANES] * keep).astype(BF16)


def adjoint(
    meta_ref, weight_ref, own_ref, g_ref, core_ref, chip_ref, tail_ref, both_ref, pair_ref,
    spread_ref,
    grad_ref, local_ref, sum_ref, above_ref, below_ref,
):
    channels = g_ref.shape[1]
    width = channels // GROUPS
    span = 3 * channels
    lane = lane_ids(channels)
    zeros = jnp.zeros((channels, LANES), BF16)
    above = from_above(core_ref, chip_ref, slice(0, RIM_EMBED))
    below = from_below(core_ref, chip_ref, slice(0, RIM_EMBED))

    def moved(rim, at, to, size, per, i):
        at += LANES * (i // per)
        x = turn(rim[:, at : at + LANES], to - size * (i % per))
        return jnp.where(within(lane, to, to + size), x, 0.0)

    for h in range(HALO // 2):
        upper, lower = [], []
        for i in (2 * h, 2 * h + 1):
            x = moved(above, 0, 0, TILE, 4, i)
            x = x + moved(above, RIM_CORNER, LANES - HALO, HALO, 16, i)
            upper.append(jnp.concatenate([x.astype(BF16), zeros], 0))
            x = moved(below, 0, TILE, TILE, 4, i)
            x = x + moved(below, RIM_CORNER, 2 * TILE, HALO, 16, i)
            y = moved(below, RIM_SIDE, 80, TILE, 4, i).astype(BF16) + tail_ref[i]
            lower.append(jnp.concatenate([x.astype(BF16), y], 0))
        x = dot(both_ref[2 * span :, :], jnp.concatenate(upper, 1))
        y = dot(both_ref[:span, :], jnp.concatenate(lower, 1))
        for m in range(2):
            above_ref[2 * h + m] = x[:, LANES * m : LANES * (m + 1)]
            below_ref[2 * h + m] = y[:, LANES * m : LANES * (m + 1)]
    spacing = [meta_ref[g] for g in range(GROUPS)]
    second = within(lane, TILE, 2 * TILE)

    def gathered(r):
        pieces = []
        for g in range(GROUPS):
            totals = []
            up, down = r - spacing[g], r + spacing[g]
            for v in range(3):
                at = channels * v + width * g
                tap = slice(at, at + width)
                total = spread_ref[r, span + at : span + at + width, :]
                last = slice(2 * span + at, 2 * span + at + width)
                if r < HALO:
                    x = spread_ref[jnp.maximum(up, 0), last, :]
                    y = above_ref[jnp.minimum(up + HALO, HALO - 1), tap, :]
                    total = total + jnp.where(up < 0, y, x)
                else:
                    total = total + spread_ref[up, last, :]
                if r >= TILE - HALO:
                    x = spread_ref[jnp.minimum(down, TILE - 1), tap, :]
                    y = below_ref[jnp.maximum(down - TILE, 0), tap, :]
                    total = total + jnp.where(down >= TILE, y, x)
                else:
                    total = total + spread_ref[down, tap, :]
                totals.append(total)
            pieces.append(
                totals[1]
                + pltpu.roll(totals[0], LANES - spacing[g], 1)
                + pltpu.roll(totals[2], spacing[g], 1)
            )
        grad = jnp.concatenate(pieces, 0)
        grad = grad + jnp.where(second, turn(grad, -48), 0.0)
        own = g_ref[r].astype(F32)
        own = own + jnp.where(pair_ref[r].astype(F32) > 0, grad, 0.0)
        return jnp.where(lane < 2 * TILE, own, 0.0).astype(BF16)

    weight = weight_ref[...].astype(F32)
    own = own_ref[...].astype(F32)
    after = unpacked(from_below(core_ref, chip_ref, slice(RIM_EMBED, RIM)))
    columns = jnp.concatenate(
        [own, after, jnp.zeros((LANES - 2 * TILE, own.shape[1]), F32)], 0
    ).astype(BF16)
    weight_part = jnp.zeros_like(weight)
    local = []
    for c in range(TILE // 8):
        rows = jnp.concatenate([gathered(8 * c + i) for i in range(8)], 0)
        grad_ref[8 * channels * c : 8 * channels * (c + 1), :] = rows
        grad_scaled = dot(rows, columns)
        for i in range(8):
            one = grad_scaled[channels * i : channels * (i + 1)]
            local.append(jnp.sum(one * weight, 0, keepdims=True))
            weight_part = weight_part + one * own[8 * c + i : 8 * c + i + 1, :]
    local_ref[...] = jnp.concatenate(local, 0)
    sum_ref[...] = weight_part


def deliver(
    meta_ref, core_ref, chip_ref, part_ref, pair_ref,
    keep_ref, send_ref, corner_ref, sum_ref, kernel_ref,
):
    channels = part_ref.shape[0]
    lane = lane_ids(channels)
    rim = from_above(core_ref, chip_ref, slice(0, RIM_SIDE))
    corner, ends = None, None
    for i in range(HALO):
        x = jnp.where(within(lane, TILE, TILE + HALO), pair_ref[i].astype(F32), 0.0)
        x = turn(jnp.maximum(x, 0.0), HALO * i - TILE)
        half = LANES * (i // 4)
        y = turn(rim[:, half : half + LANES], HALO * i - TILE * (i % 4) - (TILE - HALO))
        y = jnp.where(within(lane, HALO * i, HALO * (i + 1)), y, 0.0)
        corner, ends = (x, y) if i == 0 else (corner + x, ends + y)
    spacing = [meta_ref[g] for g in range(GROUPS)]
    share = dot(ends.astype(BF16), corner_shift(corner, spacing), NT)
    last = channels * (TAPS - 1)
    kernel_ref[:, :last] = part_ref[:, :last]
    kernel_ref[:, last:] = part_ref[:, last:] + share
    quarter = channels // 4
    corner = [corner[quarter * q : quarter * (q + 1)] for q in range(4)]
    corner = jnp.concatenate(
        [corner[0] + turn(corner[1], 64), corner[2] + turn(corner[3], 64)], 1
    )
    corner_ref[...] = corner
    rows = channels // 2
    half = half_of(lax.axis_index("blk"))
    send_ref[:quarter] = corner
    for ref, which, first in ((keep_ref, half, 0), (send_ref, 1 - half, quarter)):
        at = pl.multiple_of(rows * which, rows)
        ref[first : first + rows] = sum_ref[pl.ds(at, rows), :]
        for q in range(2):
            to = first + rows * (q + 1)
            ref[to : to + rows] = kernel_ref[pl.ds(at, rows), 256 * q : 256 * (q + 1)]
        ref[first + 3 * rows :] = jnp.concatenate(
            [kernel_ref[pl.ds(at + 8 * q, 8), 512:] for q in range(4)], 1
        )


def middle(
    meta_ref, weight_ref, own_ref, chip_ref, core_ref, dense_ref, scaled_ref, g_ref, tail_ref,
    both_ref, spread_ref,
    keep_ref, send_ref, corner_ref, local_ref, grad_ref, pair_ref, rolled_ref,
    map_ref, part_ref, above_ref, below_ref, sum_ref, kernel_ref,
):
    forward(
        meta_ref, weight_ref, own_ref, chip_ref, core_ref, dense_ref, scaled_ref,
        part_ref, pair_ref, rolled_ref, map_ref,
    )
    adjoint(
        meta_ref, weight_ref, own_ref, g_ref, core_ref, chip_ref, tail_ref, both_ref, pair_ref,
        spread_ref,
        grad_ref, local_ref, sum_ref, above_ref, below_ref,
    )
    deliver(
        meta_ref, core_ref, chip_ref, part_ref, pair_ref,
        keep_ref, send_ref, corner_ref, sum_ref, kernel_ref,
    )


def embed_terms(grad_ref, scaled_ref, local_ref, corner_ref, near_ref, far_ref, side_ref):
    both = dot(grad_ref[...], scaled_ref[...], TN)
    far = both[TILE : 2 * TILE]
    near_ref[...] = local_ref[...] + both[:TILE]
    far_ref[...] = far
    side_ref[:TILE] = far.astype(BF16)
    side_ref[TILE:] = corner_ref[...].astype(BF16)


def finish(
    mine_ref, other_ref, chip_ref, near_ref,
    weight_ref, kernel_ref, embed_ref,
):
    index, even, before, _ = place()
    channels = kernel_ref.shape[1]
    rows = channels // 2
    half = half_of(index)
    for ref, which in ((mine_ref, half), (other_ref, 1 - half)):
        at = pl.multiple_of(rows * which, rows)
        weight_ref[pl.ds(at, rows), :] = ref[:rows]
        for t in range(TAPS - 1):
            first = rows * (1 + t // 4)
            to = channels * (t % 4)
            kernel_ref[t, pl.ds(at, rows), :] = ref[first : first + rows, to : to + channels]
        for q in range(4):
            kernel_ref[TAPS - 1, pl.ds(at + 8 * q, 8), :] = ref[
                3 * rows : 3 * rows + 8, channels * q : channels * (q + 1)
            ]
    carried = other_ref[3 * rows + 8 :] * (1.0 - even)
    carried = carried + chip_ref[...].astype(F32) * (even * before)
    embed_ref[...] = near_ref[...] + carried


VMEM = pl.BlockSpec(memory_space=pltpu.VMEM)
SMEM = pl.BlockSpec(memory_space=pltpu.SMEM)
HBM = pl.BlockSpec(memory_space=pltpu.HBM)


def shape(dims, kind):
    return jax.ShapeDtypeStruct(dims, kind)


def call(kernel, outs, scalars, operands, scratch=(), flops=0, moved=0, first=None, room=32):
    specs = [first or SMEM] * scalars + [VMEM] * (len(operands) - scalars)
    return pl.pallas_call(
        kernel,
        out_shape=outs,
        in_specs=specs,
        out_specs=[SMEM if out.dtype == jnp.int32 else VMEM for out in outs],
        scratch_shapes=list(scratch),
        compiler_params=pltpu.CompilerParams(vmem_limit_bytes=room * 1024 * 1024),
        cost_estimate=pl.CostEstimate(flops=flops, bytes_accessed=moved, transcendentals=0),
    )(*operands)


def swap_with(shard, step):
    return lax.ppermute(shard, "blk", [(i, i ^ step) for i in range(lax.axis_size("blk"))])


def swap_stage(shard, first, second):
    pairs = [(i, i ^ (second if half_of(i) else first)) for i in range(lax.axis_size("blk"))]
    return lax.ppermute(shard, "blk", pairs)


def swap_chips(shard):
    count = lax.axis_size("blk")
    pairs = [(i, (i + (1 if i % 2 else -1)) % count) for i in range(count)]
    return lax.ppermute(shard, "blk", pairs)


def per_device(embed, pair_weight, conv_kernel, dilations, tile_order, cotangent):
    features = embed.shape[1]
    channels = conv_kernel.shape[0]
    count = lax.axis_size("blk")
    weight = pair_weight.T
    taps = jnp.transpose(conv_kernel, (1, 0, 2))
    cot = cotangent.reshape(2, channels, TILE * TILE)
    packed = shape((channels, RIM), BF16)
    body = shape((TILE, channels, LANES), BF16)
    to_chip, to_core = call(
        pack,
        [packed, packed],
        3,
        (tile_order, cot, embed),
        [
            pltpu.SMEM(tile_order.shape, jnp.int32),
            pltpu.VMEM(cot.shape, BF16),
            pltpu.VMEM(embed.shape, BF16),
            pltpu.SemaphoreType.DMA((3,)),
        ],
        flops=10**10,
        moved=10**6,
        first=HBM,
        room=60,
    )
    chip = swap_chips(to_chip)
    core = swap_with(to_core, 1)
    grads, dense, tail, flat, both, scaled, spread, meta = call(
        prepare,
        [
            body,
            shape((TILE // 2, channels, LANES), BF16),
            shape((HALO, channels, LANES), BF16),
            shape((channels, TAPS * channels), BF16),
            shape((TAPS * channels, 2 * channels), BF16),
            shape((TILE * channels, features), BF16),
            shape((TILE, TAPS * channels, LANES), F32),
            shape((2 * GROUPS,), jnp.int32),
        ],
        2,
        (tile_order, dilations, cot, taps, weight, embed),
        flops=2 * 10**8,
        moved=3 * 10**6,
    )
    rows = channels // 2
    sums = 3 * rows + rows * channels // features
    total, send, corner, local, grad_pair, pair, rolled = call(
        middle,
        [
            shape((sums, features), F32),
            shape((channels // 4 + sums, features), F32),
            shape((channels // 4, features), F32),
            shape((TILE, features), F32),
            shape((TILE * channels, LANES), BF16),
            body,
            shape((TILE, 3 * channels, LANES), BF16),
        ],
        1,
        (meta, weight, embed, chip, core, dense, scaled, grads, tail, both, spread),
        [
            pltpu.VMEM((TILE + 2 * HALO, channels, LANES), BF16),
            pltpu.VMEM((channels, TAPS * channels), F32),
            pltpu.VMEM((HALO, 3 * channels, LANES), F32),
            pltpu.VMEM((HALO, 3 * channels, LANES), F32),
            pltpu.VMEM((channels, features), F32),
            pltpu.VMEM((channels, TAPS * channels), F32),
        ],
        flops=2 * 10**9,
        moved=8 * 10**6,
        room=24,
    )
    by_core = swap_with(send, 1)
    near, far, sided = call(
        embed_terms,
        [
            shape((TILE, features), F32),
            shape((TILE, features), F32),
            shape((TILE + channels // 4, features), BF16),
        ],
        0,
        (grad_pair, scaled, local, corner),
        flops=2 * 10**8,
        moved=2 * 10**6,
    )
    by_chip = swap_chips(sided)
    by_core, sided = lax.optimization_barrier((by_core, sided))
    total = total + by_core[channels // 4 :]
    by_core = by_core[: channels // 4]
    steps = [1 | 1 << b for b in range(1, count.bit_length() - 1)]
    turns = list(zip(steps, steps[1:] + steps[:1]))
    for first, second in turns[:-1]:
        total = total + swap_stage(total, first, second)
    rolled, total, by_chip = lax.optimization_barrier((rolled, total, by_chip))
    last = swap_stage(total, *turns[-1])
    (out,) = call(
        respond,
        [shape((2, channels, TILE * TILE), BF16)],
        1,
        (meta, flat, rolled, pair, by_core, by_chip[TILE:]),
        [pltpu.VMEM((4 * channels, 4 * LANES), BF16)],
        flops=2 * 10**8,
        moved=2 * 10**6,
    )
    out, last = lax.optimization_barrier((out, last))
    total = total + last
    rest = swap_with(jnp.concatenate([total, far]), 1)
    grad_weight, grad_kernel, grad_embed = call(
        finish,
        [
            shape((channels, features), F32),
            shape((TAPS, channels, channels), F32),
            shape((TILE, features), F32),
        ],
        0,
        (total, rest, by_chip[:TILE], near),
        moved=10**6,
    )
    return (
        out.reshape(1, 2, channels, TILE * TILE),
        grad_embed,
        grad_weight.T,
        jnp.transpose(grad_kernel, (1, 0, 2)),
    )


def solution(mesh):
    placed = (
        P(("grp", "blk"), None),
        P(),
        P(),
        P(),
        P(("grp", "blk"), None),
        P(("grp", "blk"), None, None, None),
    )
    return jax.shard_map(
        per_device,
        mesh=mesh,
        in_specs=placed,
        out_specs=(
            P(("grp", "blk"), None, None, None),
            P(("grp", "blk"), None),
            P("grp", None),
            P("grp", None, None),
        ),
        check_vma=False,
    )
```

```python
import jax
import jax.numpy as jnp
from jax import lax
from jax.experimental import pallas as pl
from jax.experimental.pallas import tpu as pltpu
from jax.sharding import PartitionSpec as P

GROUPS = 4
HALO = 8
TILE = 32
LANES = 128
TAPS = 9
F32 = jnp.float32
BF16 = jnp.bfloat16
NN = (((1,), (0,)), ((), ()))
NT = (((1,), (1,)), ((), ()))
TN = (((0,), (0,)), ((), ()))


def dot(a, b, dims=NN):
    return lax.dot_general(a, b, dims, preferred_element_type=F32)


def turn(x, by):
    by = by % LANES
    return x if by == 0 else pltpu.roll(x, by, 1)


def lane_ids(rows):
    return lax.broadcasted_iota(jnp.int32, (rows, LANES), 1)


def within(lane, low, high):
    return jnp.logical_and(lane >= low, lane < high)


def one_hot(target, chunks):
    lane = lane_ids(target.shape[0])
    hits = [jnp.where(target == lane + LANES * c, 1.0, 0.0).astype(BF16) for c in range(chunks)]
    return jnp.concatenate(hits, 1)


def row_ids(rows):
    return lax.broadcasted_iota(jnp.int32, (rows, LANES), 0)


def spread_table(chunks):
    x = row_ids(LANES * chunks)
    return one_hot((((x >> 5) & 3) << 7) + ((x >> 7) << 5) + (x & 31), 4)


def swap_table():
    x = row_ids(HALO * TILE)
    return one_hot(((x & 31) << 3) + (x >> 5), 2)


def edge_table():
    x = row_ids(LANES)
    return one_hot(jnp.where((x & 31) < HALO, ((x & 31) << 5) + (x >> 5), -1), 2)


def corner_table(first):
    x = row_ids(HALO * TILE)
    c = (x & 31) - first
    return one_hot(jnp.where(within(c, 0, HALO), ((x >> 5) << 3) + c, -1), 1)


def as_float(flag):
    return jnp.where(flag, 1.0, 0.0).astype(F32)


def place():
    index = lax.axis_index("blk")
    last = lax.axis_size("blk") - 1
    return index, as_float(index % 2 == 0), as_float(index > 0), as_float(index < last)


def half_of(index):
    for by in (8, 4, 2, 1):
        index = index ^ (index >> by)
    return index & 1


def corner_shift(flat, spacing):
    width = flat.shape[0] // GROUPS
    lane = lane_ids(width)
    pieces = []
    for g in range(GROUPS):
        d = spacing[g]
        kept = jnp.logical_and(jnp.logical_and(lane < 8 * HALO, (lane >> 3) < d), (lane & 7) < d)
        x = jnp.where(kept, flat[width * g : width * (g + 1)], 0.0)
        pieces.append(pltpu.roll(x, (HALO + 1) * (HALO - d), 1))
    return jnp.concatenate(pieces, 0).astype(BF16)


def tiles_of(order_ref, cot_ref):
    slot = order_ref[0, 0]
    _, _, _, keep = place()
    return cot_ref[slot], (cot_ref[1 - slot].astype(F32) * keep).astype(BF16)


def fetch(sources, targets, sems):
    copies = [
        pltpu.make_async_copy(source, target, sems.at[i])
        for i, (source, target) in enumerate(zip(sources, targets))
    ]
    for copy in copies:
        copy.start()
    return copies


def pack(
    order_hbm, cot_hbm, embed_hbm,
    chip_ref, core_ref,
    order_ref, cot_ref, embed_ref, sems,
):
    copies = fetch((order_hbm, cot_hbm, embed_hbm), (order_ref, cot_ref, embed_ref), sems)
    edge, head, tail = edge_table(), corner_table(0), corner_table(TILE - HALO)
    for copy in copies:
        copy.wait()
    zero, one = tiles_of(order_ref, cot_ref)
    _, even, _, _ = place()
    channels = zero.shape[0]
    moved = dot(
        jnp.concatenate([zero[:, LANES * j : LANES * (j + 1)] for j in range(8)], 0), edge
    )
    columns = []
    for h in range(2):
        total = None
        for j in range(8):
            piece = moved[channels * j : channels * (j + 1), LANES * h : LANES * (h + 1)]
            piece = turn(piece, 4 * j)
            total = piece if total is None else total + piece
        columns.append(total)
    rim = HALO * TILE
    tail_at = TILE * (TILE - HALO)
    up = [zero[:, :rim].astype(F32)] + columns + [dot(one[:, :rim], head)]
    down = [one[:, tail_at:].astype(F32)] + [jnp.zeros_like(x) for x in columns]
    down += [dot(zero[:, tail_at:], tail)]
    up, down = jnp.concatenate(up, 1), jnp.concatenate(down, 1)
    width = up.shape[1]
    both = jnp.concatenate([embed_ref[:, :LANES], embed_ref[:, LANES:]], 0)
    core_ref[:, :width] = (down * even + up * (1.0 - even)).astype(BF16)
    core_ref[:, width:] = both
    chip_ref[:, :width] = (up * even + down * (1.0 - even)).astype(BF16)
    chip_ref[:, width:] = both


RIM_SIDE, RIM_CORNER, RIM_EMBED, RIM = 256, 512, 640, 768


def from_above(core_ref, chip_ref, at):
    _, even, before, _ = place()
    x = chip_ref[:, at].astype(F32) * (even * before)
    return x + core_ref[:, at].astype(F32) * ((1.0 - even) * before)


def from_below(core_ref, chip_ref, at):
    _, even, _, after = place()
    x = core_ref[:, at].astype(F32) * (even * after)
    return x + chip_ref[:, at].astype(F32) * ((1.0 - even) * after)


def prepare(
    order_ref, dil_ref, cot_ref, kern_ref, weight_ref, embed_ref,
    g_ref, dense_ref, tail_ref, flat_ref, both_ref, scaled_ref, spread_ref, meta_ref,
):
    for g in range(GROUPS):
        meta_ref[g] = jnp.left_shift(jnp.int32(1), dil_ref[g])
    meta_ref[GROUPS] = order_ref[0, 0]
    zero, one = tiles_of(order_ref, cot_ref)
    channels = kern_ref.shape[1]
    swap = swap_table()
    tail_at = TILE * (TILE - HALO)
    y_zero = dot(zero[:, tail_at:], swap)
    y_one = dot(one[:, tail_at:], swap)
    lane = lane_ids(channels)
    own_side = within(lane, 72, 80)
    low = lane < 2 * TILE
    pieces = []
    for j in range(4):
        at = slice(LANES * j, LANES * (j + 1))
        later = slice(LANES * (j + 4), LANES * (j + 5))
        pieces.append(
            jnp.concatenate([zero[:, at], one[:, at], zero[:, later], one[:, later]], 1)
        )
    rows = dot(jnp.concatenate(pieces, 0), spread_table(4))
    for j in range(4):
        for m in range(4):
            row = rows[channels * j : channels * (j + 1), LANES * m : LANES * (m + 1)]
            dense_ref[4 * j + m] = row.astype(BF16)
            for h in range(2):
                r = 16 * h + 4 * j + m
                side = turn(y_zero[:, LANES * h : LANES * (h + 1)], 72 - 8 * (r % 16))
                side = jnp.where(own_side, side, 0.0)
                g_ref[r] = jnp.where(low, turn(row, 64 * h), side).astype(BF16)
    for i in range(HALO):
        rest = turn(y_one[:, :LANES], 72 - 8 * i)
        tail_ref[i] = jnp.where(own_side, rest, 0.0).astype(BF16)
    eye = (
        lax.broadcasted_iota(jnp.int32, (channels, channels), 0)
        == lax.broadcasted_iota(jnp.int32, (channels, channels), 1)
    )
    eye = jnp.where(eye, 1.0, 0.0).astype(BF16)
    for u in range(3):
        for v in range(3):
            t = 3 * u + v
            pair = jnp.concatenate([kern_ref[t], kern_ref[3 * v + u]], 0)
            both_ref[channels * t : channels * (t + 1), :] = dot(eye, pair, NT).astype(BF16)
    for t in range(0, TAPS - 1, 2):
        flat_ref[:, channels * t : channels * (t + 2)] = jnp.concatenate(
            [kern_ref[t].astype(F32), kern_ref[t + 1].astype(F32)], 1
        ).astype(BF16)
    flat_ref[:, channels * (TAPS - 1) : channels * TAPS] = kern_ref[TAPS - 1]
    weight = weight_ref[...].astype(F32)
    own = embed_ref[...].astype(F32)
    for r in range(TILE):
        scaled_ref[channels * r : channels * (r + 1), :] = (own[r : r + 1, :] * weight).astype(
            BF16
        )
    inner = jnp.where(lane < 2 * TILE, 1.0, 0.0).astype(BF16)
    beside = jnp.where(own_side, 1.0, 0.0).astype(BF16)

    def spread_rows(i, carry):
        x = jnp.concatenate([g_ref[2 * i], g_ref[2 * i + 1]], 1)
        y = jnp.concatenate([inner, inner], 1), jnp.concatenate([beside, beside], 1)
        y = dot(both_ref[...], jnp.concatenate([x * y[0], x * y[1]], 0))
        spread_ref[2 * i] = y[:, :LANES]
        spread_ref[2 * i + 1] = y[:, LANES:]
        return carry

    lax.fori_loop(0, TILE // 2, spread_rows, 0, unroll=4)


def unpacked(x):
    return jnp.concatenate([x[:TILE], x[TILE:]], 1)


def forward(
    meta_ref, weight_ref, own_ref, chip_ref, core_ref, dense_ref, scaled_ref,
    pair_ref, rolled_ref, map_ref,
):
    channels = weight_ref.shape[0]
    width = channels // GROUPS
    weight = weight_ref[...].astype(F32)
    own = own_ref[...].astype(F32)
    after = unpacked(from_below(core_ref, chip_ref, slice(RIM_EMBED, RIM)))
    before = unpacked(from_above(core_ref, chip_ref, slice(RIM_EMBED, RIM)))[TILE - HALO :]
    filler = jnp.zeros((LANES - 2 * TILE - HALO, own.shape[1]), F32)
    columns = jnp.concatenate([own, after, filler, before], 0).astype(BF16)
    lane = lane_ids(channels)
    kept = (
        jnp.logical_or(lane < TILE, lane >= LANES - HALO),
        lane < 2 * TILE,
        within(lane, TILE, 2 * TILE),
    )
    for c in range(6):
        part = 0 if c == 0 else (2 if c == 5 else 1)
        if part == 1:
            scaled = scaled_ref[8 * channels * (c - 1) : 8 * channels * c, :]
        else:
            rim = before if part == 0 else after
            scaled = jnp.concatenate(
                [(rim[i : i + 1, :] * weight).astype(BF16) for i in range(HALO)], 0
            )
        pair = dot(scaled, columns, NT).astype(BF16)
        for i in range(8):
            one = pair[channels * i : channels * (i + 1)]
            if part == 1:
                pair_ref[8 * (c - 1) + i] = one
            x = jnp.where(kept[part], jnp.maximum(one.astype(F32), 0.0), 0.0)
            map_ref[8 * c + i] = x.astype(BF16)
    swap = swap_table()

    def gathered(first, per, low, high, move):
        halves = []
        for half in range(2):
            total = None
            for m in range(per):
                piece = map_ref[first + per * half + m].astype(F32)
                piece = jnp.where(within(lane, low, high), piece, 0.0)
                piece = turn(piece, move(m))
                total = piece if total is None else total + piece
            halves.append(total.astype(BF16))
        return jnp.concatenate(halves, 1)

    above = dot(gathered(0, 4, 0, TILE, lambda m: TILE * m), swap)
    below = dot(gathered(8, 16, TILE, TILE + HALO, lambda m: HALO * m - TILE), swap, NT)
    for r in range(TILE):
        half = LANES * (r // 16)
        side = turn(above[:, half : half + LANES], LANES - HALO - HALO * (r % 16))
        map_ref[HALO + r] += jnp.where(lane >= LANES - HALO, side, 0.0).astype(BF16)
    for i in range(HALO):
        half = LANES * (i // 4)
        side = turn(below[:, half : half + LANES], -TILE * (i % 4))
        map_ref[HALO + TILE + i] += jnp.where(lane < TILE, side, 0.0).astype(BF16)

    spacing = [meta_ref[g] for g in range(GROUPS)]
    source = row_ids(LANES)
    to = lane_ids(LANES)
    for g in range(GROUPS):
        tables = []
        for h in range(2):
            half = within(to, 2 * TILE * h, 2 * TILE * (h + 1))
            offset = jnp.where(half, (source - (to - 2 * TILE * h)) & (LANES - 1), LANES)
            hits = [
                jnp.where(offset == (v * spacing[g]) & (LANES - 1), 1.0, 0.0).astype(BF16)
                for v in (-1, 0, 1)
            ]
            tables.append(jnp.concatenate(hits, 1))
        table = jnp.concatenate(tables, 0)
        at = width * g
        for part in range(2):
            low = [map_ref[16 * part + i, at : at + width, :] for i in range(16)]
            high = [map_ref[16 * part + i + 16, at : at + width, :] for i in range(16)]
            x = jnp.concatenate([jnp.concatenate(low, 0), jnp.concatenate(high, 0)], 1)
            y = dot(x, table).astype(BF16)
            for i in range(16):
                for v in range(3):
                    to_row = channels * v + at
                    rolled_ref[16 * part + i, to_row : to_row + width, :] = y[
                        width * i : width * (i + 1), LANES * v : LANES * (v + 1)
                    ]


def kernel_share(meta_ref, rolled_ref, dense_ref, rows):
    spacing = [meta_ref[g] for g in range(GROUPS)]
    stack = jnp.concatenate([taps_of(rolled_ref, spacing, r) for r in rows], 1)
    return dot(jnp.concatenate([dense_ref[r] for r in rows], 1), stack, NT)


def taps_of(rolled_ref, spacing, r):
    channels = rolled_ref.shape[1] // 3
    width = channels // GROUPS
    pieces = []
    for u in range(3):
        for v in range(3):
            for g in range(GROUPS):
                at = channels * v + width * g
                pieces.append(rolled_ref[r + HALO + (u - 1) * spacing[g], at : at + width, :])
    return jnp.concatenate(pieces, 0)


def respond(
    meta_ref, flat_ref, rolled_ref, pair_ref, core_ref, chip_ref,
    out_ref,
    rows_ref,
):
    channels = flat_ref.shape[0]
    spacing = [meta_ref[g] for g in range(GROUPS)]
    lane = lane_ids(channels)
    low = lane < 2 * TILE
    _, even, _, keep = place()
    corner = core_ref[...] * even + chip_ref[...].astype(F32) * ((1.0 - even) * keep)
    low_side, high_side = corner[:, :LANES], corner[:, LANES:]
    corner = jnp.concatenate(
        [low_side, turn(low_side, 64), high_side, turn(high_side, 64)], 0
    )
    share = dot(flat_ref[:, channels * (TAPS - 1) :], corner_shift(corner, spacing))
    for j in range(4):
        rows = range(4 * j, 4 * (j + 1))
        stack = jnp.concatenate([taps_of(rolled_ref, spacing, r) for r in rows], 1)
        response = dot(flat_ref[...], stack)
        for m, r in enumerate(rows):
            row = response[:, LANES * m : LANES * (m + 1)]
            if r >= HALO:
                at = LANES - HALO
                row = row + jnp.where(lane >= at, turn(share, at - HALO * (r - HALO)), 0.0)
            near = pair_ref[r].astype(F32)
            far = turn(pair_ref[r + 16].astype(F32), 2 * TILE)
            row = jnp.where(low, near, far) + row
            rows_ref[channels * j : channels * (j + 1), LANES * m : LANES * (m + 1)] = row.astype(
                BF16
            )
    slot = meta_ref[GROUPS]
    chunks = dot(rows_ref[...], spread_table(4), NT)
    for j in range(4):
        chunk = chunks[channels * j : channels * (j + 1)]
        for h in range(2):
            at = slice(LANES * (j + 4 * h), LANES * (j + 4 * h + 1))
            to = 2 * LANES * h
            out_ref[slot, :, at] = chunk[:, to : to + LANES].astype(BF16)
            out_ref[1 - slot, :, at] = (chunk[:, to + LANES : to + 2 * LANES] * keep).astype(BF16)


def adjoint(
    meta_ref, weight_ref, own_ref, g_ref, core_ref, chip_ref, tail_ref, both_ref, pair_ref,
    spread_ref,
    rolled_ref, dense_ref,
    grad_ref, local_ref, sum_ref, part_ref, above_ref, below_ref,
):
    channels = g_ref.shape[1]
    width = channels // GROUPS
    span = 3 * channels
    lane = lane_ids(channels)
    zeros = jnp.zeros((channels, LANES), BF16)
    above = from_above(core_ref, chip_ref, slice(0, RIM_EMBED))
    below = from_below(core_ref, chip_ref, slice(0, RIM_EMBED))

    def moved(rim, at, to, size, per, i):
        at += LANES * (i // per)
        x = turn(rim[:, at : at + LANES], to - size * (i % per))
        return jnp.where(within(lane, to, to + size), x, 0.0)

    for h in range(HALO // 2):
        upper, lower = [], []
        for i in (2 * h, 2 * h + 1):
            x = moved(above, 0, 0, TILE, 4, i)
            x = x + moved(above, RIM_CORNER, LANES - HALO, HALO, 16, i)
            upper.append(jnp.concatenate([x.astype(BF16), zeros], 0))
            x = moved(below, 0, TILE, TILE, 4, i)
            x = x + moved(below, RIM_CORNER, 2 * TILE, HALO, 16, i)
            y = moved(below, RIM_SIDE, 80, TILE, 4, i).astype(BF16) + tail_ref[i]
            lower.append(jnp.concatenate([x.astype(BF16), y], 0))
        x = dot(both_ref[2 * span :, :], jnp.concatenate(upper, 1))
        y = dot(both_ref[:span, :], jnp.concatenate(lower, 1))
        for m in range(2):
            above_ref[2 * h + m] = x[:, LANES * m : LANES * (m + 1)]
            below_ref[2 * h + m] = y[:, LANES * m : LANES * (m + 1)]
    spacing = [meta_ref[g] for g in range(GROUPS)]
    second = within(lane, TILE, 2 * TILE)

    def gathered(r):
        pieces = []
        for g in range(GROUPS):
            totals = []
            up, down = r - spacing[g], r + spacing[g]
            for v in range(3):
                at = channels * v + width * g
                tap = slice(at, at + width)
                total = spread_ref[r, span + at : span + at + width, :]
                last = slice(2 * span + at, 2 * span + at + width)
                if r < HALO:
                    x = spread_ref[jnp.maximum(up, 0), last, :]
                    y = above_ref[jnp.minimum(up + HALO, HALO - 1), tap, :]
                    total = total + jnp.where(up < 0, y, x)
                else:
                    total = total + spread_ref[up, last, :]
                if r >= TILE - HALO:
                    x = spread_ref[jnp.minimum(down, TILE - 1), tap, :]
                    y = below_ref[jnp.maximum(down - TILE, 0), tap, :]
                    total = total + jnp.where(down >= TILE, y, x)
                else:
                    total = total + spread_ref[down, tap, :]
                totals.append(total)
            pieces.append(
                totals[1]
                + pltpu.roll(totals[0], LANES - spacing[g], 1)
                + pltpu.roll(totals[2], spacing[g], 1)
            )
        grad = jnp.concatenate(pieces, 0)
        grad = grad + jnp.where(second, turn(grad, -48), 0.0)
        own = g_ref[r].astype(F32)
        own = own + jnp.where(pair_ref[r].astype(F32) > 0, grad, 0.0)
        return jnp.where(lane < 2 * TILE, own, 0.0).astype(BF16)

    weight = weight_ref[...].astype(F32)
    own = own_ref[...].astype(F32)
    after = unpacked(from_below(core_ref, chip_ref, slice(RIM_EMBED, RIM)))
    columns = jnp.concatenate(
        [own, after, jnp.zeros((LANES - 2 * TILE, own.shape[1]), F32)], 0
    ).astype(BF16)
    weight_part = jnp.zeros_like(weight)
    local = []
    kernel_part = None
    for c in range(TILE // 8):
        share = kernel_share(meta_ref, rolled_ref, dense_ref, range(4 * c, 4 * (c + 1)))
        kernel_part = share if c == 0 else kernel_part + share
        rows = jnp.concatenate([gathered(8 * c + i) for i in range(8)], 0)
        grad_ref[8 * channels * c : 8 * channels * (c + 1), :] = rows
        grad_scaled = dot(rows, columns)
        for i in range(8):
            one = grad_scaled[channels * i : channels * (i + 1)]
            local.append(jnp.sum(one * weight, 0, keepdims=True))
            weight_part = weight_part + one * own[8 * c + i : 8 * c + i + 1, :]
    local_ref[...] = jnp.concatenate(local, 0)
    sum_ref[...] = weight_part
    part_ref[...] = kernel_part


def deliver(
    meta_ref, core_ref, chip_ref, part_ref, pair_ref,
    keep_ref, send_ref, corner_ref, sum_ref, kernel_ref,
):
    channels = part_ref.shape[0]
    lane = lane_ids(channels)
    rim = from_above(core_ref, chip_ref, slice(0, RIM_SIDE))
    corner, ends = None, None
    for i in range(HALO):
        x = jnp.where(within(lane, TILE, TILE + HALO), pair_ref[i].astype(F32), 0.0)
        x = turn(jnp.maximum(x, 0.0), HALO * i - TILE)
        half = LANES * (i // 4)
        y = turn(rim[:, half : half + LANES], HALO * i - TILE * (i % 4) - (TILE - HALO))
        y = jnp.where(within(lane, HALO * i, HALO * (i + 1)), y, 0.0)
        corner, ends = (x, y) if i == 0 else (corner + x, ends + y)
    spacing = [meta_ref[g] for g in range(GROUPS)]
    share = dot(ends.astype(BF16), corner_shift(corner, spacing), NT)
    last = channels * (TAPS - 1)
    kernel_ref[:, :last] = part_ref[:, :last]
    kernel_ref[:, last:] = part_ref[:, last:] + share
    quarter = channels // 4
    corner = [corner[quarter * q : quarter * (q + 1)] for q in range(4)]
    corner = jnp.concatenate(
        [corner[0] + turn(corner[1], 64), corner[2] + turn(corner[3], 64)], 1
    )
    corner_ref[...] = corner
    rows = channels // 2
    half = half_of(lax.axis_index("blk"))
    send_ref[:quarter] = corner
    for ref, which, first in ((keep_ref, half, 0), (send_ref, 1 - half, quarter)):
        at = pl.multiple_of(rows * which, rows)
        ref[first : first + rows] = sum_ref[pl.ds(at, rows), :]
        for q in range(2):
            to = first + rows * (q + 1)
            ref[to : to + rows] = kernel_ref[pl.ds(at, rows), 256 * q : 256 * (q + 1)]
        ref[first + 3 * rows :] = jnp.concatenate(
            [kernel_ref[pl.ds(at + 8 * q, 8), 512:] for q in range(4)], 1
        )


def middle(
    meta_ref, weight_ref, own_ref, chip_ref, core_ref, dense_ref, scaled_ref, g_ref, tail_ref,
    both_ref, spread_ref,
    keep_ref, send_ref, corner_ref, local_ref, grad_ref, pair_ref, rolled_ref,
    map_ref, part_ref, above_ref, below_ref, sum_ref, kernel_ref,
):
    forward(
        meta_ref, weight_ref, own_ref, chip_ref, core_ref, dense_ref, scaled_ref,
        pair_ref, rolled_ref, map_ref,
    )
    adjoint(
        meta_ref, weight_ref, own_ref, g_ref, core_ref, chip_ref, tail_ref, both_ref, pair_ref,
        spread_ref,
        rolled_ref, dense_ref,
        grad_ref, local_ref, sum_ref, part_ref, above_ref, below_ref,
    )
    deliver(
        meta_ref, core_ref, chip_ref, part_ref, pair_ref,
        keep_ref, send_ref, corner_ref, sum_ref, kernel_ref,
    )


def embed_terms(grad_ref, scaled_ref, local_ref, corner_ref, near_ref, far_ref, side_ref):
    both = dot(grad_ref[...], scaled_ref[...], TN)
    far = both[TILE : 2 * TILE]
    near_ref[...] = local_ref[...] + both[:TILE]
    far_ref[...] = far
    side_ref[:TILE] = far.astype(BF16)
    side_ref[TILE:] = corner_ref[...].astype(BF16)


def finish(
    mine_ref, other_ref, chip_ref, near_ref,
    weight_ref, kernel_ref, embed_ref,
):
    index, even, before, _ = place()
    channels = kernel_ref.shape[1]
    rows = channels // 2
    half = half_of(index)
    for ref, which in ((mine_ref, half), (other_ref, 1 - half)):
        at = pl.multiple_of(rows * which, rows)
        weight_ref[pl.ds(at, rows), :] = ref[:rows]
        for t in range(TAPS - 1):
            first = rows * (1 + t // 4)
            to = channels * (t % 4)
            kernel_ref[t, pl.ds(at, rows), :] = ref[first : first + rows, to : to + channels]
        for q in range(4):
            kernel_ref[TAPS - 1, pl.ds(at + 8 * q, 8), :] = ref[
                3 * rows : 3 * rows + 8, channels * q : channels * (q + 1)
            ]
    carried = other_ref[3 * rows + 8 :] * (1.0 - even)
    carried = carried + chip_ref[...].astype(F32) * (even * before)
    embed_ref[...] = near_ref[...] + carried


VMEM = pl.BlockSpec(memory_space=pltpu.VMEM)
SMEM = pl.BlockSpec(memory_space=pltpu.SMEM)
HBM = pl.BlockSpec(memory_space=pltpu.HBM)


def shape(dims, kind):
    return jax.ShapeDtypeStruct(dims, kind)


def call(kernel, outs, scalars, operands, scratch=(), flops=0, moved=0, first=None, room=32):
    specs = [first or SMEM] * scalars + [VMEM] * (len(operands) - scalars)
    return pl.pallas_call(
        kernel,
        out_shape=outs,
        in_specs=specs,
        out_specs=[SMEM if out.dtype == jnp.int32 else VMEM for out in outs],
        scratch_shapes=list(scratch),
        compiler_params=pltpu.CompilerParams(vmem_limit_bytes=room * 1024 * 1024),
        cost_estimate=pl.CostEstimate(flops=flops, bytes_accessed=moved, transcendentals=0),
    )(*operands)


def swap_with(shard, step):
    return lax.ppermute(shard, "blk", [(i, i ^ step) for i in range(lax.axis_size("blk"))])


def swap_stage(shard, first, second):
    pairs = [(i, i ^ (second if half_of(i) else first)) for i in range(lax.axis_size("blk"))]
    return lax.ppermute(shard, "blk", pairs)


def swap_chips(shard):
    count = lax.axis_size("blk")
    pairs = [(i, (i + (1 if i % 2 else -1)) % count) for i in range(count)]
    return lax.ppermute(shard, "blk", pairs)


def per_device(embed, pair_weight, conv_kernel, dilations, tile_order, cotangent):
    features = embed.shape[1]
    channels = conv_kernel.shape[0]
    count = lax.axis_size("blk")
    weight = pair_weight.T
    taps = jnp.transpose(conv_kernel, (1, 0, 2))
    cot = cotangent.reshape(2, channels, TILE * TILE)
    packed = shape((channels, RIM), BF16)
    body = shape((TILE, channels, LANES), BF16)
    to_chip, to_core = call(
        pack,
        [packed, packed],
        3,
        (tile_order, cot, embed),
        [
            pltpu.SMEM(tile_order.shape, jnp.int32),
            pltpu.VMEM(cot.shape, BF16),
            pltpu.VMEM(embed.shape, BF16),
            pltpu.SemaphoreType.DMA((3,)),
        ],
        flops=10**10,
        moved=10**6,
        first=HBM,
        room=60,
    )
    chip = swap_chips(to_chip)
    core = swap_with(to_core, 1)
    grads, dense, tail, flat, both, scaled, spread, meta = call(
        prepare,
        [
            body,
            shape((TILE // 2, channels, LANES), BF16),
            shape((HALO, channels, LANES), BF16),
            shape((channels, TAPS * channels), BF16),
            shape((TAPS * channels, 2 * channels), BF16),
            shape((TILE * channels, features), BF16),
            shape((TILE, TAPS * channels, LANES), F32),
            shape((2 * GROUPS,), jnp.int32),
        ],
        2,
        (tile_order, dilations, cot, taps, weight, embed),
        flops=2 * 10**8,
        moved=3 * 10**6,
    )
    rows = channels // 2
    sums = 3 * rows + rows * channels // features
    total, send, corner, local, grad_pair, pair, rolled = call(
        middle,
        [
            shape((sums, features), F32),
            shape((channels // 4 + sums, features), F32),
            shape((channels // 4, features), F32),
            shape((TILE, features), F32),
            shape((TILE * channels, LANES), BF16),
            body,
            shape((TILE, 3 * channels, LANES), BF16),
        ],
        1,
        (meta, weight, embed, chip, core, dense, scaled, grads, tail, both, spread),
        [
            pltpu.VMEM((TILE + 2 * HALO, channels, LANES), BF16),
            pltpu.VMEM((channels, TAPS * channels), F32),
            pltpu.VMEM((HALO, 3 * channels, LANES), F32),
            pltpu.VMEM((HALO, 3 * channels, LANES), F32),
            pltpu.VMEM((channels, features), F32),
            pltpu.VMEM((channels, TAPS * channels), F32),
        ],
        flops=2 * 10**9,
        moved=8 * 10**6,
        room=24,
    )
    by_core = swap_with(send, 1)
    near, far, sided = call(
        embed_terms,
        [
            shape((TILE, features), F32),
            shape((TILE, features), F32),
            shape((TILE + channels // 4, features), BF16),
        ],
        0,
        (grad_pair, scaled, local, corner),
        flops=2 * 10**8,
        moved=2 * 10**6,
    )
    by_chip = swap_chips(sided)
    by_core, sided = lax.optimization_barrier((by_core, sided))
    total = total + by_core[channels // 4 :]
    by_core = by_core[: channels // 4]
    steps = [1 | 1 << b for b in range(1, count.bit_length() - 1)]
    turns = list(zip(steps, steps[1:] + steps[:1]))
    for first, second in turns[:-1]:
        total = total + swap_stage(total, first, second)
    rolled, total, by_chip = lax.optimization_barrier((rolled, total, by_chip))
    last = swap_stage(total, *turns[-1])
    (out,) = call(
        respond,
        [shape((2, channels, TILE * TILE), BF16)],
        1,
        (meta, flat, rolled, pair, by_core, by_chip[TILE:]),
        [pltpu.VMEM((4 * channels, 4 * LANES), BF16)],
        flops=2 * 10**8,
        moved=2 * 10**6,
    )
    out, last = lax.optimization_barrier((out, last))
    total = total + last
    rest = swap_with(jnp.concatenate([total, far]), 1)
    grad_weight, grad_kernel, grad_embed = call(
        finish,
        [
            shape((channels, features), F32),
            shape((TAPS, channels, channels), F32),
            shape((TILE, features), F32),
        ],
        0,
        (total, rest, by_chip[:TILE], near),
        moved=10**6,
    )
    return (
        out.reshape(1, 2, channels, TILE * TILE),
        grad_embed,
        grad_weight.T,
        jnp.transpose(grad_kernel, (1, 0, 2)),
    )


def solution(mesh):
    placed = (
        P(("grp", "blk"), None),
        P(),
        P(),
        P(),
        P(("grp", "blk"), None),
        P(("grp", "blk"), None, None, None),
    )
    return jax.shard_map(
        per_device,
        mesh=mesh,
        in_specs=placed,
        out_specs=(
            P(("grp", "blk"), None, None, None),
            P(("grp", "blk"), None),
            P("grp", None),
            P("grp", None, None),
        ),
        check_vma=False,
    )
```

```python
import jax
import jax.numpy as jnp
from jax import lax
from jax.experimental import pallas as pl
from jax.experimental.pallas import tpu as pltpu
from jax.sharding import PartitionSpec as P

GROUPS = 4
HALO = 8
TILE = 32
LANES = 128
TAPS = 9
F32 = jnp.float32
BF16 = jnp.bfloat16
NN = (((1,), (0,)), ((), ()))
NT = (((1,), (1,)), ((), ()))
TN = (((0,), (0,)), ((), ()))


def dot(a, b, dims=NN):
    return lax.dot_general(a, b, dims, preferred_element_type=F32)


def turn(x, by):
    by = by % LANES
    return x if by == 0 else pltpu.roll(x, by, 1)


def lane_ids(rows):
    return lax.broadcasted_iota(jnp.int32, (rows, LANES), 1)


def within(lane, low, high):
    return jnp.logical_and(lane >= low, lane < high)


def one_hot(target, chunks):
    lane = lane_ids(target.shape[0])
    hits = [jnp.where(target == lane + LANES * c, 1.0, 0.0).astype(BF16) for c in range(chunks)]
    return jnp.concatenate(hits, 1)


def row_ids(rows):
    return lax.broadcasted_iota(jnp.int32, (rows, LANES), 0)


def spread_table(chunks):
    x = row_ids(LANES * chunks)
    return one_hot((((x >> 5) & 3) << 7) + ((x >> 7) << 5) + (x & 31), 4)


def swap_table():
    x = row_ids(HALO * TILE)
    return one_hot(((x & 31) << 3) + (x >> 5), 2)


def edge_table():
    x = row_ids(LANES)
    return one_hot(jnp.where((x & 31) < HALO, ((x & 31) << 5) + (x >> 5), -1), 2)


def corner_table(first):
    x = row_ids(HALO * TILE)
    c = (x & 31) - first
    return one_hot(jnp.where(within(c, 0, HALO), ((x >> 5) << 3) + c, -1), 1)


def as_float(flag):
    return jnp.where(flag, 1.0, 0.0).astype(F32)


def place():
    index = lax.axis_index("blk")
    last = lax.axis_size("blk") - 1
    return index, as_float(index % 2 == 0), as_float(index > 0), as_float(index < last)


def half_of(index):
    for by in (8, 4, 2, 1):
        index = index ^ (index >> by)
    return index & 1


def corner_shift(flat, spacing):
    width = flat.shape[0] // GROUPS
    lane = lane_ids(width)
    pieces = []
    for g in range(GROUPS):
        d = spacing[g]
        kept = jnp.logical_and(jnp.logical_and(lane < 8 * HALO, (lane >> 3) < d), (lane & 7) < d)
        x = jnp.where(kept, flat[width * g : width * (g + 1)], 0.0)
        pieces.append(pltpu.roll(x, (HALO + 1) * (HALO - d), 1))
    return jnp.concatenate(pieces, 0).astype(BF16)


def tiles_of(order_ref, cot_ref):
    slot = order_ref[0, 0]
    _, _, _, keep = place()
    return cot_ref[slot], (cot_ref[1 - slot].astype(F32) * keep).astype(BF16)


def fetch(sources, targets, sems):
    copies = [
        pltpu.make_async_copy(source, target, sems.at[i])
        for i, (source, target) in enumerate(zip(sources, targets))
    ]
    for copy in copies:
        copy.start()
    return copies


def pack(
    order_hbm, cot_hbm, embed_hbm,
    chip_ref, core_ref,
    order_ref, cot_ref, embed_ref, sems,
):
    copies = fetch((order_hbm, cot_hbm, embed_hbm), (order_ref, cot_ref, embed_ref), sems)
    edge, head, tail = edge_table(), corner_table(0), corner_table(TILE - HALO)
    for copy in copies:
        copy.wait()
    zero, one = tiles_of(order_ref, cot_ref)
    _, even, _, _ = place()
    channels = zero.shape[0]
    moved = dot(
        jnp.concatenate([zero[:, LANES * j : LANES * (j + 1)] for j in range(8)], 0), edge
    )
    columns = []
    for h in range(2):
        total = None
        for j in range(8):
            piece = moved[channels * j : channels * (j + 1), LANES * h : LANES * (h + 1)]
            piece = turn(piece, 4 * j)
            total = piece if total is None else total + piece
        columns.append(total)
    rim = HALO * TILE
    tail_at = TILE * (TILE - HALO)
    up = [zero[:, :rim].astype(F32)] + columns + [dot(one[:, :rim], head)]
    down = [one[:, tail_at:].astype(F32)] + [jnp.zeros_like(x) for x in columns]
    down += [dot(zero[:, tail_at:], tail)]
    up, down = jnp.concatenate(up, 1), jnp.concatenate(down, 1)
    width = up.shape[1]
    both = jnp.concatenate([embed_ref[:, :LANES], embed_ref[:, LANES:]], 0)
    core_ref[:, :width] = (down * even + up * (1.0 - even)).astype(BF16)
    core_ref[:, width:] = both
    chip_ref[:, :width] = (up * even + down * (1.0 - even)).astype(BF16)
    chip_ref[:, width:] = both


RIM_SIDE, RIM_CORNER, RIM_EMBED, RIM = 256, 512, 640, 768


def from_above(core_ref, chip_ref, at):
    _, even, before, _ = place()
    x = chip_ref[:, at].astype(F32) * (even * before)
    return x + core_ref[:, at].astype(F32) * ((1.0 - even) * before)


def from_below(core_ref, chip_ref, at):
    _, even, _, after = place()
    x = core_ref[:, at].astype(F32) * (even * after)
    return x + chip_ref[:, at].astype(F32) * ((1.0 - even) * after)


def prepare(
    order_ref, dil_ref, cot_ref, kern_ref, weight_ref, embed_ref,
    g_ref, dense_ref, tail_ref, flat_ref, both_ref, scaled_ref, spread_ref, meta_ref,
):
    for g in range(GROUPS):
        meta_ref[g] = jnp.left_shift(jnp.int32(1), dil_ref[g])
    meta_ref[GROUPS] = order_ref[0, 0]
    zero, one = tiles_of(order_ref, cot_ref)
    channels = kern_ref.shape[1]
    swap = swap_table()
    tail_at = TILE * (TILE - HALO)
    y_zero = dot(zero[:, tail_at:], swap)
    y_one = dot(one[:, tail_at:], swap)
    lane = lane_ids(channels)
    own_side = within(lane, 72, 80)
    low = lane < 2 * TILE
    pieces = []
    for j in range(4):
        at = slice(LANES * j, LANES * (j + 1))
        later = slice(LANES * (j + 4), LANES * (j + 5))
        pieces.append(
            jnp.concatenate([zero[:, at], one[:, at], zero[:, later], one[:, later]], 1)
        )
    rows = dot(jnp.concatenate(pieces, 0), spread_table(4))
    for j in range(4):
        for m in range(4):
            row = rows[channels * j : channels * (j + 1), LANES * m : LANES * (m + 1)]
            dense_ref[4 * j + m] = row.astype(BF16)
            for h in range(2):
                r = 16 * h + 4 * j + m
                side = turn(y_zero[:, LANES * h : LANES * (h + 1)], 72 - 8 * (r % 16))
                side = jnp.where(own_side, side, 0.0)
                g_ref[r] = jnp.where(low, turn(row, 64 * h), side).astype(BF16)
    for i in range(HALO):
        rest = turn(y_one[:, :LANES], 72 - 8 * i)
        tail_ref[i] = jnp.where(own_side, rest, 0.0).astype(BF16)
    eye = (
        lax.broadcasted_iota(jnp.int32, (channels, channels), 0)
        == lax.broadcasted_iota(jnp.int32, (channels, channels), 1)
    )
    eye = jnp.where(eye, 1.0, 0.0).astype(BF16)
    for u in range(3):
        for v in range(3):
            t = 3 * u + v
            pair = jnp.concatenate([kern_ref[t], kern_ref[3 * v + u]], 0)
            both_ref[channels * t : channels * (t + 1), :] = dot(eye, pair, NT).astype(BF16)
    for t in range(0, TAPS - 1, 2):
        flat_ref[:, channels * t : channels * (t + 2)] = jnp.concatenate(
            [kern_ref[t].astype(F32), kern_ref[t + 1].astype(F32)], 1
        ).astype(BF16)
    flat_ref[:, channels * (TAPS - 1) : channels * TAPS] = kern_ref[TAPS - 1]
    weight = weight_ref[...].astype(F32)
    own = embed_ref[...].astype(F32)
    for r in range(TILE):
        scaled_ref[channels * r : channels * (r + 1), :] = (own[r : r + 1, :] * weight).astype(
            BF16
        )
    inner = jnp.where(lane < 2 * TILE, 1.0, 0.0).astype(BF16)
    beside = jnp.where(own_side, 1.0, 0.0).astype(BF16)

    def spread_rows(i, carry):
        x = jnp.concatenate([g_ref[2 * i], g_ref[2 * i + 1]], 1)
        y = jnp.concatenate([inner, inner], 1), jnp.concatenate([beside, beside], 1)
        y = dot(both_ref[...], jnp.concatenate([x * y[0], x * y[1]], 0))
        spread_ref[2 * i] = y[:, :LANES]
        spread_ref[2 * i + 1] = y[:, LANES:]
        return carry

    lax.fori_loop(0, TILE // 2, spread_rows, 0, unroll=4)


def unpacked(x):
    return jnp.concatenate([x[:TILE], x[TILE:]], 1)


def forward(
    meta_ref, weight_ref, own_ref, chip_ref, core_ref, dense_ref, scaled_ref,
    part_ref, pair_ref, rolled_ref, map_ref,
):
    channels = weight_ref.shape[0]
    width = channels // GROUPS
    weight = weight_ref[...].astype(F32)
    own = own_ref[...].astype(F32)
    after = unpacked(from_below(core_ref, chip_ref, slice(RIM_EMBED, RIM)))
    before = unpacked(from_above(core_ref, chip_ref, slice(RIM_EMBED, RIM)))[TILE - HALO :]
    filler = jnp.zeros((LANES - 2 * TILE - HALO, own.shape[1]), F32)
    columns = jnp.concatenate([own, after, filler, before], 0).astype(BF16)
    lane = lane_ids(channels)
    kept = (
        jnp.logical_or(lane < TILE, lane >= LANES - HALO),
        lane < 2 * TILE,
        within(lane, TILE, 2 * TILE),
    )
    for c in range(6):
        part = 0 if c == 0 else (2 if c == 5 else 1)
        if part == 1:
            scaled = scaled_ref[8 * channels * (c - 1) : 8 * channels * c, :]
        else:
            rim = before if part == 0 else after
            scaled = jnp.concatenate(
                [(rim[i : i + 1, :] * weight).astype(BF16) for i in range(HALO)], 0
            )
        pair = dot(scaled, columns, NT).astype(BF16)
        for i in range(8):
            one = pair[channels * i : channels * (i + 1)]
            if part == 1:
                pair_ref[8 * (c - 1) + i] = one
            x = jnp.where(kept[part], jnp.maximum(one.astype(F32), 0.0), 0.0)
            map_ref[8 * c + i] = x.astype(BF16)
    swap = swap_table()

    def gathered(first, per, low, high, move):
        halves = []
        for half in range(2):
            total = None
            for m in range(per):
                piece = map_ref[first + per * half + m].astype(F32)
                piece = jnp.where(within(lane, low, high), piece, 0.0)
                piece = turn(piece, move(m))
                total = piece if total is None else total + piece
            halves.append(total.astype(BF16))
        return jnp.concatenate(halves, 1)

    above = dot(gathered(0, 4, 0, TILE, lambda m: TILE * m), swap)
    below = dot(gathered(8, 16, TILE, TILE + HALO, lambda m: HALO * m - TILE), swap, NT)
    for r in range(TILE):
        half = LANES * (r // 16)
        side = turn(above[:, half : half + LANES], LANES - HALO - HALO * (r % 16))
        map_ref[HALO + r] += jnp.where(lane >= LANES - HALO, side, 0.0).astype(BF16)
    for i in range(HALO):
        half = LANES * (i // 4)
        side = turn(below[:, half : half + LANES], -TILE * (i % 4))
        map_ref[HALO + TILE + i] += jnp.where(lane < TILE, side, 0.0).astype(BF16)

    spacing = [meta_ref[g] for g in range(GROUPS)]
    source = row_ids(LANES)
    to = lane_ids(LANES)
    for g in range(GROUPS):
        tables = []
        for h in range(2):
            half = within(to, 2 * TILE * h, 2 * TILE * (h + 1))
            offset = jnp.where(half, (source - (to - 2 * TILE * h)) & (LANES - 1), LANES)
            hits = [
                jnp.where(offset == (v * spacing[g]) & (LANES - 1), 1.0, 0.0).astype(BF16)
                for v in (-1, 0, 1)
            ]
            tables.append(jnp.concatenate(hits, 1))
        table = jnp.concatenate(tables, 0)
        at = width * g
        for part in range(2):
            low = [map_ref[16 * part + i, at : at + width, :] for i in range(16)]
            high = [map_ref[16 * part + i + 16, at : at + width, :] for i in range(16)]
            x = jnp.concatenate([jnp.concatenate(low, 0), jnp.concatenate(high, 0)], 1)
            y = dot(x, table).astype(BF16)
            for i in range(16):
                for v in range(3):
                    to_row = channels * v + at
                    rolled_ref[16 * part + i, to_row : to_row + width, :] = y[
                        width * i : width * (i + 1), LANES * v : LANES * (v + 1)
                    ]
    total = None
    for j in range(4):
        rows = range(4 * j, 4 * (j + 1))
        stack = jnp.concatenate([taps_of(rolled_ref, spacing, r) for r in rows], 1)
        share = dot(jnp.concatenate([dense_ref[r] for r in rows], 1), stack, NT)
        total = share if total is None else total + share
    part_ref[...] = total


def taps_of(rolled_ref, spacing, r):
    channels = rolled_ref.shape[1] // 3
    width = channels // GROUPS
    pieces = []
    for u in range(3):
        for v in range(3):
            for g in range(GROUPS):
                at = channels * v + width * g
                pieces.append(rolled_ref[r + HALO + (u - 1) * spacing[g], at : at + width, :])
    return jnp.concatenate(pieces, 0)


def respond(
    meta_ref, flat_ref, rolled_ref, pair_ref, core_ref, chip_ref,
    out_ref,
    rows_ref,
):
    channels = flat_ref.shape[0]
    spacing = [meta_ref[g] for g in range(GROUPS)]
    lane = lane_ids(channels)
    low = lane < 2 * TILE
    _, even, _, keep = place()
    corner = core_ref[...] * even + chip_ref[...].astype(F32) * ((1.0 - even) * keep)
    low_side, high_side = corner[:, :LANES], corner[:, LANES:]
    corner = jnp.concatenate(
        [low_side, turn(low_side, 64), high_side, turn(high_side, 64)], 0
    )
    share = dot(flat_ref[:, channels * (TAPS - 1) :], corner_shift(corner, spacing))
    for j in range(4):
        rows = range(4 * j, 4 * (j + 1))
        stack = jnp.concatenate([taps_of(rolled_ref, spacing, r) for r in rows], 1)
        response = dot(flat_ref[...], stack)
        for m, r in enumerate(rows):
            row = response[:, LANES * m : LANES * (m + 1)]
            if r >= HALO:
                at = LANES - HALO
                row = row + jnp.where(lane >= at, turn(share, at - HALO * (r - HALO)), 0.0)
            near = pair_ref[r].astype(F32)
            far = turn(pair_ref[r + 16].astype(F32), 2 * TILE)
            row = jnp.where(low, near, far) + row
            rows_ref[channels * j : channels * (j + 1), LANES * m : LANES * (m + 1)] = row.astype(
                BF16
            )
    slot = meta_ref[GROUPS]
    chunks = dot(rows_ref[...], spread_table(4), NT)
    for j in range(4):
        chunk = chunks[channels * j : channels * (j + 1)]
        for h in range(2):
            at = slice(LANES * (j + 4 * h), LANES * (j + 4 * h + 1))
            to = 2 * LANES * h
            out_ref[slot, :, at] = chunk[:, to : to + LANES].astype(BF16)
            out_ref[1 - slot, :, at] = (chunk[:, to + LANES : to + 2 * LANES] * keep).astype(BF16)


def adjoint(
    meta_ref, weight_ref, own_ref, g_ref, core_ref, chip_ref, tail_ref, both_ref, pair_ref,
    spread_ref,
    grad_ref, local_ref, sum_ref, above_ref, below_ref,
):
    channels = g_ref.shape[1]
    width = channels // GROUPS
    span = 3 * channels
    lane = lane_ids(channels)
    zeros = jnp.zeros((channels, LANES), BF16)
    above = from_above(core_ref, chip_ref, slice(0, RIM_EMBED))
    below = from_below(core_ref, chip_ref, slice(0, RIM_EMBED))

    def moved(rim, at, to, size, per, i):
        at += LANES * (i // per)
        x = turn(rim[:, at : at + LANES], to - size * (i % per))
        return jnp.where(within(lane, to, to + size), x, 0.0)

    for h in range(HALO // 2):
        upper, lower = [], []
        for i in (2 * h, 2 * h + 1):
            x = moved(above, 0, 0, TILE, 4, i)
            x = x + moved(above, RIM_CORNER, LANES - HALO, HALO, 16, i)
            upper.append(jnp.concatenate([x.astype(BF16), zeros], 0))
            x = moved(below, 0, TILE, TILE, 4, i)
            x = x + moved(below, RIM_CORNER, 2 * TILE, HALO, 16, i)
            y = moved(below, RIM_SIDE, 80, TILE, 4, i).astype(BF16) + tail_ref[i]
            lower.append(jnp.concatenate([x.astype(BF16), y], 0))
        x = dot(both_ref[2 * span :, :], jnp.concatenate(upper, 1))
        y = dot(both_ref[:span, :], jnp.concatenate(lower, 1))
        for m in range(2):
            above_ref[2 * h + m] = x[:, LANES * m : LANES * (m + 1)]
            below_ref[2 * h + m] = y[:, LANES * m : LANES * (m + 1)]
    spacing = [meta_ref[g] for g in range(GROUPS)]
    second = within(lane, TILE, 2 * TILE)

    def gathered(r):
        pieces = []
        for g in range(GROUPS):
            totals = []
            up, down = r - spacing[g], r + spacing[g]
            for v in range(3):
                at = channels * v + width * g
                tap = slice(at, at + width)
                total = spread_ref[r, span + at : span + at + width, :]
                last = slice(2 * span + at, 2 * span + at + width)
                if r < HALO:
                    x = spread_ref[jnp.maximum(up, 0), last, :]
                    y = above_ref[jnp.minimum(up + HALO, HALO - 1), tap, :]
                    total = total + jnp.where(up < 0, y, x)
                else:
                    total = total + spread_ref[up, last, :]
                if r >= TILE - HALO:
                    x = spread_ref[jnp.minimum(down, TILE - 1), tap, :]
                    y = below_ref[jnp.maximum(down - TILE, 0), tap, :]
                    total = total + jnp.where(down >= TILE, y, x)
                else:
                    total = total + spread_ref[down, tap, :]
                totals.append(total)
            pieces.append(
                totals[1]
                + pltpu.roll(totals[0], LANES - spacing[g], 1)
                + pltpu.roll(totals[2], spacing[g], 1)
            )
        grad = jnp.concatenate(pieces, 0)
        grad = grad + jnp.where(second, turn(grad, -48), 0.0)
        own = g_ref[r].astype(F32)
        own = own + jnp.where(pair_ref[r].astype(F32) > 0, grad, 0.0)
        return own.astype(BF16)

    weight = weight_ref[...].astype(F32)
    own = own_ref[...].astype(F32)
    after = unpacked(from_below(core_ref, chip_ref, slice(RIM_EMBED, RIM)))
    columns = jnp.concatenate(
        [own, after, jnp.zeros((LANES - 2 * TILE, own.shape[1]), F32)], 0
    ).astype(BF16)
    weight_part = jnp.zeros_like(weight)
    local = []
    for c in range(TILE // 8):
        rows = jnp.concatenate([gathered(8 * c + i) for i in range(8)], 0)
        grad_ref[8 * channels * c : 8 * channels * (c + 1), :] = rows
        grad_scaled = dot(rows, columns)
        for i in range(8):
            one = grad_scaled[channels * i : channels * (i + 1)]
            local.append(jnp.sum(one * weight, 0, keepdims=True))
            weight_part = weight_part + one * own[8 * c + i : 8 * c + i + 1, :]
    local_ref[...] = jnp.concatenate(local, 0)
    sum_ref[...] = weight_part


def deliver(
    meta_ref, core_ref, chip_ref, part_ref, pair_ref,
    keep_ref, send_ref, corner_ref, sum_ref, kernel_ref,
):
    channels = part_ref.shape[0]
    lane = lane_ids(channels)
    rim = from_above(core_ref, chip_ref, slice(0, RIM_SIDE))
    corner, ends = None, None
    for i in range(HALO):
        x = jnp.where(within(lane, TILE, TILE + HALO), pair_ref[i].astype(F32), 0.0)
        x = turn(jnp.maximum(x, 0.0), HALO * i - TILE)
        half = LANES * (i // 4)
        y = turn(rim[:, half : half + LANES], HALO * i - TILE * (i % 4) - (TILE - HALO))
        y = jnp.where(within(lane, HALO * i, HALO * (i + 1)), y, 0.0)
        corner, ends = (x, y) if i == 0 else (corner + x, ends + y)
    spacing = [meta_ref[g] for g in range(GROUPS)]
    share = dot(ends.astype(BF16), corner_shift(corner, spacing), NT)
    last = channels * (TAPS - 1)
    kernel_ref[:, :last] = part_ref[:, :last]
    kernel_ref[:, last:] = part_ref[:, last:] + share
    quarter = channels // 4
    corner = [corner[quarter * q : quarter * (q + 1)] for q in range(4)]
    corner = jnp.concatenate(
        [corner[0] + turn(corner[1], 64), corner[2] + turn(corner[3], 64)], 1
    )
    corner_ref[...] = corner
    rows = channels // 2
    half = half_of(lax.axis_index("blk"))
    send_ref[:quarter] = corner
    for ref, which, first in ((keep_ref, half, 0), (send_ref, 1 - half, quarter)):
        at = pl.multiple_of(rows * which, rows)
        ref[first : first + rows] = sum_ref[pl.ds(at, rows), :]
        for q in range(2):
            to = first + rows * (q + 1)
            ref[to : to + rows] = kernel_ref[pl.ds(at, rows), 256 * q : 256 * (q + 1)]
        ref[first + 3 * rows :] = jnp.concatenate(
            [kernel_ref[pl.ds(at + 8 * q, 8), 512:] for q in range(4)], 1
        )


def middle(
    meta_ref, weight_ref, own_ref, chip_ref, core_ref, dense_ref, scaled_ref, g_ref, tail_ref,
    both_ref, spread_ref,
    keep_ref, send_ref, corner_ref, local_ref, grad_ref, pair_ref, rolled_ref,
    map_ref, part_ref, above_ref, below_ref, sum_ref, kernel_ref,
):
    forward(
        meta_ref, weight_ref, own_ref, chip_ref, core_ref, dense_ref, scaled_ref,
        part_ref, pair_ref, rolled_ref, map_ref,
    )
    adjoint(
        meta_ref, weight_ref, own_ref, g_ref, core_ref, chip_ref, tail_ref, both_ref, pair_ref,
        spread_ref,
        grad_ref, local_ref, sum_ref, above_ref, below_ref,
    )
    deliver(
        meta_ref, core_ref, chip_ref, part_ref, pair_ref,
        keep_ref, send_ref, corner_ref, sum_ref, kernel_ref,
    )


def embed_terms(grad_ref, scaled_ref, local_ref, corner_ref, near_ref, far_ref, side_ref):
    both = dot(grad_ref[...], scaled_ref[...], TN)
    far = both[TILE : 2 * TILE]
    near_ref[...] = local_ref[...] + both[:TILE]
    far_ref[...] = far
    side_ref[:TILE] = far.astype(BF16)
    side_ref[TILE:] = corner_ref[...].astype(BF16)


def finish(
    mine_ref, other_ref, chip_ref, near_ref,
    weight_ref, kernel_ref, embed_ref,
):
    index, even, before, _ = place()
    channels = kernel_ref.shape[1]
    rows = channels // 2
    half = half_of(index)
    for ref, which in ((mine_ref, half), (other_ref, 1 - half)):
        at = pl.multiple_of(rows * which, rows)
        weight_ref[pl.ds(at, rows), :] = ref[:rows]
        for t in range(TAPS - 1):
            first = rows * (1 + t // 4)
            to = channels * (t % 4)
            kernel_ref[t, pl.ds(at, rows), :] = ref[first : first + rows, to : to + channels]
        for q in range(4):
            kernel_ref[TAPS - 1, pl.ds(at + 8 * q, 8), :] = ref[
                3 * rows : 3 * rows + 8, channels * q : channels * (q + 1)
            ]
    carried = other_ref[3 * rows + 8 :] * (1.0 - even)
    carried = carried + chip_ref[...].astype(F32) * (even * before)
    embed_ref[...] = near_ref[...] + carried


VMEM = pl.BlockSpec(memory_space=pltpu.VMEM)
SMEM = pl.BlockSpec(memory_space=pltpu.SMEM)
HBM = pl.BlockSpec(memory_space=pltpu.HBM)


def shape(dims, kind):
    return jax.ShapeDtypeStruct(dims, kind)


def call(kernel, outs, scalars, operands, scratch=(), flops=0, moved=0, first=None, room=32):
    specs = [first or SMEM] * scalars + [VMEM] * (len(operands) - scalars)
    return pl.pallas_call(
        kernel,
        out_shape=outs,
        in_specs=specs,
        out_specs=[SMEM if out.dtype == jnp.int32 else VMEM for out in outs],
        scratch_shapes=list(scratch),
        compiler_params=pltpu.CompilerParams(vmem_limit_bytes=room * 1024 * 1024),
        cost_estimate=pl.CostEstimate(flops=flops, bytes_accessed=moved, transcendentals=0),
    )(*operands)


def swap_with(shard, step):
    return lax.ppermute(shard, "blk", [(i, i ^ step) for i in range(lax.axis_size("blk"))])


def swap_stage(shard, first, second):
    pairs = [(i, i ^ (second if half_of(i) else first)) for i in range(lax.axis_size("blk"))]
    return lax.ppermute(shard, "blk", pairs)


def swap_chips(shard):
    count = lax.axis_size("blk")
    pairs = [(i, (i + (1 if i % 2 else -1)) % count) for i in range(count)]
    return lax.ppermute(shard, "blk", pairs)


def per_device(embed, pair_weight, conv_kernel, dilations, tile_order, cotangent):
    features = embed.shape[1]
    channels = conv_kernel.shape[0]
    count = lax.axis_size("blk")
    weight = pair_weight.T
    taps = jnp.transpose(conv_kernel, (1, 0, 2))
    cot = cotangent.reshape(2, channels, TILE * TILE)
    packed = shape((channels, RIM), BF16)
    body = shape((TILE, channels, LANES), BF16)
    to_chip, to_core = call(
        pack,
        [packed, packed],
        3,
        (tile_order, cot, embed),
        [
            pltpu.SMEM(tile_order.shape, jnp.int32),
            pltpu.VMEM(cot.shape, BF16),
            pltpu.VMEM(embed.shape, BF16),
            pltpu.SemaphoreType.DMA((3,)),
        ],
        flops=10**10,
        moved=10**6,
        first=HBM,
        room=60,
    )
    chip = swap_chips(to_chip)
    core = swap_with(to_core, 1)
    grads, dense, tail, flat, both, scaled, spread, meta = call(
        prepare,
        [
            body,
            shape((TILE // 2, channels, LANES), BF16),
            shape((HALO, channels, LANES), BF16),
            shape((channels, TAPS * channels), BF16),
            shape((TAPS * channels, 2 * channels), BF16),
            shape((TILE * channels, features), BF16),
            shape((TILE, TAPS * channels, LANES), F32),
            shape((2 * GROUPS,), jnp.int32),
        ],
        2,
        (tile_order, dilations, cot, taps, weight, embed),
        flops=2 * 10**8,
        moved=3 * 10**6,
    )
    rows = channels // 2
    sums = 3 * rows + rows * channels // features
    total, send, corner, local, grad_pair, pair, rolled = call(
        middle,
        [
            shape((sums, features), F32),
            shape((channels // 4 + sums, features), F32),
            shape((channels // 4, features), F32),
            shape((TILE, features), F32),
            shape((TILE * channels, LANES), BF16),
            body,
            shape((TILE, 3 * channels, LANES), BF16),
        ],
        1,
        (meta, weight, embed, chip, core, dense, scaled, grads, tail, both, spread),
        [
            pltpu.VMEM((TILE + 2 * HALO, channels, LANES), BF16),
            pltpu.VMEM((channels, TAPS * channels), F32),
            pltpu.VMEM((HALO, 3 * channels, LANES), F32),
            pltpu.VMEM((HALO, 3 * channels, LANES), F32),
            pltpu.VMEM((channels, features), F32),
            pltpu.VMEM((channels, TAPS * channels), F32),
        ],
        flops=2 * 10**9,
        moved=8 * 10**6,
        room=24,
    )
    by_core = swap_with(send, 1)
    near, far, sided = call(
        embed_terms,
        [
            shape((TILE, features), F32),
            shape((TILE, features), F32),
            shape((TILE + channels // 4, features), BF16),
        ],
        0,
        (grad_pair, scaled, local, corner),
        flops=2 * 10**8,
        moved=2 * 10**6,
    )
    by_chip = swap_chips(sided)
    by_core, sided = lax.optimization_barrier((by_core, sided))
    total = total + by_core[channels // 4 :]
    by_core = by_core[: channels // 4]
    steps = [1 | 1 << b for b in range(1, count.bit_length() - 1)]
    turns = list(zip(steps, steps[1:] + steps[:1]))
    for first, second in turns[:-1]:
        total = total + swap_stage(total, first, second)
    rolled, total = lax.optimization_barrier((rolled, total))
    last = swap_stage(total, *turns[-1])
    (out,) = call(
        respond,
        [shape((2, channels, TILE * TILE), BF16)],
        1,
        (meta, flat, rolled, pair, by_core, by_chip[TILE:]),
        [pltpu.VMEM((4 * channels, 4 * LANES), BF16)],
        flops=10**9,
        moved=2 * 10**6,
    )
    out, last = lax.optimization_barrier((out, last))
    total = total + last
    rest = swap_with(jnp.concatenate([total, far]), 1)
    grad_weight, grad_kernel, grad_embed = call(
        finish,
        [
            shape((channels, features), F32),
            shape((TAPS, channels, channels), F32),
            shape((TILE, features), F32),
        ],
        0,
        (total, rest, by_chip[:TILE], near),
        moved=10**6,
    )
    return (
        out.reshape(1, 2, channels, TILE * TILE),
        grad_embed,
        grad_weight.T,
        jnp.transpose(grad_kernel, (1, 0, 2)),
    )


def solution(mesh):
    placed = (
        P(("grp", "blk"), None),
        P(),
        P(),
        P(),
        P(("grp", "blk"), None),
        P(("grp", "blk"), None, None, None),
    )
    return jax.shard_map(
        per_device,
        mesh=mesh,
        in_specs=placed,
        out_specs=(
            P(("grp", "blk"), None, None, None),
            P(("grp", "blk"), None),
            P("grp", None),
            P("grp", None, None),
        ),
        check_vma=False,
    )
```

```python
import jax
import jax.numpy as jnp
from jax import lax
from jax.experimental import pallas as pl
from jax.experimental.pallas import tpu as pltpu
from jax.sharding import PartitionSpec as P

GROUPS = 4
HALO = 8
TILE = 32
LANES = 128
TAPS = 9
F32 = jnp.float32
BF16 = jnp.bfloat16
NN = (((1,), (0,)), ((), ()))
NT = (((1,), (1,)), ((), ()))
TN = (((0,), (0,)), ((), ()))


def dot(a, b, dims=NN):
    return lax.dot_general(a, b, dims, preferred_element_type=F32)


def turn(x, by):
    by = by % LANES
    return x if by == 0 else pltpu.roll(x, by, 1)


def lane_ids(rows):
    return lax.broadcasted_iota(jnp.int32, (rows, LANES), 1)


def within(lane, low, high):
    return jnp.logical_and(lane >= low, lane < high)


def one_hot(target, chunks):
    lane = lane_ids(target.shape[0])
    hits = [jnp.where(target == lane + LANES * c, 1.0, 0.0).astype(BF16) for c in range(chunks)]
    return jnp.concatenate(hits, 1)


def row_ids(rows):
    return lax.broadcasted_iota(jnp.int32, (rows, LANES), 0)


def spread_table(chunks):
    x = row_ids(LANES * chunks)
    return one_hot((((x >> 5) & 3) << 7) + ((x >> 7) << 5) + (x & 31), 4)


def swap_table():
    x = row_ids(HALO * TILE)
    return one_hot(((x & 31) << 3) + (x >> 5), 2)


def edge_table():
    x = row_ids(LANES)
    return one_hot(jnp.where((x & 31) < HALO, ((x & 31) << 5) + (x >> 5), -1), 2)


def corner_table(first):
    x = row_ids(HALO * TILE)
    c = (x & 31) - first
    return one_hot(jnp.where(within(c, 0, HALO), ((x >> 5) << 3) + c, -1), 1)


def as_float(flag):
    return jnp.where(flag, 1.0, 0.0).astype(F32)


def place():
    index = lax.axis_index("blk")
    last = lax.axis_size("blk") - 1
    return index, as_float(index % 2 == 0), as_float(index > 0), as_float(index < last)


def half_of(index):
    for by in (8, 4, 2, 1):
        index = index ^ (index >> by)
    return index & 1


def corner_shift(flat, spacing):
    width = flat.shape[0] // GROUPS
    lane = lane_ids(width)
    pieces = []
    for g in range(GROUPS):
        d = spacing[g]
        kept = jnp.logical_and(jnp.logical_and(lane < 8 * HALO, (lane >> 3) < d), (lane & 7) < d)
        x = jnp.where(kept, flat[width * g : width * (g + 1)], 0.0)
        pieces.append(pltpu.roll(x, (HALO + 1) * (HALO - d), 1))
    return jnp.concatenate(pieces, 0).astype(BF16)


def tiles_of(order_ref, cot_ref):
    slot = order_ref[0, 0]
    _, _, _, keep = place()
    return cot_ref[slot], (cot_ref[1 - slot].astype(F32) * keep).astype(BF16)


def fetch(sources, targets, sems):
    copies = [
        pltpu.make_async_copy(source, target, sems.at[i])
        for i, (source, target) in enumerate(zip(sources, targets))
    ]
    for copy in copies:
        copy.start()
    return copies


def pack(
    order_hbm, cot_hbm, embed_hbm,
    chip_ref, core_ref,
    order_ref, cot_ref, embed_ref, sems,
):
    copies = fetch((order_hbm, cot_hbm, embed_hbm), (order_ref, cot_ref, embed_ref), sems)
    edge, head, tail = edge_table(), corner_table(0), corner_table(TILE - HALO)
    for copy in copies:
        copy.wait()
    zero, one = tiles_of(order_ref, cot_ref)
    _, even, _, _ = place()
    channels = zero.shape[0]
    moved = dot(
        jnp.concatenate([zero[:, LANES * j : LANES * (j + 1)] for j in range(8)], 0), edge
    )
    columns = []
    for h in range(2):
        total = None
        for j in range(8):
            piece = moved[channels * j : channels * (j + 1), LANES * h : LANES * (h + 1)]
            piece = turn(piece, 4 * j)
            total = piece if total is None else total + piece
        columns.append(total)
    rim = HALO * TILE
    tail_at = TILE * (TILE - HALO)
    up = [zero[:, :rim].astype(F32)] + columns + [dot(one[:, :rim], head)]
    down = [one[:, tail_at:].astype(F32)] + [jnp.zeros_like(x) for x in columns]
    down += [dot(zero[:, tail_at:], tail)]
    up, down = jnp.concatenate(up, 1), jnp.concatenate(down, 1)
    width = up.shape[1]
    both = jnp.concatenate([embed_ref[:, :LANES], embed_ref[:, LANES:]], 0)
    core_ref[:, :width] = (down * even + up * (1.0 - even)).astype(BF16)
    core_ref[:, width:] = both
    chip_ref[:, :width] = (up * even + down * (1.0 - even)).astype(BF16)
    chip_ref[:, width:] = both


RIM_SIDE, RIM_CORNER, RIM_EMBED, RIM = 256, 512, 640, 768


def from_above(core_ref, chip_ref, at):
    _, even, before, _ = place()
    x = chip_ref[:, at].astype(F32) * (even * before)
    return x + core_ref[:, at].astype(F32) * ((1.0 - even) * before)


def from_below(core_ref, chip_ref, at):
    _, even, _, after = place()
    x = core_ref[:, at].astype(F32) * (even * after)
    return x + chip_ref[:, at].astype(F32) * ((1.0 - even) * after)


def prepare(
    order_hbm, dil_hbm, cot_ref, kern_ref, weight_ref, embed_ref,
    g_ref, dense_ref, tail_ref, flat_ref, both_ref, scaled_ref, spread_ref, meta_ref,
    order_ref, dil_ref, sems,
):
    copies = fetch((order_hbm, dil_hbm), (order_ref, dil_ref), sems)
    channels = kern_ref.shape[1]
    eye = (
        lax.broadcasted_iota(jnp.int32, (channels, channels), 0)
        == lax.broadcasted_iota(jnp.int32, (channels, channels), 1)
    )
    eye = jnp.where(eye, 1.0, 0.0).astype(BF16)
    for u in range(3):
        for v in range(3):
            t = 3 * u + v
            pair = jnp.concatenate([kern_ref[t], kern_ref[3 * v + u]], 0)
            both_ref[channels * t : channels * (t + 1), :] = dot(eye, pair, NT).astype(BF16)
    for t in range(0, TAPS - 1, 2):
        flat_ref[:, channels * t : channels * (t + 2)] = jnp.concatenate(
            [kern_ref[t].astype(F32), kern_ref[t + 1].astype(F32)], 1
        ).astype(BF16)
    flat_ref[:, channels * (TAPS - 1) : channels * TAPS] = kern_ref[TAPS - 1]
    weight = weight_ref[...].astype(F32)
    own = embed_ref[...].astype(F32)
    for r in range(TILE):
        scaled_ref[channels * r : channels * (r + 1), :] = (own[r : r + 1, :] * weight).astype(
            BF16
        )
    for copy in copies:
        copy.wait()
    for g in range(GROUPS):
        meta_ref[g] = jnp.left_shift(jnp.int32(1), dil_ref[g])
    meta_ref[GROUPS] = order_ref[0, 0]
    zero, one = tiles_of(order_ref, cot_ref)
    swap = swap_table()
    tail_at = TILE * (TILE - HALO)
    y_zero = dot(zero[:, tail_at:], swap)
    y_one = dot(one[:, tail_at:], swap)
    lane = lane_ids(channels)
    own_side = within(lane, 72, 80)
    low = lane < 2 * TILE
    pieces = []
    for j in range(4):
        at = slice(LANES * j, LANES * (j + 1))
        later = slice(LANES * (j + 4), LANES * (j + 5))
        pieces.append(
            jnp.concatenate([zero[:, at], one[:, at], zero[:, later], one[:, later]], 1)
        )
    rows = dot(jnp.concatenate(pieces, 0), spread_table(4))
    for j in range(4):
        for m in range(4):
            row = rows[channels * j : channels * (j + 1), LANES * m : LANES * (m + 1)]
            dense_ref[4 * j + m] = row.astype(BF16)
            for h in range(2):
                r = 16 * h + 4 * j + m
                side = turn(y_zero[:, LANES * h : LANES * (h + 1)], 72 - 8 * (r % 16))
                side = jnp.where(own_side, side, 0.0)
                g_ref[r] = jnp.where(low, turn(row, 64 * h), side).astype(BF16)
    for i in range(HALO):
        rest = turn(y_one[:, :LANES], 72 - 8 * i)
        tail_ref[i] = jnp.where(own_side, rest, 0.0).astype(BF16)
    inner = jnp.where(lane < 2 * TILE, 1.0, 0.0).astype(BF16)
    beside = jnp.where(own_side, 1.0, 0.0).astype(BF16)

    def spread_rows(i, carry):
        x = jnp.concatenate([g_ref[2 * i], g_ref[2 * i + 1]], 1)
        y = jnp.concatenate([inner, inner], 1), jnp.concatenate([beside, beside], 1)
        y = dot(both_ref[...], jnp.concatenate([x * y[0], x * y[1]], 0))
        spread_ref[2 * i] = y[:, :LANES]
        spread_ref[2 * i + 1] = y[:, LANES:]
        return carry

    lax.fori_loop(0, TILE // 2, spread_rows, 0, unroll=4)


def unpacked(x):
    return jnp.concatenate([x[:TILE], x[TILE:]], 1)


def forward(
    meta_ref, weight_ref, own_ref, chip_ref, core_ref, dense_ref, scaled_ref,
    part_ref, pair_ref, rolled_ref, map_ref, ready,
):
    channels = weight_ref.shape[0]
    width = channels // GROUPS
    weight = weight_ref[...].astype(F32)
    own = own_ref[...].astype(F32)
    after = unpacked(from_below(core_ref, chip_ref, slice(RIM_EMBED, RIM)))
    before = unpacked(from_above(core_ref, chip_ref, slice(RIM_EMBED, RIM)))[TILE - HALO :]
    filler = jnp.zeros((LANES - 2 * TILE - HALO, own.shape[1]), F32)
    columns = jnp.concatenate([own, after, filler, before], 0).astype(BF16)
    lane = lane_ids(channels)
    kept = (
        jnp.logical_or(lane < TILE, lane >= LANES - HALO),
        lane < 2 * TILE,
        within(lane, TILE, 2 * TILE),
    )
    for c in range(6):
        part = 0 if c == 0 else (2 if c == 5 else 1)
        if part == 1:
            scaled = scaled_ref[8 * channels * (c - 1) : 8 * channels * c, :]
        else:
            rim = before if part == 0 else after
            scaled = jnp.concatenate(
                [(rim[i : i + 1, :] * weight).astype(BF16) for i in range(HALO)], 0
            )
        pair = dot(scaled, columns, NT).astype(BF16)
        for i in range(8):
            one = pair[channels * i : channels * (i + 1)]
            if part == 1:
                pair_ref[8 * (c - 1) + i] = one
            x = jnp.where(kept[part], jnp.maximum(one.astype(F32), 0.0), 0.0)
            map_ref[8 * c + i] = x.astype(BF16)
    swap = swap_table()

    def gathered(first, per, low, high, move):
        halves = []
        for half in range(2):
            total = None
            for m in range(per):
                piece = map_ref[first + per * half + m].astype(F32)
                piece = jnp.where(within(lane, low, high), piece, 0.0)
                piece = turn(piece, move(m))
                total = piece if total is None else total + piece
            halves.append(total.astype(BF16))
        return jnp.concatenate(halves, 1)

    above = dot(gathered(0, 4, 0, TILE, lambda m: TILE * m), swap)
    below = dot(gathered(8, 16, TILE, TILE + HALO, lambda m: HALO * m - TILE), swap, NT)
    for r in range(TILE):
        half = LANES * (r // 16)
        side = turn(above[:, half : half + LANES], LANES - HALO - HALO * (r % 16))
        map_ref[HALO + r] += jnp.where(lane >= LANES - HALO, side, 0.0).astype(BF16)
    for i in range(HALO):
        half = LANES * (i // 4)
        side = turn(below[:, half : half + LANES], -TILE * (i % 4))
        map_ref[HALO + TILE + i] += jnp.where(lane < TILE, side, 0.0).astype(BF16)

    ready()
    spacing = [meta_ref[g] for g in range(GROUPS)]
    source = row_ids(LANES)
    to = lane_ids(LANES)
    for g in range(GROUPS):
        tables = []
        for h in range(2):
            half = within(to, 2 * TILE * h, 2 * TILE * (h + 1))
            offset = jnp.where(half, (source - (to - 2 * TILE * h)) & (LANES - 1), LANES)
            hits = [
                jnp.where(offset == (v * spacing[g]) & (LANES - 1), 1.0, 0.0).astype(BF16)
                for v in (-1, 0, 1)
            ]
            tables.append(jnp.concatenate(hits, 1))
        table = jnp.concatenate(tables, 0)
        at = width * g
        for part in range(2):
            low = [map_ref[16 * part + i, at : at + width, :] for i in range(16)]
            high = [map_ref[16 * part + i + 16, at : at + width, :] for i in range(16)]
            x = jnp.concatenate([jnp.concatenate(low, 0), jnp.concatenate(high, 0)], 1)
            y = dot(x, table).astype(BF16)
            for i in range(16):
                for v in range(3):
                    to_row = channels * v + at
                    rolled_ref[16 * part + i, to_row : to_row + width, :] = y[
                        width * i : width * (i + 1), LANES * v : LANES * (v + 1)
                    ]
    total = None
    for j in range(4):
        rows = range(4 * j, 4 * (j + 1))
        stack = jnp.concatenate([taps_of(rolled_ref, spacing, r) for r in rows], 1)
        share = dot(jnp.concatenate([dense_ref[r] for r in rows], 1), stack, NT)
        total = share if total is None else total + share
    part_ref[...] = total


def taps_of(rolled_ref, spacing, r):
    channels = rolled_ref.shape[1] // 3
    width = channels // GROUPS
    pieces = []
    for u in range(3):
        for v in range(3):
            for g in range(GROUPS):
                at = channels * v + width * g
                pieces.append(rolled_ref[r + HALO + (u - 1) * spacing[g], at : at + width, :])
    return jnp.concatenate(pieces, 0)


def respond(
    meta_ref, flat_ref, rolled_ref, pair_ref, core_ref, chip_ref,
    out_ref,
    rows_ref,
):
    channels = flat_ref.shape[0]
    spacing = [meta_ref[g] for g in range(GROUPS)]
    lane = lane_ids(channels)
    low = lane < 2 * TILE
    _, even, _, keep = place()
    corner = core_ref[...] * even + chip_ref[...].astype(F32) * ((1.0 - even) * keep)
    low_side, high_side = corner[:, :LANES], corner[:, LANES:]
    corner = jnp.concatenate(
        [low_side, turn(low_side, 64), high_side, turn(high_side, 64)], 0
    )
    share = dot(flat_ref[:, channels * (TAPS - 1) :], corner_shift(corner, spacing))
    for j in range(4):
        rows = range(4 * j, 4 * (j + 1))
        stack = jnp.concatenate([taps_of(rolled_ref, spacing, r) for r in rows], 1)
        response = dot(flat_ref[...], stack)
        for m, r in enumerate(rows):
            row = response[:, LANES * m : LANES * (m + 1)]
            if r >= HALO:
                at = LANES - HALO
                row = row + jnp.where(lane >= at, turn(share, at - HALO * (r - HALO)), 0.0)
            near = pair_ref[r].astype(F32)
            far = turn(pair_ref[r + 16].astype(F32), 2 * TILE)
            row = jnp.where(low, near, far) + row
            rows_ref[channels * j : channels * (j + 1), LANES * m : LANES * (m + 1)] = row.astype(
                BF16
            )
    slot = meta_ref[GROUPS]
    chunks = dot(rows_ref[...], spread_table(4), NT)
    for j in range(4):
        chunk = chunks[channels * j : channels * (j + 1)]
        for h in range(2):
            at = slice(LANES * (j + 4 * h), LANES * (j + 4 * h + 1))
            to = 2 * LANES * h
            out_ref[slot, :, at] = chunk[:, to : to + LANES].astype(BF16)
            out_ref[1 - slot, :, at] = (chunk[:, to + LANES : to + 2 * LANES] * keep).astype(BF16)


def adjoint(
    meta_ref, weight_ref, own_ref, g_ref, core_ref, chip_ref, tail_ref, both_ref, pair_ref,
    spread_ref,
    grad_ref, local_ref, sum_ref, above_ref, below_ref,
):
    channels = g_ref.shape[1]
    width = channels // GROUPS
    span = 3 * channels
    lane = lane_ids(channels)
    zeros = jnp.zeros((channels, LANES), BF16)
    above = from_above(core_ref, chip_ref, slice(0, RIM_EMBED))
    below = from_below(core_ref, chip_ref, slice(0, RIM_EMBED))

    def moved(rim, at, to, size, per, i):
        at += LANES * (i // per)
        x = turn(rim[:, at : at + LANES], to - size * (i % per))
        return jnp.where(within(lane, to, to + size), x, 0.0)

    for h in range(HALO // 2):
        upper, lower = [], []
        for i in (2 * h, 2 * h + 1):
            x = moved(above, 0, 0, TILE, 4, i)
            x = x + moved(above, RIM_CORNER, LANES - HALO, HALO, 16, i)
            upper.append(jnp.concatenate([x.astype(BF16), zeros], 0))
            x = moved(below, 0, TILE, TILE, 4, i)
            x = x + moved(below, RIM_CORNER, 2 * TILE, HALO, 16, i)
            y = moved(below, RIM_SIDE, 80, TILE, 4, i).astype(BF16) + tail_ref[i]
            lower.append(jnp.concatenate([x.astype(BF16), y], 0))
        x = dot(both_ref[2 * span :, :], jnp.concatenate(upper, 1))
        y = dot(both_ref[:span, :], jnp.concatenate(lower, 1))
        for m in range(2):
            above_ref[2 * h + m] = x[:, LANES * m : LANES * (m + 1)]
            below_ref[2 * h + m] = y[:, LANES * m : LANES * (m + 1)]
    spacing = [meta_ref[g] for g in range(GROUPS)]
    second = within(lane, TILE, 2 * TILE)

    def gathered(r):
        pieces = []
        for g in range(GROUPS):
            totals = []
            up, down = r - spacing[g], r + spacing[g]
            for v in range(3):
                at = channels * v + width * g
                tap = slice(at, at + width)
                total = spread_ref[r, span + at : span + at + width, :]
                last = slice(2 * span + at, 2 * span + at + width)
                if r < HALO:
                    x = spread_ref[jnp.maximum(up, 0), last, :]
                    y = above_ref[jnp.minimum(up + HALO, HALO - 1), tap, :]
                    total = total + jnp.where(up < 0, y, x)
                else:
                    total = total + spread_ref[up, last, :]
                if r >= TILE - HALO:
                    x = spread_ref[jnp.minimum(down, TILE - 1), tap, :]
                    y = below_ref[jnp.maximum(down - TILE, 0), tap, :]
                    total = total + jnp.where(down >= TILE, y, x)
                else:
                    total = total + spread_ref[down, tap, :]
                totals.append(total)
            pieces.append(
                totals[1]
                + pltpu.roll(totals[0], LANES - spacing[g], 1)
                + pltpu.roll(totals[2], spacing[g], 1)
            )
        grad = jnp.concatenate(pieces, 0)
        grad = grad + jnp.where(second, turn(grad, -48), 0.0)
        own = g_ref[r].astype(F32)
        own = own + jnp.where(pair_ref[r].astype(F32) > 0, grad, 0.0)
        return own.astype(BF16)

    weight = weight_ref[...].astype(F32)
    own = own_ref[...].astype(F32)
    after = unpacked(from_below(core_ref, chip_ref, slice(RIM_EMBED, RIM)))
    columns = jnp.concatenate(
        [own, after, jnp.zeros((LANES - 2 * TILE, own.shape[1]), F32)], 0
    ).astype(BF16)
    weight_part = jnp.zeros_like(weight)
    local = []
    for c in range(TILE // 8):
        rows = jnp.concatenate([gathered(8 * c + i) for i in range(8)], 0)
        grad_ref[8 * channels * c : 8 * channels * (c + 1), :] = rows
        grad_scaled = dot(rows, columns)
        for i in range(8):
            one = grad_scaled[channels * i : channels * (i + 1)]
            local.append(jnp.sum(one * weight, 0, keepdims=True))
            weight_part = weight_part + one * own[8 * c + i : 8 * c + i + 1, :]
    local_ref[...] = jnp.concatenate(local, 0)
    sum_ref[...] = weight_part


def deliver(
    meta_ref, core_ref, chip_ref, part_ref, pair_ref,
    keep_ref, send_ref, corner_ref, sum_ref, kernel_ref,
):
    channels = part_ref.shape[0]
    lane = lane_ids(channels)
    rim = from_above(core_ref, chip_ref, slice(0, RIM_SIDE))
    corner, ends = None, None
    for i in range(HALO):
        x = jnp.where(within(lane, TILE, TILE + HALO), pair_ref[i].astype(F32), 0.0)
        x = turn(jnp.maximum(x, 0.0), HALO * i - TILE)
        half = LANES * (i // 4)
        y = turn(rim[:, half : half + LANES], HALO * i - TILE * (i % 4) - (TILE - HALO))
        y = jnp.where(within(lane, HALO * i, HALO * (i + 1)), y, 0.0)
        corner, ends = (x, y) if i == 0 else (corner + x, ends + y)
    spacing = [meta_ref[g] for g in range(GROUPS)]
    share = dot(ends.astype(BF16), corner_shift(corner, spacing), NT)
    last = channels * (TAPS - 1)
    kernel_ref[:, :last] = part_ref[:, :last]
    kernel_ref[:, last:] = part_ref[:, last:] + share
    quarter = channels // 4
    corner = [corner[quarter * q : quarter * (q + 1)] for q in range(4)]
    corner = jnp.concatenate(
        [corner[0] + turn(corner[1], 64), corner[2] + turn(corner[3], 64)], 1
    )
    corner_ref[...] = corner
    rows = channels // 2
    half = half_of(lax.axis_index("blk"))
    send_ref[:quarter] = corner
    for ref, which, first in ((keep_ref, half, 0), (send_ref, 1 - half, quarter)):
        at = pl.multiple_of(rows * which, rows)
        ref[first : first + rows] = sum_ref[pl.ds(at, rows), :]
        for q in range(2):
            to = first + rows * (q + 1)
            ref[to : to + rows] = kernel_ref[pl.ds(at, rows), 256 * q : 256 * (q + 1)]
        ref[first + 3 * rows :] = jnp.concatenate(
            [kernel_ref[pl.ds(at + 8 * q, 8), 512:] for q in range(4)], 1
        )


def middle(
    meta_hbm, weight_ref, own_ref, chip_ref, core_ref, dense_ref, scaled_ref, g_ref, tail_ref,
    both_ref, spread_ref,
    keep_ref, send_ref, corner_ref, local_ref, grad_ref, pair_ref, rolled_ref,
    map_ref, part_ref, above_ref, below_ref, sum_ref, kernel_ref, meta_ref, sem,
):
    scalars = pltpu.make_async_copy(meta_hbm, meta_ref, sem)
    scalars.start()
    forward(
        meta_ref, weight_ref, own_ref, chip_ref, core_ref, dense_ref, scaled_ref,
        part_ref, pair_ref, rolled_ref, map_ref, scalars.wait,
    )
    adjoint(
        meta_ref, weight_ref, own_ref, g_ref, core_ref, chip_ref, tail_ref, both_ref, pair_ref,
        spread_ref,
        grad_ref, local_ref, sum_ref, above_ref, below_ref,
    )
    deliver(
        meta_ref, core_ref, chip_ref, part_ref, pair_ref,
        keep_ref, send_ref, corner_ref, sum_ref, kernel_ref,
    )


def embed_terms(grad_ref, scaled_ref, local_ref, corner_ref, near_ref, far_ref, side_ref):
    both = dot(grad_ref[...], scaled_ref[...], TN)
    far = both[TILE : 2 * TILE]
    near_ref[...] = local_ref[...] + both[:TILE]
    far_ref[...] = far
    side_ref[:TILE] = far.astype(BF16)
    side_ref[TILE:] = corner_ref[...].astype(BF16)


def finish(
    mine_ref, other_ref, chip_ref, near_ref,
    weight_ref, kernel_ref, embed_ref,
):
    index, even, before, _ = place()
    channels = kernel_ref.shape[1]
    rows = channels // 2
    half = half_of(index)
    for ref, which in ((mine_ref, half), (other_ref, 1 - half)):
        at = pl.multiple_of(rows * which, rows)
        weight_ref[pl.ds(at, rows), :] = ref[:rows]
        for t in range(TAPS - 1):
            first = rows * (1 + t // 4)
            to = channels * (t % 4)
            kernel_ref[t, pl.ds(at, rows), :] = ref[first : first + rows, to : to + channels]
        for q in range(4):
            kernel_ref[TAPS - 1, pl.ds(at + 8 * q, 8), :] = ref[
                3 * rows : 3 * rows + 8, channels * q : channels * (q + 1)
            ]
    carried = other_ref[3 * rows + 8 :] * (1.0 - even)
    carried = carried + chip_ref[...].astype(F32) * (even * before)
    embed_ref[...] = near_ref[...] + carried


VMEM = pl.BlockSpec(memory_space=pltpu.VMEM)
SMEM = pl.BlockSpec(memory_space=pltpu.SMEM)
HBM = pl.BlockSpec(memory_space=pltpu.HBM)


def shape(dims, kind):
    return jax.ShapeDtypeStruct(dims, kind)


def call(kernel, outs, scalars, operands, scratch=(), flops=0, moved=0, first=None, room=32):
    specs = [first or SMEM] * scalars + [VMEM] * (len(operands) - scalars)
    return pl.pallas_call(
        kernel,
        out_shape=outs,
        in_specs=specs,
        out_specs=[SMEM if out.dtype == jnp.int32 else VMEM for out in outs],
        scratch_shapes=list(scratch),
        compiler_params=pltpu.CompilerParams(vmem_limit_bytes=room * 1024 * 1024),
        cost_estimate=pl.CostEstimate(flops=flops, bytes_accessed=moved, transcendentals=0),
    )(*operands)


def swap_with(shard, step):
    return lax.ppermute(shard, "blk", [(i, i ^ step) for i in range(lax.axis_size("blk"))])


def swap_stage(shard, first, second):
    pairs = [(i, i ^ (second if half_of(i) else first)) for i in range(lax.axis_size("blk"))]
    return lax.ppermute(shard, "blk", pairs)


def swap_chips(shard):
    count = lax.axis_size("blk")
    pairs = [(i, (i + (1 if i % 2 else -1)) % count) for i in range(count)]
    return lax.ppermute(shard, "blk", pairs)


def per_device(embed, pair_weight, conv_kernel, dilations, tile_order, cotangent):
    features = embed.shape[1]
    channels = conv_kernel.shape[0]
    count = lax.axis_size("blk")
    weight = pair_weight.T
    taps = jnp.transpose(conv_kernel, (1, 0, 2))
    cot = cotangent.reshape(2, channels, TILE * TILE)
    packed = shape((channels, RIM), BF16)
    body = shape((TILE, channels, LANES), BF16)
    to_chip, to_core = call(
        pack,
        [packed, packed],
        3,
        (tile_order, cot, embed),
        [
            pltpu.SMEM(tile_order.shape, jnp.int32),
            pltpu.VMEM(cot.shape, BF16),
            pltpu.VMEM(embed.shape, BF16),
            pltpu.SemaphoreType.DMA((3,)),
        ],
        flops=10**10,
        moved=10**6,
        first=HBM,
        room=60,
    )
    chip = swap_chips(to_chip)
    core = swap_with(to_core, 1)
    grads, dense, tail, flat, both, scaled, spread, meta = call(
        prepare,
        [
            body,
            shape((TILE // 2, channels, LANES), BF16),
            shape((HALO, channels, LANES), BF16),
            shape((channels, TAPS * channels), BF16),
            shape((TAPS * channels, 2 * channels), BF16),
            shape((TILE * channels, features), BF16),
            shape((TILE, TAPS * channels, LANES), F32),
            shape((2 * GROUPS,), jnp.int32),
        ],
        2,
        (tile_order, dilations, cot, taps, weight, embed),
        [
            pltpu.SMEM(tile_order.shape, jnp.int32),
            pltpu.SMEM(dilations.shape, jnp.int32),
            pltpu.SemaphoreType.DMA((2,)),
        ],
        flops=2 * 10**8,
        moved=3 * 10**6,
        first=HBM,
    )
    rows = channels // 2
    sums = 3 * rows + rows * channels // features
    total, send, corner, local, grad_pair, pair, rolled = call(
        middle,
        [
            shape((sums, features), F32),
            shape((channels // 4 + sums, features), F32),
            shape((channels // 4, features), F32),
            shape((TILE, features), F32),
            shape((TILE * channels, LANES), BF16),
            body,
            shape((TILE, 3 * channels, LANES), BF16),
        ],
        1,
        (meta, weight, embed, chip, core, dense, scaled, grads, tail, both, spread),
        [
            pltpu.VMEM((TILE + 2 * HALO, channels, LANES), BF16),
            pltpu.VMEM((channels, TAPS * channels), F32),
            pltpu.VMEM((HALO, 3 * channels, LANES), F32),
            pltpu.VMEM((HALO, 3 * channels, LANES), F32),
            pltpu.VMEM((channels, features), F32),
            pltpu.VMEM((channels, TAPS * channels), F32),
            pltpu.SMEM(meta.shape, jnp.int32),
            pltpu.SemaphoreType.DMA,
        ],
        flops=2 * 10**9,
        moved=8 * 10**6,
        first=HBM,
        room=24,
    )
    by_core = swap_with(send, 1)
    near, far, sided = call(
        embed_terms,
        [
            shape((TILE, features), F32),
            shape((TILE, features), F32),
            shape((TILE + channels // 4, features), BF16),
        ],
        0,
        (grad_pair, scaled, local, corner),
        flops=2 * 10**8,
        moved=2 * 10**6,
    )
    by_chip = swap_chips(sided)
    by_core, sided = lax.optimization_barrier((by_core, sided))
    total = total + by_core[channels // 4 :]
    by_core = by_core[: channels // 4]
    steps = [1 | 1 << b for b in range(1, count.bit_length() - 1)]
    turns = list(zip(steps, steps[1:] + steps[:1]))
    for first, second in turns[:-1]:
        total = total + swap_stage(total, first, second)
    rolled, total = lax.optimization_barrier((rolled, total))
    last = swap_stage(total, *turns[-1])
    (out,) = call(
        respond,
        [shape((2, channels, TILE * TILE), BF16)],
        1,
        (meta, flat, rolled, pair, by_core, by_chip[TILE:]),
        [pltpu.VMEM((4 * channels, 4 * LANES), BF16)],
        flops=10**9,
        moved=2 * 10**6,
    )
    out, last = lax.optimization_barrier((out, last))
    total = total + last
    rest = swap_with(jnp.concatenate([total, far]), 1)
    grad_weight, grad_kernel, grad_embed = call(
        finish,
        [
            shape((channels, features), F32),
            shape((TAPS, channels, channels), F32),
            shape((TILE, features), F32),
        ],
        0,
        (total, rest, by_chip[:TILE], near),
        moved=10**6,
    )
    return (
        out.reshape(1, 2, channels, TILE * TILE),
        grad_embed,
        grad_weight.T,
        jnp.transpose(grad_kernel, (1, 0, 2)),
    )


def solution(mesh):
    placed = (
        P(("grp", "blk"), None),
        P(),
        P(),
        P(),
        P(("grp", "blk"), None),
        P(("grp", "blk"), None, None, None),
    )
    return jax.shard_map(
        per_device,
        mesh=mesh,
        in_specs=placed,
        out_specs=(
            P(("grp", "blk"), None, None, None),
            P(("grp", "blk"), None),
            P("grp", None),
            P("grp", None, None),
        ),
        check_vma=False,
    )
```
